32 devices in a mesh: replica: 8 (over z, x), fsdp: 4 (over y, core).
Axes of the slice: x: 2, y: 2, z: 4, core: 2. Of those that a mesh axis runs over, the one named last changes fastest.
Arguments:
- inputs: bfloat16 [16384, 4096], P(('replica', 'fsdp')), may hold values from -6 to 6
- kinds: int32 [16384], P(('replica', 'fsdp')), may hold values from 0 to 2
- weights: float32 [8, 2, 4096, 256], P('replica', None, 'fsdp'), may hold values from -0.09375 to 0.09375
- first_moment: float32 [8, 2, 4096, 256], P('replica', None, 'fsdp'), may hold values from -0.75 to 0.75
- second_moment: float32 [8, 2, 4096, 256], P('replica', None, 'fsdp'), may hold values from 0.01 to 1
- anchor: float32 [2, 4096, 256], P(None, 'fsdp'), may hold values from -0.09375 to 0.09375
- momentum: float32 [2, 4096, 256], P(None, 'fsdp'), may hold values from -0.75 to 0.75
- plan: int32 [8], replicated, may hold values from 1 to 8
Outputs:
- new_weights: float32 [8, 2, 4096, 256], P('replica', None, 'fsdp')
- new_first: float32 [8, 2, 4096, 256], P('replica', None, 'fsdp')
- new_second: float32 [8, 2, 4096, 256], P('replica', None, 'fsdp')
- new_anchor: float32 [2, 4096, 256], P(None, 'fsdp')
- new_momentum: float32 [2, 4096, 256], P(None, 'fsdp')
The draws below stay inside these ranges and needn't reach their ends.
All inputs are finite; a program needn't handle non-finite values.
Results may differ from the reference program's by a relative error of at most 0.014.
Values may be sent and summed in bfloat16 or wider, within the bound.
No kernel may reach another device: no remote copies, remote signals or barrier semaphores. Data moves between devices by JAX's collectives and lax.ppermute only.
A program may use at most 128 MiB of HBM per device.

```python
import math
import jax
import jax.numpy as jnp
from jax import lax

D = 4096
R = 256
INNER = 2
TOK_DEV = 512
TOKENS = 2048
ROWS = 16384
N_REPLICA = 8
N_FSDP = 4


def with_ends(drawn, own_key, low, top_value):
    longest = drawn.shape.index(max(drawn.shape))
    spots = []
    for shift in (0, 1):
        where = [jax.random.randint(jax.random.fold_in(own_key, axis), (), 0, length) for axis, length in enumerate(drawn.shape)]
        where[longest] = (where[longest] + shift) % drawn.shape[longest]
        spots.append(tuple(where))
    return drawn.at[spots[0]].set(low).at[spots[1]].set(top_value)


def block_levels(rng, extent, pieces, smallest, largest):
    loudness = 1.0
    for axis_at, parts in pieces:
        heights = jax.random.uniform(jax.random.fold_in(jax.random.fold_in(rng, 6), axis_at), (parts,), jnp.float32, smallest / len(pieces), largest / len(pieces))
        loudness = loudness * jnp.repeat(jnp.exp(heights), extent[axis_at] // parts).reshape((-1,) + (1,) * (len(extent) - 1 - axis_at))
    return loudness


def centred(key, dims, spread, bound, pieces=(), dtype=jnp.bfloat16):
    entries = spread * jax.random.normal(key, dims, jnp.float32)
    if pieces:
        entries = entries * block_levels(key, dims, pieces, -0.22, 0.18)
    return jnp.clip(entries, -bound, bound).astype(dtype)


def setup_inputs(seed: int = 0) -> dict:
    keys = jax.random.split(jax.random.key(seed), 9)
    return {
        "inputs": centred(keys[0], (ROWS, D), 1.0, 6.0, ((0, 32),)),
        "kinds": with_ends(jax.random.randint(keys[1], (ROWS,), 0, 3), jax.random.fold_in(keys[1], 1), 0, 2).astype(jnp.int32),
        "weights": centred(keys[2], (N_REPLICA, 2, D, R), D ** -0.5, 0.09375, ((0, 8), (2, 4)), jnp.float32),
        "first_moment": centred(keys[3], (N_REPLICA, 2, D, R), 0.05, 0.75, ((0, 8), (2, 4)), jnp.float32),
        "second_moment": jnp.clip(jnp.exp(math.log(1.0) - 4.6051702 * jax.random.uniform(keys[4], (N_REPLICA, 2, D, R), jnp.float32) ** block_levels(keys[4], (N_REPLICA, 2, D, R), ((0, 8), (2, 4)), -0.2, 0.2)), 0.01, 1.0),
        "anchor": centred(keys[5], (2, D, R), D ** -0.5, 0.09375, ((1, 4),), jnp.float32),
        "momentum": centred(keys[6], (2, D, R), 0.05, 0.75, ((1, 4),), jnp.float32),
        "plan": with_ends(jax.random.randint(keys[7], (N_REPLICA,), 1, 9), jax.random.fold_in(keys[7], 1), 1, 8).astype(jnp.int32),
    }


inner_rate = 0.003
beta_one = 0.9
beta_two = 0.95
adam_eps = 1e-08
decay_rate = 0.1
outer_rate = 0.7
outer_mu = 0.9
mix_share = 0.5

def token_weight(kinds):
    return jnp.where(kinds == 2, 1.0, jnp.where(kinds == 1, 0.25, 0.0)).astype(jnp.float32)

def silu_slope(pre):
    sig = jax.nn.sigmoid(pre)
    return sig * (1.0 + pre * (1.0 - sig))

def adam_update(theta, first, second, grad):
    first = beta_one * first + (1.0 - beta_one) * grad
    second = beta_two * second + (1.0 - beta_two) * grad * grad
    theta = theta - inner_rate * (first / (jnp.sqrt(second) + adam_eps) + decay_rate * theta)
    return (theta, first, second)

def ref_step(blocks, weight_rows, theta, first, second, scale):
    low = theta.astype(jnp.bfloat16)
    flat = blocks.reshape(-1, blocks.shape[2])
    pre = jnp.dot(flat, low[0], preferred_element_type=jnp.float32)
    hidden = jax.nn.silu(pre).astype(jnp.bfloat16)
    output = jnp.dot(hidden, low[1].T, preferred_element_type=jnp.float32)
    resid = output - flat.astype(jnp.float32)
    slope_out = (weight_rows.reshape(-1)[:, None] * resid * scale).astype(jnp.bfloat16)
    back = jnp.dot(slope_out, low[1], preferred_element_type=jnp.float32)
    slope_pre = (back * silu_slope(pre)).astype(jnp.bfloat16)
    count = blocks.shape[0]
    width = hidden.shape[1]
    xs = blocks.astype(jnp.float32)
    ds = slope_out.reshape(count, -1, flat.shape[1]).astype(jnp.float32)
    pres = slope_pre.reshape(count, -1, width).astype(jnp.float32)
    hids = hidden.reshape(count, -1, width).astype(jnp.float32)
    part_a = jnp.einsum('btd,btr->bdr', xs, pres).astype(jnp.bfloat16)
    part_b = jnp.einsum('btd,btr->bdr', ds, hids).astype(jnp.bfloat16)
    grad = jnp.stack([lax.optimization_barrier(jnp.sum(part_a.astype(jnp.float32), 0)), lax.optimization_barrier(jnp.sum(part_b.astype(jnp.float32), 0))], 0)
    return adam_update(theta, first, second, grad)

def reference(inputs, kinds, weights, first_moment, second_moment, anchor, momentum, plan):
    total_int = jnp.sum(plan).astype(jnp.int32)
    frag = (total_int % 2).astype(jnp.int32)
    counts = plan.astype(jnp.float32)
    total = jnp.sum(counts)
    pick = (lax.iota(jnp.int32, 2) == frag)[:, None, None]
    anchor_frag = lax.optimization_barrier(jnp.sum(jnp.where(pick, anchor, 0.0), 0))
    mom_frag = lax.optimization_barrier(jnp.sum(jnp.where(pick, momentum, 0.0), 0))
    theta_frag = lax.optimization_barrier(jnp.sum(jnp.where(pick[None], weights, 0.0), 1))
    outer_grad = lax.optimization_barrier(jnp.sum(counts[:, None, None] * (anchor_frag[None] - theta_frag), 0)) / total
    new_mom = outer_mu * mom_frag + outer_grad
    new_anc = anchor_frag - outer_rate * (outer_grad + outer_mu * new_mom)
    scale = 1.0 / math.sqrt(TOKENS)
    blocks_x = inputs.reshape(N_REPLICA, N_FSDP, TOK_DEV, D)
    blocks_k = token_weight(kinds).reshape(N_REPLICA, N_FSDP, TOK_DEV)

    def one_replica(packed):
        blocks, rows_w, theta, first, second = packed
        for step in range(INNER):
            theta, first, second = ref_step(blocks, rows_w, theta, first, second, scale)
            if step == 0:
                mixed = mix_share * theta + (1.0 - mix_share) * new_anc[None]
                theta = jnp.where(pick, mixed, theta)
        return (theta, first, second)
    new_w, new_f, new_s = lax.map(one_replica, (blocks_x, blocks_k, weights, first_moment, second_moment))
    anchor_out = jnp.where(pick, new_anc[None], anchor)
    momentum_out = jnp.where(pick, new_mom[None], momentum)
    return (new_w, new_f, new_s, anchor_out, momentum_out)
```

```python
import functools
import math

import jax
import jax.numpy as jnp
from jax import lax
from jax.experimental import pallas as pl
from jax.experimental.pallas import tpu as pltpu
from jax.sharding import PartitionSpec as P

INNER = 2

inner_rate = 0.003
beta_one = 0.9
beta_two = 0.95
adam_eps = 1e-08
decay_rate = 0.1
outer_rate = 0.7
outer_mu = 0.9
mix_share = 0.5

bf16 = jnp.bfloat16
f32 = jnp.float32
VMEM_LIMIT = 24 * 1024 * 1024


def token_weight(kinds):
    return jnp.where(kinds == 2, 1.0, jnp.where(kinds == 1, 0.25, 0.0)).astype(f32)


def dot(a, b):
    return jnp.dot(a, b, preferred_element_type=f32)


def dot_rows(a, b):
    return lax.dot_general(a, b, (((0,), (0,)), ((), ())), preferred_element_type=f32)


def whole(shape):
    return pl.BlockSpec(shape, lambda *_: (0,) * len(shape))


def sds(shape, dtype):
    return jax.ShapeDtypeStruct(shape, dtype)


def call(body, name, meta, ins, outs, grid=(1,), scratch=(), aliases=None, flops=0):
    arrays = [a for a, _ in ins]
    moved = sum(math.prod(o.shape) * o.dtype.itemsize for o, _ in outs)
    moved += sum(math.prod(a.shape) * a.dtype.itemsize for a, _ in ins)
    out = pl.pallas_call(
        body,
        name=name,
        out_shape=[o for o, _ in outs],
        grid_spec=pltpu.PrefetchScalarGridSpec(
            num_scalar_prefetch=1,
            grid=grid,
            in_specs=[s for _, s in ins],
            out_specs=[s for _, s in outs],
            scratch_shapes=list(scratch),
        ),
        input_output_aliases=aliases or {},
        compiler_params=pltpu.CompilerParams(vmem_limit_bytes=VMEM_LIMIT),
        cost_estimate=pl.CostEstimate(flops=flops, bytes_accessed=moved, transcendentals=0),
    )(meta, *arrays)
    return out


def cast_body(meta, theta, low):
    width = theta.shape[-1]
    low[:, :width] = theta[0, 0].astype(bf16)
    low[:, width:] = theta[0, 1].astype(bf16)


def cast_chunk(meta, weights, i, cr):
    width = weights.shape[-1]
    return call(
        cast_body, "cast_rows", meta,
        [(weights, pl.BlockSpec((1, 2, cr, width), lambda g, m: (0, 0, i, 0)))],
        [(sds((cr, 2 * width), bf16), whole((cr, 2 * width)))],
    )[0]


def turn_body(meta, x, xt):
    xt[...] = x[...].T


def turn(meta, x, slots, rows, tile):
    tokens = x.shape[0]
    per = rows // tile
    return call(
        turn_body, "turn_tokens", meta,
        [(x, pl.BlockSpec((tokens, tile), lambda g, m: (0, m[slots + g // per] * per + g % per)))],
        [(sds((_chips(meta, slots) * rows, tokens), bf16), pl.BlockSpec((tile, tokens), lambda g, m: (g, 0)))],
        grid=(_chips(meta, slots) * per,),
    )[0]


def _chips(meta, slots):
    return (meta.shape[0] - slots) // 2


def forward_body(count, first_call, *refs):
    meta, refs = refs[0], refs[1:]
    if first_call:
        acc_in = gram_in = None
    else:
        acc_in, gram_in, refs = refs[0], refs[1], refs[2:]
    lows = refs[:count]
    xs = (refs[count:2 * count], refs[2 * count:3 * count])
    acc, gram = refs[3 * count:]
    width = gram.shape[0]
    total = None if first_call else gram_in[...]
    for p in range(count):
        dec = lows[p][:, width:]
        term = dot_rows(dec, dec)
        total = term if total is None else total + term
    gram[...] = total
    for h in range(2):
        value = None if first_call else acc_in[h]
        for p in range(count):
            term = dot(xs[h][p][...], lows[p][...])
            value = term if value is None else value + term
        acc[h] = value


def forward(meta, acc, gram, pieces, x_own, x_par, cr):
    tokens = x_own.shape[0]
    wide = pieces[0][0].shape[1]
    width = wide // 2
    count = len(pieces)
    ins = []
    if acc is not None:
        ins += [(acc, whole(acc.shape)), (gram, whole(gram.shape))]
    ins += [(low, whole(low.shape)) for low, _, _ in pieces]
    for x in (x_own, x_par):
        for low, slot, i in pieces:
            ins.append((x, _columns(tokens, cr, slot, i, meta, x)))
    return call(
        functools.partial(forward_body, count, acc is None), "forward_rows", meta, ins,
        [(sds((2, tokens, wide), f32), whole((2, tokens, wide))), (sds((width, width), f32), whole((width, width)))],
        flops=4 * tokens * cr * wide * count,
    )


def _columns(tokens, cr, slot, i, meta, x):
    per = x.shape[1] // (meta.shape[0] - FIRST_SLOT) // cr
    return pl.BlockSpec((tokens, cr), lambda g, m: (0, m[slot] * per + i))


FIRST_SLOT = 4


def finish_body(scale, count, steps, *refs):
    meta, acc_in, gram_in, cw = refs[:4]
    refs = refs[4:]
    lows = refs[:count]
    xs = (refs[count:2 * count], refs[2 * count:3 * count])
    slopes, w_hi, w_lo, w_acc = refs[3 * count:]
    width = gram_in.shape[0]
    gram = gram_in[...]
    for p in range(count):
        dec = lows[p][:, width:]
        gram = gram + dot_rows(dec, dec)
    g_hi = gram.astype(bf16)
    g_lo = (gram - g_hi.astype(f32)).astype(bf16)
    w_new = None
    for h in range(2):
        value = acc_in[h]
        for p in range(count):
            value = value + dot(xs[h][p][...], lows[p][...])
        pre = value[:, :width]
        sig = 1.0 / (1.0 + jnp.exp(-pre))
        hidden = (pre * sig).astype(bf16)
        back = dot(hidden, g_hi) + dot(hidden, g_lo) - value[:, width:]
        weight = cw[h]
        slope = (weight * scale) * back * (sig * (1.0 + pre * (1.0 - sig)))
        counted = (weight * hidden.astype(f32)).astype(bf16)
        slopes[h, :, :width] = slope.astype(bf16)
        slopes[h, :, width:] = counted
        term = dot_rows(counted, hidden)
        w_new = term if w_new is None else w_new + term
    step = pl.program_id(0)

    @pl.when(step == 0)
    def _():
        w_acc[...] = w_new

    @pl.when(step > 0)
    def _():
        w_acc[...] += w_new

    @pl.when(step == steps - 1)
    def _():
        total = w_acc[...]
        hi = total.astype(bf16)
        w_hi[...] = hi
        w_lo[...] = (total - hi.astype(f32)).astype(bf16)


def finish(meta, acc, gram, cw, pieces, x_own, x_par, cr, scale):
    tokens = x_own.shape[0]
    wide = pieces[0][0].shape[1]
    width = wide // 2
    count = len(pieces)
    steps = 2
    tile = tokens // steps
    per = x_own.shape[1] // (meta.shape[0] - FIRST_SLOT) // cr
    ins = [
        (acc, pl.BlockSpec((2, tile, wide), lambda g, m: (0, g, 0))),
        (gram, whole(gram.shape)),
        (cw, pl.BlockSpec((2, tile, 1), lambda g, m: (0, g, 0))),
    ]
    ins += [(low, whole(low.shape)) for low, _, _ in pieces]
    for x in (x_own, x_par):
        for low, slot, i in pieces:
            ins.append((x, pl.BlockSpec((tile, cr), lambda g, m, slot=slot, i=i: (g, m[slot] * per + i))))
    square = (sds((width, width), bf16), whole((width, width)))
    return call(
        functools.partial(finish_body, scale, count, steps), "finish_slopes", meta, ins,
        [(sds((2, tokens, wide), bf16), pl.BlockSpec((2, tile, wide), lambda g, m: (0, g, 0))), square, square],
        grid=(steps,),
        scratch=[pltpu.VMEM((width, width), f32)],
        flops=4 * tokens * cr * wide * count + 12 * tokens * width * width,
    )


def row_grad(scale, xt_own, xt_par, slopes, w_hi, w_lo, low):
    width = w_hi.shape[0]
    both = dot(xt_own[...], slopes[0]) + dot(xt_par[...], slopes[1])
    dec = low[:, width:]
    grad_dec = scale * (dot(dec, w_hi[...]) + dot(dec, w_lo[...]) - both[:, width:])
    return both[:, :width], grad_dec


def grad_body(scale, meta, xt_own, xt_par, slopes, w_hi, w_lo, low, out):
    width = w_hi.shape[0]
    enc, dec = row_grad(scale, xt_own, xt_par, slopes, w_hi, w_lo, low)
    out[:, :width] = enc.astype(bf16)
    out[:, width:] = dec.astype(bf16)


def grad_inputs(block, cr, xt, slopes, w_hi, w_lo, low):
    tokens = xt[0].shape[1]
    ins = [(x, pl.BlockSpec((cr, tokens), lambda g, m: (block, 0))) for x in xt]
    return ins + [(a, whole(a.shape)) for a in (slopes, w_hi, w_lo, low)]


def grad_rows(meta, scale, block, cr, xt, slopes, w_hi, w_lo, low):
    wide = low.shape[1]
    return call(
        functools.partial(grad_body, scale), "grad_rows", meta,
        grad_inputs(block, cr, xt, slopes, w_hi, w_lo, low),
        [(sds((cr, wide), bf16), whole((cr, wide)))],
        flops=4 * xt[0].shape[1] * cr * wide,
    )[0]


def adam_body(scale, last, count, *refs):
    meta, xt_own, xt_par, slopes, w_hi, w_lo, low = refs[:7]
    got = refs[7:7 + count]
    theta, first, second = refs[7 + count:10 + count]
    refs = refs[10 + count:]
    width = w_hi.shape[0]
    grads = row_grad(scale, xt_own, xt_par, slopes, w_hi, w_lo, low)
    if last:
        theta_out, first_out, second_out = refs[-3:]
    else:
        anchor = refs[0]
        theta_out, first_out, second_out, low_out = refs[-4:]
    for k in range(2):
        grad = grads[k]
        for g in got:
            grad = grad + g[:, k * width:(k + 1) * width].astype(f32)
        one = beta_one * first[0, k] + (1.0 - beta_one) * grad
        two = beta_two * second[0, k] + (1.0 - beta_two) * grad * grad
        old = theta[0, k]
        new = old - inner_rate * (one / (jnp.sqrt(two) + adam_eps) + decay_rate * old)
        if not last:
            mixed = mix_share * new + (1.0 - mix_share) * anchor[...]
            new = jnp.where(meta[0] == k, mixed, new)
            low_out[:, k * width:(k + 1) * width] = new.astype(bf16)
        theta_out[0, k] = new
        first_out[0, k] = one
        second_out[0, k] = two


def adam_rows(meta, scale, i, cr, xt, slopes, w_hi, w_lo, low, got, state, state_block, new_anc, prev, full):
    width = low.shape[1] // 2
    last = new_anc is None
    block = (1, 2, cr, width)
    ins = grad_inputs(i, cr, xt, slopes, w_hi, w_lo, low)
    ins += [(g, whole(g.shape)) for g in got]
    ins += [(s, pl.BlockSpec(block, lambda g, m: (0, 0, state_block, 0))) for s in state]
    aliases = {}
    if last:
        if prev is not None:
            for n, p in enumerate(prev):
                aliases[1 + len(ins)] = n
                ins.append((p, pl.BlockSpec(memory_space=pl.ANY)))
        outs = [(sds(full, f32), pl.BlockSpec(block, lambda g, m: (0, 0, i, 0)))] * 3
    else:
        ins.append((new_anc, pl.BlockSpec((cr, width), lambda g, m: (i, 0))))
        outs = [(sds(block, f32), whole(block))] * 3 + [(sds((cr, 2 * width), bf16), whole((cr, 2 * width)))]
    return call(
        functools.partial(adam_body, scale, last, len(got)), "adam_rows", meta, ins, outs,
        aliases=aliases, flops=8 * xt[0].shape[1] * cr * width,
    )


def delta_body(order, meta, anchor, theta, *outs):
    rows = outs[0].shape[0]
    count = meta[1].astype(f32)
    for m, out in enumerate(outs):
        at = pl.ds(pl.multiple_of(order(meta[2], m) * rows, rows), rows)
        out[...] = (count * (anchor[0, at, :] - theta[0, 0, at, :])).astype(bf16)


def sum_body(meta, *refs):
    total = refs[0][...].astype(f32)
    for r in refs[1:-1]:
        total = total + r[...].astype(f32)
    refs[-1][...] = (total / meta[3].astype(f32)).astype(bf16)


def outer_body(order, meta, anchor, momentum, *refs):
    pieces = refs[:-3]
    new_anc, anchor_out, momentum_out = refs[-3:]
    rows = pieces[0].shape[0]
    frag = meta[0]
    anchor_out[...] = anchor[...]
    momentum_out[...] = momentum[...]
    for m, piece in enumerate(pieces):
        at = pl.ds(pl.multiple_of(order(meta[2], m) * rows, rows), rows)
        grad = piece[...].astype(f32)
        mom = outer_mu * momentum[frag, at, :] + grad
        anc = anchor[frag, at, :] - outer_rate * (grad + outer_mu * mom)
        new_anc[at, :] = anc
        anchor_out[frag, at, :] = anc
        momentum_out[frag, at, :] = mom


def outer(meta, anchor, momentum, weights, n):
    two, rows, width = anchor.shape
    part = rows // n
    if n & (n - 1) == 0:
        order = lambda r, m: jnp.bitwise_xor(r, m)
        dest = lambda r, m: r ^ m
    else:
        order = lambda r, m: lax.rem(r + m, n)
        dest = lambda r, m: (r + m) % n
    back = lambda r, m: dest(r, m) if n & (n - 1) == 0 else (r - m) % n
    order_back = order if n & (n - 1) == 0 else (lambda r, m: lax.rem(r + n - m, n))
    pieces = call(
        functools.partial(delta_body, order), "delta_pieces", meta,
        [
            (anchor, pl.BlockSpec((1, rows, width), lambda g, m: (m[0], 0, 0))),
            (weights, pl.BlockSpec((1, 1, rows, width), lambda g, m: (0, m[0], 0, 0))),
        ],
        [(sds((part, width), bf16), whole((part, width)))] * n,
    )
    send = lambda a, m: lax.ppermute(a, "replica", [(r, dest(r, m)) for r in range(n)])
    got = [pieces[0]] + [send(pieces[m], m) for m in range(1, n)]
    mine = call(
        sum_body, "sum_pieces", meta, [(g, whole(g.shape)) for g in got],
        [(sds((part, width), bf16), whole((part, width)))],
    )[0]
    all_pieces = [mine] + [send(mine, m) for m in range(1, n)]
    return call(
        functools.partial(outer_body, order_back), "outer_step", meta,
        [(anchor, whole(anchor.shape)), (momentum, whole(momentum.shape))] + [(p, whole(p.shape)) for p in all_pieces],
        [(sds((rows, width), f32), whole((rows, width))), (sds(anchor.shape, f32), whole(anchor.shape)), (sds(anchor.shape, f32), whole(anchor.shape))],
    )


def local(n_rep, n_fsdp, inputs, kinds, weights, first_moment, second_moment, anchor, momentum, plan):
    tokens = inputs.shape[0]
    rows, width = weights.shape[2:]
    chips = n_fsdp // 2
    scale = 1.0 / math.sqrt(tokens * n_fsdp)
    chunks = max(1, min(4, rows // 256))
    cr = rows // chunks

    me = lax.axis_index("fsdp")
    rep = lax.axis_index("replica")
    total = jnp.sum(plan)
    chip, core = me // 2, me % 2
    at = [((chip + s) % chips) * 2 for s in range(chips)]
    meta = jnp.stack(
        [total % 2, lax.dynamic_slice_in_dim(plan, rep, 1, 0)[0], rep, total]
        + [a + core for a in at] + [a + 1 - core for a in at]
    ).astype(jnp.int32)

    partner = [(f, f ^ 1) for f in range(n_fsdp)]
    to_partner = lambda a: lax.ppermute(a, "fsdp", partner)
    fetch = lambda a, s: lax.ppermute(
        a, "fsdp", [(((f // 2 + s) % chips) * 2 + f % 2, f) for f in range(n_fsdp)])
    give = lambda a, s: lax.ppermute(
        a, "fsdp", [(f, ((f // 2 + s) % chips) * 2 + f % 2) for f in range(n_fsdp)])

    low_own = [cast_chunk(meta, weights, i, cr) for i in range(chunks)]
    x_par = to_partner(inputs)
    cw_own = token_weight(kinds)
    cw = jnp.stack([cw_own, to_partner(cw_own)])[:, :, None]
    new_anc, anchor_out, momentum_out = outer(meta, anchor, momentum, weights, n_rep)
    xt = [turn(meta, x, FIRST_SLOT, rows, cr) for x in (inputs, x_par)]

    state = [(weights, first_moment, second_moment)] * chunks
    state_block = list(range(chunks))
    for step in range(INNER):
        last = step == INNER - 1
        near = [(low_own[i], FIRST_SLOT, i) for i in range(chunks)]
        near += [(to_partner(low_own[i]), FIRST_SLOT + chips, i) for i in range(chunks)]
        far, low_far = [], {}
        for i in range(chunks):
            for s in range(1, chips):
                low_far[s, i] = fetch(low_own[i], s)
                far.append((low_far[s, i], FIRST_SLOT + s, i))
                far.append((to_partner(low_far[s, i]), FIRST_SLOT + chips + s, i))
        acc, gram = forward(meta, None, None, near, inputs, x_par, cr)
        if len(far) > 2:
            acc, gram = forward(meta, acc, gram, far[:-2], inputs, x_par, cr)
        slopes, w_hi, w_lo = finish(meta, acc, gram, cw, far[-2:], inputs, x_par, cr, scale)
        got = []
        for i in range(chunks):
            got.append([
                give(grad_rows(meta, scale, s * chunks + i, cr, xt, slopes, w_hi, w_lo, low_far[s, i]), s)
                for s in range(1, chips)
            ])
        new_state, new_low, prev = [], [], None
        for i in range(chunks):
            res = adam_rows(
                meta, scale, i, cr, xt, slopes, w_hi, w_lo, low_own[i], got[i],
                state[i], state_block[i], None if last else new_anc, prev, weights.shape,
            )
            if last:
                prev = res
            else:
                new_state.append(tuple(res[:3]))
                new_low.append(res[3])
        state, state_block, low_own = new_state, [0] * chunks, new_low
    return (*prev, anchor_out, momentum_out)


def solution(mesh):
    return jax.shard_map(
        functools.partial(local, mesh.shape["replica"], mesh.shape["fsdp"]),
        mesh=mesh,
        in_specs=(
            P(("replica", "fsdp"), None),
            P(("replica", "fsdp")),
            P("replica", None, "fsdp", None),
            P("replica", None, "fsdp", None),
            P("replica", None, "fsdp", None),
            P(None, "fsdp", None),
            P(None, "fsdp", None),
            P(),
        ),
        out_specs=(
            P("replica", None, "fsdp", None),
            P("replica", None, "fsdp", None),
            P("replica", None, "fsdp", None),
            P(None, "fsdp", None),
            P(None, "fsdp", None),
        ),
        check_vma=False,
    )
```

```python
import functools
import math

import jax
import jax.numpy as jnp
from jax import lax
from jax.experimental import pallas as pl
from jax.experimental.pallas import tpu as pltpu
from jax.sharding import PartitionSpec as P

INNER = 2

inner_rate = 0.003
beta_one = 0.9
beta_two = 0.95
adam_eps = 1e-08
decay_rate = 0.1
outer_rate = 0.7
outer_mu = 0.9
mix_share = 0.5

bf16 = jnp.bfloat16
f32 = jnp.float32
VMEM_LIMIT = 16 * 1024 * 1024


def token_weight(kinds):
    return jnp.where(kinds == 2, 1.0, jnp.where(kinds == 1, 0.25, 0.0)).astype(f32)


def dot(a, b):
    return jnp.dot(a, b, preferred_element_type=f32)


def dot_rows(a, b):
    return lax.dot_general(a, b, (((0,), (0,)), ((), ())), preferred_element_type=f32)


def once(shape, index):
    return pl.BlockSpec(shape, index, pipeline_mode=pl.Buffered(1))


def whole(shape):
    return once(shape, lambda *_: (0,) * len(shape))


def sds(shape, dtype):
    return jax.ShapeDtypeStruct(shape, dtype)


def call(body, name, meta, ins, outs, grid=(1,), scratch=(), aliases=None, flops=0, after=()):
    arrays = [a for a, _ in ins] + list(after)
    moved = sum(math.prod(o.shape) * o.dtype.itemsize for o, _ in outs)
    moved += sum(math.prod(a.shape) * a.dtype.itemsize for a, _ in ins)
    n_in = len(meta) + len(ins)

    def run(*refs):
        body(*refs[:n_in], *refs[n_in + len(after):])

    return pl.pallas_call(
        run,
        name=name,
        out_shape=[o for o, _ in outs],
        grid_spec=pltpu.PrefetchScalarGridSpec(
            num_scalar_prefetch=len(meta),
            grid=grid,
            in_specs=[s for _, s in ins] + [pl.BlockSpec(memory_space=pl.ANY)] * len(after),
            out_specs=[s for _, s in outs],
            scratch_shapes=list(scratch),
        ),
        input_output_aliases=aliases or {},
        compiler_params=pltpu.CompilerParams(vmem_limit_bytes=VMEM_LIMIT),
        cost_estimate=pl.CostEstimate(flops=flops, bytes_accessed=moved, transcendentals=0),
    )(*meta, *arrays)


def plan_sum(plan):
    total = plan[0]
    for r in range(1, plan.shape[0]):
        total = total + plan[r]
    return total


def fragment(plan):
    return lax.rem(plan_sum(plan), 2)


def cast_body(chunks, theta, *refs):
    outs, (held, sems) = refs[:len(chunks)], refs[len(chunks):]
    cr, wide = outs[0].shape
    width = wide // 2
    copies = []
    for n, i in enumerate(chunks):
        copy = pltpu.make_async_copy(theta.at[0, :, pl.ds(i * cr, cr), :], held.at[n], sems.at[n])
        copy.start()
        copies.append(copy)
    for n, copy in enumerate(copies):
        copy.wait()
        for k in range(2):
            outs[n][:, k * width:(k + 1) * width] = held[n, k].astype(bf16)


def cast_chunks(weights, chunks, cr):
    width = weights.shape[-1]
    return call(
        functools.partial(cast_body, chunks), "cast_rows", (),
        [(weights, pl.BlockSpec(memory_space=pltpu.HBM))],
        [(sds((cr, 2 * width), bf16), whole((cr, 2 * width)))] * len(chunks),
        scratch=[
            pltpu.VMEM((len(chunks), 2, cr, width), f32),
            pltpu.SemaphoreType.DMA((len(chunks),)),
        ],
    )


def weigh_body(kinds, out):
    out[...] = token_weight(kinds[...])


def copy_body(x, out):
    out[...] = x[...]


def relay(x, after):
    return call(copy_body, "relay_rows", (), [(x, whole(x.shape))], [(sds(x.shape, x.dtype), whole(x.shape))], after=after)[0]


def turn_body(pos, x, xt):
    xt[...] = x[...].T


def turn(pos, x, chips, rows, tile):
    tokens = x.shape[0]
    per = rows // tile
    return call(
        turn_body, "turn_tokens", (pos,),
        [(x, pl.BlockSpec((tokens, tile), lambda g, m: (0, m[1 + g // per] * per + g % per)))],
        [(sds((chips * rows, tokens), bf16), pl.BlockSpec((tile, tokens), lambda g, m: (g, 0)))],
        grid=(chips * per,),
    )[0]


def forward_body(count, first_call, pos, *refs):
    if first_call:
        acc_in = gram_in = None
    else:
        acc_in, gram_in, refs = refs[0], refs[1], refs[2:]
    lows = refs[:count]
    xs = (refs[count:2 * count], refs[2 * count:3 * count])
    acc, gram = refs[3 * count:]
    width = gram.shape[0]
    total = None if first_call else gram_in[...]
    for p in range(count):
        dec = lows[p][:, width:]
        term = dot_rows(dec, dec)
        total = term if total is None else total + term
    gram[...] = total
    for h in range(2):
        value = None if first_call else acc_in[h]
        for p in range(count):
            term = dot(xs[h][p][...], lows[p][...])
            value = term if value is None else value + term
        acc[h] = value


def column(slot, i, per):
    return lambda g, m: (0, m[slot] * per + i)


def forward(pos, acc, gram, pieces, xs, cr, per, after=()):
    tokens = xs[0].shape[0]
    wide = pieces[0][0].shape[1]
    width = wide // 2
    count = len(pieces)
    ins = []
    if acc is not None:
        ins += [(acc, whole(acc.shape)), (gram, whole(gram.shape))]
    ins += [(low, whole(low.shape)) for low, _, _ in pieces]
    for x in xs:
        ins += [(x, once((tokens, cr), column(slot, i, per))) for _, slot, i in pieces]
    return call(
        functools.partial(forward_body, count, acc is None), "forward_rows", (pos,), ins,
        [(sds((2, tokens, wide), f32), whole((2, tokens, wide))), (sds((width, width), f32), whole((width, width)))],
        flops=4 * tokens * cr * wide * count, after=after,
    )


def finish_body(scale, count, steps, pos, acc_in, gram_in, cw, *refs):
    lows = refs[:count]
    xs = (refs[count:2 * count], refs[2 * count:3 * count])
    slopes, w_hi, w_lo, w_acc = refs[3 * count:]
    width = gram_in.shape[0]
    gram = gram_in[...]
    for p in range(count):
        dec = lows[p][:, width:]
        gram = gram + dot_rows(dec, dec)
    g_hi = gram.astype(bf16)
    g_lo = (gram - g_hi.astype(f32)).astype(bf16)
    w_new = None
    for h in range(2):
        value = acc_in[h]
        for p in range(count):
            value = value + dot(xs[h][p][...], lows[p][...])
        pre = value[:, :width]
        sig = 1.0 / (1.0 + jnp.exp(-pre))
        hidden = (pre * sig).astype(bf16)
        back = dot(hidden, g_hi) + dot(hidden, g_lo) - value[:, width:]
        weight = cw[h]
        slope = (weight * scale) * back * (sig * (1.0 + pre * (1.0 - sig)))
        counted = (weight * hidden.astype(f32)).astype(bf16)
        slopes[h, :, :width] = slope.astype(bf16)
        slopes[h, :, width:] = counted
        term = dot_rows(counted, hidden)
        w_new = term if w_new is None else w_new + term
    step = pl.program_id(0)

    @pl.when(step == 0)
    def _():
        w_acc[...] = w_new

    @pl.when(step > 0)
    def _():
        w_acc[...] += w_new

    @pl.when(step == steps - 1)
    def _():
        total = w_acc[...]
        hi = total.astype(bf16)
        w_hi[...] = hi
        w_lo[...] = (total - hi.astype(f32)).astype(bf16)


def finish(pos, acc, gram, cw, pieces, xs, cr, per, scale):
    tokens = xs[0].shape[0]
    wide = pieces[0][0].shape[1]
    width = wide // 2
    count = len(pieces)
    steps = 2
    tile = tokens // steps
    ins = [
        (acc, pl.BlockSpec((2, tile, wide), lambda g, m: (0, g, 0))),
        (gram, whole(gram.shape)),
        (cw, pl.BlockSpec((2, tile, 1), lambda g, m: (0, g, 0))),
    ]
    ins += [(low, whole(low.shape)) for low, _, _ in pieces]
    for x in xs:
        for _, slot, i in pieces:
            ins.append((x, pl.BlockSpec((tile, cr), lambda g, m, slot=slot, i=i: (g, m[slot] * per + i))))
    square = (sds((width, width), bf16), whole((width, width)))
    return call(
        functools.partial(finish_body, scale, count, steps), "finish_slopes", (pos,), ins,
        [(sds((2, tokens, wide), bf16), pl.BlockSpec((2, tile, wide), lambda g, m: (0, g, 0))), square, square],
        grid=(steps,),
        scratch=[pltpu.VMEM((width, width), f32)],
        flops=4 * tokens * cr * wide * count + 12 * tokens * width * width,
    )


def grad_body(scale, xt_own, xt_par, slopes, w_hi, w_lo, low, out):
    width = w_hi.shape[0]
    both = dot(xt_own[...], slopes[0]) + dot(xt_par[...], slopes[1])
    dec = low[:, width:]
    grad_dec = scale * (dot(dec, w_hi[...]) + dot(dec, w_lo[...]) - both[:, width:])
    out[:, :width] = both[:, :width].astype(out.dtype)
    out[:, width:] = grad_dec.astype(out.dtype)


def grad_rows(scale, block, cr, xt, slopes, w_hi, w_lo, low, dtype, after=()):
    tokens = xt[0].shape[1]
    wide = low.shape[1]
    ins = [(x, once((cr, tokens), lambda g: (block, 0))) for x in xt]
    ins += [(a, whole(a.shape)) for a in (slopes, w_hi, w_lo, low)]
    return call(
        functools.partial(grad_body, scale), "grad_rows", (), ins,
        [(sds((cr, wide), dtype), whole((cr, wide)))],
        flops=4 * tokens * cr * wide, after=after,
    )[0]


def adam_body(last, count, plan, own, *refs):
    got = refs[:count]
    theta, first, second = refs[count:3 + count]
    refs = refs[3 + count:]
    width = own.shape[1] // 2
    if last:
        theta_out, first_out, second_out = refs[-3:]
    else:
        anchor = refs[0]
        theta_out, first_out, second_out, low_out = refs[-4:]
        frag = fragment(plan)
    for k in range(2):
        grad = own[:, k * width:(k + 1) * width]
        for g in got:
            grad = grad + g[:, k * width:(k + 1) * width].astype(f32)
        one = beta_one * first[0, k] + (1.0 - beta_one) * grad
        two = beta_two * second[0, k] + (1.0 - beta_two) * grad * grad
        old = theta[0, k]
        new = old - inner_rate * (one / (jnp.sqrt(two) + adam_eps) + decay_rate * old)
        if not last:
            mixed = mix_share * new + (1.0 - mix_share) * anchor[...]
            new = jnp.where(frag == k, mixed, new)
            low_out[:, k * width:(k + 1) * width] = new.astype(bf16)
        theta_out[0, k] = new
        first_out[0, k] = one
        second_out[0, k] = two


def adam_rows(plan, i, cr, own, got, state, state_block, new_anc, prev, full):
    width = own.shape[1] // 2
    last = new_anc is None
    block = (1, 2, cr, width)
    ins = [(g, whole(g.shape)) for g in [own] + got]
    ins += [(s, once(block, lambda g, m: (0, 0, state_block, 0))) for s in state]
    aliases = {}
    if last:
        if prev is not None:
            for n, p in enumerate(prev):
                aliases[1 + len(ins)] = n
                ins.append((p, pl.BlockSpec(memory_space=pl.ANY)))
        outs = [(sds(full, f32), once(block, lambda g, m: (0, 0, i, 0)))] * 3
    else:
        ins.append((new_anc, once((cr, width), lambda g, m: (i, 0))))
        outs = [(sds(block, f32), whole(block))] * 3 + [(sds((cr, 2 * width), bf16), whole((cr, 2 * width)))]
    return call(
        functools.partial(adam_body, last, len(got)), "adam_rows", (plan,), ins, outs, aliases=aliases,
    )


def delta_body(pos, plan, anchor, theta, anchor_off, theta_off, keep, send):
    count = plan[pos[0]].astype(f32)
    keep[...] = count * (anchor[0] - theta[0, 0])
    send[...] = (count * (anchor_off[0] - theta_off[0, 0])).astype(bf16)


def add_body(final, plan, a, b, out):
    total = a[...].astype(f32) + b[...].astype(f32)
    if final:
        total = total / plan_sum(plan).astype(f32)
    out[...] = total.astype(bf16)


def outer_body(pos, plan, anchor, momentum, own, other, new_anc, anchor_out, momentum_out):
    half = own.shape[0]
    frag = fragment(plan)
    bit = lax.rem(pos[0], 2)
    anchor_out[...] = anchor[...]
    momentum_out[...] = momentum[...]
    for piece, where in ((own, bit), (other, 1 - bit)):
        at = pl.ds(pl.multiple_of(where * half, half), half)
        grad = piece[...].astype(f32)
        mom = outer_mu * momentum[frag, at, :] + grad
        anc = anchor[frag, at, :] - outer_rate * (grad + outer_mu * mom)
        new_anc[at, :] = anc
        anchor_out[frag, at, :] = anc
        momentum_out[frag, at, :] = mom


def outer_start(pos, plan, anchor, weights, after):
    _, rows, width = anchor.shape
    half = rows // 2

    def at(off):
        def anchor_at(g, p, q):
            return (fragment(q), lax.rem(p[0] + off, 2), 0)

        def theta_at(g, p, q):
            return (0, fragment(q), lax.rem(p[0] + off, 2), 0)

        return [(anchor, once((1, half, width), anchor_at)), (weights, once((1, 1, half, width), theta_at))]

    return call(
        delta_body, "delta_halves", (pos, plan), at(0) + at(1),
        [(sds((half, width), f32), whole((half, width))), (sds((half, width), bf16), whole((half, width)))],
        after=after,
    )


def outer_add(plan, a, b, final, after):
    return call(
        functools.partial(add_body, final), "add_halves", (plan,), [(a, whole(a.shape)), (b, whole(b.shape))],
        [(sds(a.shape, bf16), whole(a.shape))], after=after,
    )[0]


def outer_end(pos, plan, anchor, momentum, own, other):
    _, rows, width = anchor.shape
    return call(
        outer_body, "outer_step", (pos, plan),
        [(a, whole(a.shape)) for a in (anchor, momentum, own, other)],
        [(sds((rows, width), f32), whole((rows, width)))] + [(sds(anchor.shape, f32), whole(anchor.shape))] * 2,
    )


def local(n_rep, n_fsdp, inputs, kinds, weights, first_moment, second_moment, anchor, momentum, plan):
    tokens = inputs.shape[0]
    rows, width = weights.shape[2:]
    chips = n_fsdp // 2
    scale = 1.0 / math.sqrt(tokens * n_fsdp)
    chunks = max(1, min(4, rows // 256))
    cr = rows // chunks

    partner = [(f, f ^ 1) for f in range(n_fsdp)]
    to_partner = lambda a: lax.ppermute(a, "fsdp", partner)
    fetch = lambda a, s: lax.ppermute(
        a, "fsdp", [(((f // 2 + s) % chips) * 2 + f % 2, f) for f in range(n_fsdp)])
    give = lambda a, s: lax.ppermute(
        a, "fsdp", [(f, ((f // 2 + s) % chips) * 2 + f % 2) for f in range(n_fsdp)])
    across = lambda a, bit: lax.ppermute(a, "replica", [(r, r ^ bit) for r in range(n_rep)])

    low_own = cast_chunks(weights, [0], cr)
    if chunks > 1:
        low_own = list(low_own) + list(cast_chunks(weights, list(range(1, chunks)), cr))

    chip = lax.axis_index("fsdp") // 2
    core = lax.axis_index("fsdp") % 2
    at = [((chip + s) % chips) * 2 for s in range(chips)]
    pos = jnp.stack([lax.axis_index("replica")] + [a + core for a in at] + [a + 1 - core for a in at]).astype(jnp.int32)

    x_par = to_partner(inputs)
    xs = (inputs, x_par)
    keep, send = outer_start(pos, plan, anchor, weights, after=[low_own[-1]])
    outer_in = across(send, 1)
    lanes = kinds.reshape(-1, 128)
    cw_own = call(
        weigh_body, "weigh_tokens", (), [(lanes, whole(lanes.shape))],
        [(sds(lanes.shape, f32), whole(lanes.shape))], after=[send],
    )[0]
    cw = jnp.stack([cw_own, to_partner(cw_own)]).reshape(2, tokens, 1)
    xt = [turn(pos, x, chips, rows, cr) for x in xs]

    state = [(weights, first_moment, second_moment)] * chunks
    state_block = list(range(chunks))
    for step in range(INNER):
        last = step == INNER - 1
        near = [(low_own[i], 1, i) for i in range(chunks)]
        near += [(to_partner(low_own[i]), 1 + chips, i) for i in range(chunks)]
        acc, gram = forward(pos, None, None, near, xs, cr, chunks)
        far = [(i, s) for i in range(chunks) for s in range(1, chips)]
        low_far = {(i, s): fetch(low_own[i], s) for i, s in far}

        stages = []
        if step == 0:
            bits = [1 << b for b in range(1, n_rep.bit_length() - 1)]
            own = keep
            took = outer_in
        wait_for = []
        pending = None
        for n, (i, s) in enumerate(far):
            handed = to_partner(relay(low_far[i, s], [acc] + wait_for))
            pieces = [(low_far[i, s], 1 + s, i)]
            if pending is not None:
                pieces = [pending] + pieces
            acc, gram = forward(pos, acc, gram, pieces, xs, cr, chunks)
            pending = (handed, 1 + chips + s, i)
            if step == 0 and bits and n in (0, len(far) - 2):
                own = outer_add(plan, own, took, False, [acc])
                took = across(own, bits.pop(0))
                wait_for = [own]
        slopes, w_hi, w_lo = finish(pos, acc, gram, cw, [pending], xs, cr, chunks, scale)

        mine, got = [], []
        for i in range(chunks):
            sent = [
                grad_rows(scale, s * chunks + i, cr, xt, slopes, w_hi, w_lo, low_far[i, s], bf16)
                for s in range(1, chips)
            ]
            got.append([give(g, s) for s, g in enumerate(sent, 1)])
        for i in range(chunks):
            mine.append(grad_rows(scale, i, cr, xt, slopes, w_hi, w_lo, low_own[i], f32, after=sent))
        if step == 0:
            while bits:
                own = outer_add(plan, own, took, False, sent)
                took = across(own, bits.pop(0))
            own = outer_add(plan, own, took, True, mine[-1:])
            new_anc, anchor_out, momentum_out = outer_end(pos, plan, anchor, momentum, own, across(own, 1))

        new_state, new_low, prev = [], [], None
        for i in range(chunks):
            res = adam_rows(
                plan, i, cr, mine[i], got[i], state[i], state_block[i],
                None if last else new_anc, prev, weights.shape,
            )
            if last:
                prev = res
            else:
                new_state.append(tuple(res[:3]))
                new_low.append(res[3])
        state, state_block, low_own = new_state, [0] * chunks, new_low
    return (*prev, anchor_out, momentum_out)


def solution(mesh):
    return jax.shard_map(
        functools.partial(local, mesh.shape["replica"], mesh.shape["fsdp"]),
        mesh=mesh,
        in_specs=(
            P(("replica", "fsdp"), None),
            P(("replica", "fsdp")),
            P("replica", None, "fsdp", None),
            P("replica", None, "fsdp", None),
            P("replica", None, "fsdp", None),
            P(None, "fsdp", None),
            P(None, "fsdp", None),
            P(),
        ),
        out_specs=(
            P("replica", None, "fsdp", None),
            P("replica", None, "fsdp", None),
            P("replica", None, "fsdp", None),
            P(None, "fsdp", None),
            P(None, "fsdp", None),
        ),
        check_vma=False,
    )
```

```python
import functools
import math

import jax
import jax.numpy as jnp
from jax import lax
from jax.experimental import pallas as pl
from jax.experimental.pallas import tpu as pltpu
from jax.sharding import PartitionSpec as P

INNER = 2

inner_rate = 0.003
beta_one = 0.9
beta_two = 0.95
adam_eps = 1e-08
decay_rate = 0.1
outer_rate = 0.7
outer_mu = 0.9
mix_share = 0.5

bf16 = jnp.bfloat16
f32 = jnp.float32
VMEM_LIMIT = 16 * 1024 * 1024
CAST_VMEM = 63 * 1024 * 1024


def token_weight(kinds):
    return jnp.where(kinds == 2, 1.0, jnp.where(kinds == 1, 0.25, 0.0)).astype(f32)


def dot(a, b):
    return jnp.dot(a, b, preferred_element_type=f32)


def dot_rows(a, b):
    return lax.dot_general(a, b, (((0,), (0,)), ((), ())), preferred_element_type=f32)


def once(shape, index):
    return pl.BlockSpec(shape, index, pipeline_mode=pl.Buffered(1))


def whole(shape):
    return once(shape, lambda *_: (0,) * len(shape))


def sds(shape, dtype):
    return jax.ShapeDtypeStruct(shape, dtype)


def call(body, name, meta, ins, outs, grid=(1,), scratch=(), aliases=None, after=(), vmem=VMEM_LIMIT):
    arrays = [a for a, _ in ins] + list(after)
    n_in = len(meta) + len(ins)

    def run(*refs):
        body(*refs[:n_in], *refs[n_in + len(after):])

    return pl.pallas_call(
        run,
        name=name,
        out_shape=[o for o, _ in outs],
        grid_spec=pltpu.PrefetchScalarGridSpec(
            num_scalar_prefetch=len(meta),
            grid=grid,
            in_specs=[s for _, s in ins] + [pl.BlockSpec(memory_space=pl.ANY)] * len(after),
            out_specs=[s for _, s in outs],
            scratch_shapes=list(scratch),
        ),
        input_output_aliases=aliases or {},
        compiler_params=pltpu.CompilerParams(vmem_limit_bytes=vmem),
        cost_estimate=pl.CostEstimate(flops=1, bytes_accessed=1, transcendentals=0),
    )(*meta, *arrays)


def plan_sum(plan):
    total = plan[0]
    for r in range(1, plan.shape[0]):
        total = total + plan[r]
    return total


def fragment(plan):
    return lax.rem(plan_sum(plan), 2)


def cast_body(blocks, theta, *refs):
    outs, (held, sems) = refs[:len(blocks)], refs[len(blocks):]
    copies = []
    for n, (off, size) in enumerate(blocks):
        copy = pltpu.make_async_copy(
            theta.at[0, :, pl.ds(off, size), :], held.at[:, pl.ds(off, size), :], sems.at[n])
        if (off, size) not in blocks[:n]:
            copy.start()
        copies.append(copy)
    width = held.shape[2]
    for n, (off, size) in enumerate(blocks):
        copies[n].wait()
        for k in range(2):
            outs[n][:, k * width:(k + 1) * width] = held[k, off:off + size].astype(bf16)


def cast_blocks(weights, blocks, after=(), vmem=VMEM_LIMIT):
    _, _, rows, width = weights.shape
    shapes = [(size, 2 * width) for _, size in blocks]
    return call(
        functools.partial(cast_body, blocks), "cast_rows", (),
        [(weights, pl.BlockSpec(memory_space=pltpu.HBM))],
        [(sds(shape, bf16), whole(shape)) for shape in shapes],
        scratch=[pltpu.VMEM((2, rows, width), f32), pltpu.SemaphoreType.DMA((len(blocks),))],
        after=after, vmem=vmem,
    )


def join_body(first, *refs):
    out = refs[-1]
    off = 0
    for part in (first,) + refs[:-1]:
        out[off:off + part.shape[0], :] = part[...]
        off += part.shape[0]


def join_rows(parts, after=()):
    shape = (sum(p.shape[0] for p in parts), parts[0].shape[1])
    return call(
        join_body, "join_rows", (), [(p, whole(p.shape)) for p in parts],
        [(sds(shape, parts[0].dtype), whole(shape))], after=after,
    )[0]


def weigh_body(own, other, out):
    for h, kinds in enumerate((own, other)):
        lanes = kinds.shape[0]
        pad = jnp.zeros((8 - lanes % 8, 128), f32)
        value = token_weight(kinds[...])
        if lanes % 8:
            value = jnp.concatenate([value, pad], 0)
        turned = value.T
        for j in range(lanes):
            out[h, j * 128:(j + 1) * 128, :] = turned[:, j:j + 1]


def copy_body(x, out):
    out[...] = x[...]


def relay(x, after):
    return call(copy_body, "relay_rows", (), [(x, whole(x.shape))], [(sds(x.shape, x.dtype), whole(x.shape))], after=after)[0]


def forward_body(count, first_call, pos, *refs):
    if first_call:
        acc_in = gram_in = None
    else:
        acc_in, gram_in, refs = refs[0], refs[1], refs[2:]
    lows = refs[:count]
    xs = (refs[count:2 * count], refs[2 * count:3 * count])
    acc, gram = refs[3 * count:]
    width = gram.shape[0]
    total = None if first_call else gram_in[...]
    for p in range(count):
        dec = lows[p][:, width:]
        term = dot_rows(dec, dec)
        total = term if total is None else total + term
    gram[...] = total
    for h in range(2):
        value = None if first_call else acc_in[h]
        for p in range(count):
            term = dot(xs[h][p][...], lows[p][...])
            value = term if value is None else value + term
        acc[h] = value


def column(slot, i, per):
    return lambda g, m: (0, m[slot] * per + i)


def forward(pos, acc, gram, pieces, xs, rows, after=()):
    tokens = xs[0].shape[0]
    wide = pieces[0][0].shape[1]
    width = wide // 2
    count = len(pieces)
    ins = []
    if acc is not None:
        ins += [(acc, whole(acc.shape)), (gram, whole(gram.shape))]
    ins += [(low, whole(low.shape)) for low, _, _ in pieces]
    for x in xs:
        ins += [
            (x, once((tokens, low.shape[0]), column(slot, i, rows // low.shape[0])))
            for low, slot, i in pieces
        ]
    return call(
        functools.partial(forward_body, count, acc is None), "forward_rows", (pos,), ins,
        [(sds((2, tokens, wide), f32), whole((2, tokens, wide))), (sds((width, width), f32), whole((width, width)))],
        after=after,
    )


def finish_body(scale, count, steps, pos, acc_in, gram_in, cw, *refs):
    lows = refs[:count]
    xs = (refs[count:2 * count], refs[2 * count:3 * count])
    slopes, w_hi, w_lo, w_acc, g_hi, g_lo = refs[3 * count:]
    width = gram_in.shape[0]
    step = pl.program_id(0)

    @pl.when(step == 0)
    def _():
        gram = gram_in[...]
        for p in range(count):
            dec = lows[p][:, width:]
            gram = gram + dot_rows(dec, dec)
        hi = gram.astype(bf16)
        g_hi[...] = hi
        g_lo[...] = (gram - hi.astype(f32)).astype(bf16)
        w_acc[...] = jnp.zeros_like(w_acc)

    w_new = None
    for h in range(2):
        value = acc_in[h]
        for p in range(count):
            value = value + dot(xs[h][p][...], lows[p][...])
        pre = value[:, :width]
        sig = 0.5 + 0.5 * jnp.tanh(0.5 * pre)
        hidden = (pre * sig).astype(bf16)
        back = dot(hidden, g_hi[...]) + dot(hidden, g_lo[...]) - value[:, width:]
        weight = cw[h]
        slope = (weight * scale) * back * (sig * (1.0 + pre * (1.0 - sig)))
        counted = (weight * hidden.astype(f32)).astype(bf16)
        slopes[h, :, :width] = slope.astype(bf16)
        slopes[h, :, width:] = counted
        term = dot_rows(counted, hidden)
        w_new = term if w_new is None else w_new + term
    w_acc[...] += w_new

    @pl.when(step == steps - 1)
    def _():
        total = w_acc[...]
        hi = total.astype(bf16)
        w_hi[...] = hi
        w_lo[...] = (total - hi.astype(f32)).astype(bf16)


def finish(pos, acc, gram, cw, pieces, xs, rows, scale):
    tokens = xs[0].shape[0]
    wide = pieces[0][0].shape[1]
    width = wide // 2
    count = len(pieces)
    steps = 2
    tile = tokens // steps
    ins = [
        (acc, pl.BlockSpec((2, tile, wide), lambda g, m: (0, g, 0))),
        (gram, whole(gram.shape)),
        (cw, pl.BlockSpec((2, tile, 1), lambda g, m: (0, g, 0))),
    ]
    ins += [(low, whole(low.shape)) for low, _, _ in pieces]
    for x in xs:
        for low, slot, i in pieces:
            cr = low.shape[0]
            ins.append((x, pl.BlockSpec(
                (tile, cr), lambda g, m, slot=slot, i=i, per=rows // cr: (g, m[slot] * per + i))))
    square = (sds((width, width), bf16), whole((width, width)))
    return call(
        functools.partial(finish_body, scale, count, steps), "finish_slopes", (pos,), ins,
        [(sds((2, tokens, wide), bf16), pl.BlockSpec((2, tile, wide), lambda g, m: (0, g, 0))), square, square],
        grid=(steps,),
        scratch=[pltpu.VMEM((width, width), f32)] + [pltpu.VMEM((width, width), bf16)] * 2,
    )


def grad_body(scale, pos, x_own, x_par, slopes, w_hi, w_lo, low, out):
    width = w_hi.shape[0]
    both = dot_rows(x_own[...], slopes[0]) + dot_rows(x_par[...], slopes[1])
    dec = low[:, width:]
    grad_dec = scale * (dot(dec, w_hi[...]) + dot(dec, w_lo[...]) - both[:, width:])
    out[:, :width] = both[:, :width].astype(out.dtype)
    out[:, width:] = grad_dec.astype(out.dtype)


def grad_rows(pos, scale, slot, i, xs, rows, slopes, w_hi, w_lo, low, dtype, after=()):
    tokens = xs[0].shape[0]
    cr, wide = low.shape
    ins = [(x, once((tokens, cr), column(slot, i, rows // cr))) for x in xs]
    ins += [(a, whole(a.shape)) for a in (slopes, w_hi, w_lo, low)]
    return call(
        functools.partial(grad_body, scale), "grad_rows", (pos,), ins,
        [(sds((cr, wide), dtype), whole((cr, wide)))], after=after,
    )[0]


def adam_body(last, count, plan, own, *refs):
    got = refs[:count]
    theta, first, second = refs[count:3 + count]
    refs = refs[3 + count:]
    width = own.shape[1] // 2
    if last:
        theta_out, first_out, second_out = refs[-3:]
    else:
        anchor = refs[0]
        theta_out, first_out, second_out, low_out = refs[-4:]
        frag = fragment(plan)
    for k in range(2):
        grad = own[:, k * width:(k + 1) * width]
        for g in got:
            grad = grad + g[:, k * width:(k + 1) * width].astype(f32)
        one = beta_one * first[0, k] + (1.0 - beta_one) * grad
        two = beta_two * second[0, k] + (1.0 - beta_two) * grad * grad
        old = theta[0, k]
        new = old - inner_rate * (one / (jnp.sqrt(two) + adam_eps) + decay_rate * old)
        if not last:
            mixed = mix_share * new + (1.0 - mix_share) * anchor[...]
            new = jnp.where(frag == k, mixed, new)
            low_out[:, k * width:(k + 1) * width] = new.astype(bf16)
        theta_out[0, k] = new
        first_out[0, k] = one
        second_out[0, k] = two


def adam_rows(plan, i, cr, own, got, state, state_block, new_anc, prev, full):
    width = own.shape[1] // 2
    last = new_anc is None
    block = (1, 2, cr, width)
    ins = [(g, whole(g.shape)) for g in [own] + got]
    ins += [(s, once(block, lambda g, m: (0, 0, state_block, 0))) for s in state]
    aliases = {}
    if last:
        if prev is not None:
            for n, p in enumerate(prev):
                aliases[1 + len(ins)] = n
                ins.append((p, pl.BlockSpec(memory_space=pl.ANY)))
        outs = [(sds(full, f32), once(block, lambda g, m: (0, 0, i, 0)))] * 3
    else:
        ins.append((new_anc, once((cr, width), lambda g, m: (i, 0))))
        outs = [(sds(block, f32), whole(block))] * 3 + [(sds((cr, 2 * width), bf16), whole((cr, 2 * width)))]
    return call(
        functools.partial(adam_body, last, len(got)), "adam_rows", (plan,), ins, outs, aliases=aliases,
    )


def delta_body(pos, plan, anchor, theta, anchor_off, theta_off, keep, send):
    count = plan[pos[0]].astype(f32)
    keep[...] = count * (anchor[0] - theta[0, 0])
    send[...] = (count * (anchor_off[0] - theta_off[0, 0])).astype(bf16)


def add_body(final, plan, a, b, out):
    total = a[...].astype(f32) + b[...].astype(f32)
    if final:
        total = total / plan_sum(plan).astype(f32)
    out[...] = total.astype(bf16)


def outer_body(pos, plan, anchor, momentum, own, other, new_anc, anchor_out, momentum_out):
    half = own.shape[0]
    frag = fragment(plan)
    bit = lax.rem(pos[0], 2)
    anchor_out[...] = anchor[...]
    momentum_out[...] = momentum[...]
    for piece, where in ((own, bit), (other, 1 - bit)):
        at = pl.ds(pl.multiple_of(where * half, half), half)
        grad = piece[...].astype(f32)
        mom = outer_mu * momentum[frag, at, :] + grad
        anc = anchor[frag, at, :] - outer_rate * (grad + outer_mu * mom)
        new_anc[at, :] = anc
        anchor_out[frag, at, :] = anc
        momentum_out[frag, at, :] = mom


def outer_start(pos, plan, anchor, weights, after):
    _, rows, width = anchor.shape
    half = rows // 2

    def at(off):
        def anchor_at(g, p, q):
            return (fragment(q), lax.rem(p[0] + off, 2), 0)

        def theta_at(g, p, q):
            return (0, fragment(q), lax.rem(p[0] + off, 2), 0)

        return [(anchor, once((1, half, width), anchor_at)), (weights, once((1, 1, half, width), theta_at))]

    return call(
        delta_body, "delta_halves", (pos, plan), at(0) + at(1),
        [(sds((half, width), f32), whole((half, width))), (sds((half, width), bf16), whole((half, width)))],
        after=after,
    )


def outer_add(plan, a, b, final, after):
    return call(
        functools.partial(add_body, final), "add_halves", (plan,), [(a, whole(a.shape)), (b, whole(b.shape))],
        [(sds(a.shape, bf16), whole(a.shape))], after=after,
    )[0]


def outer_end(pos, plan, anchor, momentum, own, other):
    _, rows, width = anchor.shape
    return call(
        outer_body, "outer_step", (pos, plan),
        [(a, whole(a.shape)) for a in (anchor, momentum, own, other)],
        [(sds((rows, width), f32), whole((rows, width)))] + [(sds(anchor.shape, f32), whole(anchor.shape))] * 2,
    )


def local(n_rep, n_fsdp, inputs, kinds, weights, first_moment, second_moment, anchor, momentum, plan):
    tokens = inputs.shape[0]
    rows, width = weights.shape[2:]
    chips = n_fsdp // 2
    scale = 1.0 / math.sqrt(tokens * n_fsdp)
    chunks = max(1, min(4, rows // 256))
    cr = rows // chunks

    partner = [(f, f ^ 1) for f in range(n_fsdp)]
    to_partner = lambda a: lax.ppermute(a, "fsdp", partner)
    fetch = lambda a, s: lax.ppermute(
        a, "fsdp", [(((f // 2 + s) % chips) * 2 + f % 2, f) for f in range(n_fsdp)])
    give = lambda a, s: lax.ppermute(
        a, "fsdp", [(f, ((f // 2 + s) % chips) * 2 + f % 2) for f in range(n_fsdp)])
    across = lambda a, bit: lax.ppermute(a, "replica", [(r, r ^ bit) for r in range(n_rep)])

    blocks = [(i * cr, cr) for i in range(chunks)]
    low_own = list(cast_blocks(weights, blocks[:1], vmem=CAST_VMEM))
    if chunks > 1:
        low_own += list(cast_blocks(weights, blocks[1:], low_own, vmem=CAST_VMEM))

    chip = lax.axis_index("fsdp") // 2
    core = lax.axis_index("fsdp") % 2
    at = [((chip + s) % chips) * 2 for s in range(chips)]
    pos = jnp.stack([lax.axis_index("replica")] + [a + core for a in at] + [a + 1 - core for a in at]).astype(jnp.int32)

    x_par = to_partner(inputs)
    xs = (inputs, x_par)
    keep, send = outer_start(pos, plan, anchor, weights, after=[low_own[-1]])
    outer_in = across(send, 1)
    lanes = kinds.reshape(-1, 128)
    cw = call(
        weigh_body, "weigh_tokens", (),
        [(lanes, whole(lanes.shape)), (to_partner(lanes), whole(lanes.shape))],
        [(sds((2, tokens, 1), f32), whole((2, tokens, 1)))], after=[send],
    )[0]

    state = [(weights, first_moment, second_moment)] * chunks
    state_block = list(range(chunks))
    for step in range(INNER):
        last = step == INNER - 1
        far = [(i, s) for i in range(chunks) for s in range(1, chips)]
        low_far = {(i, s): fetch(low_own[i], s) for i, s in far}
        low_all = join_rows(low_own) if chunks > 1 else low_own[0]
        near = [(low_all, 1, 0), (to_partner(low_all), 1 + chips, 0)]
        acc, gram = forward(pos, None, None, near, xs, rows)

        if step == 0:
            bits = [1 << b for b in range(1, n_rep.bit_length() - 1)]
            own = keep
            took = outer_in
        wait_for = []
        pending = []
        for n, (i, s) in enumerate(far):
            handed = to_partner(relay(low_far[i, s], [acc] + wait_for))
            pending.append((low_far[i, s], 1 + s, i))
            if n > 0 or len(far) == 1:
                acc, gram = forward(pos, acc, gram, pending, xs, rows)
                pending = []
            pending.append((handed, 1 + chips + s, i))
            if step == 0 and bits and n in (0, len(far) - 2):
                own = outer_add(plan, own, took, False, [acc])
                took = across(own, bits.pop(0))
                wait_for = [own]
        slopes, w_hi, w_lo = finish(pos, acc, gram, cw, pending, xs, rows, scale)

        mine, got, sent = [], [], []
        for i in range(chunks):
            now = []
            for s in range(1, chips):
                now.append(grad_rows(
                    pos, scale, 1 + s, i, xs, rows, slopes, w_hi, w_lo, low_far[i, s], bf16, after=sent[-1:]))
                sent.append(now[-1])
            got.append([give(g, s) for s, g in enumerate(now, 1)])
        for i in range(chunks):
            mine.append(grad_rows(
                pos, scale, 1, i, xs, rows, slopes, w_hi, w_lo, low_own[i], f32, after=(sent + mine)[-1:]))
        if step == 0:
            while bits:
                own = outer_add(plan, own, took, False, sent[-1:])
                took = across(own, bits.pop(0))
            own = outer_add(plan, own, took, True, mine[-1:])
            new_anc, anchor_out, momentum_out = outer_end(pos, plan, anchor, momentum, own, across(own, 1))

        new_state, new_low, prev = [], [], None
        for i in range(chunks):
            res = adam_rows(
                plan, i, cr, mine[i], got[i], state[i], state_block[i],
                None if last else new_anc, prev, weights.shape,
            )
            if last:
                prev = res
            else:
                new_state.append(tuple(res[:3]))
                new_low.append(res[3])
        state, state_block, low_own = new_state, [0] * chunks, new_low
    return (*prev, anchor_out, momentum_out)


def solution(mesh):
    return jax.shard_map(
        functools.partial(local, mesh.shape["replica"], mesh.shape["fsdp"]),
        mesh=mesh,
        in_specs=(
            P(("replica", "fsdp"), None),
            P(("replica", "fsdp")),
            P("replica", None, "fsdp", None),
            P("replica", None, "fsdp", None),
            P("replica", None, "fsdp", None),
            P(None, "fsdp", None),
            P(None, "fsdp", None),
            P(),
        ),
        out_specs=(
            P("replica", None, "fsdp", None),
            P("replica", None, "fsdp", None),
            P("replica", None, "fsdp", None),
            P(None, "fsdp", None),
            P(None, "fsdp", None),
        ),
        check_vma=False,
    )
```

```python
import functools
import math

import jax
import jax.numpy as jnp
from jax import lax
from jax.experimental import pallas as pl
from jax.experimental.pallas import tpu as pltpu
from jax.sharding import PartitionSpec as P

INNER = 2

inner_rate = 0.003
beta_one = 0.9
beta_two = 0.95
adam_eps = 1e-08
decay_rate = 0.1
outer_rate = 0.7
outer_mu = 0.9
mix_share = 0.5

bf16 = jnp.bfloat16
f32 = jnp.float32
VMEM_LIMIT = 16 * 1024 * 1024


def token_weight(kinds):
    return jnp.where(kinds == 2, 1.0, jnp.where(kinds == 1, 0.25, 0.0)).astype(f32)


def dot(a, b):
    return jnp.dot(a, b, preferred_element_type=f32)


def dot_rows(a, b):
    return lax.dot_general(a, b, (((0,), (0,)), ((), ())), preferred_element_type=f32)


def once(shape, index):
    return pl.BlockSpec(shape, index, pipeline_mode=pl.Buffered(1))


def whole(shape):
    return once(shape, lambda *_: (0,) * len(shape))


def sds(shape, dtype):
    return jax.ShapeDtypeStruct(shape, dtype)


def call(body, name, meta, ins, outs, grid=(1,), scratch=(), aliases=None, flops=0, after=()):
    arrays = [a for a, _ in ins] + list(after)
    n_in = len(meta) + len(ins)
    moved = sum(math.prod(o.shape) * o.dtype.itemsize for o, _ in outs)
    moved += sum(math.prod(s.block_shape or a.shape) * a.dtype.itemsize for a, s in ins)

    def run(*refs):
        body(*refs[:n_in], *refs[n_in + len(after):])

    return pl.pallas_call(
        run,
        name=name,
        out_shape=[o for o, _ in outs],
        grid_spec=pltpu.PrefetchScalarGridSpec(
            num_scalar_prefetch=len(meta),
            grid=grid,
            in_specs=[s for _, s in ins] + [pl.BlockSpec(memory_space=pl.ANY)] * len(after),
            out_specs=[s for _, s in outs],
            scratch_shapes=list(scratch),
        ),
        input_output_aliases=aliases or {},
        compiler_params=pltpu.CompilerParams(vmem_limit_bytes=VMEM_LIMIT),
        cost_estimate=pl.CostEstimate(flops=flops, bytes_accessed=moved, transcendentals=0),
    )(*meta, *arrays)


def plan_sum(plan):
    total = plan[0]
    for r in range(1, plan.shape[0]):
        total = total + plan[r]
    return total


def fragment(plan):
    return lax.rem(plan_sum(plan), 2)


def cast_body(theta, low):
    width = theta.shape[3]
    for k in range(2):
        low[:, k * width:(k + 1) * width] = theta[0, k].astype(bf16)


def cast_rows(weights):
    _, _, rows, width = weights.shape
    return call(
        cast_body, "cast_rows", (), [(weights, whole(weights.shape))],
        [(sds((rows, 2 * width), bf16), whole((rows, 2 * width)))],
    )[0]


def weigh_body(own, other, out):
    for h, kinds in enumerate((own, other)):
        lanes = kinds.shape[0]
        pad = jnp.zeros((8 - lanes % 8, 128), f32)
        value = token_weight(kinds[...])
        if lanes % 8:
            value = jnp.concatenate([value, pad], 0)
        turned = value.T
        for j in range(lanes):
            out[h, j * 128:(j + 1) * 128, :] = turned[:, j:j + 1]


def copy_body(x, out):
    out[...] = x[...]


def relay(x, after):
    return call(copy_body, "relay_rows", (), [(x, whole(x.shape))], [(sds(x.shape, x.dtype), whole(x.shape))], after=after)[0]


def turn_body(pos, x, xt):
    xt[...] = x[...].T


def turn(pos, x, chips, rows):
    tokens = x.shape[0]
    tile = min(256, tokens)
    return call(
        turn_body, "turn_tokens", (pos,),
        [(x, pl.BlockSpec((tile, rows), lambda s, t, m: (t, m[1 + s])))],
        [(sds((chips * rows, tokens), bf16), pl.BlockSpec((rows, tile), lambda s, t, m: (s, t)))],
        grid=(chips, tokens // tile),
    )[0]


def forward_body(count, tile, first_call, pos, *refs):
    if first_call:
        acc_in = gram_in = None
    else:
        acc_in, gram_in, refs = refs[0], refs[1], refs[2:]
    lows = refs[:count]
    xs = (refs[count:2 * count], refs[2 * count:3 * count])
    acc, gram = refs[3 * count:]
    width = gram.shape[0]
    step = pl.program_id(0)
    at = pl.ds(pl.multiple_of(step * tile, tile), tile)

    @pl.when(step == 0)
    def _():
        total = None if first_call else gram_in[...]
        for p in range(count):
            dec = lows[p][:, width:]
            term = dot_rows(dec, dec)
            total = term if total is None else total + term
        gram[...] = total

    for h in range(2):
        value = None if first_call else acc_in[h, at, :]
        for p in range(count):
            term = dot(xs[h][p][...], lows[p][...])
            value = term if value is None else value + term
        acc[h, at, :] = value


def column(slot):
    return lambda g, m: (g, m[slot])


def token_blocks(x, tile, pieces):
    return [(x, pl.BlockSpec((tile, low.shape[0]), column(slot))) for low, slot in pieces]


def forward(pos, acc, gram, pieces, xs, after=()):
    tokens = xs[0].shape[0]
    tile = min(128, tokens)
    wide = pieces[0][0].shape[1]
    width = wide // 2
    ins = []
    if acc is not None:
        ins += [(acc, whole(acc.shape)), (gram, whole(gram.shape))]
    ins += [(low, whole(low.shape)) for low, _ in pieces]
    for x in xs:
        ins += token_blocks(x, tile, pieces)
    return call(
        functools.partial(forward_body, len(pieces), tile, acc is None), "forward_rows", (pos,), ins,
        [(sds((2, tokens, wide), f32), whole((2, tokens, wide))), (sds((width, width), f32), whole((width, width)))],
        grid=(tokens // tile,), after=after,
    )


def finish_body(scale, tile, count, steps, pos, acc_in, gram_in, cw, *refs):
    lows = refs[:count]
    xs = (refs[count:2 * count], refs[2 * count:3 * count])
    slopes, w_hi, w_lo, w_acc, g_hi, g_lo = refs[3 * count:]
    width = gram_in.shape[0]
    step = pl.program_id(0)
    at = pl.ds(pl.multiple_of(step * tile, tile), tile)

    @pl.when(step == 0)
    def _():
        gram = gram_in[...]
        for p in range(count):
            dec = lows[p][:, width:]
            gram = gram + dot_rows(dec, dec)
        hi = gram.astype(bf16)
        g_hi[...] = hi
        g_lo[...] = (gram - hi.astype(f32)).astype(bf16)
        w_acc[...] = jnp.zeros_like(w_acc)

    total = w_acc[...]
    for h in range(2):
        value = acc_in[h, at, :]
        for p in range(count):
            value = value + dot(xs[h][p][...], lows[p][...])
        pre = value[:, :width]
        sig = 0.5 + 0.5 * jnp.tanh(0.5 * pre)
        hidden = (pre * sig).astype(bf16)
        back = dot(hidden, g_hi[...]) + dot(hidden, g_lo[...]) - value[:, width:]
        weight = cw[h, at, :]
        slope = (weight * scale) * back * (sig * (1.0 + pre * (1.0 - sig)))
        counted = (weight * hidden.astype(f32)).astype(bf16)
        slopes[h, at, :width] = slope.astype(bf16)
        slopes[h, at, width:] = counted
        total = total + dot_rows(counted, hidden)
    w_acc[...] = total

    @pl.when(step == steps - 1)
    def _():
        hi = total.astype(bf16)
        w_hi[...] = hi
        w_lo[...] = (total - hi.astype(f32)).astype(bf16)


def finish(pos, acc, gram, cw, pieces, xs, scale):
    tokens = xs[0].shape[0]
    tile = min(256, tokens)
    wide = pieces[0][0].shape[1]
    width = wide // 2
    ins = [(a, whole(a.shape)) for a in [acc, gram, cw] + [low for low, _ in pieces]]
    for x in xs:
        ins += token_blocks(x, tile, pieces)
    square = (sds((width, width), bf16), whole((width, width)))
    return call(
        functools.partial(finish_body, scale, tile, len(pieces), tokens // tile), "finish_slopes", (pos,), ins,
        [(sds((2, tokens, wide), bf16), whole((2, tokens, wide))), square, square],
        grid=(tokens // tile,),
        scratch=[pltpu.VMEM((width, width), f32)] + [pltpu.VMEM((width, width), bf16)] * 2,
    )


def grad_body(scale, off, xt_own, xt_par, slopes, w_hi, w_lo, low, out):
    width = w_hi.shape[0]
    both = dot(xt_own[...], slopes[0]) + dot(xt_par[...], slopes[1])
    dec = low[off:off + out.shape[0], width:]
    grad_dec = scale * (dot(dec, w_hi[...]) + dot(dec, w_lo[...]) - both[:, width:])
    out[:, :width] = both[:, :width].astype(out.dtype)
    out[:, width:] = grad_dec.astype(out.dtype)


def grad_rows(scale, s, i, cr, xt, slopes, w_hi, w_lo, low, dtype, after=()):
    tokens = xt[0].shape[1]
    rows, wide = low.shape
    block = s * (rows // cr) + i
    ins = [(x, once((cr, tokens), lambda g: (block, 0))) for x in xt]
    ins += [(a, whole(a.shape)) for a in (slopes, w_hi, w_lo, low)]
    return call(
        functools.partial(grad_body, scale, i * cr), "grad_rows", (), ins,
        [(sds((cr, wide), dtype), whole((cr, wide)))], after=after,
    )[0]


def adam_body(last, count, plan, own, *refs):
    got = refs[:count]
    theta, first, second = refs[count:3 + count]
    anchor = refs[3 + count]
    theta_out, first_out, second_out = refs[-3:]
    width = own.shape[1] // 2
    for k in range(2):
        grad = own[:, k * width:(k + 1) * width]
        for g in got:
            grad = grad + g[:, k * width:(k + 1) * width].astype(f32)
        one = beta_one * first[0, k] + (1.0 - beta_one) * grad
        two = beta_two * second[0, k] + (1.0 - beta_two) * grad * grad
        old = theta[0, k]
        if last:
            old = mixed(plan, k, old, anchor[...])
        theta_out[0, k] = old - inner_rate * (one / (jnp.sqrt(two) + adam_eps) + decay_rate * old)
        first_out[0, k] = one
        second_out[0, k] = two


def mixed(plan, k, theta, anchor):
    return jnp.where(fragment(plan) == k, mix_share * theta + (1.0 - mix_share) * anchor, theta)


def adam_rows(plan, i, cr, own, got, state, state_block, new_anc, prev, full):
    width = own.shape[1] // 2
    last = new_anc is not None
    block = (1, 2, cr, width)
    ins = [(g, whole(g.shape)) for g in [own] + got]
    ins += [(s, once(block, lambda g, m: (0, 0, state_block, 0))) for s in state]
    aliases = {}
    if last:
        ins.append((new_anc, once((cr, width), lambda g, m: (i, 0))))
        if prev is not None:
            for n, p in enumerate(prev):
                aliases[1 + len(ins)] = n
                ins.append((p, pl.BlockSpec(memory_space=pl.ANY)))
        outs = [(sds(full, f32), once(block, lambda g, m: (0, 0, i, 0)))] * 3
    else:
        outs = [(sds(block, f32), whole(block))] * 3
    return call(
        functools.partial(adam_body, last, len(got)), "adam_rows", (plan,), ins, outs, aliases=aliases,
    )


def quarter(pos, m, size):
    where = jnp.bitwise_xor(lax.rem(pos[0], 4), m)
    return pl.ds(pl.multiple_of(where * size, size), size)


def delta_body(pos, plan, anchor, theta, *outs):
    count = plan[pos[0]].astype(f32)
    for m, out in enumerate(outs):
        at = quarter(pos, m, out.shape[0])
        out[...] = (count * (anchor[0, at, :] - theta[0, 0, at, :])).astype(out.dtype)


def outer_start(pos, plan, anchor, weights, after):
    _, rows, width = anchor.shape
    part = (rows // 4, width)
    return call(
        delta_body, "delta_quarters", (pos, plan),
        [
            (anchor, once((1, rows, width), lambda g, p, q: (fragment(q), 0, 0))),
            (weights, once((1, 1, rows, width), lambda g, p, q: (0, fragment(q), 0, 0))),
        ],
        [(sds(part, f32), whole(part))] + [(sds(part, bf16), whole(part))] * 3, after=after,
    )


def add_body(final, plan, *refs):
    total = refs[0][...].astype(f32)
    for r in refs[1:-1]:
        total = total + r[...].astype(f32)
    if final:
        total = total / plan_sum(plan).astype(f32)
    refs[-1][...] = total.astype(bf16)


def outer_add(plan, parts, final):
    shape = parts[0].shape
    return call(
        functools.partial(add_body, final), "add_quarters", (plan,), [(a, whole(shape)) for a in parts],
        [(sds(shape, bf16), whole(shape))],
    )[0]


def outer_update(frag, at, anchor, momentum, grad):
    mom = outer_mu * momentum[frag, at, :] + grad
    return anchor[frag, at, :] - outer_rate * (grad + outer_mu * mom), mom


def mix_body(count, pos, plan, anchor, momentum, *refs):
    quarters, thetas = refs[:4], refs[4:4 + count]
    new_anc, low = refs[-2:]
    frag = fragment(plan)
    for m, piece in enumerate(quarters):
        at = quarter(pos, m, piece.shape[0])
        new_anc[at, :] = outer_update(frag, at, anchor, momentum, piece[...].astype(f32))[0]
    cr, width = thetas[0].shape[2:]
    for i, theta in enumerate(thetas):
        for k in range(2):
            value = mixed(plan, k, theta[0, k], new_anc[i * cr:(i + 1) * cr, :])
            low[i * cr:(i + 1) * cr, k * width:(k + 1) * width] = value.astype(bf16)


def outer_mix(pos, plan, anchor, momentum, quarters, thetas):
    _, rows, width = anchor.shape
    return call(
        functools.partial(mix_body, len(thetas)), "mix_rows", (pos, plan),
        [(a, whole(a.shape)) for a in [anchor, momentum] + quarters + thetas],
        [(sds((rows, width), f32), whole((rows, width))), (sds((rows, 2 * width), bf16), whole((rows, 2 * width)))],
    )


def outer_body(pos, plan, anchor, momentum, *refs):
    quarters = refs[:4]
    anchor_out, momentum_out = refs[4:]
    frag = fragment(plan)
    anchor_out[...] = anchor[...]
    momentum_out[...] = momentum[...]
    for m, piece in enumerate(quarters):
        at = quarter(pos, m, piece.shape[0])
        anc, mom = outer_update(frag, at, anchor, momentum, piece[...].astype(f32))
        anchor_out[frag, at, :] = anc
        momentum_out[frag, at, :] = mom


def outer_end(pos, plan, anchor, momentum, quarters, after):
    return call(
        outer_body, "outer_step", (pos, plan),
        [(a, whole(a.shape)) for a in [anchor, momentum] + quarters],
        [(sds(anchor.shape, f32), whole(anchor.shape))] * 2, after=after,
    )


def local(n_rep, n_fsdp, inputs, kinds, weights, first_moment, second_moment, anchor, momentum, plan):
    tokens = inputs.shape[0]
    rows, width = weights.shape[2:]
    chips = n_fsdp // 2
    scale = 1.0 / math.sqrt(tokens * n_fsdp)
    chunks = max(1, min(4, rows // 256))
    cr = rows // chunks

    partner = [(f, f ^ 1) for f in range(n_fsdp)]
    to_partner = lambda a: lax.ppermute(a, "fsdp", partner)
    fetch = lambda a, s: lax.ppermute(
        a, "fsdp", [(((f // 2 + s) % chips) * 2 + f % 2, f) for f in range(n_fsdp)])
    give = lambda a, s: lax.ppermute(
        a, "fsdp", [(f, ((f // 2 + s) % chips) * 2 + f % 2) for f in range(n_fsdp)])
    across = lambda a, bit: lax.ppermute(a, "replica", [(r, r ^ bit) for r in range(n_rep)])

    blocks = [(i * cr, cr) for i in range(chunks)]
    low_own = cast_rows(weights)

    chip = lax.axis_index("fsdp") // 2
    core = lax.axis_index("fsdp") % 2
    at = [((chip + s) % chips) * 2 for s in range(chips)]
    pos = jnp.stack([lax.axis_index("replica")] + [a + core for a in at] + [a + 1 - core for a in at]).astype(jnp.int32)

    x_par = to_partner(inputs)
    xs = (inputs, x_par)
    lanes = kinds.reshape(-1, 128)
    cw = call(
        weigh_body, "weigh_tokens", (),
        [(lanes, whole(lanes.shape)), (to_partner(lanes), whole(lanes.shape))],
        [(sds((2, tokens, 1), f32), whole((2, tokens, 1)))], after=[low_own],
    )[0]

    parts = outer_start(pos, plan, anchor, weights, [low_own])
    own = outer_add(plan, [parts[0]] + [across(parts[m], m) for m in range(1, 4)], n_rep == 4)
    bit = 4
    while bit < n_rep:
        own = outer_add(plan, [own, across(own, bit)], 2 * bit == n_rep)
        bit *= 2
    xt = [turn(pos, x, chips, rows) for x in xs]

    ready = [cw, own] + xt
    state = [(weights, first_moment, second_moment)] * chunks
    state_block = list(range(chunks))
    new_anc = None
    for step in range(INNER):
        last = step == INNER - 1
        low_far = {s: fetch(low_own, s) for s in range(1, chips)}
        near = [(low_own, 1), (to_partner(low_own), 1 + chips)]
        acc, gram = forward(pos, None, None, near, xs)
        far = [(low_far[s], 1 + s) for s in low_far]
        handed = [(to_partner(relay(low, [acc] + ready)), slot + chips) for low, slot in far]
        acc, gram = forward(pos, acc, gram, far, xs)
        slopes, w_hi, w_lo = finish(pos, acc, gram, cw, handed, xs, scale)

        mine, got, sent = [], [], []
        for i in range(chunks):
            now = []
            for s in low_far:
                now.append(grad_rows(
                    scale, s, i, cr, xt, slopes, w_hi, w_lo, low_far[s], bf16, after=sent[-1:]))
                sent.append(now[-1])
            got.append([give(g, s) for s, g in zip(low_far, now)])
        for i in range(chunks):
            mine.append(grad_rows(
                scale, 0, i, cr, xt, slopes, w_hi, w_lo, low_own, f32, after=(sent + mine)[-1:]))

        new_state, prev = [], None
        for i in range(chunks):
            res = adam_rows(
                plan, i, cr, mine[i], got[i], state[i], state_block[i], new_anc, prev, weights.shape)
            if last:
                prev = res
            else:
                new_state.append(tuple(res))
        if not last:
            quarters = [own] + [across(own, m) for m in range(1, 4)]
            new_anc, low_own = outer_mix(pos, plan, anchor, momentum, quarters, [t for t, _, _ in new_state])
            anchor_out, momentum_out = outer_end(pos, plan, anchor, momentum, quarters, [low_own])
            ready = [anchor_out]
            state, state_block = new_state, [0] * chunks
    return (*prev, anchor_out, momentum_out)


def solution(mesh):
    return jax.shard_map(
        functools.partial(local, mesh.shape["replica"], mesh.shape["fsdp"]),
        mesh=mesh,
        in_specs=(
            P(("replica", "fsdp"), None),
            P(("replica", "fsdp")),
            P("replica", None, "fsdp", None),
            P("replica", None, "fsdp", None),
            P("replica", None, "fsdp", None),
            P(None, "fsdp", None),
            P(None, "fsdp", None),
            P(),
        ),
        out_specs=(
            P("replica", None, "fsdp", None),
            P("replica", None, "fsdp", None),
            P("replica", None, "fsdp", None),
            P(None, "fsdp", None),
            P(None, "fsdp", None),
        ),
        check_vma=False,
    )
```

```python
import functools
import math

import jax
import jax.numpy as jnp
from jax import lax
from jax.experimental import pallas as pl
from jax.experimental.pallas import tpu as pltpu
from jax.sharding import PartitionSpec as P

INNER = 2

inner_rate = 0.003
beta_one = 0.9
beta_two = 0.95
adam_eps = 1e-08
decay_rate = 0.1
outer_rate = 0.7
outer_mu = 0.9
mix_share = 0.5

bf16 = jnp.bfloat16
f32 = jnp.float32
VMEM_LIMIT = 12 * 1024 * 1024


def token_weight(kinds):
    return jnp.where(kinds == 2, 1.0, jnp.where(kinds == 1, 0.25, 0.0)).astype(f32)


def dot(a, b):
    return jnp.dot(a, b, preferred_element_type=f32)


def dot_rows(a, b):
    return lax.dot_general(a, b, (((0,), (0,)), ((), ())), preferred_element_type=f32)


def once(shape, index):
    return pl.BlockSpec(shape, index, pipeline_mode=pl.Buffered(1))


def whole(shape):
    return once(shape, lambda *_: (0,) * len(shape))


def sds(shape, dtype):
    return jax.ShapeDtypeStruct(shape, dtype)


def call(body, name, meta, ins, outs, grid=(1,), scratch=(), aliases=None, flops=0, after=()):
    arrays = [a for a, _ in ins] + list(after)
    n_in = len(meta) + len(ins)
    moved = sum(math.prod(o.shape) * o.dtype.itemsize for o, _ in outs)
    moved += sum(math.prod(s.block_shape or a.shape) * a.dtype.itemsize for a, s in ins)

    def run(*refs):
        body(*refs[:n_in], *refs[n_in + len(after):])

    return pl.pallas_call(
        run,
        name=name,
        out_shape=[o for o, _ in outs],
        grid_spec=pltpu.PrefetchScalarGridSpec(
            num_scalar_prefetch=len(meta),
            grid=grid,
            in_specs=[s for _, s in ins] + [pl.BlockSpec(memory_space=pl.ANY)] * len(after),
            out_specs=[s for _, s in outs],
            scratch_shapes=list(scratch),
        ),
        input_output_aliases=aliases or {},
        compiler_params=pltpu.CompilerParams(vmem_limit_bytes=VMEM_LIMIT),
        cost_estimate=pl.CostEstimate(flops=flops, bytes_accessed=moved, transcendentals=0),
    )(*meta, *arrays)


def plan_sum(plan):
    total = plan[0]
    for r in range(1, plan.shape[0]):
        total = total + plan[r]
    return total


def fragment(plan):
    return lax.rem(plan_sum(plan), 2)


def cast_body(theta, *lows):
    sub, wide = lows[0].shape
    width = wide // 2
    for j, low in enumerate(lows):
        for k in range(2):
            low[:, k * width:(k + 1) * width] = theta[0, k, j * sub:(j + 1) * sub, :].astype(bf16)


def cast_rows(weights, parts):
    _, _, rows, width = weights.shape
    shape = (rows // parts, 2 * width)
    return call(
        cast_body, "cast_rows", (), [(weights, whole(weights.shape))],
        [(sds(shape, bf16), whole(shape))] * parts,
    )


def weigh_body(own, other, out):
    for h, kinds in enumerate((own, other)):
        lanes = kinds.shape[0]
        pad = jnp.zeros((8 - lanes % 8, 128), f32)
        value = token_weight(kinds[...])
        if lanes % 8:
            value = jnp.concatenate([value, pad], 0)
        turned = value.T
        for j in range(lanes):
            out[h, j * 128:(j + 1) * 128, :] = turned[:, j:j + 1]


def copy_body(x, out):
    out[...] = x[...]


def relay(x, after):
    return call(copy_body, "relay_rows", (), [(x, whole(x.shape))], [(sds(x.shape, x.dtype), whole(x.shape))], after=after)[0]


def turn_body(pos, x, xt):
    xt[...] = x[...].T


def turn(pos, x, chips, rows):
    tokens = x.shape[0]
    tile = min(256, tokens)
    return call(
        turn_body, "turn_tokens", (pos,),
        [(x, pl.BlockSpec((tile, rows), lambda s, t, m: (t, m[1 + s])))],
        [(sds((chips * rows, tokens), bf16), pl.BlockSpec((rows, tile), lambda s, t, m: (s, t)))],
        grid=(chips, tokens // tile),
    )[0]


def forward_body(offs, first_call, pos, *refs):
    count = len(offs)
    if first_call:
        acc_in = gram_in = None
    else:
        acc_in, gram_in, refs = refs[0], refs[1], refs[2:]
    lows, xs = refs[:count], refs[count:count + 2]
    acc, gram = refs[count + 2:]
    width = gram.shape[0]

    def step(n):
        low = lows[n][pl.ds(offs[n], xs[0].shape[1]), :]
        term = dot_rows(low[:, width:], low[:, width:])
        prods = [dot(x[...], low) for x in xs]
        if n > 0:
            gram[...] += term
            for h in range(2):
                acc[h] += prods[h]
        elif first_call:
            gram[...] = term
            for h in range(2):
                acc[h] = prods[h]
        else:
            gram[...] = gram_in[...] + term
            for h in range(2):
                acc[h] = acc_in[h] + prods[h]

    for n in range(count):
        pl.when(pl.program_id(0) == n)(functools.partial(step, n))


def token_blocks(xs, pieces, sub):

    def column(g, m):
        at = 0
        for n, (_, _, slot, part) in enumerate(pieces):
            per = xs[0].shape[1] // (m.shape[0] - 1) // sub
            at = jnp.where(g == n, m[slot] * per + part, at)
        return (0, at)

    return [(x, pl.BlockSpec((x.shape[0], sub), column)) for x in xs]


def forward(pos, acc, gram, pieces, xs, sub, after=()):
    tokens = xs[0].shape[0]
    wide = pieces[0][0].shape[1]
    width = wide // 2
    ins = []
    if acc is not None:
        ins += [(acc, whole(acc.shape)), (gram, whole(gram.shape))]
    ins += [(low, whole(low.shape)) for low, _, _, _ in pieces]
    return call(
        functools.partial(forward_body, [off for _, off, _, _ in pieces], acc is None), "forward_rows", (pos,),
        ins + token_blocks(xs, pieces, sub),
        [(sds((2, tokens, wide), f32), whole((2, tokens, wide))), (sds((width, width), f32), whole((width, width)))],
        grid=(len(pieces),), after=after,
    )


def finish_body(scale, tile, offs, pos, acc_in, gram_in, cw, *refs):
    count = len(offs)
    lows, xs = refs[:count], refs[count:count + 2]
    slopes, w_hi, w_lo, acc, gram = refs[count + 2:]
    width = gram_in.shape[0]

    def step(n):
        low = lows[n][pl.ds(offs[n], xs[0].shape[1]), :]
        term = dot_rows(low[:, width:], low[:, width:])
        before = (acc_in, gram_in) if n == 0 else (acc, gram)
        gram[...] = before[1][...] + term
        for h in range(2):
            acc[h] = before[0][h] + dot(xs[h][...], low)

    for n in range(count):
        pl.when(pl.program_id(0) == n)(functools.partial(step, n))

    @pl.when(pl.program_id(0) == count - 1)
    def _():
        g_all = gram[...]
        g_hi = g_all.astype(bf16)
        g_lo = (g_all - g_hi.astype(f32)).astype(bf16)
        total = None
        for h in range(2):
            for t in range(0, acc.shape[1], tile):
                at = pl.ds(t, tile)
                pre = acc[h, at, :width]
                sig = 0.5 + 0.5 * jnp.tanh(0.5 * pre)
                hidden = (pre * sig).astype(bf16)
                back = dot(hidden, g_hi) + dot(hidden, g_lo) - acc[h, at, width:]
                weight = cw[h, at, :]
                slope = (weight * scale) * back * (sig * (1.0 + pre * (1.0 - sig)))
                counted = (weight * hidden.astype(f32)).astype(bf16)
                slopes[h, at, :width] = slope.astype(bf16)
                slopes[h, at, width:] = counted
                term = dot_rows(counted, hidden)
                total = term if total is None else total + term
        hi = total.astype(bf16)
        w_hi[...] = hi
        w_lo[...] = (total - hi.astype(f32)).astype(bf16)


def finish(pos, acc, gram, cw, pieces, xs, sub, scale):
    tokens = xs[0].shape[0]
    wide = pieces[0][0].shape[1]
    width = wide // 2
    ins = [(a, whole(a.shape)) for a in [acc, gram, cw] + [low for low, _, _, _ in pieces]]
    square = (sds((width, width), bf16), whole((width, width)))
    return call(
        functools.partial(finish_body, scale, min(256, tokens), [off for _, off, _, _ in pieces]), "finish_slopes", (pos,),
        ins + token_blocks(xs, pieces, sub),
        [(sds((2, tokens, wide), bf16), whole((2, tokens, wide))), square, square],
        grid=(len(pieces),),
        scratch=[pltpu.VMEM((2, tokens, wide), f32), pltpu.VMEM((width, width), f32)],
    )


def grad_body(scale, off, xt_own, xt_par, slopes, w_hi, w_lo, low, out):
    width = w_hi.shape[0]
    both = dot(xt_own[...], slopes[0]) + dot(xt_par[...], slopes[1])
    dec = low[off:off + out.shape[0], width:]
    grad_dec = scale * (dot(dec, w_hi[...]) + dot(dec, w_lo[...]) - both[:, width:])
    out[:, :width] = both[:, :width].astype(out.dtype)
    out[:, width:] = grad_dec.astype(out.dtype)


def grad_rows(scale, s, i, cr, xt, slopes, w_hi, w_lo, lows, dtype, after=()):
    tokens = xt[0].shape[1]
    sub, wide = lows[0].shape
    low = lows[i * cr // sub]
    block = s * (sub * len(lows) // cr) + i
    ins = [(x, once((cr, tokens), lambda g: (block, 0))) for x in xt]
    ins += [(a, whole(a.shape)) for a in (slopes, w_hi, w_lo, low)]
    return call(
        functools.partial(grad_body, scale, i * cr % sub), "grad_rows", (), ins,
        [(sds((cr, wide), dtype), whole((cr, wide)))], after=after,
    )[0]


def adam_body(last, count, plan, own, *refs):
    got = refs[:count]
    theta, first, second = refs[count:3 + count]
    anchor = refs[3 + count]
    theta_out, first_out, second_out = refs[-3:]
    width = own.shape[1] // 2
    for k in range(2):
        grad = own[:, k * width:(k + 1) * width]
        for g in got:
            grad = grad + g[:, k * width:(k + 1) * width].astype(f32)
        one = beta_one * first[0, k] + (1.0 - beta_one) * grad
        two = beta_two * second[0, k] + (1.0 - beta_two) * grad * grad
        old = theta[0, k]
        if last:
            old = mixed(plan, k, old, anchor[...])
        theta_out[0, k] = old - inner_rate * (one / (jnp.sqrt(two) + adam_eps) + decay_rate * old)
        first_out[0, k] = one
        second_out[0, k] = two


def mixed(plan, k, theta, anchor):
    return jnp.where(fragment(plan) == k, mix_share * theta + (1.0 - mix_share) * anchor, theta)


def adam_rows(plan, i, cr, own, got, state, state_block, new_anc, prev, full, after=()):
    width = own.shape[1] // 2
    last = new_anc is not None
    block = (1, 2, cr, width)
    ins = [(g, whole(g.shape)) for g in [own] + got]
    ins += [(s, once(block, lambda g, m: (0, 0, state_block, 0))) for s in state]
    aliases = {}
    if last:
        ins.append((new_anc, once((cr, width), lambda g, m: (i, 0))))
        if prev is not None:
            for n, p in enumerate(prev):
                aliases[1 + len(ins)] = n
                ins.append((p, pl.BlockSpec(memory_space=pl.ANY)))
        outs = [(sds(full, f32), once(block, lambda g, m: (0, 0, i, 0)))] * 3
    else:
        outs = [(sds(block, f32), whole(block))] * 3
    return call(
        functools.partial(adam_body, last, len(got)), "adam_rows", (plan,), ins, outs, aliases=aliases,
        after=after,
    )


def quarter(pos, m, size):
    where = jnp.bitwise_xor(lax.rem(pos[0], 4), m)
    return pl.ds(pl.multiple_of(where * size, size), size)


def delta_body(pos, plan, anchor, theta, *outs):
    count = plan[pos[0]].astype(f32)
    for m, out in enumerate(outs):
        at = quarter(pos, m, out.shape[0])
        out[...] = (count * (anchor[0, at, :] - theta[0, 0, at, :])).astype(out.dtype)


def outer_start(pos, plan, anchor, weights, after):
    _, rows, width = anchor.shape
    part = (rows // 4, width)
    return call(
        delta_body, "delta_quarters", (pos, plan),
        [
            (anchor, once((1, rows, width), lambda g, p, q: (fragment(q), 0, 0))),
            (weights, once((1, 1, rows, width), lambda g, p, q: (0, fragment(q), 0, 0))),
        ],
        [(sds(part, f32), whole(part))] + [(sds(part, bf16), whole(part))] * 3, after=after,
    )


def add_body(final, plan, *refs):
    total = refs[0][...].astype(f32)
    for r in refs[1:-1]:
        total = total + r[...].astype(f32)
    if final:
        total = total / plan_sum(plan).astype(f32)
    refs[-1][...] = total.astype(bf16)


def outer_add(plan, parts, final, after=()):
    shape = parts[0].shape
    return call(
        functools.partial(add_body, final), "add_quarters", (plan,), [(a, whole(shape)) for a in parts],
        [(sds(shape, bf16), whole(shape))], after=after,
    )[0]


def outer_update(frag, at, anchor, momentum, grad):
    mom = outer_mu * momentum[frag, at, :] + grad
    return anchor[frag, at, :] - outer_rate * (grad + outer_mu * mom), mom


def new_anchor_body(pos, plan, anchor, momentum, *refs):
    for m, piece in enumerate(refs[:4]):
        at = quarter(pos, m, piece.shape[0])
        refs[4][at, :] = outer_update(0, at, anchor, momentum, piece[...].astype(f32))[0]


def outer_anchor(pos, plan, anchor, momentum, quarters, after):
    _, rows, width = anchor.shape
    part = once((1, rows, width), lambda g, p, q: (fragment(q), 0, 0))
    return call(
        new_anchor_body, "new_anchor", (pos, plan),
        [(anchor, part), (momentum, part)] + [(a, whole(a.shape)) for a in quarters],
        [(sds((rows, width), f32), whole((rows, width)))], after=after,
    )[0]


def mix_body(off, plan, new_anc, *refs):
    thetas, low = refs[:-1], refs[-1]
    cr, width = thetas[0].shape[2:]
    for i, theta in enumerate(thetas):
        for k in range(2):
            value = mixed(plan, k, theta[0, k], new_anc[off + i * cr:off + (i + 1) * cr, :])
            low[i * cr:(i + 1) * cr, k * width:(k + 1) * width] = value.astype(bf16)


def mix_rows(plan, new_anc, off, thetas):
    cr, width = thetas[0].shape[2:]
    shape = (cr * len(thetas), 2 * width)
    return call(
        functools.partial(mix_body, off), "mix_rows", (plan,),
        [(a, whole(a.shape)) for a in [new_anc] + thetas], [(sds(shape, bf16), whole(shape))],
    )[0]


def outer_body(pos, plan, anchor, momentum, *refs):
    quarters = refs[:4]
    anchor_out, momentum_out = refs[4:]
    frag = fragment(plan)
    anchor_out[...] = anchor[...]
    momentum_out[...] = momentum[...]
    for m, piece in enumerate(quarters):
        at = quarter(pos, m, piece.shape[0])
        anc, mom = outer_update(frag, at, anchor, momentum, piece[...].astype(f32))
        anchor_out[frag, at, :] = anc
        momentum_out[frag, at, :] = mom


def outer_end(pos, plan, anchor, momentum, quarters, after):
    return call(
        outer_body, "outer_step", (pos, plan),
        [(a, whole(a.shape)) for a in [anchor, momentum] + quarters],
        [(sds(anchor.shape, f32), whole(anchor.shape))] * 2, after=after,
    )


def local(n_rep, n_fsdp, inputs, kinds, weights, first_moment, second_moment, anchor, momentum, plan):
    tokens = inputs.shape[0]
    rows, width = weights.shape[2:]
    chips = n_fsdp // 2
    scale = 1.0 / math.sqrt(tokens * n_fsdp)
    chunks = max(1, min(4, rows // 256))
    cr = rows // chunks
    parts = max(1, chunks // 2)
    sub = rows // parts

    partner = [(f, f ^ 1) for f in range(n_fsdp)]
    to_partner = lambda a: lax.ppermute(a, "fsdp", partner)
    fetch = lambda a, s: lax.ppermute(
        a, "fsdp", [(((f // 2 + s) % chips) * 2 + f % 2, f) for f in range(n_fsdp)])
    give = lambda a, s: lax.ppermute(
        a, "fsdp", [(f, ((f // 2 + s) % chips) * 2 + f % 2) for f in range(n_fsdp)])
    across = lambda a, bit: lax.ppermute(a, "replica", [(r, r ^ bit) for r in range(n_rep)])

    blocks = [(i * cr, cr) for i in range(chunks)]
    low_own = cast_rows(weights, 1)

    chip = lax.axis_index("fsdp") // 2
    core = lax.axis_index("fsdp") % 2
    at = [((chip + s) % chips) * 2 for s in range(chips)]
    pos = jnp.stack([lax.axis_index("replica")] + [a + core for a in at] + [a + 1 - core for a in at]).astype(jnp.int32)

    x_par = to_partner(inputs)
    xs = (inputs, x_par)
    lanes = kinds.reshape(-1, 128)
    cw = call(
        weigh_body, "weigh_tokens", (),
        [(lanes, whole(lanes.shape)), (to_partner(lanes), whole(lanes.shape))],
        [(sds((2, tokens, 1), f32), whole((2, tokens, 1)))], after=low_own,
    )[0]

    quarters = outer_start(pos, plan, anchor, weights, low_own)
    xt = [turn(pos, x, chips, rows) for x in xs]
    own = outer_add(plan, [quarters[0]] + [across(quarters[m], m) for m in range(1, 4)], n_rep == 4, [xt[0], cw])

    state = [(weights, first_moment, second_moment)] * chunks
    state_block = list(range(chunks))
    new_anc = None
    for step in range(INNER):
        last = step == INNER - 1
        def pieces(lows, slot, cut=sub):
            return [
                (low, off, slot, (j * low.shape[0] + off) // cut)
                for j, low in enumerate(lows) for off in range(0, low.shape[0], cut)
            ]

        low_far = {s: [fetch(low, s) for low in low_own] for s in range(1, chips)}
        low_near = [to_partner(low) for low in low_own]
        acc, gram = forward(pos, None, None, pieces(low_own, 1), xs, sub)
        pending = pieces(low_near, 1 + chips)
        if step == 0:
            acc, gram = forward(pos, acc, gram, pending, xs, sub)
            pending = []
            bit = 4
            while bit < n_rep:
                own = outer_add(plan, [own, across(own, bit)], 2 * bit == n_rep, [acc, xt[1]])
                bit *= 2
            ready = [own]
        for j in range(len(low_own)):
            handed = {s: to_partner(relay(low_far[s][j], [acc] + ready)) for s in low_far}
            place = lambda lows, slot: [
                (low, off, slot + s, j * (rows // len(low_own)) // sub + off // sub)
                for s, low in lows.items() for off in range(0, low.shape[0], sub)
            ]
            acc, gram = forward(
                pos, acc, gram, pending + place({s: low_far[s][j] for s in low_far}, 1), xs, sub)
            pending = place(handed, 1 + chips)
        slopes, w_hi, w_lo = finish(pos, acc, gram, cw, pending, xs, sub, scale)

        mine, got, sent = [], [], []
        for i in range(chunks):
            now = []
            for s in low_far:
                now.append(grad_rows(
                    scale, s, i, cr, xt, slopes, w_hi, w_lo, low_far[s], bf16, after=sent[-1:]))
                sent.append(now[-1])
            got.append([give(g, s) for s, g in zip(low_far, now)])
        for i in range(chunks):
            mine.append(grad_rows(
                scale, 0, i, cr, xt, slopes, w_hi, w_lo, low_own, f32, after=(sent + mine)[-1:]))

        new_state, prev = [], None
        if not last:
            quarters = [own] + [across(own, m) for m in range(1, 4)]
            new_anc = outer_anchor(pos, plan, anchor, momentum, quarters, mine[-1:])
            low_next = []
        for i in range(chunks):
            res = adam_rows(
                plan, i, cr, mine[i], got[i], state[i], state_block[i], new_anc if last else None, prev,
                weights.shape, [] if last else low_next[-1:])
            if last:
                prev = res
                continue
            new_state.append(tuple(res))
            if (i + 1) * cr % sub == 0:
                thetas = [t for t, _, _ in new_state[len(low_next) * (sub // cr):]]
                low_next.append(mix_rows(plan, new_anc, len(low_next) * sub, thetas))
        if not last:
            anchor_out, momentum_out = outer_end(pos, plan, anchor, momentum, quarters, low_next)
            ready = [anchor_out]
            state, state_block, low_own = new_state, [0] * chunks, low_next
    return (*prev, anchor_out, momentum_out)


def solution(mesh):
    return jax.shard_map(
        functools.partial(local, mesh.shape["replica"], mesh.shape["fsdp"]),
        mesh=mesh,
        in_specs=(
            P(("replica", "fsdp"), None),
            P(("replica", "fsdp")),
            P("replica", None, "fsdp", None),
            P("replica", None, "fsdp", None),
            P("replica", None, "fsdp", None),
            P(None, "fsdp", None),
            P(None, "fsdp", None),
            P(),
        ),
        out_specs=(
            P("replica", None, "fsdp", None),
            P("replica", None, "fsdp", None),
            P("replica", None, "fsdp", None),
            P(None, "fsdp", None),
            P(None, "fsdp", None),
        ),
        check_vma=False,
    )
```

```python
import functools
import math

import jax
import jax.numpy as jnp
from jax import lax
from jax.experimental import pallas as pl
from jax.experimental.pallas import tpu as pltpu
from jax.sharding import PartitionSpec as P

INNER = 2

inner_rate = 0.003
beta_one = 0.9
beta_two = 0.95
adam_eps = 1e-08
decay_rate = 0.1
outer_rate = 0.7
outer_mu = 0.9
mix_share = 0.5

bf16 = jnp.bfloat16
f32 = jnp.float32
VMEM_LIMIT = 16 * 1024 * 1024


def token_weight(kinds):
    return jnp.where(kinds == 2, 1.0, jnp.where(kinds == 1, 0.25, 0.0)).astype(f32)


def dot(a, b):
    return jnp.dot(a, b, preferred_element_type=f32)


def dot_rows(a, b):
    return lax.dot_general(a, b, (((0,), (0,)), ((), ())), preferred_element_type=f32)


def once(shape, index):
    return pl.BlockSpec(shape, index, pipeline_mode=pl.Buffered(1))


def whole(shape):
    return once(shape, lambda *_: (0,) * len(shape))


def sds(shape, dtype):
    return jax.ShapeDtypeStruct(shape, dtype)


def call(body, name, meta, ins, outs, grid=(1,), scratch=(), aliases=None, flops=0, after=()):
    arrays = [a for a, _ in ins] + list(after)
    n_in = len(meta) + len(ins)
    moved = sum(math.prod(o.shape) * o.dtype.itemsize for o, _ in outs)
    moved += sum(math.prod(s.block_shape or a.shape) * a.dtype.itemsize for a, s in ins)

    def run(*refs):
        body(*refs[:n_in], *refs[n_in + len(after):])

    return pl.pallas_call(
        run,
        name=name,
        out_shape=[o for o, _ in outs],
        grid_spec=pltpu.PrefetchScalarGridSpec(
            num_scalar_prefetch=len(meta),
            grid=grid,
            in_specs=[s for _, s in ins] + [pl.BlockSpec(memory_space=pl.ANY)] * len(after),
            out_specs=[s for _, s in outs],
            scratch_shapes=list(scratch),
        ),
        input_output_aliases=aliases or {},
        compiler_params=pltpu.CompilerParams(vmem_limit_bytes=VMEM_LIMIT),
        cost_estimate=pl.CostEstimate(flops=flops, bytes_accessed=moved, transcendentals=0),
    )(*meta, *arrays)


def plan_sum(plan):
    total = plan[0]
    for r in range(1, plan.shape[0]):
        total = total + plan[r]
    return total


def fragment(plan):
    return lax.rem(plan_sum(plan), 2)


EXTRA = 16


def cast_body(theta, kinds, low, more):
    rows, wide = low.shape
    width = wide // 2
    for k in range(2):
        value = theta[0, k].astype(bf16)
        low[:, k * width:(k + 1) * width] = value
        more[:rows, k * width:(k + 1) * width] = value
    weight = token_weight(kinds[...])
    pad = jnp.zeros((EXTRA - kinds.shape[0], wide), f32)
    more[rows:, :] = jnp.concatenate([weight, pad], 0).astype(bf16)


def cast_rows(weights, kinds):
    _, _, rows, width = weights.shape
    lanes = kinds.reshape(-1, 2 * width)
    shapes = [(rows, 2 * width), (rows + EXTRA, 2 * width)]
    return call(
        cast_body, "cast_rows", (), [(weights, whole(weights.shape)), (lanes, whole(lanes.shape))],
        [(sds(shape, bf16), whole(shape)) for shape in shapes],
    )


def weigh_body(own, other, out):
    wide = own.shape[1]
    for h, rows in enumerate((own, other)):
        turned = rows[...].astype(f32).T
        for j in range(out.shape[1] // wide):
            out[h, j * wide:(j + 1) * wide, :] = turned[:, j:j + 1]


def weigh(own, other, tokens):
    rows, wide = own.shape
    last = once((EXTRA, wide), lambda g: (rows // EXTRA - 1, 0))
    return call(
        weigh_body, "weigh_tokens", (), [(own, last), (other, last)],
        [(sds((2, tokens, 1), f32), whole((2, tokens, 1)))],
    )[0]


def copy_body(x, out):
    out[...] = x[...]


def relay(x, after):
    return call(copy_body, "relay_rows", (), [(x, whole(x.shape))], [(sds(x.shape, x.dtype), whole(x.shape))], after=after)[0]


def turn_block(pos, x, xt, t, tile):
    rows = x.shape[1] // (pos.shape[0] - 1)
    for s in range(xt.shape[0] // rows):
        xt[s * rows:(s + 1) * rows, t:t + tile] = x[t:t + tile, columns(pos, 1 + s, 0, rows, rows)].T


def columns(pos, slot, off, size, rows):
    return pl.ds(pl.multiple_of(pos[slot] * rows + off, size), size)


def turn_body(tile, pos, x, xt):
    for t in range(0, x.shape[0], tile):
        turn_block(pos, x, xt, t, tile)


def stage_body(tile, pos, x, held, xt, sems):
    copies = []
    for n, t in enumerate(range(0, x.shape[0], tile)):
        copy = pltpu.make_async_copy(x.at[pl.ds(t, tile), :], held.at[pl.ds(t, tile), :], sems.at[n])
        copy.start()
        copies.append(copy)
    for n, t in enumerate(range(0, x.shape[0], tile)):
        copies[n].wait()
        turn_block(pos, held, xt, t, tile)


def turn(pos, x, chips, stage):
    tokens, depth = x.shape
    tile = min(128, tokens)
    xt = [(sds((depth // 2, tokens), bf16), whole((depth // 2, tokens)))]
    if not stage:
        return x, call(functools.partial(turn_body, tile), "turn_tokens", (pos,), [(x, whole(x.shape))], xt)[0]
    return call(
        functools.partial(stage_body, tile), "stage_tokens", (pos,), [(x, pl.BlockSpec(memory_space=pl.ANY))],
        [(sds(x.shape, bf16), whole(x.shape))] + xt,
        scratch=[pltpu.SemaphoreType.DMA((tokens // tile,))],
    )


def product(pos, x, low, slot, off, rows):
    size = low.shape[0]
    return dot(x[:, columns(pos, slot, off, size, rows)], low[...])


def gram_sum(lows, before):
    for low in lows:
        dec = low[:, low.shape[1] // 2:]
        term = dot_rows(dec, dec)
        before = term if before is None else before + term
    return before


def forward_body(places, rows, first_call, pos, *refs):
    if first_call:
        acc_in = gram_in = None
    else:
        acc_in, gram_in, refs = refs[0], refs[1], refs[2:]
    count = len(places)
    lows, xs = refs[:count], refs[count:count + 2]
    acc, gram = refs[count + 2:]
    gram[...] = gram_sum(lows, None if first_call else gram_in[...])
    for h in range(2):
        value = None if first_call else acc_in[h]
        for low, (slot, off) in zip(lows, places):
            term = product(pos, xs[h], low, slot, off, rows)
            value = term if value is None else value + term
        acc[h] = value


def forward(pos, acc, gram, pieces, xs, rows, after=()):
    tokens = xs[0].shape[0]
    wide = pieces[0][0].shape[1]
    width = wide // 2
    ins = []
    if acc is not None:
        ins += [(acc, whole(acc.shape)), (gram, whole(gram.shape))]
    ins += [(a, whole((min(a.shape[0], rows), wide))) for a, _, _ in pieces] + [(x, whole(x.shape)) for x in xs]
    return call(
        functools.partial(forward_body, [(slot, off) for _, slot, off in pieces], rows, acc is None),
        "forward_rows", (pos,), ins,
        [(sds((2, tokens, wide), f32), whole((2, tokens, wide))), (sds((width, width), f32), whole((width, width)))],
        after=after,
    )


def finish_body(scale, tile, places, rows, pos, acc_in, gram_in, cw, *refs):
    count = len(places)
    lows, xs = refs[:count], refs[count:count + 2]
    slopes, w_hi, w_lo, acc = refs[count + 2:]
    width = gram_in.shape[0]
    gram = gram_sum(lows, gram_in[...])
    g_hi = gram.astype(bf16)
    g_lo = (gram - g_hi.astype(f32)).astype(bf16)
    total = None
    for h in range(2):
        value = acc_in[h]
        for low, (slot, off) in zip(lows, places):
            value = value + product(pos, xs[h], low, slot, off, rows)
        acc[h] = value
        for t in range(0, acc.shape[1], tile):
            at = pl.ds(t, tile)
            pre = acc[h, at, :width]
            sig = 0.5 + 0.5 * jnp.tanh(0.5 * pre)
            hidden = (pre * sig).astype(bf16)
            back = dot(hidden, g_hi) + dot(hidden, g_lo) - acc[h, at, width:]
            weight = cw[h, at, :]
            slope = (weight * scale) * back * (sig * (1.0 + pre * (1.0 - sig)))
            counted = (weight * hidden.astype(f32)).astype(bf16)
            slopes[h, at, :width] = slope.astype(bf16)
            slopes[h, at, width:] = counted
            term = dot_rows(counted, hidden)
            total = term if total is None else total + term
    hi = total.astype(bf16)
    w_hi[...] = hi
    w_lo[...] = (total - hi.astype(f32)).astype(bf16)


def finish(pos, acc, gram, cw, pieces, xs, rows, scale):
    tokens = xs[0].shape[0]
    wide = pieces[0][0].shape[1]
    width = wide // 2
    ins = [(a, whole(a.shape)) for a in [acc, gram, cw] + [low for low, _, _ in pieces] + list(xs)]
    square = (sds((width, width), bf16), whole((width, width)))
    return call(
        functools.partial(
            finish_body, scale, min(256, tokens), [(slot, off) for _, slot, off in pieces], rows),
        "finish_slopes", (pos,), ins,
        [(sds((2, tokens, wide), bf16), whole((2, tokens, wide))), square, square],
        scratch=[pltpu.VMEM((2, tokens, wide), f32)],
    )


def grad_body(scale, off, xt_own, xt_par, slopes, w_hi, w_lo, low, out):
    width = w_hi.shape[0]
    both = dot(xt_own[...], slopes[0]) + dot(xt_par[...], slopes[1])
    dec = low[off:off + out.shape[0], width:]
    grad_dec = scale * (dot(dec, w_hi[...]) + dot(dec, w_lo[...]) - both[:, width:])
    out[:, :width] = both[:, :width].astype(out.dtype)
    out[:, width:] = grad_dec.astype(out.dtype)


def grad_rows(scale, s, i, cr, xt, slopes, w_hi, w_lo, lows, dtype, after=()):
    tokens = xt[0].shape[1]
    sub, wide = lows[0].shape
    low = lows[i * cr // sub]
    block = s * (sub * len(lows) // cr) + i
    ins = [(x, once((cr, tokens), lambda g: (block, 0))) for x in xt]
    ins += [(a, whole(a.shape)) for a in (slopes, w_hi, w_lo, low)]
    return call(
        functools.partial(grad_body, scale, i * cr % sub), "grad_rows", (), ins,
        [(sds((cr, wide), dtype), whole((cr, wide)))], after=after,
    )[0]


def adam_body(last, count, plan, own, *refs):
    got = refs[:count]
    theta, first, second = refs[count:3 + count]
    anchor = refs[3 + count]
    theta_out, first_out, second_out = refs[-3:]
    width = own.shape[1] // 2
    for k in range(2):
        grad = own[:, k * width:(k + 1) * width]
        for g in got:
            grad = grad + g[:, k * width:(k + 1) * width].astype(f32)
        one = beta_one * first[0, k] + (1.0 - beta_one) * grad
        two = beta_two * second[0, k] + (1.0 - beta_two) * grad * grad
        old = theta[0, k]
        if last:
            old = mixed(plan, k, old, anchor[...])
        theta_out[0, k] = old - inner_rate * (one / (jnp.sqrt(two) + adam_eps) + decay_rate * old)
        first_out[0, k] = one
        second_out[0, k] = two


def mixed(plan, k, theta, anchor):
    return jnp.where(fragment(plan) == k, mix_share * theta + (1.0 - mix_share) * anchor, theta)


def adam_rows(plan, i, cr, own, got, state, state_block, new_anc, prev, full, after=()):
    width = own.shape[1] // 2
    last = new_anc is not None
    block = (1, 2, cr, width)
    ins = [(g, whole(g.shape)) for g in [own] + got]
    ins += [(s, once(block, lambda g, m: (0, 0, state_block, 0))) for s in state]
    aliases = {}
    if last:
        ins.append((new_anc, once((cr, width), lambda g, m: (i, 0))))
        if prev is not None:
            for n, p in enumerate(prev):
                aliases[1 + len(ins)] = n
                ins.append((p, pl.BlockSpec(memory_space=pl.ANY)))
        outs = [(sds(full, f32), once(block, lambda g, m: (0, 0, i, 0)))] * 3
    else:
        outs = [(sds(block, f32), whole(block))] * 3
    return call(
        functools.partial(adam_body, last, len(got)), "adam_rows", (plan,), ins, outs, aliases=aliases,
        after=after,
    )


def quarter(pos, m, size):
    where = jnp.bitwise_xor(lax.rem(pos[0], 4), m)
    return pl.ds(pl.multiple_of(where * size, size), size)


def delta_body(pos, plan, anchor, theta, *outs):
    count = plan[pos[0]].astype(f32)
    for m, out in enumerate(outs):
        at = quarter(pos, m, out.shape[0])
        out[...] = (count * (anchor[0, at, :] - theta[0, 0, at, :])).astype(out.dtype)


def outer_start(pos, plan, anchor, weights, after):
    _, rows, width = anchor.shape
    part = (rows // 4, width)
    return call(
        delta_body, "delta_quarters", (pos, plan),
        [
            (anchor, once((1, rows, width), lambda g, p, q: (fragment(q), 0, 0))),
            (weights, once((1, 1, rows, width), lambda g, p, q: (0, fragment(q), 0, 0))),
        ],
        [(sds(part, f32), whole(part))] + [(sds(part, bf16), whole(part))] * 3, after=after,
    )


def add_body(final, plan, *refs):
    total = refs[0][...].astype(f32)
    for r in refs[1:-1]:
        total = total + r[...].astype(f32)
    if final:
        total = total / plan_sum(plan).astype(f32)
    refs[-1][...] = total.astype(bf16)


def outer_add(plan, parts, final, after=()):
    shape = parts[0].shape
    return call(
        functools.partial(add_body, final), "add_quarters", (plan,), [(a, whole(shape)) for a in parts],
        [(sds(shape, bf16), whole(shape))], after=after,
    )[0]


def outer_update(frag, at, anchor, momentum, grad):
    mom = outer_mu * momentum[frag, at, :] + grad
    return anchor[frag, at, :] - outer_rate * (grad + outer_mu * mom), mom


def new_anchor_body(pos, plan, anchor, momentum, *refs):
    for m, piece in enumerate(refs[:4]):
        at = quarter(pos, m, piece.shape[0])
        refs[4][at, :] = outer_update(0, at, anchor, momentum, piece[...].astype(f32))[0]


def outer_anchor(pos, plan, anchor, momentum, quarters, after):
    _, rows, width = anchor.shape
    part = once((1, rows, width), lambda g, p, q: (fragment(q), 0, 0))
    return call(
        new_anchor_body, "new_anchor", (pos, plan),
        [(anchor, part), (momentum, part)] + [(a, whole(a.shape)) for a in quarters],
        [(sds((rows, width), f32), whole((rows, width)))], after=after,
    )[0]


def mix_body(off, plan, new_anc, *refs):
    thetas, low = refs[:-1], refs[-1]
    cr, width = thetas[0].shape[2:]
    for i, theta in enumerate(thetas):
        for k in range(2):
            value = mixed(plan, k, theta[0, k], new_anc[off + i * cr:off + (i + 1) * cr, :])
            low[i * cr:(i + 1) * cr, k * width:(k + 1) * width] = value.astype(bf16)


def mix_rows(plan, new_anc, off, thetas):
    cr, width = thetas[0].shape[2:]
    shape = (cr * len(thetas), 2 * width)
    return call(
        functools.partial(mix_body, off), "mix_rows", (plan,),
        [(a, whole(a.shape)) for a in [new_anc] + thetas], [(sds(shape, bf16), whole(shape))],
    )[0]


def outer_body(pos, plan, anchor, momentum, *refs):
    quarters = refs[:4]
    anchor_out, momentum_out, token = refs[4:]
    token[...] = jnp.zeros_like(token)
    frag = fragment(plan)
    anchor_out[...] = anchor[...]
    momentum_out[...] = momentum[...]
    for m, piece in enumerate(quarters):
        at = quarter(pos, m, piece.shape[0])
        anc, mom = outer_update(frag, at, anchor, momentum, piece[...].astype(f32))
        anchor_out[frag, at, :] = anc
        momentum_out[frag, at, :] = mom


def outer_end(pos, plan, anchor, momentum, quarters, after):
    return call(
        outer_body, "outer_step", (pos, plan),
        [(a, whole(a.shape)) for a in [anchor, momentum] + quarters],
        [(sds(anchor.shape, f32), whole(anchor.shape))] * 2 + [(sds((8, 128), f32), whole((8, 128)))], after=after,
    )


def local(n_rep, n_fsdp, inputs, kinds, weights, first_moment, second_moment, anchor, momentum, plan):
    tokens = inputs.shape[0]
    rows, width = weights.shape[2:]
    chips = n_fsdp // 2
    scale = 1.0 / math.sqrt(tokens * n_fsdp)
    chunks = max(1, min(4, rows // 256))
    cr = rows // chunks
    parts = max(1, chunks // 2)
    sub = rows // parts

    partner = [(f, f ^ 1) for f in range(n_fsdp)]
    to_partner = lambda a: lax.ppermute(a, "fsdp", partner)
    fetch = lambda a, s: lax.ppermute(
        a, "fsdp", [(((f // 2 + s) % chips) * 2 + f % 2, f) for f in range(n_fsdp)])
    give = lambda a, s: lax.ppermute(
        a, "fsdp", [(f, ((f // 2 + s) % chips) * 2 + f % 2) for f in range(n_fsdp)])
    across = lambda a, bit: lax.ppermute(a, "replica", [(r, r ^ bit) for r in range(n_rep)])

    low, more = cast_rows(weights, kinds)
    low_own, low_send = [low], [more]

    chip = lax.axis_index("fsdp") // 2
    core = lax.axis_index("fsdp") % 2
    at = [((chip + s) % chips) * 2 for s in range(chips)]
    pos = jnp.stack([lax.axis_index("replica")] + [a + core for a in at] + [a + 1 - core for a in at]).astype(jnp.int32)

    x_par = to_partner(inputs)
    low_near = [to_partner(more)]
    cw = weigh(more, low_near[0], tokens)

    quarters = outer_start(pos, plan, anchor, weights, low_own)
    xs, xt = zip(*[turn(pos, x, chips, stage) for x, stage in ((inputs, False), (x_par, True))])
    own = outer_add(plan, [quarters[0]] + [across(quarters[m], m) for m in range(1, 4)], n_rep == 4, xt)

    state = [(weights, first_moment, second_moment)] * chunks
    state_block = list(range(chunks))
    new_anc = None
    for step in range(INNER):
        last = step == INNER - 1
        size = low_own[0].shape[0]
        low_far = {s: [fetch(low, s) for low in low_own] for s in range(1, chips)}
        if step:
            low_near = [to_partner(low) for low in low_own]
        acc, gram = forward(pos, None, None, [(low, 1, j * size) for j, low in enumerate(low_own)], xs, rows)
        pending = [(low, 1 + chips, j * size) for j, low in enumerate(low_near)]
        if step == 0:
            acc, gram = forward(pos, acc, gram, pending, xs, rows)
            pending = []
            bit = 4
            while bit < n_rep:
                own = outer_add(plan, [own, across(own, bit)], 2 * bit == n_rep, [acc, cw])
                bit *= 2
            ready = [own]
        for j in range(len(low_own)):
            for s in low_far:
                low_far[s][j] = relay(low_far[s][j], [acc] + ready)
            acc, gram = forward(
                pos, acc, gram, pending + [(low_far[s][j], 1 + s, j * size) for s in low_far], xs, rows)
            pending = [(to_partner(low_far[s][j]), 1 + chips + s, j * size) for s in low_far]
        slopes, w_hi, w_lo = finish(pos, acc, gram, cw, pending, xs, rows, scale)

        mine, got, sent = [], [], []
        for i in range(chunks):
            now = []
            for s in low_far:
                now.append(grad_rows(
                    scale, s, i, cr, xt, slopes, w_hi, w_lo, low_far[s], bf16, after=sent[-1:]))
                sent.append(now[-1])
            got.append([give(g, s) for s, g in zip(low_far, now)])
        for i in range(chunks):
            mine.append(grad_rows(
                scale, 0, i, cr, xt, slopes, w_hi, w_lo, low_own, f32, after=(sent + mine)[-1:]))

        new_state, prev = [], None
        if not last:
            quarters = [own] + [across(own, m) for m in range(1, 4)]
            new_anc = outer_anchor(pos, plan, anchor, momentum, quarters, mine[-1:])
            low_next = []
        for i in range(chunks):
            res = adam_rows(
                plan, i, cr, mine[i], got[i], state[i], state_block[i], new_anc if last else None, prev,
                weights.shape, [] if last else low_next[-1:])
            if last:
                prev = res
                continue
            new_state.append(tuple(res))
            if (i + 1) * cr % sub == 0:
                thetas = [t for t, _, _ in new_state[len(low_next) * (sub // cr):]]
                low_next.append(mix_rows(plan, new_anc, len(low_next) * sub, thetas))
        if not last:
            anchor_out, momentum_out, token = outer_end(pos, plan, anchor, momentum, quarters, low_next)
            ready = [token]
            state, state_block, low_own = new_state, [0] * chunks, low_next
    return (*prev, anchor_out, momentum_out)


def solution(mesh):
    return jax.shard_map(
        functools.partial(local, mesh.shape["replica"], mesh.shape["fsdp"]),
        mesh=mesh,
        in_specs=(
            P(("replica", "fsdp"), None),
            P(("replica", "fsdp")),
            P("replica", None, "fsdp", None),
            P("replica", None, "fsdp", None),
            P("replica", None, "fsdp", None),
            P(None, "fsdp", None),
            P(None, "fsdp", None),
            P(),
        ),
        out_specs=(
            P("replica", None, "fsdp", None),
            P("replica", None, "fsdp", None),
            P("replica", None, "fsdp", None),
            P(None, "fsdp", None),
            P(None, "fsdp", None),
        ),
        check_vma=False,
    )
```

```python
import functools
import math

import jax
import jax.numpy as jnp
from jax import lax
from jax.experimental import pallas as pl
from jax.experimental.pallas import tpu as pltpu
from jax.sharding import PartitionSpec as P

INNER = 2

inner_rate = 0.003
beta_one = 0.9
beta_two = 0.95
adam_eps = 1e-08
decay_rate = 0.1
outer_rate = 0.7
outer_mu = 0.9
mix_share = 0.5

bf16 = jnp.bfloat16
f32 = jnp.float32
VMEM_LIMIT = 16 * 1024 * 1024


def token_weight(kinds):
    return jnp.where(kinds == 2, 1.0, jnp.where(kinds == 1, 0.25, 0.0)).astype(f32)


def dot(a, b):
    return jnp.dot(a, b, preferred_element_type=f32)


def dot_rows(a, b):
    return lax.dot_general(a, b, (((0,), (0,)), ((), ())), preferred_element_type=f32)


def once(shape, index):
    return pl.BlockSpec(shape, index, pipeline_mode=pl.Buffered(1))


def whole(shape):
    return once(shape, lambda *_: (0,) * len(shape))


def sds(shape, dtype):
    return jax.ShapeDtypeStruct(shape, dtype)


def call(body, name, meta, ins, outs, grid=(1,), scratch=(), aliases=None, flops=0, after=()):
    arrays = [a for a, _ in ins] + list(after)
    n_in = len(meta) + len(ins)
    moved = sum(math.prod(o.shape) * o.dtype.itemsize for o, _ in outs)
    moved += sum(math.prod(s.block_shape or a.shape) * a.dtype.itemsize for a, s in ins)

    def run(*refs):
        body(*refs[:n_in], *refs[n_in + len(after):])

    return pl.pallas_call(
        run,
        name=name,
        out_shape=[o for o, _ in outs],
        grid_spec=pltpu.PrefetchScalarGridSpec(
            num_scalar_prefetch=len(meta),
            grid=grid,
            in_specs=[s for _, s in ins] + [pl.BlockSpec(memory_space=pl.ANY)] * len(after),
            out_specs=[s for _, s in outs],
            scratch_shapes=list(scratch),
        ),
        input_output_aliases=aliases or {},
        compiler_params=pltpu.CompilerParams(vmem_limit_bytes=VMEM_LIMIT),
        cost_estimate=pl.CostEstimate(flops=flops, bytes_accessed=moved, transcendentals=0),
    )(*meta, *arrays)


def plan_sum(plan):
    total = plan[0]
    for r in range(1, plan.shape[0]):
        total = total + plan[r]
    return total


def fragment(plan):
    return lax.rem(plan_sum(plan), 2)


EXTRA = 16


def cast_body(theta, *lows):
    for k, low in enumerate(lows):
        low[...] = theta[0, k].astype(bf16)


def cast_rows(weights):
    _, _, rows, width = weights.shape
    return call(
        cast_body, "cast_rows", (), [(weights, whole(weights.shape))],
        [(sds((rows, width), bf16), whole((rows, width)))] * 2,
    )


def extend_body(low, kinds, more):
    rows, width = low.shape
    more[:rows, :] = low[...]
    pad = jnp.zeros((EXTRA - kinds.shape[0], width), f32)
    more[rows:, :] = jnp.concatenate([token_weight(kinds[...]), pad], 0).astype(bf16)


def extend(low, kinds):
    rows, width = low.shape
    lanes = kinds.reshape(-1, width)
    shape = (rows + EXTRA, width)
    return call(
        extend_body, "extend_rows", (), [(a, whole(a.shape)) for a in (low, lanes)],
        [(sds(shape, bf16), whole(shape))],
    )[0]


def weigh_body(own, other, out):
    wide = own.shape[1]
    for h, rows in enumerate((own, other)):
        turned = rows[...].astype(f32).T
        for j in range(out.shape[1] // wide):
            out[h, j * wide:(j + 1) * wide, :] = turned[:, j:j + 1]


def weigh(own, other, tokens):
    rows, wide = own.shape
    last = once((EXTRA, wide), lambda g: (rows // EXTRA - 1, 0))
    return call(
        weigh_body, "weigh_tokens", (), [(own, last), (other, last)],
        [(sds((2, tokens, 1), f32), whole((2, tokens, 1)))],
    )[0]


def relay_body(x, *outs):
    size = outs[0].shape[0]
    for n, out in enumerate(outs):
        out[...] = x[n * size:(n + 1) * size, :]


def relay(x, cuts, after):
    shape = (x.shape[0] // cuts, x.shape[1])
    return call(
        relay_body, "relay_rows", (), [(x, whole(x.shape))],
        [(sds(shape, x.dtype), whole(shape))] * cuts, after=after,
    )


def turn_block(pos, x, xt, t, tile):
    rows = x.shape[1] // (pos.shape[0] - 1)
    for s in range(xt.shape[0] // rows):
        xt[s * rows:(s + 1) * rows, t:t + tile] = x[t:t + tile, columns(pos, 1 + s, 0, rows, rows)].T


def columns(pos, slot, off, size, rows):
    return pl.ds(pl.multiple_of(pos[slot] * rows + off, size), size)


def turn_body(tile, pos, x, xt):
    for t in range(0, x.shape[0], tile):
        turn_block(pos, x, xt, t, tile)


def stage_body(tile, pos, x, held, xt, sems):
    copies = []
    for n, t in enumerate(range(0, x.shape[0], tile)):
        copy = pltpu.make_async_copy(x.at[pl.ds(t, tile), :], held.at[pl.ds(t, tile), :], sems.at[n])
        copy.start()
        copies.append(copy)
    for n, t in enumerate(range(0, x.shape[0], tile)):
        copies[n].wait()
        turn_block(pos, held, xt, t, tile)


def turn(pos, x, chips, stage):
    tokens, depth = x.shape
    tile = min(128, tokens)
    xt = [(sds((depth // 2, tokens), bf16), whole((depth // 2, tokens)))]
    if not stage:
        return x, call(functools.partial(turn_body, tile), "turn_tokens", (pos,), [(x, whole(x.shape))], xt)[0]
    return call(
        functools.partial(stage_body, tile), "stage_tokens", (pos,), [(x, pl.BlockSpec(memory_space=pl.ANY))],
        [(sds(x.shape, bf16), whole(x.shape))] + xt,
        scratch=[pltpu.SemaphoreType.DMA((tokens // tile,))],
    )


def product(pos, x, low, place, rows):
    slot, off, size = place
    return dot(x[:, columns(pos, slot, off, size, rows)], low[:size, :])


def gram_sum(lows, before):
    for low in lows:
        term = dot_rows(low[...], low[...])
        before = term if before is None else before + term
    return before


def forward_body(places, rows, with_gram, first_call, pos, *refs):
    carry = 2 if with_gram else 1
    before = (None, None) if first_call else refs[:carry]
    if not first_call:
        refs = refs[carry:]
    count = len(places)
    lows, xs = refs[:count], refs[count:count + 2]
    outs = refs[count + 2:]
    if with_gram:
        outs[1][...] = gram_sum(lows, None if first_call else before[1][...])
    for h in range(2):
        value = None if first_call else before[0][h]
        for low, place in zip(lows, places):
            term = product(pos, xs[h], low, place, rows)
            value = term if value is None else value + term
        outs[0][h] = value


def forward(pos, carry, pieces, xs, rows, with_gram, after=()):
    tokens = xs[0].shape[0]
    width = pieces[0][0].shape[1]
    ins = [(a, whole(a.shape)) for a in carry]
    ins += [(p[0], whole((p[3], width))) for p in pieces] + [(x, whole(x.shape)) for x in xs]
    shapes = [(2, tokens, width)] + [(width, width)] * with_gram
    return call(
        functools.partial(forward_body, [p[1:] for p in pieces], rows, with_gram, not carry),
        "forward_decoder" if with_gram else "forward_encoder", (pos,), ins,
        [(sds(shape, f32), whole(shape)) for shape in shapes], after=after,
    )


def split(total):
    hi = total.astype(bf16)
    return hi, (total - hi.astype(f32)).astype(bf16)


def hidden_body(scale, tile, places, rows, pos, acc_in, cw, *refs):
    count = len(places)
    lows, xs = refs[:count], refs[count:count + 2]
    hidden_out, slope_out, counted_out, w_hi, w_lo, acc = refs[count + 2:]
    total = None
    for h in range(2):
        value = acc_in[h]
        for low, place in zip(lows, places):
            value = value + product(pos, xs[h], low, place, rows)
        acc[h] = value
        for t in range(0, acc.shape[1], tile):
            at = pl.ds(t, tile)
            pre = acc[h, at, :]
            sig = 0.5 + 0.5 * jnp.tanh(0.5 * pre)
            hidden = (pre * sig).astype(bf16)
            weight = cw[h, at, :]
            counted = (weight * hidden.astype(f32)).astype(bf16)
            hidden_out[h, at, :] = hidden
            slope_out[h, at, :] = (weight * scale) * (sig * (1.0 + pre * (1.0 - sig)))
            counted_out[h, at, :] = counted
            term = dot_rows(counted, hidden)
            total = term if total is None else total + term
    w_hi[...], w_lo[...] = split(total)


def hidden_rows(pos, acc, cw, pieces, xs, rows, scale):
    shape = acc.shape
    width = shape[2]
    ins = [(a, whole(a.shape)) for a in [acc, cw] + [p[0] for p in pieces] + list(xs)]
    square = (sds((width, width), bf16), whole((width, width)))
    return call(
        functools.partial(hidden_body, scale, min(256, shape[1]), [p[1:] for p in pieces], rows),
        "hidden_units", (pos,), ins,
        [(sds(shape, bf16), whole(shape)), (sds(shape, f32), whole(shape)), (sds(shape, bf16), whole(shape)), square, square],
        scratch=[pltpu.VMEM(shape, f32)],
    )


def slope_body(places, rows, pos, acc_in, gram_in, hidden, slope, *refs):
    count = len(places)
    lows, xs, out = refs[:count], refs[count:count + 2], refs[count + 2]
    g_hi, g_lo = split(gram_sum(lows, gram_in[...]))
    for h in range(2):
        value = acc_in[h]
        for low, place in zip(lows, places):
            value = value + product(pos, xs[h], low, place, rows)
        back = dot(hidden[h], g_hi) + dot(hidden[h], g_lo) - value
        out[h] = (slope[h] * back).astype(bf16)


def slope_rows(pos, acc, gram, hidden, slope, pieces, xs, rows):
    ins = [(a, whole(a.shape)) for a in [acc, gram, hidden, slope] + [p[0] for p in pieces] + list(xs)]
    return call(
        functools.partial(slope_body, [p[1:] for p in pieces], rows), "slope_pre", (pos,), ins,
        [(sds(acc.shape, bf16), whole(acc.shape))],
    )[0]


def encoder_body(xt_own, xt_par, slopes, out):
    out[...] = (dot(xt_own[...], slopes[0]) + dot(xt_par[...], slopes[1])).astype(out.dtype)


def decoder_body(scale, xt_own, xt_par, counted, w_hi, w_lo, low, out):
    dec = low[...]
    both = dot(xt_own[...], counted[0]) + dot(xt_par[...], counted[1])
    out[...] = (scale * (dot(dec, w_hi[...]) + dot(dec, w_lo[...]) - both)).astype(out.dtype)


def grad_rows(body, name, block, cr, xt, others, dtype, after=()):
    tokens = xt[0].shape[1]
    width = others[0].shape[2]
    ins = [(x, once((cr, tokens), lambda g: (block, 0))) for x in xt]
    ins += [(a, whole(a.shape)) for a in others]
    return call(body, name, (), ins, [(sds((cr, width), dtype), whole((cr, width)))], after=after)[0]


def adam_body(last, count, k, i, n_low, plan, own, *refs):
    got = refs[:count]
    theta, first, second = refs[count:3 + count]
    refs = refs[3 + count:]
    grad = own[...]
    for g in got:
        grad = grad + g[...].astype(f32)
    one = beta_one * first[0, 0] + (1.0 - beta_one) * grad
    two = beta_two * second[0, 0] + (1.0 - beta_two) * grad * grad
    old = theta[0, 0]
    if last:
        old = mixed(plan, k, old, refs[0][...])
    new = old - inner_rate * (one / (jnp.sqrt(two) + adam_eps) + decay_rate * old)
    if n_low is not None:
        cr = own.shape[0]
        anchor, before, low = refs[0], refs[1:1 + n_low], refs[1 + n_low]
        for j, b in enumerate(before):
            low[j * cr:(j + 1) * cr, :] = b[...]
        low[n_low * cr:(n_low + 1) * cr, :] = mixed(plan, k, new, anchor[i * cr:(i + 1) * cr, :]).astype(bf16)
    theta_out, first_out, second_out = refs[-3:]
    theta_out[0, 0] = new
    first_out[0, 0] = one
    second_out[0, 0] = two


def mixed(plan, k, theta, anchor):
    return jnp.where(fragment(plan) == k, mix_share * theta + (1.0 - mix_share) * anchor, theta)


def adam_rows(plan, k, i, own, got, state, at, new_anc, prev, full, last, lows=None, after=()):
    cr, width = own.shape
    block = (1, 1, cr, width)
    ins = [(g, whole(g.shape)) for g in [own] + got]
    ins += [(s, once(block, lambda g, m: (0, at[0], at[1], 0))) for s in state]
    aliases = {}
    outs = []
    if last:
        ins.append((new_anc, once((cr, width), lambda g, m: (i, 0))))
        if prev is not None:
            for n, p in enumerate(prev):
                aliases[1 + len(ins)] = n
                ins.append((p, pl.BlockSpec(memory_space=pl.ANY)))
        outs = [(sds(full, f32), once(block, lambda g, m: (0, k, i, 0)))] * 3
    else:
        if lows is not None:
            ins += [(a, whole(a.shape)) for a in [new_anc] + lows]
            shape = (cr * (1 + len(lows)), width)
            outs = [(sds(shape, bf16), whole(shape))]
        outs += [(sds(block, f32), whole(block))] * 3
    return call(
        functools.partial(adam_body, last, len(got), k, i, None if lows is None else len(lows)), "adam_rows",
        (plan,), ins, outs, aliases=aliases, after=after,
    )


def quarter(pos, m, size):
    where = jnp.bitwise_xor(lax.rem(pos[0], 4), m)
    return pl.ds(pl.multiple_of(where * size, size), size)


def delta_body(pos, plan, anchor, theta, *outs):
    count = plan[pos[0]].astype(f32)
    for m, out in enumerate(outs):
        at = quarter(pos, m, out.shape[0])
        out[...] = (count * (anchor[0, at, :] - theta[0, 0, at, :])).astype(out.dtype)


def outer_start(pos, plan, anchor, weights, after):
    _, rows, width = anchor.shape
    part = (rows // 4, width)
    return call(
        delta_body, "delta_quarters", (pos, plan),
        [
            (anchor, once((1, rows, width), lambda g, p, q: (fragment(q), 0, 0))),
            (weights, once((1, 1, rows, width), lambda g, p, q: (0, fragment(q), 0, 0))),
        ],
        [(sds(part, f32), whole(part))] + [(sds(part, bf16), whole(part))] * 3, after=after,
    )


def add_body(final, plan, *refs):
    total = refs[0][...].astype(f32)
    for r in refs[1:-1]:
        total = total + r[...].astype(f32)
    if final:
        total = total / plan_sum(plan).astype(f32)
    refs[-1][...] = total.astype(bf16)


def outer_add(plan, parts, final, after=()):
    shape = parts[0].shape
    return call(
        functools.partial(add_body, final), "add_quarters", (plan,), [(a, whole(shape)) for a in parts],
        [(sds(shape, bf16), whole(shape))], after=after,
    )[0]


def outer_update(frag, at, anchor, momentum, grad):
    mom = outer_mu * momentum[frag, at, :] + grad
    return anchor[frag, at, :] - outer_rate * (grad + outer_mu * mom), mom


def new_anchor_body(pos, plan, anchor, momentum, *refs):
    for m, piece in enumerate(refs[:4]):
        at = quarter(pos, m, piece.shape[0])
        refs[4][at, :] = outer_update(0, at, anchor, momentum, piece[...].astype(f32))[0]


def outer_anchor(pos, plan, anchor, momentum, quarters, after):
    _, rows, width = anchor.shape
    part = once((1, rows, width), lambda g, p, q: (fragment(q), 0, 0))
    return call(
        new_anchor_body, "new_anchor", (pos, plan),
        [(anchor, part), (momentum, part)] + [(a, whole(a.shape)) for a in quarters],
        [(sds((rows, width), f32), whole((rows, width)))], after=after,
    )[0]


def mix_body(k, plan, new_anc, theta, low):
    low[...] = mixed(plan, k, theta[0, 0], new_anc[...]).astype(bf16)


def mix_rows(plan, new_anc, k, theta, after):
    shape = new_anc.shape
    return call(
        functools.partial(mix_body, k), "mix_rows", (plan,), [(a, whole(a.shape)) for a in (new_anc, theta)],
        [(sds(shape, bf16), whole(shape))], after=after,
    )[0]


def outer_body(pos, plan, anchor, momentum, *refs):
    quarters = refs[:4]
    anchor_out, momentum_out, token = refs[4:]
    token[...] = jnp.zeros_like(token)
    frag = fragment(plan)
    anchor_out[...] = anchor[...]
    momentum_out[...] = momentum[...]
    for m, piece in enumerate(quarters):
        at = quarter(pos, m, piece.shape[0])
        anc, mom = outer_update(frag, at, anchor, momentum, piece[...].astype(f32))
        anchor_out[frag, at, :] = anc
        momentum_out[frag, at, :] = mom


def outer_end(pos, plan, anchor, momentum, quarters, after):
    return call(
        outer_body, "outer_step", (pos, plan),
        [(a, whole(a.shape)) for a in [anchor, momentum] + quarters],
        [(sds(anchor.shape, f32), whole(anchor.shape))] * 2 + [(sds((8, 128), f32), whole((8, 128)))], after=after,
    )


def local(n_rep, n_fsdp, inputs, kinds, weights, first_moment, second_moment, anchor, momentum, plan):
    tokens = inputs.shape[0]
    rows, width = weights.shape[2:]
    chips = n_fsdp // 2
    scale = 1.0 / math.sqrt(tokens * n_fsdp)
    chunks = max(1, rows // 512)
    cr = rows // chunks
    cuts = chunks
    cut = rows // cuts
    others = range(1, chips)

    partner = [(f, f ^ 1) for f in range(n_fsdp)]
    to_partner = lambda a: lax.ppermute(a, "fsdp", partner)
    fetch = lambda a, s: lax.ppermute(
        a, "fsdp", [(((f // 2 + s) % chips) * 2 + f % 2, f) for f in range(n_fsdp)])
    give = lambda a, s: lax.ppermute(
        a, "fsdp", [(f, ((f // 2 + s) % chips) * 2 + f % 2) for f in range(n_fsdp)])
    across = lambda a, bit: lax.ppermute(a, "replica", [(r, r ^ bit) for r in range(n_rep)])

    enc, dec = cast_rows(weights)

    chip = lax.axis_index("fsdp") // 2
    core = lax.axis_index("fsdp") % 2
    at = [((chip + s) % chips) * 2 for s in range(chips)]
    pos = jnp.stack([lax.axis_index("replica")] + [a + core for a in at] + [a + 1 - core for a in at]).astype(jnp.int32)

    x_par = to_partner(inputs)
    more = extend(enc, kinds)
    enc_near = to_partner(more)
    cw = weigh(more, enc_near, tokens)

    quarters = outer_start(pos, plan, anchor, weights, [enc])
    xs, xt = zip(*[turn(pos, x, chips, stage) for x, stage in ((inputs, False), (x_par, True))])
    own = outer_add(plan, [quarters[0]] + [across(quarters[m], m) for m in range(1, 4)], n_rep == 4, xt)

    blocks = [(1, 0)] + [(0, i) for i in range(chunks)]
    state = {key: (weights, first_moment, second_moment) for key in blocks}
    state_at = {key: key for key in blocks}
    new_anc = None
    for step in range(INNER):
        last = step == INNER - 1
        enc_far = {s: fetch(enc, s) for s in others}
        dec_far = {s: fetch(dec, s) for s in others}
        if step:
            enc_near = to_partner(enc)
        dec_near = to_partner(dec)

        carry = forward(pos, [], [(enc, 1, 0, rows)], xs, rows, False)
        carry = forward(pos, list(carry), [(enc_near, 1 + chips, 0, rows)], xs, rows, False)
        ready = [cw, own, *xt] if step == 0 else [token]
        part = [(p, 1 + s, n * cut, cut) for s in others for n, p in enumerate(relay(enc_far[s], cuts, [*carry, *ready]))]
        pending = [(to_partner(p), slot + chips, off, size) for p, slot, off, size in part]
        carry = forward(pos, carry, part, xs, rows, False)
        hidden, slope, counted, w_hi, w_lo = hidden_rows(pos, carry[0], cw, pending, xs, rows, scale)
        if step == 0:
            bit = 4
            while bit < n_rep:
                own = outer_add(plan, [own, across(own, bit)], 2 * bit == n_rep)
                bit *= 2

        dec_grad = lambda block, low, dtype, after: grad_rows(
            functools.partial(decoder_body, scale), "decoder_grad", block, rows, xt,
            [counted, w_hi, w_lo, low], dtype, after)
        enc_grad = lambda block, dtype, after: grad_rows(
            encoder_body, "encoder_grad", block, cr, xt, [slopes], dtype, after)
        sent = [own] if step == 0 else []
        got = {key: [] for key in blocks}
        for s in others:
            sent.append(dec_grad(s, dec_far[s], bf16, sent[-1:]))
            got[1, 0].append(give(sent[-1], s))

        carry = forward(pos, [], [(dec, 1, 0, rows)], xs, rows, True, sent[-1:])
        carry = forward(pos, carry, [(dec_near, 1 + chips, 0, rows)], xs, rows, True)
        part = [(p, 1 + s, n * cut, cut) for s in others for n, p in enumerate(relay(dec_far[s], cuts, sent[-1:]))]
        pending = [(to_partner(p), slot + chips, off, size) for p, slot, off, size in part]
        carry = forward(pos, carry, part, xs, rows, True)
        slopes = slope_rows(pos, *carry, hidden, slope, pending, xs, rows)
        for i in range(chunks):
            for s in others:
                sent.append(enc_grad(s * chunks + i, bf16, sent[-1:]))
                got[0, i].append(give(sent[-1], s))
        mine = {(1, 0): dec_grad(0, dec, f32, sent[-1:])}
        for i in range(chunks):
            mine[0, i] = enc_grad(i, f32, sent[-1:])

        if not last:
            quarters = [own] + [across(own, m) for m in range(1, 4)]
            new_anc = outer_anchor(pos, plan, anchor, momentum, quarters, [mine[1, 0]])
        new_state, prev, lows, after = {}, None, [], []
        for key in blocks:
            k, i = key
            more_out = [] if last or k else [lows]
            res = adam_rows(
                plan, k, i, mine[key], got[key], state[key], state_at[key], new_anc, prev, weights.shape, last,
                *more_out, after=after)
            if last:
                prev = res
                continue
            if k == 0:
                lows = lows + [res[0]]
            new_state[key] = tuple(res[-3:])
            after = [] if k == 0 else [res[0]]
        if not last:
            enc = lows[-1]
            dec = mix_rows(plan, new_anc, 1, new_state[1, 0][0], [enc])
            anchor_out, momentum_out, token = outer_end(pos, plan, anchor, momentum, quarters, [dec])
            state, state_at = new_state, {key: (0, 0) for key in blocks}
    return (*prev, anchor_out, momentum_out)


def solution(mesh):
    return jax.shard_map(
        functools.partial(local, mesh.shape["replica"], mesh.shape["fsdp"]),
        mesh=mesh,
        in_specs=(
            P(("replica", "fsdp"), None),
            P(("replica", "fsdp")),
            P("replica", None, "fsdp", None),
            P("replica", None, "fsdp", None),
            P("replica", None, "fsdp", None),
            P(None, "fsdp", None),
            P(None, "fsdp", None),
            P(),
        ),
        out_specs=(
            P("replica", None, "fsdp", None),
            P("replica", None, "fsdp", None),
            P("replica", None, "fsdp", None),
            P(None, "fsdp", None),
            P(None, "fsdp", None),
        ),
        check_vma=False,
    )
```

```python
import functools
import math

import jax
import jax.numpy as jnp
from jax import lax
from jax.experimental import pallas as pl
from jax.experimental.pallas import tpu as pltpu
from jax.sharding import PartitionSpec as P

INNER = 2

inner_rate = 0.003
beta_one = 0.9
beta_two = 0.95
adam_eps = 1e-08
decay_rate = 0.1
outer_rate = 0.7
outer_mu = 0.9
mix_share = 0.5

bf16 = jnp.bfloat16
f32 = jnp.float32
VMEM_LIMIT = 10 * 1024 * 1024


def token_weight(kinds):
    return jnp.where(kinds == 2, 1.0, jnp.where(kinds == 1, 0.25, 0.0)).astype(f32)


def dot(a, b):
    return jnp.dot(a, b, preferred_element_type=f32)


def dot_rows(a, b):
    return lax.dot_general(a, b, (((0,), (0,)), ((), ())), preferred_element_type=f32)


def once(shape, index):
    return pl.BlockSpec(shape, index, pipeline_mode=pl.Buffered(1))


def whole(shape):
    return once(shape, lambda *_: (0,) * len(shape))


def sds(shape, dtype):
    return jax.ShapeDtypeStruct(shape, dtype)


def call(body, name, meta, ins, outs, grid=(1,), scratch=(), aliases=None, flops=0, after=()):
    arrays = [a for a, _ in ins] + list(after)
    n_in = len(meta) + len(ins)
    moved = sum(math.prod(o.shape) * o.dtype.itemsize for o, _ in outs)
    moved += sum(math.prod(s.block_shape or a.shape) * a.dtype.itemsize for a, s in ins)

    def run(*refs):
        body(*refs[:n_in], *refs[n_in + len(after):])

    return pl.pallas_call(
        run,
        name=name,
        out_shape=[o for o, _ in outs],
        grid_spec=pltpu.PrefetchScalarGridSpec(
            num_scalar_prefetch=len(meta),
            grid=grid,
            in_specs=[s for _, s in ins] + [pl.BlockSpec(memory_space=pl.ANY)] * len(after),
            out_specs=[s for _, s in outs],
            scratch_shapes=list(scratch),
        ),
        input_output_aliases=aliases or {},
        compiler_params=pltpu.CompilerParams(vmem_limit_bytes=VMEM_LIMIT),
        cost_estimate=pl.CostEstimate(flops=flops, bytes_accessed=moved, transcendentals=0),
    )(*meta, *arrays)


def plan_sum(plan):
    total = plan[0]
    for r in range(1, plan.shape[0]):
        total = total + plan[r]
    return total


def fragment(plan):
    return lax.rem(plan_sum(plan), 2)


EXTRA = 16


def cast_body(theta, *lows):
    for k, low in enumerate(lows):
        low[...] = theta[0, k].astype(bf16)


def cast_rows(weights):
    _, _, rows, width = weights.shape
    return call(
        cast_body, "cast_rows", (), [(weights, whole(weights.shape))],
        [(sds((rows, width), bf16), whole((rows, width)))] * 2,
    )


def weigh_body(kinds, other, out):
    lanes, wide = kinds.shape
    pad = jnp.zeros((EXTRA - lanes, wide), f32)
    own = jnp.concatenate([token_weight(kinds[...]), pad], 0)
    for h, rows in enumerate((own, other[other.shape[0] - EXTRA:, :].astype(f32))):
        turned = rows.T
        for j in range(lanes):
            out[h, j * wide:(j + 1) * wide, :] = turned[:, j:j + 1]


def weigh(lanes, other, tokens):
    return call(
        weigh_body, "weigh_tokens", (), [(a, whole(a.shape)) for a in (lanes, other)],
        [(sds((2, tokens, 1), f32), whole((2, tokens, 1)))],
    )[0]


def relay_body(cut, x, *refs):
    outs = refs
    if refs[0].dtype != bf16:
        kinds, outs = refs[0], refs[1:]
        pad = jnp.zeros((EXTRA - kinds.shape[0], kinds.shape[1]), f32)
        outs[-1][cut:, :] = jnp.concatenate([token_weight(kinds[...]), pad], 0).astype(bf16)
    for n, out in enumerate(outs):
        out[:cut, :] = x[n * cut:(n + 1) * cut, :]


def relay(x, cuts, after, lanes=None):
    rows, width = x.shape
    cut = rows // cuts
    shapes = [(cut, width)] * (cuts - 1) + [(cut + (0 if lanes is None else EXTRA), width)]
    ins = [x] if lanes is None else [x, lanes]
    return call(
        functools.partial(relay_body, cut), "relay_rows", (), [(a, whole(a.shape)) for a in ins],
        [(sds(shape, x.dtype), whole(shape)) for shape in shapes], after=after,
    )


def turn_block(pos, x, xt, t, tile):
    rows = x.shape[1] // (pos.shape[0] - 1)
    for s in range(xt.shape[0] // rows):
        xt[s * rows:(s + 1) * rows, t:t + tile] = x[t:t + tile, columns(pos, 1 + s, 0, rows, rows)].T


def columns(pos, slot, off, size, rows):
    return pl.ds(pl.multiple_of(pos[slot] * rows + off, size), size)


def turn_body(tile, pos, x, xt):
    for t in range(0, x.shape[0], tile):
        turn_block(pos, x, xt, t, tile)


def stage_body(tile, pos, x, held, xt, sems):
    copies = []
    for n, t in enumerate(range(0, x.shape[0], tile)):
        copy = pltpu.make_async_copy(x.at[pl.ds(t, tile), :], held.at[pl.ds(t, tile), :], sems.at[n])
        copy.start()
        copies.append(copy)
    for n, t in enumerate(range(0, x.shape[0], tile)):
        copies[n].wait()
        turn_block(pos, held, xt, t, tile)


def turn(pos, x, chips, stage):
    tokens, depth = x.shape
    tile = min(128, tokens)
    xt = [(sds((depth // 2, tokens), bf16), whole((depth // 2, tokens)))]
    if not stage:
        return x, call(functools.partial(turn_body, tile), "turn_tokens", (pos,), [(x, whole(x.shape))], xt)[0]
    return call(
        functools.partial(stage_body, tile), "stage_tokens", (pos,), [(x, pl.BlockSpec(memory_space=pl.ANY))],
        [(sds(x.shape, bf16), whole(x.shape))] + xt,
        scratch=[pltpu.SemaphoreType.DMA((tokens // tile,))],
    )


def product(pos, x, low, place, rows):
    slot, off, size = place
    return dot(x[:, columns(pos, slot, off, size, rows)], low[:size, :])


def gram_sum(lows, before):
    for low in lows:
        term = dot_rows(low[...], low[...])
        before = term if before is None else before + term
    return before


def forward_body(places, rows, with_gram, first_call, pos, *refs):
    carry = 2 if with_gram else 1
    before = (None, None) if first_call else refs[:carry]
    if not first_call:
        refs = refs[carry:]
    count = len(places)
    lows, xs = refs[:count], refs[count:count + 2]
    outs = refs[count + 2:]
    if with_gram:
        outs[1][...] = gram_sum(lows, None if first_call else before[1][...])
    for h in range(2):
        value = None if first_call else before[0][h]
        for low, place in zip(lows, places):
            term = product(pos, xs[h], low, place, rows)
            value = term if value is None else value + term
        outs[0][h] = value


def forward(pos, carry, pieces, xs, rows, with_gram, after=()):
    tokens = xs[0].shape[0]
    width = pieces[0][0].shape[1]
    ins = [(a, whole(a.shape)) for a in carry]
    ins += [(p[0], whole(p[0].shape)) for p in pieces] + [(x, whole(x.shape)) for x in xs]
    shapes = [(2, tokens, width)] + [(width, width)] * with_gram
    return call(
        functools.partial(forward_body, [p[1:] for p in pieces], rows, with_gram, not carry),
        "forward_decoder" if with_gram else "forward_encoder", (pos,), ins,
        [(sds(shape, f32), whole(shape)) for shape in shapes], after=after,
    )


def split(total):
    hi = total.astype(bf16)
    return hi, (total - hi.astype(f32)).astype(bf16)


def hidden_body(scale, tile, places, rows, pos, acc_in, cw, *refs):
    count = len(places)
    lows, xs = refs[:count], refs[count:count + 2]
    hidden_out, slope_out, counted_out, w_hi, w_lo, acc = refs[count + 2:]
    total = None
    for h in range(2):
        value = acc_in[h]
        for low, place in zip(lows, places):
            value = value + product(pos, xs[h], low, place, rows)
        acc[h] = value
        for t in range(0, acc.shape[1], tile):
            at = pl.ds(t, tile)
            pre = acc[h, at, :]
            sig = 0.5 + 0.5 * jnp.tanh(0.5 * pre)
            hidden = (pre * sig).astype(bf16)
            weight = cw[h, at, :]
            counted = (weight * hidden.astype(f32)).astype(bf16)
            hidden_out[h, at, :] = hidden
            slope_out[h, at, :] = (weight * scale) * (sig * (1.0 + pre * (1.0 - sig)))
            counted_out[h, at, :] = counted
            term = dot_rows(counted, hidden)
            total = term if total is None else total + term
    w_hi[...], w_lo[...] = split(total)


def hidden_rows(pos, acc, cw, pieces, xs, rows, scale):
    shape = acc.shape
    width = shape[2]
    ins = [(a, whole(a.shape)) for a in [acc, cw] + [p[0] for p in pieces] + list(xs)]
    square = (sds((width, width), bf16), whole((width, width)))
    return call(
        functools.partial(hidden_body, scale, min(256, shape[1]), [p[1:] for p in pieces], rows),
        "hidden_units", (pos,), ins,
        [(sds(shape, bf16), whole(shape)), (sds(shape, f32), whole(shape)), (sds(shape, bf16), whole(shape)), square, square],
        scratch=[pltpu.VMEM(shape, f32)],
    )


def slope_body(places, rows, pos, acc_in, gram_in, hidden, slope, *refs):
    count = len(places)
    lows, xs, out = refs[:count], refs[count:count + 2], refs[count + 2]
    g_hi, g_lo = split(gram_sum(lows, gram_in[...]))
    for h in range(2):
        value = acc_in[h]
        for low, place in zip(lows, places):
            value = value + product(pos, xs[h], low, place, rows)
        back = dot(hidden[h], g_hi) + dot(hidden[h], g_lo) - value
        out[h] = (slope[h] * back).astype(bf16)


def slope_rows(pos, acc, gram, hidden, slope, pieces, xs, rows):
    ins = [(a, whole(a.shape)) for a in [acc, gram, hidden, slope] + [p[0] for p in pieces] + list(xs)]
    return call(
        functools.partial(slope_body, [p[1:] for p in pieces], rows), "slope_pre", (pos,), ins,
        [(sds(acc.shape, bf16), whole(acc.shape))],
    )[0]


def token_sum(start, size, xts, weights):
    at = pl.ds(start, size)
    return dot(xts[0][at, :], weights[0]) + dot(xts[1][at, :], weights[1])


def encoder_body(start, xt_own, xt_par, slopes, out):
    out[...] = token_sum(start, out.shape[0], (xt_own, xt_par), slopes).astype(out.dtype)


def decoder_body(scale, start, xt_own, xt_par, counted, w_hi, w_lo, low, out):
    both = token_sum(start, out.shape[0], (xt_own, xt_par), counted)
    dec = low[:out.shape[0], :]
    out[...] = (scale * (dot(dec, w_hi[...]) + dot(dec, w_lo[...]) - both)).astype(out.dtype)


def grad_rows(body, name, size, xt, others, dtype, after=()):
    shape = (size, others[0].shape[2])
    ins = [(a, whole(a.shape)) for a in [*xt, *others]]
    return call(body, name, (), ins, [(sds(shape, dtype), whole(shape))], after=after)[0]


def adam_body(last, count, k, off, n_low, plan, own, *refs):
    got = refs[:count]
    theta, first, second = refs[count:3 + count]
    refs = refs[3 + count:]
    grad = own[...]
    for g in got:
        grad = grad + g[...].astype(f32)
    one = beta_one * first[0, 0] + (1.0 - beta_one) * grad
    two = beta_two * second[0, 0] + (1.0 - beta_two) * grad * grad
    old = theta[0, 0]
    if last:
        old = mixed(plan, k, old, refs[0][...])
    new = old - inner_rate * (one / (jnp.sqrt(two) + adam_eps) + decay_rate * old)
    if n_low is not None:
        anchor, before, low = refs[0], refs[1:1 + n_low], refs[1 + n_low]
        for b in before:
            low[:off, :] = b[...]
        low[off:, :] = mixed(plan, k, new, anchor[off:off + own.shape[0], :]).astype(bf16)
    theta_out, first_out, second_out = refs[-3:]
    theta_out[0, 0] = new
    first_out[0, 0] = one
    second_out[0, 0] = two


def mixed(plan, k, theta, anchor):
    return jnp.where(fragment(plan) == k, mix_share * theta + (1.0 - mix_share) * anchor, theta)


def adam_rows(plan, key, own, got, state, at, new_anc, prev, full, last, lows=None, after=()):
    k, off, cr = key
    i = off // cr
    width = own.shape[1]
    block = (1, 1, cr, width)
    ins = [(g, whole(g.shape)) for g in [own] + got]
    ins += [(s, once(block, lambda g, m: (0, at[0], at[1], 0))) for s in state]
    aliases = {}
    outs = []
    if last:
        ins.append((new_anc, once((cr, width), lambda g, m: (i, 0))))
        if prev is not None:
            for n, p in enumerate(prev):
                aliases[1 + len(ins)] = n
                ins.append((p, pl.BlockSpec(memory_space=pl.ANY)))
        outs = [(sds(full, f32), once(block, lambda g, m: (0, k, i, 0)))] * 3
    else:
        if lows is not None:
            ins += [(a, whole(a.shape)) for a in [new_anc] + lows]
            shape = (off + cr, width)
            outs = [(sds(shape, bf16), whole(shape))]
        outs += [(sds(block, f32), whole(block))] * 3
    return call(
        functools.partial(adam_body, last, len(got), k, off, None if lows is None else len(lows)), "adam_rows",
        (plan,), ins, outs, aliases=aliases, after=after,
    )


def quarter(pos, m, size):
    where = jnp.bitwise_xor(lax.rem(pos[0], 4), m)
    return pl.ds(pl.multiple_of(where * size, size), size)


def delta_body(pos, plan, anchor, theta, *outs):
    count = plan[pos[0]].astype(f32)
    for m, out in enumerate(outs):
        at = quarter(pos, m, out.shape[0])
        out[...] = (count * (anchor[0, at, :] - theta[0, 0, at, :])).astype(out.dtype)


def outer_start(pos, plan, anchor, weights, after):
    _, rows, width = anchor.shape
    part = (rows // 4, width)
    return call(
        delta_body, "delta_quarters", (pos, plan),
        [
            (anchor, once((1, rows, width), lambda g, p, q: (fragment(q), 0, 0))),
            (weights, once((1, 1, rows, width), lambda g, p, q: (0, fragment(q), 0, 0))),
        ],
        [(sds(part, f32), whole(part))] + [(sds(part, bf16), whole(part))] * 3, after=after,
    )


def add_body(final, plan, *refs):
    total = refs[0][...].astype(f32)
    for r in refs[1:-1]:
        total = total + r[...].astype(f32)
    if final:
        total = total / plan_sum(plan).astype(f32)
    refs[-1][...] = total.astype(bf16)


def outer_add(plan, parts, final, after=()):
    shape = parts[0].shape
    return call(
        functools.partial(add_body, final), "add_quarters", (plan,), [(a, whole(shape)) for a in parts],
        [(sds(shape, bf16), whole(shape))], after=after,
    )[0]


def outer_update(frag, at, anchor, momentum, grad):
    mom = outer_mu * momentum[frag, at, :] + grad
    return anchor[frag, at, :] - outer_rate * (grad + outer_mu * mom), mom


def new_anchor_body(pos, plan, anchor, momentum, *refs):
    for m, piece in enumerate(refs[:4]):
        at = quarter(pos, m, piece.shape[0])
        refs[4][at, :] = outer_update(0, at, anchor, momentum, piece[...].astype(f32))[0]


def outer_anchor(pos, plan, anchor, momentum, quarters, after):
    _, rows, width = anchor.shape
    part = once((1, rows, width), lambda g, p, q: (fragment(q), 0, 0))
    return call(
        new_anchor_body, "new_anchor", (pos, plan),
        [(anchor, part), (momentum, part)] + [(a, whole(a.shape)) for a in quarters],
        [(sds((rows, width), f32), whole((rows, width)))], after=after,
    )[0]


def mix_body(k, plan, new_anc, theta, low):
    low[...] = mixed(plan, k, theta[0, 0], new_anc[...]).astype(bf16)


def mix_rows(plan, new_anc, k, theta, after):
    shape = new_anc.shape
    return call(
        functools.partial(mix_body, k), "mix_rows", (plan,), [(a, whole(a.shape)) for a in (new_anc, theta)],
        [(sds(shape, bf16), whole(shape))], after=after,
    )[0]


def outer_body(pos, plan, anchor, momentum, *refs):
    quarters = refs[:4]
    anchor_out, momentum_out, token = refs[4:]
    token[...] = jnp.zeros_like(token)
    frag = fragment(plan)
    anchor_out[...] = anchor[...]
    momentum_out[...] = momentum[...]
    for m, piece in enumerate(quarters):
        at = quarter(pos, m, piece.shape[0])
        anc, mom = outer_update(frag, at, anchor, momentum, piece[...].astype(f32))
        anchor_out[frag, at, :] = anc
        momentum_out[frag, at, :] = mom


def outer_end(pos, plan, anchor, momentum, quarters, after):
    return call(
        outer_body, "outer_step", (pos, plan),
        [(a, whole(a.shape)) for a in [anchor, momentum] + quarters],
        [(sds(anchor.shape, f32), whole(anchor.shape))] * 2 + [(sds((8, 128), f32), whole((8, 128)))], after=after,
    )


def local(n_rep, n_fsdp, inputs, kinds, weights, first_moment, second_moment, anchor, momentum, plan):
    tokens = inputs.shape[0]
    rows, width = weights.shape[2:]
    chips = n_fsdp // 2
    scale = 1.0 / math.sqrt(tokens * n_fsdp)
    cuts = max(1, rows // 512)
    cut = rows // cuts
    others = range(1, chips)

    partner = [(f, f ^ 1) for f in range(n_fsdp)]
    to_partner = lambda a: lax.ppermute(a, "fsdp", partner)
    fetch = lambda a, s: lax.ppermute(
        a, "fsdp", [(((f // 2 + s) % chips) * 2 + f % 2, f) for f in range(n_fsdp)])
    give = lambda a, s: lax.ppermute(
        a, "fsdp", [(f, ((f // 2 + s) % chips) * 2 + f % 2) for f in range(n_fsdp)])
    across = lambda a, bit: lax.ppermute(a, "replica", [(r, r ^ bit) for r in range(n_rep)])

    enc, dec = cast_rows(weights)

    chip = lax.axis_index("fsdp") // 2
    core = lax.axis_index("fsdp") % 2
    at = [((chip + s) % chips) * 2 for s in range(chips)]
    pos = jnp.stack([lax.axis_index("replica")] + [a + core for a in at] + [a + 1 - core for a in at]).astype(jnp.int32)

    x_par = to_partner(inputs)
    quarters = outer_start(pos, plan, anchor, weights, [enc])
    lanes = kinds.reshape(-1, width)
    xs, xt = zip(*[turn(pos, x, chips, stage) for x, stage in ((inputs, False), (x_par, True))])
    own = outer_add(plan, [quarters[0]] + [across(quarters[m], m) for m in range(1, 4)], n_rep == 4, xt)

    most = rows - rows // 4 if rows >= 1024 else rows
    blocks = [(1, 0, rows), (0, 0, most)] + [(0, off, rows - most) for off in range(most, rows, max(1, rows - most))]
    state = {key: (weights, first_moment, second_moment) for key in blocks}
    state_at = {(k, off, size): (k, off // size) for k, off, size in blocks}
    new_anc = None
    for step in range(INNER):
        last = step == INNER - 1
        enc_far = {s: fetch(enc, s) for s in others}
        dec_far = {s: fetch(dec, s) for s in others}
        enc_near, dec_near = to_partner(enc), to_partner(dec)

        carry = forward(pos, [], [(enc, 1, 0, rows)], xs, rows, False)
        carry = forward(pos, list(carry), [(enc_near, 1 + chips, 0, rows)], xs, rows, False)
        ready = [own, *xt] if step == 0 else [token]
        riders = [lanes] if step == 0 else []
        part = [(p, 1 + s, n * cut, cut) for s in others for n, p in enumerate(
            relay(enc_far[s], cuts, [*carry, *ready], *riders))]
        pending = [(to_partner(p), slot + chips, off, size) for p, slot, off, size in part]
        carry = forward(pos, carry, part, xs, rows, False)
        if step == 0:
            cw = weigh(lanes, pending[-1][0], tokens)
        hidden, slope, counted, w_hi, w_lo = hidden_rows(pos, carry[0], cw, pending, xs, rows, scale)
        if step == 0:
            bit = 4
            while bit < n_rep:
                own = outer_add(plan, [own, across(own, bit)], 2 * bit == n_rep)
                bit *= 2

        dec_grad = lambda s, low, dtype, after: grad_rows(
            functools.partial(decoder_body, scale, s * rows), "decoder_grad", rows, xt,
            [counted, w_hi, w_lo, low], dtype, after)
        enc_grad = lambda s, off, size, dtype, after: grad_rows(
            functools.partial(encoder_body, s * rows + off), "encoder_grad", size, xt, [slopes], dtype, after)
        sent = []
        got = {key: [] for key in blocks}
        for s in others:
            sent.append(dec_grad(s, dec_far[s], bf16, sent[-1:]))
            got[blocks[0]].append(give(sent[-1], s))

        carry = forward(pos, [], [(dec, 1, 0, rows)], xs, rows, True, sent[-1:])
        part = [(p, 1 + s, n * cut, cut) for s in others for n, p in enumerate(relay(dec_far[s], cuts, sent[-1:]))]
        carry = forward(pos, carry, [(dec_near, 1 + chips, 0, rows)], xs, rows, True)
        pending = [(to_partner(p), slot + chips, off, size) for p, slot, off, size in part]
        carry = forward(pos, carry, part, xs, rows, True)
        slopes = slope_rows(pos, *carry, hidden, slope, pending, xs, rows)
        for key in blocks[1:]:
            for s in others:
                sent.append(enc_grad(s, *key[1:], bf16, sent[-1:]))
                got[key].append(give(sent[-1], s))
        mine = {blocks[0]: dec_grad(0, dec, f32, sent[-1:])}
        for key in blocks[1:]:
            mine[key] = enc_grad(0, *key[1:], f32, sent[-1:])

        if not last:
            quarters = [own] + [across(own, m) for m in range(1, 4)]
            new_anc = outer_anchor(pos, plan, anchor, momentum, quarters, [mine[blocks[0]]])
        new_state, prev, lows, after = {}, None, [], []
        for key in blocks:
            k = key[0]
            more_out = [] if last or k else [lows]
            res = adam_rows(
                plan, key, mine[key], got[key], state[key], state_at[key], new_anc, prev, weights.shape, last,
                *more_out, after=after)
            if last:
                prev = res
                continue
            if k == 0:
                lows = [res[0]]
            new_state[key] = tuple(res[-3:])
            after = [] if k == 0 else [res[0]]
        if not last:
            enc = lows[-1]
            dec = mix_rows(plan, new_anc, 1, new_state[blocks[0]][0], [enc])
            anchor_out, momentum_out, token = outer_end(pos, plan, anchor, momentum, quarters, [dec])
            state, state_at = new_state, {key: (0, 0) for key in blocks}
    return (*prev, anchor_out, momentum_out)


def solution(mesh):
    return jax.shard_map(
        functools.partial(local, mesh.shape["replica"], mesh.shape["fsdp"]),
        mesh=mesh,
        in_specs=(
            P(("replica", "fsdp"), None),
            P(("replica", "fsdp")),
            P("replica", None, "fsdp", None),
            P("replica", None, "fsdp", None),
            P("replica", None, "fsdp", None),
            P(None, "fsdp", None),
            P(None, "fsdp", None),
            P(),
        ),
        out_specs=(
            P("replica", None, "fsdp", None),
            P("replica", None, "fsdp", None),
            P("replica", None, "fsdp", None),
            P(None, "fsdp", None),
            P(None, "fsdp", None),
        ),
        check_vma=False,
    )
```

```python
import functools
import math

import jax
import jax.numpy as jnp
from jax import lax
from jax.experimental import pallas as pl
from jax.experimental.pallas import tpu as pltpu
from jax.sharding import PartitionSpec as P

INNER = 2

inner_rate = 0.003
beta_one = 0.9
beta_two = 0.95
adam_eps = 1e-08
decay_rate = 0.1
outer_rate = 0.7
outer_mu = 0.9
mix_share = 0.5

bf16 = jnp.bfloat16
f32 = jnp.float32
VMEM_LIMIT = 10 * 1024 * 1024


def token_weight(kinds):
    return jnp.where(kinds == 2, 1.0, jnp.where(kinds == 1, 0.25, 0.0)).astype(f32)


def dot(a, b):
    return jnp.dot(a, b, preferred_element_type=f32)


def dot_rows(a, b):
    return lax.dot_general(a, b, (((0,), (0,)), ((), ())), preferred_element_type=f32)


def once(shape, index):
    return pl.BlockSpec(shape, index, pipeline_mode=pl.Buffered(1))


def whole(shape):
    return once(shape, lambda *_: (0,) * len(shape))


def sds(shape, dtype):
    return jax.ShapeDtypeStruct(shape, dtype)


def call(body, name, meta, ins, outs, grid=(1,), scratch=(), aliases=None, flops=0, after=()):
    arrays = [a for a, _ in ins] + list(after)
    n_in = len(meta) + len(ins)
    moved = sum(math.prod(o.shape) * o.dtype.itemsize for o, _ in outs)
    moved += sum(math.prod(s.block_shape or a.shape) * a.dtype.itemsize for a, s in ins)

    def run(*refs):
        body(*refs[:n_in], *refs[n_in + len(after):])

    return pl.pallas_call(
        run,
        name=name,
        out_shape=[o for o, _ in outs],
        grid_spec=pltpu.PrefetchScalarGridSpec(
            num_scalar_prefetch=len(meta),
            grid=grid,
            in_specs=[s for _, s in ins] + [pl.BlockSpec(memory_space=pl.ANY)] * len(after),
            out_specs=[s for _, s in outs],
            scratch_shapes=list(scratch),
        ),
        input_output_aliases=aliases or {},
        compiler_params=pltpu.CompilerParams(vmem_limit_bytes=VMEM_LIMIT),
        cost_estimate=pl.CostEstimate(flops=flops, bytes_accessed=moved, transcendentals=0),
    )(*meta, *arrays)


def plan_sum(plan):
    total = plan[0]
    for r in range(1, plan.shape[0]):
        total = total + plan[r]
    return total


def fragment(plan):
    return lax.rem(plan_sum(plan), 2)


EXTRA = 16


def cast_body(theta, *lows):
    for k, low in enumerate(lows):
        low[...] = theta[0, k].astype(bf16)


def cast_rows(weights):
    _, _, rows, width = weights.shape
    return call(
        cast_body, "cast_rows", (), [(weights, whole(weights.shape))],
        [(sds((rows, width), bf16), whole((rows, width)))] * 2,
    )


def weigh_body(kinds, other, out):
    lanes, wide = kinds.shape
    pad = jnp.zeros((EXTRA - lanes, wide), f32)
    own = jnp.concatenate([token_weight(kinds[...]), pad], 0)
    for h, rows in enumerate((own, other[other.shape[0] - EXTRA:, :].astype(f32))):
        turned = rows.T
        for j in range(lanes):
            out[h, j * wide:(j + 1) * wide, :] = turned[:, j:j + 1]


def weigh(lanes, other, tokens):
    return call(
        weigh_body, "weigh_tokens", (), [(a, whole(a.shape)) for a in (lanes, other)],
        [(sds((2, tokens, 1), f32), whole((2, tokens, 1)))],
    )[0]


def relay_body(cut, x, *refs):
    outs = refs
    if refs[0].dtype != bf16:
        kinds, outs = refs[0], refs[1:]
        pad = jnp.zeros((EXTRA - kinds.shape[0], kinds.shape[1]), f32)
        outs[-1][cut:, :] = jnp.concatenate([token_weight(kinds[...]), pad], 0).astype(bf16)
    for n, out in enumerate(outs):
        out[:cut, :] = x[n * cut:(n + 1) * cut, :]


def relay(x, cuts, after, lanes=None):
    rows, width = x.shape
    cut = rows // cuts
    shapes = [(cut, width)] * (cuts - 1) + [(cut + (0 if lanes is None else EXTRA), width)]
    ins = [x] if lanes is None else [x, lanes]
    return call(
        functools.partial(relay_body, cut), "relay_rows", (), [(a, whole(a.shape)) for a in ins],
        [(sds(shape, x.dtype), whole(shape)) for shape in shapes], after=after,
    )


def turn_block(pos, x, xt, t, tile):
    rows = x.shape[1] // (pos.shape[0] - 1)
    for s in range(xt.shape[0] // rows):
        xt[s * rows:(s + 1) * rows, t:t + tile] = x[t:t + tile, columns(pos, 1 + s, 0, rows, rows)].T


def columns(pos, slot, off, size, rows):
    return pl.ds(pl.multiple_of(pos[slot] * rows + off, size), size)


def turn_body(tile, pos, x, xt):
    for t in range(0, x.shape[0], tile):
        turn_block(pos, x, xt, t, tile)


def stage_body(tile, pos, x, held, xt, sems):
    copies = []
    for n, t in enumerate(range(0, x.shape[0], tile)):
        copy = pltpu.make_async_copy(x.at[pl.ds(t, tile), :], held.at[pl.ds(t, tile), :], sems.at[n])
        copy.start()
        copies.append(copy)
    for n, t in enumerate(range(0, x.shape[0], tile)):
        copies[n].wait()
        turn_block(pos, held, xt, t, tile)


def turn(pos, x, chips, stage):
    tokens, depth = x.shape
    tile = min(128, tokens)
    xt = [(sds((depth // 2, tokens), bf16), whole((depth // 2, tokens)))]
    if not stage:
        return x, call(functools.partial(turn_body, tile), "turn_tokens", (pos,), [(x, whole(x.shape))], xt)[0]
    return call(
        functools.partial(stage_body, tile), "stage_tokens", (pos,), [(x, pl.BlockSpec(memory_space=pl.ANY))],
        [(sds(x.shape, bf16), whole(x.shape))] + xt,
        scratch=[pltpu.SemaphoreType.DMA((tokens // tile,))],
    )


def product(pos, x, low, place, rows):
    slot, off, size = place
    return dot(x[:, columns(pos, slot, off, size, rows)], low[:size, :])


def gram_sum(lows, before):
    for low in lows:
        term = dot_rows(low[...], low[...])
        before = term if before is None else before + term
    return before


def forward_body(places, rows, with_gram, first_call, pos, *refs):
    carry = 2 if with_gram else 1
    before = (None, None) if first_call else refs[:carry]
    if not first_call:
        refs = refs[carry:]
    count = len(places)
    lows, xs = refs[:count], refs[count:count + 2]
    outs = refs[count + 2:]
    if with_gram:
        outs[1][...] = gram_sum(lows, None if first_call else before[1][...])
    for h in range(2):
        value = None if first_call else before[0][h]
        for low, place in zip(lows, places):
            term = product(pos, xs[h], low, place, rows)
            value = term if value is None else value + term
        outs[0][h] = value


def forward(pos, carry, pieces, xs, rows, with_gram, after=()):
    tokens = xs[0].shape[0]
    width = pieces[0][0].shape[1]
    ins = [(a, whole(a.shape)) for a in carry]
    ins += [(p[0], whole(p[0].shape)) for p in pieces] + [(x, whole(x.shape)) for x in xs]
    shapes = [(2, tokens, width)] + [(width, width)] * with_gram
    return call(
        functools.partial(forward_body, [p[1:] for p in pieces], rows, with_gram, not carry),
        "forward_decoder" if with_gram else "forward_encoder", (pos,), ins,
        [(sds(shape, f32), whole(shape)) for shape in shapes], after=after,
    )


def split(total):
    hi = total.astype(bf16)
    return hi, (total - hi.astype(f32)).astype(bf16)


def hidden_body(scale, tile, places, rows, pos, acc_in, cw, *refs):
    count = len(places)
    lows, xs = refs[:count], refs[count:count + 2]
    hidden_out, slope_out, counted_out, w_hi, w_lo, acc = refs[count + 2:]
    total = None
    for h in range(2):
        value = acc_in[h]
        for low, place in zip(lows, places):
            value = value + product(pos, xs[h], low, place, rows)
        acc[h] = value
        for t in range(0, acc.shape[1], tile):
            at = pl.ds(t, tile)
            pre = acc[h, at, :]
            sig = 0.5 + 0.5 * jnp.tanh(0.5 * pre)
            hidden = (pre * sig).astype(bf16)
            weight = cw[h, at, :]
            counted = (weight * hidden.astype(f32)).astype(bf16)
            hidden_out[h, at, :] = hidden
            slope_out[h, at, :] = (weight * scale) * (sig * (1.0 + pre * (1.0 - sig)))
            counted_out[h, at, :] = counted
            term = dot_rows(counted, hidden)
            total = term if total is None else total + term
    w_hi[...], w_lo[...] = split(total)


def hidden_rows(pos, acc, cw, pieces, xs, rows, scale):
    shape = acc.shape
    width = shape[2]
    ins = [(a, whole(a.shape)) for a in [acc, cw] + [p[0] for p in pieces] + list(xs)]
    square = (sds((width, width), bf16), whole((width, width)))
    return call(
        functools.partial(hidden_body, scale, min(256, shape[1]), [p[1:] for p in pieces], rows),
        "hidden_units", (pos,), ins,
        [(sds(shape, bf16), whole(shape)), (sds(shape, f32), whole(shape)), (sds(shape, bf16), whole(shape)), square, square],
        scratch=[pltpu.VMEM(shape, f32)],
    )


def slope_body(places, rows, pos, acc_in, gram_in, hidden, slope, *refs):
    count = len(places)
    lows, xs, out = refs[:count], refs[count:count + 2], refs[count + 2]
    g_hi, g_lo = split(gram_sum(lows, gram_in[...]))
    for h in range(2):
        value = acc_in[h]
        for low, place in zip(lows, places):
            value = value + product(pos, xs[h], low, place, rows)
        back = dot(hidden[h], g_hi) + dot(hidden[h], g_lo) - value
        out[h] = (slope[h] * back).astype(bf16)


def slope_rows(pos, acc, gram, hidden, slope, pieces, xs, rows):
    ins = [(a, whole(a.shape)) for a in [acc, gram, hidden, slope] + [p[0] for p in pieces] + list(xs)]
    return call(
        functools.partial(slope_body, [p[1:] for p in pieces], rows), "slope_pre", (pos,), ins,
        [(sds(acc.shape, bf16), whole(acc.shape))],
    )[0]


def token_sum(start, size, xts, weights):
    at = pl.ds(start, size)
    return dot(xts[0][at, :], weights[0]) + dot(xts[1][at, :], weights[1])


def encoder_body(start, xt_own, xt_par, slopes, out):
    out[...] = token_sum(start, out.shape[0], (xt_own, xt_par), slopes).astype(out.dtype)


def decoder_body(scale, start, pieces, xt_own, xt_par, counted, w_hi, w_lo, *refs):
    lows, got, out = refs[:pieces], refs[pieces:-1], refs[-1]
    off = 0
    for low in lows:
        size = low.shape[0]
        both = token_sum(start + off, size, (xt_own, xt_par), counted)
        value = scale * (dot(low[...], w_hi[...]) + dot(low[...], w_lo[...]) - both)
        for g in got:
            value = value + g[off:off + size, :].astype(f32)
        out[off:off + size, :] = value.astype(out.dtype)
        off += size


def grad_rows(body, name, size, xt, others, dtype, after=()):
    shape = (size, others[0].shape[2])
    ins = [(a, whole(a.shape)) for a in [*xt, *others]]
    return call(body, name, (), ins, [(sds(shape, dtype), whole(shape))], after=after)[0]


def adam_body(last, count, k, off, n_low, plan, own, *refs):
    got = refs[:count]
    theta, first, second = refs[count:3 + count]
    refs = refs[3 + count:]
    grad = own[...]
    for g in got:
        grad = grad + g[...].astype(f32)
    one = beta_one * first[0, 0] + (1.0 - beta_one) * grad
    two = beta_two * second[0, 0] + (1.0 - beta_two) * grad * grad
    old = theta[0, 0]
    if last:
        old = mixed(plan, k, old, refs[0][...])
    new = old - inner_rate * (one / (jnp.sqrt(two) + adam_eps) + decay_rate * old)
    if n_low is not None:
        anchor, before, low = refs[0], refs[1:1 + n_low], refs[1 + n_low]
        for b in before:
            low[:off, :] = b[...]
        low[off:, :] = mixed(plan, k, new, anchor[off:off + own.shape[0], :]).astype(bf16)
    theta_out, first_out, second_out = refs[-3:]
    theta_out[0, 0] = new
    first_out[0, 0] = one
    second_out[0, 0] = two


def mixed(plan, k, theta, anchor):
    return jnp.where(fragment(plan) == k, mix_share * theta + (1.0 - mix_share) * anchor, theta)


def adam_rows(plan, key, own, got, state, at, new_anc, prev, full, last, lows=None, after=()):
    k, off, cr = key
    i = off // cr
    width = own.shape[1]
    block = (1, 1, cr, width)
    ins = [(g, whole(g.shape)) for g in [own] + got]
    ins += [(s, once(block, lambda g, m: (0, at[0], at[1], 0))) for s in state]
    aliases = {}
    outs = []
    if last:
        ins.append((new_anc, once((cr, width), lambda g, m: (i, 0))))
        if prev is not None:
            for n, p in enumerate(prev):
                aliases[1 + len(ins)] = n
                ins.append((p, pl.BlockSpec(memory_space=pl.ANY)))
        outs = [(sds(full, f32), once(block, lambda g, m: (0, k, i, 0)))] * 3
    else:
        if lows is not None:
            ins += [(a, whole(a.shape)) for a in [new_anc] + lows]
            shape = (off + cr, width)
            outs = [(sds(shape, bf16), whole(shape))]
        outs += [(sds(block, f32), whole(block))] * 3
    return call(
        functools.partial(adam_body, last, len(got), k, off, None if lows is None else len(lows)), "adam_rows",
        (plan,), ins, outs, aliases=aliases, after=after,
    )


def quarter(pos, m, size):
    where = jnp.bitwise_xor(lax.rem(pos[0], 4), m)
    return pl.ds(pl.multiple_of(where * size, size), size)


def delta_body(pos, plan, anchor, theta, *outs):
    count = plan[pos[0]].astype(f32)
    for m, out in enumerate(outs):
        at = quarter(pos, m, out.shape[0])
        out[...] = (count * (anchor[0, at, :] - theta[0, 0, at, :])).astype(out.dtype)


def outer_start(pos, plan, anchor, weights, after):
    _, rows, width = anchor.shape
    part = (rows // 4, width)
    return call(
        delta_body, "delta_quarters", (pos, plan),
        [
            (anchor, once((1, rows, width), lambda g, p, q: (fragment(q), 0, 0))),
            (weights, once((1, 1, rows, width), lambda g, p, q: (0, fragment(q), 0, 0))),
        ],
        [(sds(part, f32), whole(part))] + [(sds(part, bf16), whole(part))] * 3, after=after,
    )


def add_body(final, plan, *refs):
    total = refs[0][...].astype(f32)
    for r in refs[1:-1]:
        total = total + r[...].astype(f32)
    if final:
        total = total / plan_sum(plan).astype(f32)
    refs[-1][...] = total.astype(bf16)


def outer_add(plan, parts, final, after=()):
    shape = parts[0].shape
    return call(
        functools.partial(add_body, final), "add_quarters", (plan,), [(a, whole(shape)) for a in parts],
        [(sds(shape, bf16), whole(shape))], after=after,
    )[0]


def outer_update(frag, at, anchor, momentum, grad):
    mom = outer_mu * momentum[frag, at, :] + grad
    return anchor[frag, at, :] - outer_rate * (grad + outer_mu * mom), mom


def new_anchor_body(pos, plan, anchor, momentum, *refs):
    for m, piece in enumerate(refs[:4]):
        at = quarter(pos, m, piece.shape[0])
        refs[4][at, :] = outer_update(0, at, anchor, momentum, piece[...].astype(f32))[0]


def outer_anchor(pos, plan, anchor, momentum, quarters, after):
    _, rows, width = anchor.shape
    part = once((1, rows, width), lambda g, p, q: (fragment(q), 0, 0))
    return call(
        new_anchor_body, "new_anchor", (pos, plan),
        [(anchor, part), (momentum, part)] + [(a, whole(a.shape)) for a in quarters],
        [(sds((rows, width), f32), whole((rows, width)))], after=after,
    )[0]


def mix_body(k, plan, new_anc, theta, low):
    low[...] = mixed(plan, k, theta[0, 0], new_anc[...]).astype(bf16)


def mix_rows(plan, new_anc, k, theta, after):
    shape = new_anc.shape
    return call(
        functools.partial(mix_body, k), "mix_rows", (plan,), [(a, whole(a.shape)) for a in (new_anc, theta)],
        [(sds(shape, bf16), whole(shape))], after=after,
    )[0]


def outer_body(pos, plan, anchor, momentum, *refs):
    quarters = refs[:4]
    anchor_out, momentum_out, token = refs[4:]
    token[...] = jnp.zeros_like(token)
    frag = fragment(plan)
    anchor_out[...] = anchor[...]
    momentum_out[...] = momentum[...]
    for m, piece in enumerate(quarters):
        at = quarter(pos, m, piece.shape[0])
        anc, mom = outer_update(frag, at, anchor, momentum, piece[...].astype(f32))
        anchor_out[frag, at, :] = anc
        momentum_out[frag, at, :] = mom


def outer_end(pos, plan, anchor, momentum, quarters, after):
    return call(
        outer_body, "outer_step", (pos, plan),
        [(a, whole(a.shape)) for a in [anchor, momentum] + quarters],
        [(sds(anchor.shape, f32), whole(anchor.shape))] * 2 + [(sds((8, 128), f32), whole((8, 128)))], after=after,
    )


def local(n_rep, n_fsdp, inputs, kinds, weights, first_moment, second_moment, anchor, momentum, plan):
    tokens = inputs.shape[0]
    rows, width = weights.shape[2:]
    chips = n_fsdp // 2
    scale = 1.0 / math.sqrt(tokens * n_fsdp)
    cuts = max(1, rows // 512)
    cut = rows // cuts
    others = range(1, chips)

    partner = [(f, f ^ 1) for f in range(n_fsdp)]
    to_partner = lambda a: lax.ppermute(a, "fsdp", partner)
    fetch = lambda a, s: lax.ppermute(
        a, "fsdp", [(((f // 2 + s) % chips) * 2 + f % 2, f) for f in range(n_fsdp)])
    give = lambda a, s: lax.ppermute(
        a, "fsdp", [(f, ((f // 2 + s) % chips) * 2 + f % 2) for f in range(n_fsdp)])
    across = lambda a, bit: lax.ppermute(a, "replica", [(r, r ^ bit) for r in range(n_rep)])

    enc, dec = cast_rows(weights)

    chip = lax.axis_index("fsdp") // 2
    core = lax.axis_index("fsdp") % 2
    at = [((chip + s) % chips) * 2 for s in range(chips)]
    pos = jnp.stack([lax.axis_index("replica")] + [a + core for a in at] + [a + 1 - core for a in at]).astype(jnp.int32)

    x_par = to_partner(inputs)
    quarters = outer_start(pos, plan, anchor, weights, [enc])
    lanes = kinds.reshape(-1, width)
    xs, xt = zip(*[turn(pos, x, chips, stage) for x, stage in ((inputs, False), (x_par, True))])
    own = outer_add(plan, [quarters[0]] + [across(quarters[m], m) for m in range(1, 4)], n_rep == 4, xt)

    most = rows - rows // 4 if rows >= 1024 else rows
    blocks = [(1, 0, rows), (0, 0, most)] + [(0, off, rows - most) for off in range(most, rows, max(1, rows - most))]
    state = {key: (weights, first_moment, second_moment) for key in blocks}
    state_at = {(k, off, size): (k, off // size) for k, off, size in blocks}
    new_anc = None
    for step in range(INNER):
        last = step == INNER - 1
        enc_far = {s: fetch(enc, s) for s in others}
        dec_far = {s: fetch(dec, s) for s in others}
        enc_near, dec_near = to_partner(enc), to_partner(dec)

        carry = forward(pos, [], [(enc, 1, 0, rows), (enc_near, 1 + chips, 0, rows)], xs, rows, False)
        ready = [own, *xt] if step == 0 else [token]
        riders = [lanes] if step == 0 else []
        part = [(p, 1 + s, n * cut, cut) for s in others for n, p in enumerate(
            relay(enc_far[s], cuts, [*carry, *ready], *riders))]
        pending = [(to_partner(p), slot + chips, off, size) for p, slot, off, size in part]
        carry = forward(pos, carry, part, xs, rows, False)
        if step == 0:
            cw = weigh(lanes, pending[-1][0], tokens)
        hidden, slope, counted, w_hi, w_lo = hidden_rows(pos, carry[0], cw, pending, xs, rows, scale)
        dec_grad = lambda s, lows, more, dtype, after: grad_rows(
            functools.partial(decoder_body, scale, s * rows, len(lows)), "decoder_grad", rows, xt,
            [counted, w_hi, w_lo, *lows, *more], dtype, after)
        enc_grad = lambda s, off, size, dtype, after: grad_rows(
            functools.partial(encoder_body, s * rows + off), "encoder_grad", size, xt, [slopes], dtype, after)
        sent = []
        got = {key: [] for key in blocks}
        far = {s: relay(dec_far[s], cuts, [counted]) for s in others}
        for s in others:
            sent.append(dec_grad(s, far[s], [], bf16, sent[-1:]))
            got[blocks[0]].append(give(sent[-1], s))

        part = [(p, 1 + s, n * cut, cut) for s in others for n, p in enumerate(far[s])]
        pending = [(to_partner(p), slot + chips, off, size) for p, slot, off, size in part]
        carry = forward(
            pos, [], [(dec, 1, 0, rows), (dec_near, 1 + chips, 0, rows)] + part, xs, rows, True, sent[-1:])
        slopes = slope_rows(pos, *carry, hidden, slope, pending, xs, rows)
        if step == 0:
            bit = 4
            while bit < n_rep:
                own = outer_add(plan, [own, across(own, bit)], 2 * bit == n_rep, [slopes])
                bit *= 2
            sent.append(own)
        for n, key in enumerate(blocks[1:]):
            for s in others:
                sent.append(enc_grad(s, *key[1:], bf16, sent[-1:]))
                got[key].append(give(sent[-1], s))
            if n == 0:
                mine = {blocks[0]: dec_grad(0, [dec], got[blocks[0]], f32, sent[-1:])}
                got[blocks[0]] = []
                sent.append(mine[blocks[0]])
        for key in blocks[1:]:
            mine[key] = enc_grad(0, *key[1:], f32, sent[-1:])

        if not last:
            quarters = [own] + [across(own, m) for m in range(1, 4)]
            new_anc = outer_anchor(pos, plan, anchor, momentum, quarters, [mine[blocks[0]]])
        new_state, prev, lows = {}, None, []
        adam = lambda key, prev, *more, after=(): adam_rows(
            plan, key, mine[key], got[key], state[key], state_at[key], new_anc, prev, weights.shape, last,
            *more, after=after)
        if last:
            for key in blocks:
                prev = adam(key, prev)
        else:
            for key in blocks[1:]:
                enc, *new_state[key] = adam(key, None, lows)
                lows = [enc]
            new_state[blocks[0]] = adam(blocks[0], None, after=[enc])
            dec = mix_rows(plan, new_anc, 1, new_state[blocks[0]][0], [enc])
            anchor_out, momentum_out, token = outer_end(pos, plan, anchor, momentum, quarters, [dec])
            state, state_at = new_state, {key: (0, 0) for key in blocks}
    return (*prev, anchor_out, momentum_out)


def solution(mesh):
    return jax.shard_map(
        functools.partial(local, mesh.shape["replica"], mesh.shape["fsdp"]),
        mesh=mesh,
        in_specs=(
            P(("replica", "fsdp"), None),
            P(("replica", "fsdp")),
            P("replica", None, "fsdp", None),
            P("replica", None, "fsdp", None),
            P("replica", None, "fsdp", None),
            P(None, "fsdp", None),
            P(None, "fsdp", None),
            P(),
        ),
        out_specs=(
            P("replica", None, "fsdp", None),
            P("replica", None, "fsdp", None),
            P("replica", None, "fsdp", None),
            P(None, "fsdp", None),
            P(None, "fsdp", None),
        ),
        check_vma=False,
    )
```

```python
import functools
import math

import jax
import jax.numpy as jnp
from jax import lax
from jax.experimental import pallas as pl
from jax.experimental.pallas import tpu as pltpu
from jax.sharding import PartitionSpec as P

INNER = 2

inner_rate = 0.003
beta_one = 0.9
beta_two = 0.95
adam_eps = 1e-08
decay_rate = 0.1
outer_rate = 0.7
outer_mu = 0.9
mix_share = 0.5

bf16 = jnp.bfloat16
f32 = jnp.float32
VMEM_LIMIT = 10 * 1024 * 1024


def token_weight(kinds):
    return jnp.where(kinds == 2, 1.0, jnp.where(kinds == 1, 0.25, 0.0)).astype(f32)


def dot(a, b):
    return jnp.dot(a, b, preferred_element_type=f32)


def dot_rows(a, b):
    return lax.dot_general(a, b, (((0,), (0,)), ((), ())), preferred_element_type=f32)


def once(shape, index):
    return pl.BlockSpec(shape, index, pipeline_mode=pl.Buffered(1))


def whole(shape):
    return once(shape, lambda *_: (0,) * len(shape))


def sds(shape, dtype):
    return jax.ShapeDtypeStruct(shape, dtype)


def call(body, name, meta, ins, outs, grid=(1,), scratch=(), aliases=None, flops=0, after=()):
    arrays = [a for a, _ in ins] + list(after)
    n_in = len(meta) + len(ins)
    moved = sum(math.prod(o.shape) * o.dtype.itemsize for o, _ in outs)
    moved += sum(math.prod(s.block_shape or a.shape) * a.dtype.itemsize for a, s in ins)

    def run(*refs):
        body(*refs[:n_in], *refs[n_in + len(after):])

    return pl.pallas_call(
        run,
        name=name,
        out_shape=[o for o, _ in outs],
        grid_spec=pltpu.PrefetchScalarGridSpec(
            num_scalar_prefetch=len(meta),
            grid=grid,
            in_specs=[s for _, s in ins] + [pl.BlockSpec(memory_space=pl.ANY)] * len(after),
            out_specs=[s for _, s in outs],
            scratch_shapes=list(scratch),
        ),
        input_output_aliases=aliases or {},
        compiler_params=pltpu.CompilerParams(vmem_limit_bytes=VMEM_LIMIT),
        cost_estimate=pl.CostEstimate(flops=flops, bytes_accessed=moved, transcendentals=0),
    )(*meta, *arrays)


def plan_sum(plan):
    total = plan[0]
    for r in range(1, plan.shape[0]):
        total = total + plan[r]
    return total


def fragment(plan):
    return lax.rem(plan_sum(plan), 2)


EXTRA = 16


def cast_body(theta, *lows):
    for k, low in enumerate(lows):
        low[...] = theta[0, k].astype(bf16)


def cast_rows(weights, pos):
    _, _, rows, width = weights.shape
    return call(
        cast_body, "cast_rows", (), [(weights, whole(weights.shape))],
        [(sds((rows, width), bf16), whole((rows, width)))] * 2, after=[pos],
    )


def weight_rows(kinds, wide):
    rows = [token_weight(kinds[j:j + wide].reshape(1, wide)) for j in range(0, kinds.shape[0], wide)]
    return jnp.concatenate(rows + [jnp.zeros((EXTRA - len(rows), wide), f32)], 0)


def weigh_body(kinds, other, out):
    wide = other.shape[1]
    lanes = kinds.shape[0] // wide
    own = weight_rows(kinds, wide)
    for h, rows in enumerate((own, other[other.shape[0] - EXTRA:, :].astype(f32))):
        turned = rows.T
        for j in range(lanes):
            out[h, j * wide:(j + 1) * wide, :] = turned[:, j:j + 1]


def weigh(lanes, other, tokens):
    return call(
        weigh_body, "weigh_tokens", (), [(a, whole(a.shape)) for a in (lanes, other)],
        [(sds((2, tokens, 1), f32), whole((2, tokens, 1)))],
    )[0]


def relay_body(cut, x, *refs):
    outs = refs
    if refs[0].dtype != bf16:
        kinds, outs = refs[0], refs[1:]
        outs[-1][cut:, :] = weight_rows(kinds, x.shape[1]).astype(bf16)
    for n, out in enumerate(outs):
        out[:cut, :] = x[n * cut:(n + 1) * cut, :]


def relay(x, cuts, after, lanes=None):
    rows, width = x.shape
    cut = rows // cuts
    shapes = [(cut, width)] * (cuts - 1) + [(cut + (0 if lanes is None else EXTRA), width)]
    ins = [x] if lanes is None else [x, lanes]
    return call(
        functools.partial(relay_body, cut), "relay_rows", (), [(a, whole(a.shape)) for a in ins],
        [(sds(shape, x.dtype), whole(shape)) for shape in shapes], after=after,
    )


def turn_block(pos, x, xt, t, tile):
    rows = x.shape[1] // (pos.shape[0] - 1)
    for s in range(xt.shape[0] // rows):
        xt[s * rows:(s + 1) * rows, t:t + tile] = x[t:t + tile, columns(pos, 1 + s, 0, rows, rows)].T


def columns(pos, slot, off, size, rows):
    return pl.ds(pl.multiple_of(pos[slot] * rows + off, size), size)


def turn_body(tile, pos, x, xt):
    for t in range(0, x.shape[0], tile):
        turn_block(pos, x, xt, t, tile)


def stage_body(tile, pos, x, held, xt, sems):
    copies = []
    for n, t in enumerate(range(0, x.shape[0], tile)):
        copy = pltpu.make_async_copy(x.at[pl.ds(t, tile), :], held.at[pl.ds(t, tile), :], sems.at[n])
        copy.start()
        copies.append(copy)
    for n, t in enumerate(range(0, x.shape[0], tile)):
        copies[n].wait()
        turn_block(pos, held, xt, t, tile)


def turn(pos, x, chips, stage):
    tokens, depth = x.shape
    tile = min(128, tokens)
    xt = [(sds((depth // 2, tokens), bf16), whole((depth // 2, tokens)))]
    if not stage:
        return x, call(functools.partial(turn_body, tile), "turn_tokens", (pos,), [(x, whole(x.shape))], xt)[0]
    return call(
        functools.partial(stage_body, tile), "stage_tokens", (pos,), [(x, pl.BlockSpec(memory_space=pl.ANY))],
        [(sds(x.shape, bf16), whole(x.shape))] + xt,
        scratch=[pltpu.SemaphoreType.DMA((tokens // tile,))],
    )


def product(pos, x, low, place, rows):
    slot, off, size = place
    return dot(x[:, columns(pos, slot, off, size, rows)], low[:size, :])


def gram_sum(lows, before):
    for low in lows:
        term = dot_rows(low[...], low[...])
        before = term if before is None else before + term
    return before


def forward_body(places, rows, with_gram, first_call, pos, *refs):
    carry = 2 if with_gram else 1
    before = (None, None) if first_call else refs[:carry]
    if not first_call:
        refs = refs[carry:]
    count = len(places)
    lows, xs = refs[:count], refs[count:count + 2]
    outs = refs[count + 2:]
    if with_gram:
        outs[1][...] = gram_sum(lows, None if first_call else before[1][...])
    for h in range(2):
        value = None if first_call else before[0][h]
        for low, place in zip(lows, places):
            term = product(pos, xs[h], low, place, rows)
            value = term if value is None else value + term
        outs[0][h] = value


def forward(pos, carry, pieces, xs, rows, with_gram, after=()):
    tokens = xs[0].shape[0]
    width = pieces[0][0].shape[1]
    ins = [(a, whole(a.shape)) for a in carry]
    ins += [(p[0], whole(p[0].shape)) for p in pieces] + [(x, whole(x.shape)) for x in xs]
    shapes = [(2, tokens, width)] + [(width, width)] * with_gram
    return call(
        functools.partial(forward_body, [p[1:] for p in pieces], rows, with_gram, not carry),
        "forward_decoder" if with_gram else "forward_encoder", (pos,), ins,
        [(sds(shape, f32), whole(shape)) for shape in shapes], after=after,
    )


def split(total):
    hi = total.astype(bf16)
    return hi, (total - hi.astype(f32)).astype(bf16)


def hidden_body(scale, tile, places, rows, pos, acc_in, cw, *refs):
    count = len(places)
    lows, xs = refs[:count], refs[count:count + 2]
    hidden_out, slope_out, counted_out, w_hi, w_lo, acc = refs[count + 2:]
    total = None
    for h in range(2):
        value = acc_in[h]
        for low, place in zip(lows, places):
            value = value + product(pos, xs[h], low, place, rows)
        acc[h] = value
        for t in range(0, acc.shape[1], tile):
            at = pl.ds(t, tile)
            pre = acc[h, at, :]
            sig = 0.5 + 0.5 * jnp.tanh(0.5 * pre)
            hidden = (pre * sig).astype(bf16)
            weight = cw[h, at, :]
            counted = (weight * hidden.astype(f32)).astype(bf16)
            hidden_out[h, at, :] = hidden
            slope_out[h, at, :] = (weight * scale) * (sig * (1.0 + pre * (1.0 - sig)))
            counted_out[h, at, :] = counted
            term = dot_rows(counted, hidden)
            total = term if total is None else total + term
    w_hi[...], w_lo[...] = split(total)


def hidden_rows(pos, acc, cw, pieces, xs, rows, scale):
    shape = acc.shape
    width = shape[2]
    ins = [(a, whole(a.shape)) for a in [acc, cw] + [p[0] for p in pieces] + list(xs)]
    square = (sds((width, width), bf16), whole((width, width)))
    return call(
        functools.partial(hidden_body, scale, min(256, shape[1]), [p[1:] for p in pieces], rows),
        "hidden_units", (pos,), ins,
        [(sds(shape, bf16), whole(shape)), (sds(shape, f32), whole(shape)), (sds(shape, bf16), whole(shape)), square, square],
        scratch=[pltpu.VMEM(shape, f32)],
    )


def slope_body(places, rows, pos, acc_in, gram_in, hidden, slope, *refs):
    count = len(places)
    lows, xs, out = refs[:count], refs[count:count + 2], refs[count + 2]
    g_hi, g_lo = split(gram_sum(lows, gram_in[...]))
    for h in range(2):
        value = acc_in[h]
        for low, place in zip(lows, places):
            value = value + product(pos, xs[h], low, place, rows)
        back = dot(hidden[h], g_hi) + dot(hidden[h], g_lo) - value
        out[h] = (slope[h] * back).astype(bf16)


def slope_rows(pos, acc, gram, hidden, slope, pieces, xs, rows):
    ins = [(a, whole(a.shape)) for a in [acc, gram, hidden, slope] + [p[0] for p in pieces] + list(xs)]
    return call(
        functools.partial(slope_body, [p[1:] for p in pieces], rows), "slope_pre", (pos,), ins,
        [(sds(acc.shape, bf16), whole(acc.shape))],
    )[0]


def token_sum(start, size, xts, weights):
    at = pl.ds(start, size)
    return dot(xts[0][at, :], weights[0]) + dot(xts[1][at, :], weights[1])


def encoder_body(start, xt_own, xt_par, slopes, out):
    out[...] = token_sum(start, out.shape[0], (xt_own, xt_par), slopes).astype(out.dtype)


def decoder_body(scale, start, pieces, xt_own, xt_par, counted, w_hi, w_lo, *refs):
    lows, got, out = refs[:pieces], refs[pieces:-1], refs[-1]
    off = 0
    for low in lows:
        size = low.shape[0]
        both = token_sum(start + off, size, (xt_own, xt_par), counted)
        value = scale * (dot(low[...], w_hi[...]) + dot(low[...], w_lo[...]) - both)
        for g in got:
            value = value + g[off:off + size, :].astype(f32)
        out[off:off + size, :] = value.astype(out.dtype)
        off += size


def grad_rows(body, name, size, xt, others, dtype, after=()):
    shape = (size, others[0].shape[2])
    ins = [(a, whole(a.shape)) for a in [*xt, *others]]
    return call(body, name, (), ins, [(sds(shape, dtype), whole(shape))], after=after)[0]


def adam_body(last, count, k, off, n_low, plan, own, *refs):
    got = refs[:count]
    theta, first, second = refs[count:3 + count]
    refs = refs[3 + count:]
    grad = own[...]
    for g in got:
        grad = grad + g[...].astype(f32)
    one = beta_one * first[0, 0] + (1.0 - beta_one) * grad
    two = beta_two * second[0, 0] + (1.0 - beta_two) * grad * grad
    old = theta[0, 0]
    if last:
        old = mixed(plan, k, old, refs[0][...])
    new = old - inner_rate * (one / (jnp.sqrt(two) + adam_eps) + decay_rate * old)
    if n_low is not None:
        anchor, before, low = refs[0], refs[1:1 + n_low], refs[1 + n_low]
        for b in before:
            low[:off, :] = b[...]
        low[off:, :] = mixed(plan, k, new, anchor[off:off + own.shape[0], :]).astype(bf16)
    theta_out, first_out, second_out = refs[-3:]
    theta_out[0, 0] = new
    first_out[0, 0] = one
    second_out[0, 0] = two


def mixed(plan, k, theta, anchor):
    return jnp.where(fragment(plan) == k, mix_share * theta + (1.0 - mix_share) * anchor, theta)


def adam_rows(plan, key, own, got, state, at, new_anc, prev, full, last, lows=None, after=()):
    k, off, cr = key
    i = off // cr
    width = own.shape[1]
    block = (1, 1, cr, width)
    ins = [(g, whole(g.shape)) for g in [own] + got]
    ins += [(s, once(block, lambda g, m: (0, at[0], at[1], 0))) for s in state]
    aliases = {}
    outs = []
    if last:
        ins.append((new_anc, once((cr, width), lambda g, m: (i, 0))))
        if prev is not None:
            for n, p in enumerate(prev):
                aliases[1 + len(ins)] = n
                ins.append((p, pl.BlockSpec(memory_space=pl.ANY)))
        outs = [(sds(full, f32), once(block, lambda g, m: (0, k, i, 0)))] * 3
    else:
        if lows is not None:
            ins += [(a, whole(a.shape)) for a in [new_anc] + lows]
            shape = (off + cr, width)
            outs = [(sds(shape, bf16), whole(shape))]
        outs += [(sds(block, f32), whole(block))] * 3
    return call(
        functools.partial(adam_body, last, len(got), k, off, None if lows is None else len(lows)), "adam_rows",
        (plan,), ins, outs, aliases=aliases, after=after,
    )


def quarter(pos, m, size):
    where = jnp.bitwise_xor(lax.rem(pos[0], 4), m)
    return pl.ds(pl.multiple_of(where * size, size), size)


def delta_body(pos, plan, anchor, theta, *outs):
    count = plan[pos[0]].astype(f32)
    for m, out in enumerate(outs):
        at = quarter(pos, m, out.shape[0])
        out[...] = (count * (anchor[0, at, :] - theta[0, 0, at, :])).astype(out.dtype)


def outer_start(pos, plan, anchor, weights, after):
    _, rows, width = anchor.shape
    part = (rows // 4, width)
    return call(
        delta_body, "delta_quarters", (pos, plan),
        [
            (anchor, once((1, rows, width), lambda g, p, q: (fragment(q), 0, 0))),
            (weights, once((1, 1, rows, width), lambda g, p, q: (0, fragment(q), 0, 0))),
        ],
        [(sds(part, f32), whole(part))] + [(sds(part, bf16), whole(part))] * 3, after=after,
    )


def add_body(final, plan, *refs):
    total = refs[0][...].astype(f32)
    for r in refs[1:-1]:
        total = total + r[...].astype(f32)
    if final:
        total = total / plan_sum(plan).astype(f32)
    refs[-1][...] = total.astype(bf16)


def outer_add(plan, parts, final, after=()):
    shape = parts[0].shape
    return call(
        functools.partial(add_body, final), "add_quarters", (plan,), [(a, whole(shape)) for a in parts],
        [(sds(shape, bf16), whole(shape))], after=after,
    )[0]


def outer_update(frag, at, anchor, momentum, grad):
    mom = outer_mu * momentum[frag, at, :] + grad
    return anchor[frag, at, :] - outer_rate * (grad + outer_mu * mom), mom


def new_anchor_body(pos, plan, anchor, momentum, *refs):
    for m, piece in enumerate(refs[:4]):
        at = quarter(pos, m, piece.shape[0])
        refs[4][at, :] = outer_update(0, at, anchor, momentum, piece[...].astype(f32))[0]


def outer_anchor(pos, plan, anchor, momentum, quarters, after):
    _, rows, width = anchor.shape
    part = once((1, rows, width), lambda g, p, q: (fragment(q), 0, 0))
    return call(
        new_anchor_body, "new_anchor", (pos, plan),
        [(anchor, part), (momentum, part)] + [(a, whole(a.shape)) for a in quarters],
        [(sds((rows, width), f32), whole((rows, width)))], after=after,
    )[0]


def mix_body(k, plan, new_anc, theta, low):
    low[...] = mixed(plan, k, theta[0, 0], new_anc[...]).astype(bf16)


def mix_rows(plan, new_anc, k, theta, after):
    shape = new_anc.shape
    return call(
        functools.partial(mix_body, k), "mix_rows", (plan,), [(a, whole(a.shape)) for a in (new_anc, theta)],
        [(sds(shape, bf16), whole(shape))], after=after,
    )[0]


def outer_body(pos, plan, anchor, momentum, *refs):
    quarters = refs[:4]
    anchor_out, momentum_out, token = refs[4:]
    token[...] = jnp.zeros_like(token)
    frag = fragment(plan)
    anchor_out[...] = anchor[...]
    momentum_out[...] = momentum[...]
    for m, piece in enumerate(quarters):
        at = quarter(pos, m, piece.shape[0])
        anc, mom = outer_update(frag, at, anchor, momentum, piece[...].astype(f32))
        anchor_out[frag, at, :] = anc
        momentum_out[frag, at, :] = mom


def outer_end(pos, plan, anchor, momentum, quarters, after):
    return call(
        outer_body, "outer_step", (pos, plan),
        [(a, whole(a.shape)) for a in [anchor, momentum] + quarters],
        [(sds(anchor.shape, f32), whole(anchor.shape))] * 2 + [(sds((8, 128), f32), whole((8, 128)))], after=after,
    )


def local(n_rep, n_fsdp, inputs, kinds, weights, first_moment, second_moment, anchor, momentum, plan):
    tokens = inputs.shape[0]
    rows, width = weights.shape[2:]
    chips = n_fsdp // 2
    scale = 1.0 / math.sqrt(tokens * n_fsdp)
    cuts = max(1, rows // 512)
    cut = rows // cuts
    others = range(1, chips)

    partner = [(f, f ^ 1) for f in range(n_fsdp)]
    to_partner = lambda a: lax.ppermute(a, "fsdp", partner)
    fetch = lambda a, s: lax.ppermute(
        a, "fsdp", [(((f // 2 + s) % chips) * 2 + f % 2, f) for f in range(n_fsdp)])
    give = lambda a, s: lax.ppermute(
        a, "fsdp", [(f, ((f // 2 + s) % chips) * 2 + f % 2) for f in range(n_fsdp)])
    across = lambda a, bit: lax.ppermute(a, "replica", [(r, r ^ bit) for r in range(n_rep)])

    chip = lax.axis_index("fsdp") // 2
    core = lax.axis_index("fsdp") % 2
    at = [((chip + s) % chips) * 2 for s in range(chips)]
    pos = jnp.stack([lax.axis_index("replica")] + [a + core for a in at] + [a + 1 - core for a in at]).astype(jnp.int32)

    enc, dec = cast_rows(weights, pos)
    x_par = to_partner(inputs)
    quarters = outer_start(pos, plan, anchor, weights, [enc])
    xs, xt = zip(*[turn(pos, x, chips, stage) for x, stage in ((inputs, False), (x_par, True))])
    own = outer_add(plan, [quarters[0]] + [across(quarters[m], m) for m in range(1, 4)], n_rep == 4, xt)

    most = rows - rows // 4 if rows >= 1024 else rows
    blocks = [(1, 0, rows), (0, 0, most)] + [(0, off, rows - most) for off in range(most, rows, max(1, rows - most))]
    state = {key: (weights, first_moment, second_moment) for key in blocks}
    state_at = {(k, off, size): (k, off // size) for k, off, size in blocks}
    new_anc = None
    for step in range(INNER):
        last = step == INNER - 1
        enc_far = {s: fetch(enc, s) for s in others}
        dec_far = {s: fetch(dec, s) for s in others}
        enc_near, dec_near = to_partner(enc), to_partner(dec)

        carry = forward(pos, [], [(enc, 1, 0, rows), (enc_near, 1 + chips, 0, rows)], xs, rows, False)
        ready = [own, *xt] if step == 0 else [token]
        riders = [kinds] if step == 0 else []
        part = [(p, 1 + s, n * cut, cut) for s in others for n, p in enumerate(
            relay(enc_far[s], cuts, [*carry, *ready], *riders))]
        pending = [(to_partner(p), slot + chips, off, size) for p, slot, off, size in part]
        carry = forward(pos, carry, part, xs, rows, False)
        if step == 0:
            cw = weigh(kinds, pending[-1][0], tokens)
        hidden, slope, counted, w_hi, w_lo = hidden_rows(pos, carry[0], cw, pending, xs, rows, scale)
        dec_grad = lambda s, lows, more, dtype, after: grad_rows(
            functools.partial(decoder_body, scale, s * rows, len(lows)), "decoder_grad", rows, xt,
            [counted, w_hi, w_lo, *lows, *more], dtype, after)
        enc_grad = lambda s, off, size, dtype, after: grad_rows(
            functools.partial(encoder_body, s * rows + off), "encoder_grad", size, xt, [slopes], dtype, after)
        sent = []
        got = {key: [] for key in blocks}
        far = {s: relay(dec_far[s], cuts, [counted]) for s in others}
        for s in others:
            sent.append(dec_grad(s, far[s], [], bf16, sent[-1:]))
            got[blocks[0]].append(give(sent[-1], s))

        part = [(p, 1 + s, n * cut, cut) for s in others for n, p in enumerate(far[s])]
        pending = [(to_partner(p), slot + chips, off, size) for p, slot, off, size in part]
        carry = forward(
            pos, [], [(dec, 1, 0, rows), (dec_near, 1 + chips, 0, rows)] + part, xs, rows, True, sent[-1:])
        slopes = slope_rows(pos, *carry, hidden, slope, pending, xs, rows)
        if step == 0:
            bit = 4
            while bit < n_rep:
                own = outer_add(plan, [own, across(own, bit)], 2 * bit == n_rep, [slopes])
                bit *= 2
            sent.append(own)
        for n, key in enumerate(blocks[1:]):
            for s in others:
                sent.append(enc_grad(s, *key[1:], bf16, sent[-1:]))
                got[key].append(give(sent[-1], s))
            if n == 0:
                mine = {blocks[0]: dec_grad(0, [dec], got[blocks[0]], f32, sent[-1:])}
                got[blocks[0]] = []
                sent.append(mine[blocks[0]])
        for key in blocks[1:]:
            mine[key] = enc_grad(0, *key[1:], f32, sent[-1:])

        if not last:
            quarters = [own] + [across(own, m) for m in range(1, 4)]
            new_anc = outer_anchor(pos, plan, anchor, momentum, quarters, [mine[blocks[0]]])
        new_state, prev, lows = {}, None, []
        adam = lambda key, prev, *more, after=(): adam_rows(
            plan, key, mine[key], got[key], state[key], state_at[key], new_anc, prev, weights.shape, last,
            *more, after=after)
        if last:
            for key in blocks:
                prev = adam(key, prev)
        else:
            for key in blocks[1:]:
                enc, *new_state[key] = adam(key, None, lows)
                lows = [enc]
            new_state[blocks[0]] = adam(blocks[0], None, after=[enc])
            dec = mix_rows(plan, new_anc, 1, new_state[blocks[0]][0], [enc])
            anchor_out, momentum_out, token = outer_end(pos, plan, anchor, momentum, quarters, [dec])
            state, state_at = new_state, {key: (0, 0) for key in blocks}
    return (*prev, anchor_out, momentum_out)


def solution(mesh):
    return jax.shard_map(
        functools.partial(local, mesh.shape["replica"], mesh.shape["fsdp"]),
        mesh=mesh,
        in_specs=(
            P(("replica", "fsdp"), None),
            P(("replica", "fsdp")),
            P("replica", None, "fsdp", None),
            P("replica", None, "fsdp", None),
            P("replica", None, "fsdp", None),
            P(None, "fsdp", None),
            P(None, "fsdp", None),
            P(),
        ),
        out_specs=(
            P("replica", None, "fsdp", None),
            P("replica", None, "fsdp", None),
            P("replica", None, "fsdp", None),
            P(None, "fsdp", None),
            P(None, "fsdp", None),
        ),
        check_vma=False,
    )
```

```python
import functools
import math

import jax
import jax.numpy as jnp
from jax import lax
from jax.experimental import pallas as pl
from jax.experimental.pallas import tpu as pltpu
from jax.sharding import PartitionSpec as P

INNER = 2

inner_rate = 0.003
beta_one = 0.9
beta_two = 0.95
adam_eps = 1e-08
decay_rate = 0.1
outer_rate = 0.7
outer_mu = 0.9
mix_share = 0.5

bf16 = jnp.bfloat16
f32 = jnp.float32
VMEM_LIMIT = 10 * 1024 * 1024


def token_weight(kinds):
    return jnp.where(kinds == 2, 1.0, jnp.where(kinds == 1, 0.25, 0.0)).astype(f32)


def dot(a, b):
    return jnp.dot(a, b, preferred_element_type=f32)


def dot_rows(a, b):
    return lax.dot_general(a, b, (((0,), (0,)), ((), ())), preferred_element_type=f32)


def once(shape, index):
    return pl.BlockSpec(shape, index, pipeline_mode=pl.Buffered(1))


def whole(shape):
    return once(shape, lambda *_: (0,) * len(shape))


def sds(shape, dtype):
    return jax.ShapeDtypeStruct(shape, dtype)


def call(body, name, meta, ins, outs, grid=(1,), scratch=(), aliases=None, flops=0, after=()):
    arrays = [a for a, _ in ins] + list(after)
    n_in = len(meta) + len(ins)
    moved = sum(math.prod(o.shape) * o.dtype.itemsize for o, _ in outs)
    moved += sum(math.prod(s.block_shape or a.shape) * a.dtype.itemsize for a, s in ins)

    def run(*refs):
        body(*refs[:n_in], *refs[n_in + len(after):])

    return pl.pallas_call(
        run,
        name=name,
        out_shape=[o for o, _ in outs],
        grid_spec=pltpu.PrefetchScalarGridSpec(
            num_scalar_prefetch=len(meta),
            grid=grid,
            in_specs=[s for _, s in ins] + [pl.BlockSpec(memory_space=pl.ANY)] * len(after),
            out_specs=[s for _, s in outs],
            scratch_shapes=list(scratch),
        ),
        input_output_aliases=aliases or {},
        compiler_params=pltpu.CompilerParams(vmem_limit_bytes=VMEM_LIMIT),
        cost_estimate=pl.CostEstimate(flops=flops, bytes_accessed=moved, transcendentals=0),
    )(*meta, *arrays)


def plan_sum(plan):
    total = plan[0]
    for r in range(1, plan.shape[0]):
        total = total + plan[r]
    return total


def fragment(plan):
    return lax.rem(plan_sum(plan), 2)


EXTRA = 16


def cast_body(sizes, theta, enc, dec, *parts):
    enc[...] = theta[0, 0].astype(bf16)
    value = theta[0, 1].astype(bf16)
    dec[...] = value
    put_parts(value, sizes, parts)


def put_parts(value, sizes, parts):
    off = 0
    for size, part in zip(sizes, parts):
        part[...] = value[off:off + size, :]
        off += size


def cast_rows(weights, sizes, pos):
    _, _, rows, width = weights.shape
    shapes = [(rows, width)] * 2 + [(size, width) for size in sizes]
    return call(
        functools.partial(cast_body, sizes), "cast_rows", (), [(weights, whole(weights.shape))],
        [(sds(shape, bf16), whole(shape)) for shape in shapes], after=[pos],
    )


def weight_rows(kinds, wide):
    rows = [token_weight(kinds[j:j + wide].reshape(1, wide)) for j in range(0, kinds.shape[0], wide)]
    return jnp.concatenate(rows + [jnp.zeros((EXTRA - len(rows), wide), f32)], 0)


def weigh_body(kinds, other, out):
    wide = other.shape[1]
    lanes = kinds.shape[0] // wide
    own = weight_rows(kinds, wide)
    for h, rows in enumerate((own, other[other.shape[0] - EXTRA:, :].astype(f32))):
        turned = rows.T
        for j in range(lanes):
            out[h, j * wide:(j + 1) * wide, :] = turned[:, j:j + 1]


def weigh(lanes, other, tokens):
    return call(
        weigh_body, "weigh_tokens", (), [(a, whole(a.shape)) for a in (lanes, other)],
        [(sds((2, tokens, 1), f32), whole((2, tokens, 1)))],
    )[0]


def relay_body(cut, x, *refs):
    outs = refs
    if refs[0].dtype != bf16:
        kinds, outs = refs[0], refs[1:]
        outs[-1][cut:, :] = weight_rows(kinds, x.shape[1]).astype(bf16)
    for n, out in enumerate(outs):
        out[:cut, :] = x[n * cut:(n + 1) * cut, :]


def relay(x, cuts, after, lanes=None):
    rows, width = x.shape
    cut = rows // cuts
    shapes = [(cut, width)] * (cuts - 1) + [(cut + (0 if lanes is None else EXTRA), width)]
    ins = [x] if lanes is None else [x, lanes]
    return call(
        functools.partial(relay_body, cut), "relay_rows", (), [(a, whole(a.shape)) for a in ins],
        [(sds(shape, x.dtype), whole(shape)) for shape in shapes], after=after,
    )


def turn_block(pos, x, xt, t, tile):
    rows = x.shape[1] // (pos.shape[0] - 1)
    for s in range(xt.shape[0] // rows):
        xt[s * rows:(s + 1) * rows, t:t + tile] = x[t:t + tile, columns(pos, 1 + s, 0, rows, rows)].T


def columns(pos, slot, off, size, rows):
    return pl.ds(pl.multiple_of(pos[slot] * rows + off, 128), size)


def turn_body(tile, pos, x, xt):
    for t in range(0, x.shape[0], tile):
        turn_block(pos, x, xt, t, tile)


def stage_body(tile, pos, x, held, xt, sems):
    copies = []
    for n, t in enumerate(range(0, x.shape[0], tile)):
        copy = pltpu.make_async_copy(x.at[pl.ds(t, tile), :], held.at[pl.ds(t, tile), :], sems.at[n])
        copy.start()
        copies.append(copy)
    for n, t in enumerate(range(0, x.shape[0], tile)):
        copies[n].wait()
        turn_block(pos, held, xt, t, tile)


def turn(pos, x, chips, stage):
    tokens, depth = x.shape
    tile = min(128, tokens)
    xt = [(sds((depth // 2, tokens), bf16), whole((depth // 2, tokens)))]
    if not stage:
        return x, call(functools.partial(turn_body, tile), "turn_tokens", (pos,), [(x, whole(x.shape))], xt)[0]
    return call(
        functools.partial(stage_body, tile), "stage_tokens", (pos,), [(x, pl.BlockSpec(memory_space=pl.ANY))],
        [(sds(x.shape, bf16), whole(x.shape))] + xt,
        scratch=[pltpu.SemaphoreType.DMA((tokens // tile,))],
    )


def product(pos, x, low, place, rows):
    slot, off, size = place
    return dot(x[:, columns(pos, slot, off, size, rows)], low[:size, :])


def gram_sum(lows, before):
    for low in lows:
        term = dot_rows(low[...], low[...])
        before = term if before is None else before + term
    return before


def forward_body(places, rows, with_gram, first_call, pos, *refs):
    carry = 2 if with_gram else 1
    before = (None, None) if first_call else refs[:carry]
    if not first_call:
        refs = refs[carry:]
    count = len(places)
    lows, xs = refs[:count], refs[count:count + 2]
    outs = refs[count + 2:]
    if with_gram:
        outs[1][...] = gram_sum(lows, None if first_call else before[1][...])
    for h in range(2):
        value = None if first_call else before[0][h]
        for low, place in zip(lows, places):
            term = product(pos, xs[h], low, place, rows)
            value = term if value is None else value + term
        outs[0][h] = value


def forward(pos, carry, pieces, xs, rows, with_gram, after=()):
    tokens = xs[0].shape[0]
    width = pieces[0][0].shape[1]
    ins = [(a, whole(a.shape)) for a in carry]
    ins += [(p[0], whole(p[0].shape)) for p in pieces] + [(x, whole(x.shape)) for x in xs]
    shapes = [(2, tokens, width)] + [(width, width)] * with_gram
    return call(
        functools.partial(forward_body, [p[1:] for p in pieces], rows, with_gram, not carry),
        "forward_decoder" if with_gram else "forward_encoder", (pos,), ins,
        [(sds(shape, f32), whole(shape)) for shape in shapes], after=after,
    )


def split(total):
    hi = total.astype(bf16)
    return hi, (total - hi.astype(f32)).astype(bf16)


def hidden_body(scale, tile, places, rows, pos, acc_in, cw, *refs):
    count = len(places)
    lows, xs = refs[:count], refs[count:count + 2]
    hidden_out, slope_out, counted_out, w_hi, w_lo, acc = refs[count + 2:]
    total = None
    for h in range(2):
        value = acc_in[h]
        for low, place in zip(lows, places):
            value = value + product(pos, xs[h], low, place, rows)
        acc[h] = value
        for t in range(0, acc.shape[1], tile):
            at = pl.ds(t, tile)
            pre = acc[h, at, :]
            sig = 0.5 + 0.5 * jnp.tanh(0.5 * pre)
            hidden = (pre * sig).astype(bf16)
            weight = cw[h, at, :]
            counted = (weight * hidden.astype(f32)).astype(bf16)
            hidden_out[h, at, :] = hidden
            slope_out[h, at, :] = (weight * scale) * (sig * (1.0 + pre * (1.0 - sig)))
            counted_out[h, at, :] = counted
            term = dot_rows(counted, hidden)
            total = term if total is None else total + term
    w_hi[...], w_lo[...] = split(total)


def hidden_rows(pos, acc, cw, pieces, xs, rows, scale):
    shape = acc.shape
    width = shape[2]
    ins = [(a, whole(a.shape)) for a in [acc, cw] + [p[0] for p in pieces] + list(xs)]
    square = (sds((width, width), bf16), whole((width, width)))
    return call(
        functools.partial(hidden_body, scale, min(256, shape[1]), [p[1:] for p in pieces], rows),
        "hidden_units", (pos,), ins,
        [(sds(shape, bf16), whole(shape)), (sds(shape, f32), whole(shape)), (sds(shape, bf16), whole(shape)), square, square],
        scratch=[pltpu.VMEM(shape, f32)],
    )


def slope_body(places, rows, pos, acc_in, gram_in, hidden, slope, *refs):
    count = len(places)
    lows, xs, out = refs[:count], refs[count:count + 2], refs[count + 2]
    g_hi, g_lo = split(gram_sum(lows, gram_in[...]))
    for h in range(2):
        value = acc_in[h]
        for low, place in zip(lows, places):
            value = value + product(pos, xs[h], low, place, rows)
        back = dot(hidden[h], g_hi) + dot(hidden[h], g_lo) - value
        out[h] = (slope[h] * back).astype(bf16)


def slope_rows(pos, acc, gram, hidden, slope, pieces, xs, rows):
    ins = [(a, whole(a.shape)) for a in [acc, gram, hidden, slope] + [p[0] for p in pieces] + list(xs)]
    return call(
        functools.partial(slope_body, [p[1:] for p in pieces], rows), "slope_pre", (pos,), ins,
        [(sds(acc.shape, bf16), whole(acc.shape))],
    )[0]


def token_sum(start, size, xts, weights):
    at = pl.ds(start, size)
    return dot(xts[0][at, :], weights[0]) + dot(xts[1][at, :], weights[1])


def encoder_body(start, xt_own, xt_par, slopes, out):
    out[...] = token_sum(start, out.shape[0], (xt_own, xt_par), slopes).astype(out.dtype)


def decoder_body(scale, start, pieces, front, xt_own, xt_par, counted, w_hi, w_lo, *refs):
    lows, more, out = refs[:pieces], refs[pieces:-1], refs[-1]
    off = 0
    got = more
    if front:
        off = more[0].shape[0]
        out[:off, :] = more[0][...]
        got = ()
    for low in lows:
        size = low.shape[0]
        both = token_sum(start + off, size, (xt_own, xt_par), counted)
        value = scale * (dot(low[...], w_hi[...]) + dot(low[...], w_lo[...]) - both)
        for g in got:
            value = value + g[off:off + size, :].astype(f32)
        out[off:off + size, :] = value.astype(out.dtype)
        off += size


def grad_rows(body, name, size, xt, others, dtype, after=()):
    shape = (size, others[0].shape[2])
    ins = [(a, whole(a.shape)) for a in [*xt, *others]]
    return call(body, name, (), ins, [(sds(shape, dtype), whole(shape))], after=after)[0]


def adam_body(last, count, k, off, n_low, plan, own, *refs):
    got = refs[:count]
    theta, first, second = refs[count:3 + count]
    refs = refs[3 + count:]
    grad = own[...]
    for g in got:
        grad = grad + g[...].astype(f32)
    one = beta_one * first[0, 0] + (1.0 - beta_one) * grad
    two = beta_two * second[0, 0] + (1.0 - beta_two) * grad * grad
    old = theta[0, 0]
    if last:
        old = mixed(plan, k, old, refs[0][...])
    new = old - inner_rate * (one / (jnp.sqrt(two) + adam_eps) + decay_rate * old)
    if n_low is not None:
        anchor, before, lows = refs[0], refs[1:1 + n_low], refs[1 + n_low:-3]
        value = mixed(plan, k, new, anchor[off:off + own.shape[0], :]).astype(bf16)
        lows[0][...] = value
        if before:
            lows[1][:off, :] = before[0][...]
            lows[1][off:, :] = value
    theta_out, first_out, second_out = refs[-3:]
    theta_out[0, 0] = new
    first_out[0, 0] = one
    second_out[0, 0] = two


def mixed(plan, k, theta, anchor):
    return jnp.where(fragment(plan) == k, mix_share * theta + (1.0 - mix_share) * anchor, theta)


def adam_rows(plan, key, own, got, state, at, new_anc, prev, full, last, lows=None, after=()):
    k, off, cr = key
    i = off // cr
    width = own.shape[1]
    block = (1, 1, cr, width)
    ins = [(g, whole(g.shape)) for g in [own] + got]
    ins += [(s, once(block, lambda g, m: (0, at[0], at[1], 0))) for s in state]
    aliases = {}
    outs = []
    if last:
        ins.append((new_anc, once((cr, width), lambda g, m: (i, 0))))
        if prev is not None:
            for n, p in enumerate(prev):
                aliases[1 + len(ins)] = n
                ins.append((p, pl.BlockSpec(memory_space=pl.ANY)))
        outs = [(sds(full, f32), once(block, lambda g, m: (0, k, i, 0)))] * 3
    else:
        if lows is not None:
            ins += [(a, whole(a.shape)) for a in [new_anc] + lows]
            shapes = [(cr, width)] + [(off + cr, width)] * len(lows)
            outs = [(sds(shape, bf16), whole(shape)) for shape in shapes]
        outs += [(sds(block, f32), whole(block))] * 3
    return call(
        functools.partial(adam_body, last, len(got), k, off, None if lows is None else len(lows)), "adam_rows",
        (plan,), ins, outs, aliases=aliases, after=after,
    )


def quarter(pos, m, size):
    where = jnp.bitwise_xor(lax.rem(pos[0], 4), m)
    return pl.ds(pl.multiple_of(where * size, size), size)


def delta_body(pos, plan, anchor, theta, *outs):
    count = plan[pos[0]].astype(f32)
    for m, out in enumerate(outs):
        at = quarter(pos, m, out.shape[0])
        out[...] = (count * (anchor[0, at, :] - theta[0, 0, at, :])).astype(out.dtype)


def outer_start(pos, plan, anchor, weights, after):
    _, rows, width = anchor.shape
    part = (rows // 4, width)
    return call(
        delta_body, "delta_quarters", (pos, plan),
        [
            (anchor, once((1, rows, width), lambda g, p, q: (fragment(q), 0, 0))),
            (weights, once((1, 1, rows, width), lambda g, p, q: (0, fragment(q), 0, 0))),
        ],
        [(sds(part, f32), whole(part))] + [(sds(part, bf16), whole(part))] * 3, after=after,
    )


def add_body(final, plan, *refs):
    total = refs[0][...].astype(f32)
    for r in refs[1:-1]:
        total = total + r[...].astype(f32)
    if final:
        total = total / plan_sum(plan).astype(f32)
    refs[-1][...] = total.astype(bf16)


def outer_add(plan, parts, final, after=()):
    shape = parts[0].shape
    return call(
        functools.partial(add_body, final), "add_quarters", (plan,), [(a, whole(shape)) for a in parts],
        [(sds(shape, bf16), whole(shape))], after=after,
    )[0]


def outer_update(frag, at, anchor, momentum, grad):
    mom = outer_mu * momentum[frag, at, :] + grad
    return anchor[frag, at, :] - outer_rate * (grad + outer_mu * mom), mom


def new_anchor_body(pos, plan, anchor, momentum, *refs):
    for m, piece in enumerate(refs[:4]):
        at = quarter(pos, m, piece.shape[0])
        refs[4][at, :] = outer_update(0, at, anchor, momentum, piece[...].astype(f32))[0]


def outer_anchor(pos, plan, anchor, momentum, quarters, after):
    _, rows, width = anchor.shape
    part = once((1, rows, width), lambda g, p, q: (fragment(q), 0, 0))
    return call(
        new_anchor_body, "new_anchor", (pos, plan),
        [(anchor, part), (momentum, part)] + [(a, whole(a.shape)) for a in quarters],
        [(sds((rows, width), f32), whole((rows, width)))], after=after,
    )[0]


def mix_body(k, sizes, plan, new_anc, theta, low, *parts):
    value = mixed(plan, k, theta[0, 0], new_anc[...]).astype(bf16)
    low[...] = value
    put_parts(value, sizes, parts)


def mix_rows(plan, new_anc, k, theta, sizes, after):
    rows, width = new_anc.shape
    shapes = [(rows, width)] + [(size, width) for size in sizes]
    return call(
        functools.partial(mix_body, k, sizes), "mix_rows", (plan,), [(a, whole(a.shape)) for a in (new_anc, theta)],
        [(sds(shape, bf16), whole(shape)) for shape in shapes], after=after,
    )


def outer_body(pos, plan, anchor, momentum, *refs):
    quarters = refs[:4]
    anchor_out, momentum_out, token = refs[4:]
    token[...] = jnp.zeros_like(token)
    frag = fragment(plan)
    anchor_out[...] = anchor[...]
    momentum_out[...] = momentum[...]
    for m, piece in enumerate(quarters):
        at = quarter(pos, m, piece.shape[0])
        anc, mom = outer_update(frag, at, anchor, momentum, piece[...].astype(f32))
        anchor_out[frag, at, :] = anc
        momentum_out[frag, at, :] = mom


def outer_end(pos, plan, anchor, momentum, quarters, after):
    return call(
        outer_body, "outer_step", (pos, plan),
        [(a, whole(a.shape)) for a in [anchor, momentum] + quarters],
        [(sds(anchor.shape, f32), whole(anchor.shape))] * 2 + [(sds((8, 128), f32), whole((8, 128)))], after=after,
    )


def local(n_rep, n_fsdp, inputs, kinds, weights, first_moment, second_moment, anchor, momentum, plan):
    tokens = inputs.shape[0]
    rows, width = weights.shape[2:]
    chips = n_fsdp // 2
    scale = 1.0 / math.sqrt(tokens * n_fsdp)
    most = rows - rows // 4 if rows >= 1024 else rows
    sizes = [most] + [rows - most] * (most < rows)
    starts = [sum(sizes[:n]) for n in range(len(sizes))]
    others = range(1, chips)

    partner = [(f, f ^ 1) for f in range(n_fsdp)]
    to_partner = lambda a: lax.ppermute(a, "fsdp", partner)
    fetch = lambda a, s: lax.ppermute(
        a, "fsdp", [(((f // 2 + s) % chips) * 2 + f % 2, f) for f in range(n_fsdp)])
    give = lambda a, s: lax.ppermute(
        a, "fsdp", [(f, ((f // 2 + s) % chips) * 2 + f % 2) for f in range(n_fsdp)])
    across = lambda a, bit: lax.ppermute(a, "replica", [(r, r ^ bit) for r in range(n_rep)])

    chip = lax.axis_index("fsdp") // 2
    core = lax.axis_index("fsdp") % 2
    at = [((chip + s) % chips) * 2 for s in range(chips)]
    pos = jnp.stack([lax.axis_index("replica")] + [a + core for a in at] + [a + 1 - core for a in at]).astype(jnp.int32)

    enc, dec, *dec_parts = cast_rows(weights, sizes, pos)
    enc_parts = [enc]
    x_par = to_partner(inputs)
    quarters = outer_start(pos, plan, anchor, weights, [enc])
    xs, xt = zip(*[turn(pos, x, chips, stage) for x, stage in ((inputs, False), (x_par, True))])
    own = outer_add(plan, [quarters[0]] + [across(quarters[m], m) for m in range(1, 4)], n_rep == 4, xt)

    blocks = [(1, 0, rows)] + [(0, off, size) for off, size in zip(starts, sizes)]
    state = {key: (weights, first_moment, second_moment) for key in blocks}
    state_at = {(k, off, size): (k, off // size) for k, off, size in blocks}
    new_anc = None
    for step in range(INNER):
        last = step == INNER - 1
        enc_far = [{s: fetch(part, s) for s in others} for part in enc_parts]
        dec_far = [{s: fetch(part, s) for s in others} for part in dec_parts]
        enc_near, dec_near = to_partner(enc), to_partner(dec)

        def take(far, off, after, *riders):
            pieces = []
            for s in others:
                cuts = max(1, far[s].shape[0] // 384)
                cut = far[s].shape[0] // cuts
                got = relay(far[s], cuts, after, *riders)
                pieces += [(p, 1 + s, off + n * cut, cut) for n, p in enumerate(got)]
            return pieces, [(to_partner(p), slot + chips, o, size) for p, slot, o, size in pieces]

        carry = forward(pos, [], [(enc, 1, 0, rows), (enc_near, 1 + chips, 0, rows)], xs, rows, False)
        ready = [own, *xt] if step == 0 else [token]
        pending = []
        off = 0
        for part in enc_far:
            pieces, handed = take(part, off, [*carry, *ready], *([kinds] if step == 0 else []))
            carry = forward(pos, carry, pending + pieces, xs, rows, False)
            pending = handed
            off += part[1].shape[0]
        if step == 0:
            cw = weigh(kinds, pending[-1][0], tokens)
        hidden, slope, counted, w_hi, w_lo = hidden_rows(pos, carry[0], cw, pending, xs, rows, scale)
        dec_grad = lambda s, size, lows, more, front, dtype, after: grad_rows(
            functools.partial(decoder_body, scale, s * rows, len(lows), front), "decoder_grad", size, xt,
            [counted, w_hi, w_lo, *lows, *more], dtype, after)
        enc_grad = lambda s, off, size, dtype, after: grad_rows(
            functools.partial(encoder_body, s * rows + off), "encoder_grad", size, xt, [slopes], dtype, after)
        sent = []
        got = {key: [] for key in blocks}
        part, pending = [], []
        whole_grad = {s: [] for s in others}
        for n, far in enumerate(dec_far):
            pieces, handed = take(far, starts[n], [counted] + sent[-1:])
            part += pieces
            pending += handed
            for s in others:
                rows_in = [p[0] for p in pieces if p[1] == 1 + s]
                whole_grad[s] = [dec_grad(
                    s, starts[n] + sizes[n], rows_in, whole_grad[s], n > 0, bf16, sent[-1:])]
                sent.append(whole_grad[s][0])
        back = [give(whole_grad[s][0], s) for s in others]

        carry = forward(
            pos, [], [(dec, 1, 0, rows), (dec_near, 1 + chips, 0, rows)] + part, xs, rows, True, sent[-1:])
        slopes = slope_rows(pos, *carry, hidden, slope, pending, xs, rows)
        if step == 0:
            bit = 4
            while bit < n_rep:
                own = outer_add(plan, [own, across(own, bit)], 2 * bit == n_rep, [slopes])
                bit *= 2
            sent.append(own)
        for n, key in enumerate(blocks[1:]):
            for s in others:
                sent.append(enc_grad(s, *key[1:], bf16, sent[-1:]))
                got[key].append(give(sent[-1], s))
            if n == 0:
                mine = {blocks[0]: dec_grad(0, rows, dec_parts, back, False, f32, sent[-1:])}
                sent.append(mine[blocks[0]])
        for key in blocks[1:]:
            mine[key] = enc_grad(0, *key[1:], f32, sent[-1:])

        if not last:
            quarters = [own] + [across(own, m) for m in range(1, 4)]
            new_anc = outer_anchor(pos, plan, anchor, momentum, quarters, [mine[blocks[0]]])
        new_state, prev, lows = {}, None, []
        adam = lambda key, prev, *more, after=(): adam_rows(
            plan, key, mine[key], got[key], state[key], state_at[key], new_anc, prev, weights.shape, last,
            *more, after=after)
        if last:
            for key in blocks:
                prev = adam(key, prev)
        else:
            for key in blocks[1:]:
                *new, a, b, c = adam(key, None, lows)
                lows.append(new[0])
                new_state[key] = (a, b, c)
            enc = new[-1]
            enc_parts = [enc]
            new_state[blocks[0]] = adam(blocks[0], None, after=[enc])
            dec, *dec_parts = mix_rows(plan, new_anc, 1, new_state[blocks[0]][0], sizes, [enc])
            anchor_out, momentum_out, token = outer_end(pos, plan, anchor, momentum, quarters, [dec])
            state, state_at = new_state, {key: (0, 0) for key in blocks}
    return (*prev, anchor_out, momentum_out)


def solution(mesh):
    return jax.shard_map(
        functools.partial(local, mesh.shape["replica"], mesh.shape["fsdp"]),
        mesh=mesh,
        in_specs=(
            P(("replica", "fsdp"), None),
            P(("replica", "fsdp")),
            P("replica", None, "fsdp", None),
            P("replica", None, "fsdp", None),
            P("replica", None, "fsdp", None),
            P(None, "fsdp", None),
            P(None, "fsdp", None),
            P(),
        ),
        out_specs=(
            P("replica", None, "fsdp", None),
            P("replica", None, "fsdp", None),
            P("replica", None, "fsdp", None),
            P(None, "fsdp", None),
            P(None, "fsdp", None),
        ),
        check_vma=False,
    )
```

```python
import functools
import math

import jax
import jax.numpy as jnp
from jax import lax
from jax.experimental import pallas as pl
from jax.experimental.pallas import tpu as pltpu
from jax.sharding import PartitionSpec as P

INNER = 2

inner_rate = 0.003
beta_one = 0.9
beta_two = 0.95
adam_eps = 1e-08
decay_rate = 0.1
outer_rate = 0.7
outer_mu = 0.9
mix_share = 0.5

bf16 = jnp.bfloat16
f32 = jnp.float32
VMEM_LIMIT = 10 * 1024 * 1024


def token_weight(kinds):
    return jnp.where(kinds == 2, 1.0, jnp.where(kinds == 1, 0.25, 0.0)).astype(f32)


def dot(a, b):
    return jnp.dot(a, b, preferred_element_type=f32)


def dot_rows(a, b):
    return lax.dot_general(a, b, (((0,), (0,)), ((), ())), preferred_element_type=f32)


def once(shape, index):
    return pl.BlockSpec(shape, index, pipeline_mode=pl.Buffered(1))


def whole(shape):
    return once(shape, lambda *_: (0,) * len(shape))


def sds(shape, dtype):
    return jax.ShapeDtypeStruct(shape, dtype)


def call(body, name, meta, ins, outs, grid=(1,), scratch=(), aliases=None, flops=0, after=()):
    arrays = [a for a, _ in ins] + list(after)
    n_in = len(meta) + len(ins)
    moved = sum(math.prod(o.shape) * o.dtype.itemsize for o, _ in outs)
    moved += sum(math.prod(s.block_shape or a.shape) * a.dtype.itemsize for a, s in ins)

    def run(*refs):
        body(*refs[:n_in], *refs[n_in + len(after):])

    return pl.pallas_call(
        run,
        name=name,
        out_shape=[o for o, _ in outs],
        grid_spec=pltpu.PrefetchScalarGridSpec(
            num_scalar_prefetch=len(meta),
            grid=grid,
            in_specs=[s for _, s in ins] + [pl.BlockSpec(memory_space=pl.ANY)] * len(after),
            out_specs=[s for _, s in outs],
            scratch_shapes=list(scratch),
        ),
        input_output_aliases=aliases or {},
        compiler_params=pltpu.CompilerParams(vmem_limit_bytes=VMEM_LIMIT),
        cost_estimate=pl.CostEstimate(flops=flops, bytes_accessed=moved, transcendentals=0),
    )(*meta, *arrays)


def plan_sum(plan):
    total = plan[0]
    for r in range(1, plan.shape[0]):
        total = total + plan[r]
    return total


def fragment(plan):
    return lax.rem(plan_sum(plan), 2)


EXTRA = 16


def cast_body(sizes, theta, enc, dec, *parts):
    enc[...] = theta[0, 0].astype(bf16)
    value = theta[0, 1].astype(bf16)
    dec[...] = value
    put_parts(value, sizes, parts)


def put_parts(value, sizes, parts):
    off = 0
    for size, part in zip(sizes, parts):
        part[...] = value[off:off + size, :]
        off += size


def cast_rows(weights, sizes, pos):
    _, _, rows, width = weights.shape
    shapes = [(rows, width)] * 2 + [(size, width) for size in sizes]
    return call(
        functools.partial(cast_body, sizes), "cast_rows", (), [(weights, whole(weights.shape))],
        [(sds(shape, bf16), whole(shape)) for shape in shapes], after=[pos],
    )


def weight_rows(kinds, wide):
    rows = [token_weight(kinds[j:j + wide].reshape(1, wide)) for j in range(0, kinds.shape[0], wide)]
    return jnp.concatenate(rows + [jnp.zeros((EXTRA - len(rows), wide), f32)], 0)


def weigh_body(kinds, other, out):
    wide = other.shape[1]
    lanes = kinds.shape[0] // wide
    own = weight_rows(kinds, wide)
    for h, rows in enumerate((own, other[other.shape[0] - EXTRA:, :].astype(f32))):
        turned = rows.T
        for j in range(lanes):
            out[h, j * wide:(j + 1) * wide, :] = turned[:, j:j + 1]


def weigh(lanes, other, tokens):
    return call(
        weigh_body, "weigh_tokens", (), [(a, whole(a.shape)) for a in (lanes, other)],
        [(sds((2, tokens, 1), f32), whole((2, tokens, 1)))],
    )[0]


def relay_body(cut, x, *refs):
    outs = refs
    if refs[0].dtype != bf16:
        kinds, outs = refs[0], refs[1:]
        outs[-1][cut:, :] = weight_rows(kinds, x.shape[1]).astype(bf16)
    for n, out in enumerate(outs):
        out[:cut, :] = x[n * cut:(n + 1) * cut, :]


def relay(x, cuts, after, lanes=None):
    rows, width = x.shape
    cut = rows // cuts
    shapes = [(cut, width)] * (cuts - 1) + [(cut + (0 if lanes is None else EXTRA), width)]
    ins = [x] if lanes is None else [x, lanes]
    return call(
        functools.partial(relay_body, cut), "relay_rows", (), [(a, whole(a.shape)) for a in ins],
        [(sds(shape, x.dtype), whole(shape)) for shape in shapes], after=after,
    )


def turn_block(pos, x, xt, t, tile):
    rows = x.shape[1] // (pos.shape[0] - 1)
    for s in range(xt.shape[0] // rows):
        xt[s * rows:(s + 1) * rows, t:t + tile] = x[t:t + tile, columns(pos, 1 + s, 0, rows, rows)].T


def columns(pos, slot, off, size, rows):
    return pl.ds(pl.multiple_of(pos[slot] * rows + off, 128), size)


def turn_body(tile, pos, x, xt):
    for t in range(0, x.shape[0], tile):
        turn_block(pos, x, xt, t, tile)


def stage_body(tile, pos, x, held, xt, sems):
    copies = []
    for n, t in enumerate(range(0, x.shape[0], tile)):
        copy = pltpu.make_async_copy(x.at[pl.ds(t, tile), :], held.at[pl.ds(t, tile), :], sems.at[n])
        copy.start()
        copies.append(copy)
    for n, t in enumerate(range(0, x.shape[0], tile)):
        copies[n].wait()
        turn_block(pos, held, xt, t, tile)


def turn(pos, x, chips, stage):
    tokens, depth = x.shape
    tile = min(128, tokens)
    xt = [(sds((depth // 2, tokens), bf16), whole((depth // 2, tokens)))]
    if not stage:
        return x, call(functools.partial(turn_body, tile), "turn_tokens", (pos,), [(x, whole(x.shape))], xt)[0]
    return call(
        functools.partial(stage_body, tile), "stage_tokens", (pos,), [(x, pl.BlockSpec(memory_space=pl.ANY))],
        [(sds(x.shape, bf16), whole(x.shape))] + xt,
        scratch=[pltpu.SemaphoreType.DMA((tokens // tile,))],
    )


def product(pos, x, low, place, rows):
    slot, off, size = place
    return dot(x[:, columns(pos, slot, off, size, rows)], low[:size, :])


def gram_sum(lows, before):
    for low in lows:
        term = dot_rows(low[...], low[...])
        before = term if before is None else before + term
    return before


def forward_body(places, rows, with_gram, first_call, pos, *refs):
    carry = 2 if with_gram else 1
    before = (None, None) if first_call else refs[:carry]
    if not first_call:
        refs = refs[carry:]
    count = len(places)
    lows, xs = refs[:count], refs[count:count + 2]
    outs = refs[count + 2:]
    if with_gram:
        outs[1][...] = gram_sum(lows, None if first_call else before[1][...])
    for h in range(2):
        value = None if first_call else before[0][h]
        for low, place in zip(lows, places):
            term = product(pos, xs[h], low, place, rows)
            value = term if value is None else value + term
        outs[0][h] = value


def forward(pos, carry, pieces, xs, rows, with_gram, after=()):
    tokens = xs[0].shape[0]
    width = pieces[0][0].shape[1]
    ins = [(a, whole(a.shape)) for a in carry]
    ins += [(p[0], whole(p[0].shape)) for p in pieces] + [(x, whole(x.shape)) for x in xs]
    shapes = [(2, tokens, width)] + [(width, width)] * with_gram
    return call(
        functools.partial(forward_body, [p[1:] for p in pieces], rows, with_gram, not carry),
        "forward_decoder" if with_gram else "forward_encoder", (pos,), ins,
        [(sds(shape, f32), whole(shape)) for shape in shapes], after=after,
    )


def split(total):
    hi = total.astype(bf16)
    return hi, (total - hi.astype(f32)).astype(bf16)


def hidden_body(scale, tile, places, rows, pos, acc_in, cw, *refs):
    count = len(places)
    lows, xs = refs[:count], refs[count:count + 2]
    hidden_out, slope_out, counted_out, w_hi, w_lo, acc = refs[count + 2:]
    total = None
    for h in range(2):
        value = acc_in[h]
        for low, place in zip(lows, places):
            value = value + product(pos, xs[h], low, place, rows)
        acc[h] = value
        for t in range(0, acc.shape[1], tile):
            at = pl.ds(t, tile)
            pre = acc[h, at, :]
            sig = 0.5 + 0.5 * jnp.tanh(0.5 * pre)
            hidden = (pre * sig).astype(bf16)
            weight = cw[h, at, :]
            counted = (weight * hidden.astype(f32)).astype(bf16)
            hidden_out[h, at, :] = hidden
            slope_out[h, at, :] = (weight * scale) * (sig * (1.0 + pre * (1.0 - sig)))
            counted_out[h, at, :] = counted
            term = dot_rows(counted, hidden)
            total = term if total is None else total + term
    w_hi[...], w_lo[...] = split(total)


def hidden_rows(pos, acc, cw, pieces, xs, rows, scale):
    shape = acc.shape
    width = shape[2]
    ins = [(a, whole(a.shape)) for a in [acc, cw] + [p[0] for p in pieces] + list(xs)]
    square = (sds((width, width), bf16), whole((width, width)))
    return call(
        functools.partial(hidden_body, scale, min(256, shape[1]), [p[1:] for p in pieces], rows),
        "hidden_units", (pos,), ins,
        [(sds(shape, bf16), whole(shape)), (sds(shape, f32), whole(shape)), (sds(shape, bf16), whole(shape)), square, square],
        scratch=[pltpu.VMEM(shape, f32)],
    )


def slope_body(places, rows, pos, acc_in, gram_in, hidden, slope, *refs):
    count = len(places)
    lows, xs, out = refs[:count], refs[count:count + 2], refs[count + 2]
    g_hi, g_lo = split(gram_sum(lows, gram_in[...]))
    for h in range(2):
        value = acc_in[h]
        for low, place in zip(lows, places):
            value = value + product(pos, xs[h], low, place, rows)
        back = dot(hidden[h], g_hi) + dot(hidden[h], g_lo) - value
        out[h] = (slope[h] * back).astype(bf16)


def slope_rows(pos, acc, gram, hidden, slope, pieces, xs, rows):
    ins = [(a, whole(a.shape)) for a in [acc, gram, hidden, slope] + [p[0] for p in pieces] + list(xs)]
    return call(
        functools.partial(slope_body, [p[1:] for p in pieces], rows), "slope_pre", (pos,), ins,
        [(sds(acc.shape, bf16), whole(acc.shape))],
    )[0]


def token_sum(start, size, xts, weights):
    at = pl.ds(start, size)
    return dot(xts[0][at, :], weights[0]) + dot(xts[1][at, :], weights[1])


def encoder_body(start, xt_own, xt_par, slopes, out):
    out[...] = token_sum(start, out.shape[0], (xt_own, xt_par), slopes).astype(out.dtype)


def decoder_body(scale, start, pieces, front, xt_own, xt_par, counted, w_hi, w_lo, *refs):
    lows, more, out = refs[:pieces], refs[pieces:-1], refs[-1]
    off = 0
    got = more
    if front:
        off = more[0].shape[0]
        out[:off, :] = more[0][...]
        got = ()
    for low in lows:
        size = low.shape[0]
        both = token_sum(start + off, size, (xt_own, xt_par), counted)
        value = scale * (dot(low[...], w_hi[...]) + dot(low[...], w_lo[...]) - both)
        for g in got:
            value = value + g[off:off + size, :].astype(f32)
        out[off:off + size, :] = value.astype(out.dtype)
        off += size


def grad_rows(body, name, size, xt, others, dtype, after=()):
    shape = (size, others[0].shape[2])
    ins = [(a, whole(a.shape)) for a in [*xt, *others]]
    return call(body, name, (), ins, [(sds(shape, dtype), whole(shape))], after=after)[0]


def adam_body(last, count, k, off, n_low, plan, own, *refs):
    got = refs[:count]
    theta, first, second = refs[count:3 + count]
    refs = refs[3 + count:]
    grad = own[...]
    for g in got:
        grad = grad + g[...].astype(f32)
    one = beta_one * first[0, 0] + (1.0 - beta_one) * grad
    two = beta_two * second[0, 0] + (1.0 - beta_two) * grad * grad
    old = theta[0, 0]
    if last:
        old = mixed(plan, k, old, refs[0][...])
    new = old - inner_rate * (one / (jnp.sqrt(two) + adam_eps) + decay_rate * old)
    if n_low is not None:
        anchor, before, lows = refs[0], refs[1:1 + n_low], refs[1 + n_low:-3]
        value = mixed(plan, k, new, anchor[off:off + own.shape[0], :]).astype(bf16)
        for b in before:
            lows[0][:off, :] = b[...]
        lows[0][off:, :] = value
    if last and k:
        refs[-4][...] = jnp.zeros_like(refs[-4])
    theta_out, first_out, second_out = refs[-3:]
    theta_out[0, 0] = new
    first_out[0, 0] = one
    second_out[0, 0] = two


def mixed(plan, k, theta, anchor):
    return jnp.where(fragment(plan) == k, mix_share * theta + (1.0 - mix_share) * anchor, theta)


def adam_rows(plan, key, own, got, state, at, new_anc, prev, full, last, lows=None, after=()):
    k, off, cr = key
    i = off // cr
    width = own.shape[1]
    block = (1, 1, cr, width)
    ins = [(g, whole(g.shape)) for g in [own] + got]
    ins += [(s, once(block, lambda g, m: (0, at[0], at[1], 0))) for s in state]
    aliases = {}
    outs = []
    if last:
        ins.append((new_anc, once((cr, width), lambda g, m: (i, 0))))
        if prev is not None:
            for n, p in enumerate(prev):
                aliases[1 + len(ins)] = n
                ins.append((p, pl.BlockSpec(memory_space=pl.ANY)))
        outs = [(sds(full, f32), once(block, lambda g, m: (0, k, i, 0)))] * 3
        if prev is None:
            outs = [(sds((8, 128), f32), whole((8, 128)))] + outs
    else:
        if lows is not None:
            ins += [(a, whole(a.shape)) for a in [new_anc] + lows]
            shape = (off + cr, width)
            outs = [(sds(shape, bf16), whole(shape))]
        outs += [(sds(block, f32), whole(block))] * 3
    return call(
        functools.partial(adam_body, last, len(got), k, off, None if lows is None else len(lows)), "adam_rows",
        (plan,), ins, outs, aliases=aliases, after=after,
    )


def quarter(pos, m, size):
    where = jnp.bitwise_xor(lax.rem(pos[0], 4), m)
    return pl.ds(pl.multiple_of(where * size, size), size)


def delta_body(pos, plan, anchor, theta, *outs):
    count = plan[pos[0]].astype(f32)
    for m, out in enumerate(outs):
        at = quarter(pos, m, out.shape[0])
        out[...] = (count * (anchor[0, at, :] - theta[0, 0, at, :])).astype(out.dtype)


def outer_start(pos, plan, anchor, weights, after):
    _, rows, width = anchor.shape
    part = (rows // 4, width)
    return call(
        delta_body, "delta_quarters", (pos, plan),
        [
            (anchor, once((1, rows, width), lambda g, p, q: (fragment(q), 0, 0))),
            (weights, once((1, 1, rows, width), lambda g, p, q: (0, fragment(q), 0, 0))),
        ],
        [(sds(part, f32), whole(part))] + [(sds(part, bf16), whole(part))] * 3, after=after,
    )


def add_body(final, plan, *refs):
    total = refs[0][...].astype(f32)
    for r in refs[1:-1]:
        total = total + r[...].astype(f32)
    if final:
        total = total / plan_sum(plan).astype(f32)
    refs[-1][...] = total.astype(bf16)


def outer_add(plan, parts, final, after=()):
    shape = parts[0].shape
    return call(
        functools.partial(add_body, final), "add_quarters", (plan,), [(a, whole(shape)) for a in parts],
        [(sds(shape, bf16), whole(shape))], after=after,
    )[0]


def outer_update(frag, at, anchor, momentum, grad):
    mom = outer_mu * momentum[frag, at, :] + grad
    return anchor[frag, at, :] - outer_rate * (grad + outer_mu * mom), mom


def new_anchor_body(pos, plan, anchor, momentum, *refs):
    for m, piece in enumerate(refs[:4]):
        at = quarter(pos, m, piece.shape[0])
        refs[4][at, :] = outer_update(0, at, anchor, momentum, piece[...].astype(f32))[0]


def outer_anchor(pos, plan, anchor, momentum, quarters, after):
    _, rows, width = anchor.shape
    part = once((1, rows, width), lambda g, p, q: (fragment(q), 0, 0))
    return call(
        new_anchor_body, "new_anchor", (pos, plan),
        [(anchor, part), (momentum, part)] + [(a, whole(a.shape)) for a in quarters],
        [(sds((rows, width), f32), whole((rows, width)))], after=after,
    )[0]


def mix_body(k, sizes, plan, new_anc, theta, low, *parts):
    value = mixed(plan, k, theta[0, 0], new_anc[...]).astype(bf16)
    low[...] = value
    put_parts(value, sizes, parts)


def mix_rows(plan, new_anc, k, theta, sizes, after):
    rows, width = new_anc.shape
    shapes = [(rows, width)] + [(size, width) for size in sizes]
    return call(
        functools.partial(mix_body, k, sizes), "mix_rows", (plan,), [(a, whole(a.shape)) for a in (new_anc, theta)],
        [(sds(shape, bf16), whole(shape)) for shape in shapes], after=after,
    )


def outer_body(pos, plan, anchor, momentum, *refs):
    quarters = refs[:4]
    anchor_out, momentum_out, token = refs[4:]
    token[...] = jnp.zeros_like(token)
    frag = fragment(plan)
    anchor_out[...] = anchor[...]
    momentum_out[...] = momentum[...]
    for m, piece in enumerate(quarters):
        at = quarter(pos, m, piece.shape[0])
        anc, mom = outer_update(frag, at, anchor, momentum, piece[...].astype(f32))
        anchor_out[frag, at, :] = anc
        momentum_out[frag, at, :] = mom


def outer_end(pos, plan, anchor, momentum, quarters, after):
    return call(
        outer_body, "outer_step", (pos, plan),
        [(a, whole(a.shape)) for a in [anchor, momentum] + quarters],
        [(sds(anchor.shape, f32), whole(anchor.shape))] * 2 + [(sds((8, 128), f32), whole((8, 128)))], after=after,
    )


def local(n_rep, n_fsdp, inputs, kinds, weights, first_moment, second_moment, anchor, momentum, plan):
    tokens = inputs.shape[0]
    rows, width = weights.shape[2:]
    chips = n_fsdp // 2
    scale = 1.0 / math.sqrt(tokens * n_fsdp)
    most = rows - rows // 4 if rows >= 1024 else rows
    sizes = [most] + [rows - most] * (most < rows)
    starts = [sum(sizes[:n]) for n in range(len(sizes))]
    others = range(1, chips)

    partner = [(f, f ^ 1) for f in range(n_fsdp)]
    to_partner = lambda a: lax.ppermute(a, "fsdp", partner)
    fetch = lambda a, s: lax.ppermute(
        a, "fsdp", [(((f // 2 + s) % chips) * 2 + f % 2, f) for f in range(n_fsdp)])
    give = lambda a, s: lax.ppermute(
        a, "fsdp", [(f, ((f // 2 + s) % chips) * 2 + f % 2) for f in range(n_fsdp)])
    across = lambda a, bit: lax.ppermute(a, "replica", [(r, r ^ bit) for r in range(n_rep)])

    chip = lax.axis_index("fsdp") // 2
    core = lax.axis_index("fsdp") % 2
    at = [((chip + s) % chips) * 2 for s in range(chips)]
    pos = jnp.stack([lax.axis_index("replica")] + [a + core for a in at] + [a + 1 - core for a in at]).astype(jnp.int32)

    enc, dec, *dec_parts = cast_rows(weights, sizes, pos)
    enc_parts = [enc]
    x_par = to_partner(inputs)
    quarters = outer_start(pos, plan, anchor, weights, [enc])
    xs, xt = zip(*[turn(pos, x, chips, stage) for x, stage in ((inputs, False), (x_par, True))])
    own = outer_add(plan, [quarters[0]] + [across(quarters[m], m) for m in range(1, 4)], n_rep == 4, xt)

    blocks = [(1, 0, rows)] + [(0, off, size) for off, size in zip(starts, sizes)]
    state = {key: (weights, first_moment, second_moment) for key in blocks}
    state_at = {(k, off, size): (k, off // size) for k, off, size in blocks}
    new_anc = None
    for step in range(INNER):
        last = step == INNER - 1
        enc_far = [{s: fetch(part, s) for s in others} for part in enc_parts]
        dec_far = [{s: fetch(part, s) for s in others} for part in dec_parts]
        enc_near, dec_near = to_partner(enc), to_partner(dec)

        def take(far, off, after, *riders):
            pieces = []
            for s in others:
                cuts = max(1, far[s].shape[0] // 384)
                cut = far[s].shape[0] // cuts
                got = relay(far[s], cuts, after, *riders)
                pieces += [(p, 1 + s, off + n * cut, cut) for n, p in enumerate(got)]
            return pieces, [(to_partner(p), slot + chips, o, size) for p, slot, o, size in pieces]

        carry = forward(pos, [], [(enc, 1, 0, rows), (enc_near, 1 + chips, 0, rows)], xs, rows, False)
        ready = [own, *xt] if step == 0 else [token]
        pending = []
        off = 0
        for part in enc_far:
            pieces, handed = take(part, off, [*carry, *ready], *([kinds] if step == 0 else []))
            carry = forward(pos, carry, pending + pieces, xs, rows, False)
            pending = handed
            off += part[1].shape[0]
        if step == 0:
            cw = weigh(kinds, pending[-1][0], tokens)
        hidden, slope, counted, w_hi, w_lo = hidden_rows(pos, carry[0], cw, pending, xs, rows, scale)
        dec_grad = lambda s, size, lows, more, front, dtype, after: grad_rows(
            functools.partial(decoder_body, scale, s * rows, len(lows), front), "decoder_grad", size, xt,
            [counted, w_hi, w_lo, *lows, *more], dtype, after)
        enc_grad = lambda s, off, size, dtype, after: grad_rows(
            functools.partial(encoder_body, s * rows + off), "encoder_grad", size, xt, [slopes], dtype, after)
        sent = []
        got = {key: [] for key in blocks}
        part, pending = [], []
        whole_grad = {s: [] for s in others}
        for n, far in enumerate(dec_far):
            pieces, handed = take(far, starts[n], [counted] + sent[-1:])
            part += pieces
            pending += handed
            for s in others:
                rows_in = [p[0] for p in pieces if p[1] == 1 + s]
                whole_grad[s] = [dec_grad(
                    s, starts[n] + sizes[n], rows_in, whole_grad[s], n > 0, bf16, sent[-1:])]
                sent.append(whole_grad[s][0])
        back = [give(whole_grad[s][0], s) for s in others]

        carry = forward(
            pos, [], [(dec, 1, 0, rows), (dec_near, 1 + chips, 0, rows)] + part, xs, rows, True, sent[-1:])
        slopes = slope_rows(pos, *carry, hidden, slope, pending, xs, rows)
        if step == 0:
            bit = 4
            while bit < n_rep:
                own = outer_add(plan, [own, across(own, bit)], 2 * bit == n_rep, [slopes])
                bit *= 2
            sent.append(own)
        adam = lambda key, prev, *more, after=(): adam_rows(
            plan, key, mine[key], got[key], state[key], state_at[key], new_anc, prev, weights.shape, last,
            *more, after=after)
        prev = None
        mine = {}
        for n, key in enumerate(blocks[1:]):
            for s in others:
                sent.append(enc_grad(s, *key[1:], bf16, sent[-1:]))
                got[key].append(give(sent[-1], s))
            if n == 0:
                mine[blocks[0]] = dec_grad(0, rows, dec_parts, back, False, f32, sent[-1:])
                sent.append(mine[blocks[0]])
                for other in blocks[1:]:
                    mine[other] = enc_grad(0, *other[1:], f32, sent[-1:])
                    sent.append(mine[other])
                if last:
                    token, *prev = adam(blocks[0], None)
                    sent.append(token)

        if not last:
            quarters = [own] + [across(own, m) for m in range(1, 4)]
            new_anc = outer_anchor(pos, plan, anchor, momentum, quarters, [mine[blocks[0]]])
        new_state, lows = {}, []
        if last:
            for key in blocks[1:]:
                prev = adam(key, prev)
        else:
            for key in blocks[1:]:
                enc, *new_state[key] = adam(key, None, lows)
                lows = [enc]
            enc_parts = [enc]
            new_state[blocks[0]] = adam(blocks[0], None, after=[enc])
            dec, *dec_parts = mix_rows(plan, new_anc, 1, new_state[blocks[0]][0], sizes, [enc])
            anchor_out, momentum_out, token = outer_end(pos, plan, anchor, momentum, quarters, [dec])
            state, state_at = new_state, {key: (0, 0) for key in blocks}
    return (*prev, anchor_out, momentum_out)


def solution(mesh):
    return jax.shard_map(
        functools.partial(local, mesh.shape["replica"], mesh.shape["fsdp"]),
        mesh=mesh,
        in_specs=(
            P(("replica", "fsdp"), None),
            P(("replica", "fsdp")),
            P("replica", None, "fsdp", None),
            P("replica", None, "fsdp", None),
            P("replica", None, "fsdp", None),
            P(None, "fsdp", None),
            P(None, "fsdp", None),
            P(),
        ),
        out_specs=(
            P("replica", None, "fsdp", None),
            P("replica", None, "fsdp", None),
            P("replica", None, "fsdp", None),
            P(None, "fsdp", None),
            P(None, "fsdp", None),
        ),
        check_vma=False,
    )
```

```python
import functools
import math

import jax
import jax.numpy as jnp
from jax import lax
from jax.experimental import pallas as pl
from jax.experimental.pallas import tpu as pltpu
from jax.sharding import PartitionSpec as P

INNER = 2

inner_rate = 0.003
beta_one = 0.9
beta_two = 0.95
adam_eps = 1e-08
decay_rate = 0.1
outer_rate = 0.7
outer_mu = 0.9
mix_share = 0.5

bf16 = jnp.bfloat16
f32 = jnp.float32
VMEM_LIMIT = 10 * 1024 * 1024


def token_weight(kinds):
    return jnp.where(kinds == 2, 1.0, jnp.where(kinds == 1, 0.25, 0.0)).astype(f32)


def dot(a, b):
    return jnp.dot(a, b, preferred_element_type=f32)


def dot_rows(a, b):
    return lax.dot_general(a, b, (((0,), (0,)), ((), ())), preferred_element_type=f32)


def once(shape, index):
    return pl.BlockSpec(shape, index, pipeline_mode=pl.Buffered(1))


def whole(shape):
    return once(shape, lambda *_: (0,) * len(shape))


def sds(shape, dtype):
    return jax.ShapeDtypeStruct(shape, dtype)


def call(body, name, meta, ins, outs, grid=(1,), scratch=(), aliases=None, flops=0, after=()):
    arrays = [a for a, _ in ins] + list(after)
    n_in = len(meta) + len(ins)
    moved = sum(math.prod(o.shape) * o.dtype.itemsize for o, _ in outs)
    moved += sum(math.prod(s.block_shape or a.shape) * a.dtype.itemsize for a, s in ins)

    def run(*refs):
        body(*refs[:n_in], *refs[n_in + len(after):])

    return pl.pallas_call(
        run,
        name=name,
        out_shape=[o for o, _ in outs],
        grid_spec=pltpu.PrefetchScalarGridSpec(
            num_scalar_prefetch=len(meta),
            grid=grid,
            in_specs=[s for _, s in ins] + [pl.BlockSpec(memory_space=pl.ANY)] * len(after),
            out_specs=[s for _, s in outs],
            scratch_shapes=list(scratch),
        ),
        input_output_aliases=aliases or {},
        compiler_params=pltpu.CompilerParams(vmem_limit_bytes=VMEM_LIMIT),
        cost_estimate=pl.CostEstimate(flops=flops, bytes_accessed=moved, transcendentals=0),
    )(*meta, *arrays)


def plan_sum(plan):
    total = plan[0]
    for r in range(1, plan.shape[0]):
        total = total + plan[r]
    return total


def fragment(plan):
    return lax.rem(plan_sum(plan), 2)


EXTRA = 16


def cast_body(sizes, theta, enc, dec, *parts):
    enc[...] = theta[0, 0].astype(bf16)
    value = theta[0, 1].astype(bf16)
    dec[...] = value
    put_parts(value, sizes, parts)


def put_parts(value, sizes, parts):
    off = 0
    for size, part in zip(sizes, parts):
        part[...] = value[off:off + size, :]
        off += size


def cast_rows(weights, sizes, pos):
    _, _, rows, width = weights.shape
    shapes = [(rows, width)] * 2 + [(size, width) for size in sizes]
    return call(
        functools.partial(cast_body, sizes), "cast_rows", (), [(weights, whole(weights.shape))],
        [(sds(shape, bf16), whole(shape)) for shape in shapes], after=[pos],
    )


def weight_rows(kinds, wide):
    rows = [token_weight(kinds[j:j + wide].reshape(1, wide)) for j in range(0, kinds.shape[0], wide)]
    return jnp.concatenate(rows + [jnp.zeros((EXTRA - len(rows), wide), f32)], 0)


def weigh_body(kinds, other, out):
    wide = other.shape[1]
    lanes = kinds.shape[0] // wide
    own = weight_rows(kinds, wide)
    for h, rows in enumerate((own, other[other.shape[0] - EXTRA:, :].astype(f32))):
        turned = rows.T
        for j in range(lanes):
            out[h, j * wide:(j + 1) * wide, :] = turned[:, j:j + 1]


def weigh(lanes, other, tokens):
    return call(
        weigh_body, "weigh_tokens", (), [(a, whole(a.shape)) for a in (lanes, other)],
        [(sds((2, tokens, 1), f32), whole((2, tokens, 1)))],
    )[0]


def relay_body(cut, x, *refs):
    outs = refs
    if refs[0].dtype != bf16:
        kinds, outs = refs[0], refs[1:]
        outs[-1][cut:, :] = weight_rows(kinds, x.shape[1]).astype(bf16)
    for n, out in enumerate(outs):
        out[:cut, :] = x[n * cut:(n + 1) * cut, :]


def relay(x, cuts, after, lanes=None):
    rows, width = x.shape
    cut = rows // cuts
    shapes = [(cut, width)] * (cuts - 1) + [(cut + (0 if lanes is None else EXTRA), width)]
    ins = [x] if lanes is None else [x, lanes]
    return call(
        functools.partial(relay_body, cut), "relay_rows", (), [(a, whole(a.shape)) for a in ins],
        [(sds(shape, x.dtype), whole(shape)) for shape in shapes], after=after,
    )


def turn_block(pos, x, xt, t, tile):
    rows = x.shape[1] // (pos.shape[0] - 1)
    for s in range(xt.shape[0] // rows):
        xt[s * rows:(s + 1) * rows, t:t + tile] = x[t:t + tile, columns(pos, 1 + s, 0, rows, rows)].T


def columns(pos, slot, off, size, rows):
    return pl.ds(pl.multiple_of(pos[slot] * rows + off, 128), size)


def turn_body(tile, pos, x, xt):
    for t in range(0, x.shape[0], tile):
        turn_block(pos, x, xt, t, tile)


def stage_body(tile, pos, x, held, xt, sems):
    copies = []
    for n, t in enumerate(range(0, x.shape[0], tile)):
        copy = pltpu.make_async_copy(x.at[pl.ds(t, tile), :], held.at[pl.ds(t, tile), :], sems.at[n])
        copy.start()
        copies.append(copy)
    for n, t in enumerate(range(0, x.shape[0], tile)):
        copies[n].wait()
        turn_block(pos, held, xt, t, tile)


def turn(pos, x, chips, stage):
    tokens, depth = x.shape
    tile = min(128, tokens)
    xt = [(sds((depth // 2, tokens), bf16), whole((depth // 2, tokens)))]
    if not stage:
        return x, call(functools.partial(turn_body, tile), "turn_tokens", (pos,), [(x, whole(x.shape))], xt)[0]
    return call(
        functools.partial(stage_body, tile), "stage_tokens", (pos,), [(x, pl.BlockSpec(memory_space=pl.ANY))],
        [(sds(x.shape, bf16), whole(x.shape))] + xt,
        scratch=[pltpu.SemaphoreType.DMA((tokens // tile,))],
    )


def product(pos, x, low, place, rows):
    slot, off, size = place
    return dot(x[:, columns(pos, slot, off, size, rows)], low[:size, :])


def gram_sum(lows, before):
    for low in lows:
        term = dot_rows(low[...], low[...])
        before = term if before is None else before + term
    return before


def forward_body(places, rows, with_gram, first_call, pos, *refs):
    carry = 2 if with_gram else 1
    before = (None, None) if first_call else refs[:carry]
    if not first_call:
        refs = refs[carry:]
    count = len(places)
    lows, xs = refs[:count], refs[count:count + 2]
    outs = refs[count + 2:]
    if with_gram:
        outs[1][...] = gram_sum(lows, None if first_call else before[1][...])
    for h in range(2):
        value = None if first_call else before[0][h]
        for low, place in zip(lows, places):
            term = product(pos, xs[h], low, place, rows)
            value = term if value is None else value + term
        outs[0][h] = value


def forward(pos, carry, pieces, xs, rows, with_gram, after=()):
    tokens = xs[0].shape[0]
    width = pieces[0][0].shape[1]
    ins = [(a, whole(a.shape)) for a in carry]
    ins += [(p[0], whole(p[0].shape)) for p in pieces] + [(x, whole(x.shape)) for x in xs]
    shapes = [(2, tokens, width)] + [(width, width)] * with_gram
    return call(
        functools.partial(forward_body, [p[1:] for p in pieces], rows, with_gram, not carry),
        "forward_decoder" if with_gram else "forward_encoder", (pos,), ins,
        [(sds(shape, f32), whole(shape)) for shape in shapes], after=after,
    )


def split(total):
    hi = total.astype(bf16)
    return hi, (total - hi.astype(f32)).astype(bf16)


def hidden_body(scale, tile, places, rows, pos, acc_in, cw, *refs):
    count = len(places)
    lows, xs = refs[:count], refs[count:count + 2]
    hidden_out, slope_out, counted_out, w_hi, w_lo, acc = refs[count + 2:]
    total = None
    for h in range(2):
        value = acc_in[h]
        for low, place in zip(lows, places):
            value = value + product(pos, xs[h], low, place, rows)
        acc[h] = value
        for t in range(0, acc.shape[1], tile):
            at = pl.ds(t, tile)
            pre = acc[h, at, :]
            sig = 0.5 + 0.5 * jnp.tanh(0.5 * pre)
            hidden = (pre * sig).astype(bf16)
            weight = cw[h, at, :]
            counted = (weight * hidden.astype(f32)).astype(bf16)
            hidden_out[h, at, :] = hidden
            slope_out[h, at, :] = (weight * scale) * (sig * (1.0 + pre * (1.0 - sig)))
            counted_out[h, at, :] = counted
            term = dot_rows(counted, hidden)
            total = term if total is None else total + term
    w_hi[...], w_lo[...] = split(total)


def hidden_rows(pos, acc, cw, pieces, xs, rows, scale):
    shape = acc.shape
    width = shape[2]
    ins = [(a, whole(a.shape)) for a in [acc, cw] + [p[0] for p in pieces] + list(xs)]
    square = (sds((width, width), bf16), whole((width, width)))
    return call(
        functools.partial(hidden_body, scale, min(256, shape[1]), [p[1:] for p in pieces], rows),
        "hidden_units", (pos,), ins,
        [(sds(shape, bf16), whole(shape)), (sds(shape, f32), whole(shape)), (sds(shape, bf16), whole(shape)), square, square],
        scratch=[pltpu.VMEM(shape, f32)],
    )


def slope_body(places, rows, pos, acc_in, gram_in, hidden, slope, *refs):
    count = len(places)
    lows, xs, out = refs[:count], refs[count:count + 2], refs[count + 2]
    g_hi, g_lo = split(gram_sum(lows, gram_in[...]))
    for h in range(2):
        value = acc_in[h]
        for low, place in zip(lows, places):
            value = value + product(pos, xs[h], low, place, rows)
        back = dot(hidden[h], g_hi) + dot(hidden[h], g_lo) - value
        out[h] = (slope[h] * back).astype(bf16)


def slope_rows(pos, acc, gram, hidden, slope, pieces, xs, rows):
    ins = [(a, whole(a.shape)) for a in [acc, gram, hidden, slope] + [p[0] for p in pieces] + list(xs)]
    return call(
        functools.partial(slope_body, [p[1:] for p in pieces], rows), "slope_pre", (pos,), ins,
        [(sds(acc.shape, bf16), whole(acc.shape))],
    )[0]


def token_sum(start, size, xts, weights):
    at = pl.ds(start, size)
    return dot(xts[0][at, :], weights[0]) + dot(xts[1][at, :], weights[1])


def encoder_body(start, xt_own, xt_par, slopes, out):
    out[...] = token_sum(start, out.shape[0], (xt_own, xt_par), slopes).astype(out.dtype)


def decoder_body(scale, start, pieces, front, xt_own, xt_par, counted, w_hi, w_lo, *refs):
    lows, more, out = refs[:pieces], refs[pieces:-1], refs[-1]
    off = 0
    got = more
    if front:
        off = more[0].shape[0]
        out[:off, :] = more[0][...]
        got = ()
    for low in lows:
        size = low.shape[0]
        both = token_sum(start + off, size, (xt_own, xt_par), counted)
        value = scale * (dot(low[...], w_hi[...]) + dot(low[...], w_lo[...]) - both)
        for g in got:
            value = value + g[off:off + size, :].astype(f32)
        out[off:off + size, :] = value.astype(out.dtype)
        off += size


def grad_rows(body, name, size, xt, others, dtype, after=()):
    shape = (size, others[0].shape[2])
    ins = [(a, whole(a.shape)) for a in [*xt, *others]]
    return call(body, name, (), ins, [(sds(shape, dtype), whole(shape))], after=after)[0]


def adam_body(last, count, k, off, n_low, plan, own, *refs):
    got = refs[:count]
    theta, first, second = refs[count:3 + count]
    refs = refs[3 + count:]
    grad = own[...]
    for g in got:
        grad = grad + g[...].astype(f32)
    one = beta_one * first[0, 0] + (1.0 - beta_one) * grad
    two = beta_two * second[0, 0] + (1.0 - beta_two) * grad * grad
    old = theta[0, 0]
    if last:
        old = mixed(plan, k, old, refs[0][...])
    new = old - inner_rate * (one / (jnp.sqrt(two) + adam_eps) + decay_rate * old)
    if n_low is not None:
        anchor, before, lows = refs[0], refs[1:1 + n_low], refs[1 + n_low:-3]
        value = mixed(plan, k, new, anchor[off:off + own.shape[0], :]).astype(bf16)
        for b in before:
            lows[0][:off, :] = b[...]
        lows[0][off:, :] = value
    if last and k:
        refs[-4][...] = jnp.zeros_like(refs[-4])
    theta_out, first_out, second_out = refs[-3:]
    theta_out[0, 0] = new
    first_out[0, 0] = one
    second_out[0, 0] = two


def mixed(plan, k, theta, anchor):
    return jnp.where(fragment(plan) == k, mix_share * theta + (1.0 - mix_share) * anchor, theta)


def adam_rows(plan, key, own, got, state, at, new_anc, prev, full, last, lows=None, after=()):
    k, off, cr = key
    i = off // cr
    width = own.shape[1]
    block = (1, 1, cr, width)
    ins = [(g, whole(g.shape)) for g in [own] + got]
    ins += [(s, once(block, lambda g, m: (0, at[0], at[1], 0))) for s in state]
    aliases = {}
    outs = []
    if last:
        ins.append((new_anc, once((cr, width), lambda g, m: (i, 0))))
        if prev is not None:
            for n, p in enumerate(prev):
                aliases[1 + len(ins)] = n
                ins.append((p, pl.BlockSpec(memory_space=pl.ANY)))
        outs = [(sds(full, f32), once(block, lambda g, m: (0, k, i, 0)))] * 3
        if prev is None:
            outs = [(sds((8, 128), f32), whole((8, 128)))] + outs
    else:
        if lows is not None:
            ins += [(a, whole(a.shape)) for a in [new_anc] + lows]
            shape = (off + cr, width)
            outs = [(sds(shape, bf16), whole(shape))]
        outs += [(sds(block, f32), whole(block))] * 3
    return call(
        functools.partial(adam_body, last, len(got), k, off, None if lows is None else len(lows)), "adam_rows",
        (plan,), ins, outs, aliases=aliases, after=after,
    )


def quarter(pos, m, size):
    where = jnp.bitwise_xor(lax.rem(pos[0], 4), m)
    return pl.ds(pl.multiple_of(where * size, size), size)


def delta_body(pos, plan, anchor, theta, *outs):
    count = plan[pos[0]].astype(f32)
    for m, out in enumerate(outs):
        at = quarter(pos, m, out.shape[0])
        out[...] = (count * (anchor[0, at, :] - theta[0, 0, at, :])).astype(out.dtype)


def outer_start(pos, plan, anchor, weights, after):
    _, rows, width = anchor.shape
    part = (rows // 4, width)
    return call(
        delta_body, "delta_quarters", (pos, plan),
        [
            (anchor, once((1, rows, width), lambda g, p, q: (fragment(q), 0, 0))),
            (weights, once((1, 1, rows, width), lambda g, p, q: (0, fragment(q), 0, 0))),
        ],
        [(sds(part, f32), whole(part))] + [(sds(part, bf16), whole(part))] * 3, after=after,
    )


def add_body(final, plan, *refs):
    total = refs[0][...].astype(f32)
    for r in refs[1:-1]:
        total = total + r[...].astype(f32)
    if final:
        total = total / plan_sum(plan).astype(f32)
    refs[-1][...] = total.astype(bf16)


def outer_add(plan, parts, final, after=()):
    shape = parts[0].shape
    return call(
        functools.partial(add_body, final), "add_quarters", (plan,), [(a, whole(shape)) for a in parts],
        [(sds(shape, bf16), whole(shape))], after=after,
    )[0]


def outer_update(frag, at, anchor, momentum, grad):
    mom = outer_mu * momentum[frag, at, :] + grad
    return anchor[frag, at, :] - outer_rate * (grad + outer_mu * mom), mom


def new_anchor_body(pos, plan, anchor, momentum, *refs):
    for m, piece in enumerate(refs[:4]):
        at = quarter(pos, m, piece.shape[0])
        refs[4][at, :] = outer_update(0, at, anchor, momentum, piece[...].astype(f32))[0]


def outer_anchor(pos, plan, anchor, momentum, quarters, after):
    _, rows, width = anchor.shape
    part = once((1, rows, width), lambda g, p, q: (fragment(q), 0, 0))
    return call(
        new_anchor_body, "new_anchor", (pos, plan),
        [(anchor, part), (momentum, part)] + [(a, whole(a.shape)) for a in quarters],
        [(sds((rows, width), f32), whole((rows, width)))], after=after,
    )[0]


def mix_body(k, sizes, plan, new_anc, theta, low, *parts):
    value = mixed(plan, k, theta[0, 0], new_anc[...]).astype(bf16)
    low[...] = value
    put_parts(value, sizes, parts)


def mix_rows(plan, new_anc, k, theta, sizes, after):
    rows, width = new_anc.shape
    shapes = [(rows, width)] + [(size, width) for size in sizes]
    return call(
        functools.partial(mix_body, k, sizes), "mix_rows", (plan,), [(a, whole(a.shape)) for a in (new_anc, theta)],
        [(sds(shape, bf16), whole(shape)) for shape in shapes], after=after,
    )


def outer_body(pos, plan, anchor, momentum, *refs):
    quarters = refs[:4]
    anchor_out, momentum_out, token = refs[4:]
    token[...] = jnp.zeros_like(token)
    frag = fragment(plan)
    anchor_out[...] = anchor[...]
    momentum_out[...] = momentum[...]
    for m, piece in enumerate(quarters):
        at = quarter(pos, m, piece.shape[0])
        anc, mom = outer_update(frag, at, anchor, momentum, piece[...].astype(f32))
        anchor_out[frag, at, :] = anc
        momentum_out[frag, at, :] = mom


def outer_end(pos, plan, anchor, momentum, quarters, after):
    return call(
        outer_body, "outer_step", (pos, plan),
        [(a, whole(a.shape)) for a in [anchor, momentum] + quarters],
        [(sds(anchor.shape, f32), whole(anchor.shape))] * 2 + [(sds((8, 128), f32), whole((8, 128)))], after=after,
    )


def local(n_rep, n_fsdp, inputs, kinds, weights, first_moment, second_moment, anchor, momentum, plan):
    tokens = inputs.shape[0]
    rows, width = weights.shape[2:]
    chips = n_fsdp // 2
    scale = 1.0 / math.sqrt(tokens * n_fsdp)
    most = rows - rows // 4 if rows >= 1024 else rows
    sizes = [most] + [rows - most] * (most < rows)
    starts = [sum(sizes[:n]) for n in range(len(sizes))]
    others = range(1, chips)

    partner = [(f, f ^ 1) for f in range(n_fsdp)]
    to_partner = lambda a: lax.ppermute(a, "fsdp", partner)
    fetch = lambda a, s: lax.ppermute(
        a, "fsdp", [(((f // 2 + s) % chips) * 2 + f % 2, f) for f in range(n_fsdp)])
    give = lambda a, s: lax.ppermute(
        a, "fsdp", [(f, ((f // 2 + s) % chips) * 2 + f % 2) for f in range(n_fsdp)])
    across = lambda a, bit: lax.ppermute(a, "replica", [(r, r ^ bit) for r in range(n_rep)])

    chip = lax.axis_index("fsdp") // 2
    core = lax.axis_index("fsdp") % 2
    at = [((chip + s) % chips) * 2 for s in range(chips)]
    pos = jnp.stack([lax.axis_index("replica")] + [a + core for a in at] + [a + 1 - core for a in at]).astype(jnp.int32)

    enc, dec, *dec_parts = cast_rows(weights, sizes, pos)
    enc_parts = [enc]
    x_par = to_partner(inputs)
    quarters = outer_start(pos, plan, anchor, weights, [enc])
    xs, xt = zip(*[turn(pos, x, chips, stage) for x, stage in ((inputs, False), (x_par, True))])
    own = outer_add(plan, [quarters[0]] + [across(quarters[m], m) for m in range(1, 4)], n_rep == 4, xt)

    half, rest = (rows // 2, rows // 4) if rows >= 1024 else (rows, rows)
    blocks = [(1, 0, rows), (0, 0, half)] + [(0, off, rest) for off in range(half, rows, rest)]
    state = {key: (weights, first_moment, second_moment) for key in blocks}
    state_at = {(k, off, size): (k, off // size) for k, off, size in blocks}
    new_anc = None
    for step in range(INNER):
        last = step == INNER - 1
        enc_far = [{s: fetch(part, s) for s in others} for part in enc_parts]
        dec_far = [{s: fetch(part, s) for s in others} for part in dec_parts]
        enc_near, dec_near = to_partner(enc), to_partner(dec)

        def take(far, off, after, *riders):
            pieces = []
            for s in others:
                cuts = max(1, far[s].shape[0] // 384)
                cut = far[s].shape[0] // cuts
                got = relay(far[s], cuts, after, *riders)
                pieces += [(p, 1 + s, off + n * cut, cut) for n, p in enumerate(got)]
            return pieces, [(to_partner(p), slot + chips, o, size) for p, slot, o, size in pieces]

        carry = forward(pos, [], [(enc, 1, 0, rows), (enc_near, 1 + chips, 0, rows)], xs, rows, False)
        ready = [own, *xt] if step == 0 else [token]
        pending = []
        off = 0
        for part in enc_far:
            pieces, handed = take(part, off, [*carry, *ready], *([kinds] if step == 0 else []))
            carry = forward(pos, carry, pending + pieces, xs, rows, False)
            pending = handed
            off += part[1].shape[0]
        if step == 0:
            cw = weigh(kinds, pending[-1][0], tokens)
        hidden, slope, counted, w_hi, w_lo = hidden_rows(pos, carry[0], cw, pending, xs, rows, scale)
        dec_grad = lambda s, size, lows, more, front, dtype, after: grad_rows(
            functools.partial(decoder_body, scale, s * rows, len(lows), front), "decoder_grad", size, xt,
            [counted, w_hi, w_lo, *lows, *more], dtype, after)
        enc_grad = lambda s, off, size, dtype, after: grad_rows(
            functools.partial(encoder_body, s * rows + off), "encoder_grad", size, xt, [slopes], dtype, after)
        sent = []
        got = {key: [] for key in blocks}
        part, pending = [], []
        whole_grad = {s: [] for s in others}
        for n, far in enumerate(dec_far):
            pieces, handed = take(far, starts[n], [counted] + sent[-1:])
            part += pieces
            pending += handed
            for s in others:
                rows_in = [p[0] for p in pieces if p[1] == 1 + s]
                whole_grad[s] = [dec_grad(
                    s, starts[n] + sizes[n], rows_in, whole_grad[s], n > 0, bf16, sent[-1:])]
                sent.append(whole_grad[s][0])
        back = [give(whole_grad[s][0], s) for s in others]

        carry = forward(
            pos, [], [(dec, 1, 0, rows), (dec_near, 1 + chips, 0, rows)] + part, xs, rows, True, sent[-1:])
        slopes = slope_rows(pos, *carry, hidden, slope, pending, xs, rows)
        adam = lambda key, prev, *more, after=(): adam_rows(
            plan, key, mine[key], got[key], state[key], state_at[key], new_anc, prev, weights.shape, last,
            *more, after=after)
        prev = None
        mine = {}
        for n, key in enumerate(blocks[1:]):
            for s in others:
                sent.append(enc_grad(s, *key[1:], bf16, sent[-1:]))
                got[key].append(give(sent[-1], s))
            if n == 0:
                if step == 0:
                    bit = 4
                    while bit < n_rep:
                        own = outer_add(plan, [own, across(own, bit)], 2 * bit == n_rep, sent[-1:])
                        bit *= 2
                    sent.append(own)
                mine[blocks[0]] = dec_grad(0, rows, dec_parts, back, False, f32, sent[-1:])
                sent.append(mine[blocks[0]])
            if n == len(blocks) - 3 or len(blocks) == 2:
                if last:
                    token, *prev = adam(blocks[0], None)
                    sent.append(token)
                for other in blocks[1:]:
                    mine[other] = enc_grad(0, *other[1:], f32, sent[-1:])
                    sent.append(mine[other])

        if not last:
            quarters = [own] + [across(own, m) for m in range(1, 4)]
            new_anc = outer_anchor(pos, plan, anchor, momentum, quarters, [mine[blocks[0]]])
        new_state, lows = {}, []
        if last:
            for key in blocks[1:]:
                prev = adam(key, prev)
        else:
            for key in blocks[1:]:
                enc, *new_state[key] = adam(key, None, lows)
                lows = [enc]
            enc_parts = [enc]
            new_state[blocks[0]] = adam(blocks[0], None, after=[enc])
            dec, *dec_parts = mix_rows(plan, new_anc, 1, new_state[blocks[0]][0], sizes, [enc])
            anchor_out, momentum_out, token = outer_end(pos, plan, anchor, momentum, quarters, [dec])
            state, state_at = new_state, {key: (0, 0) for key in blocks}
    return (*prev, anchor_out, momentum_out)


def solution(mesh):
    return jax.shard_map(
        functools.partial(local, mesh.shape["replica"], mesh.shape["fsdp"]),
        mesh=mesh,
        in_specs=(
            P(("replica", "fsdp"), None),
            P(("replica", "fsdp")),
            P("replica", None, "fsdp", None),
            P("replica", None, "fsdp", None),
            P("replica", None, "fsdp", None),
            P(None, "fsdp", None),
            P(None, "fsdp", None),
            P(),
        ),
        out_specs=(
            P("replica", None, "fsdp", None),
            P("replica", None, "fsdp", None),
            P("replica", None, "fsdp", None),
            P(None, "fsdp", None),
            P(None, "fsdp", None),
        ),
        check_vma=False,
    )
```

```python
import functools
import math

import jax
import jax.numpy as jnp
from jax import lax
from jax.experimental import pallas as pl
from jax.experimental.pallas import tpu as pltpu
from jax.sharding import PartitionSpec as P

INNER = 2

inner_rate = 0.003
beta_one = 0.9
beta_two = 0.95
adam_eps = 1e-08
decay_rate = 0.1
outer_rate = 0.7
outer_mu = 0.9
mix_share = 0.5

bf16 = jnp.bfloat16
f32 = jnp.float32
VMEM_LIMIT = 10 * 1024 * 1024


def token_weight(kinds):
    return jnp.where(kinds == 2, 1.0, jnp.where(kinds == 1, 0.25, 0.0)).astype(f32)


def dot(a, b):
    return jnp.dot(a, b, preferred_element_type=f32)


def dot_rows(a, b):
    return lax.dot_general(a, b, (((0,), (0,)), ((), ())), preferred_element_type=f32)


def once(shape, index):
    return pl.BlockSpec(shape, index, pipeline_mode=pl.Buffered(1))


def whole(shape):
    return once(shape, lambda *_: (0,) * len(shape))


def sds(shape, dtype):
    return jax.ShapeDtypeStruct(shape, dtype)


def call(body, name, meta, ins, outs, grid=(1,), scratch=(), aliases=None, flops=0, after=()):
    arrays = [a for a, _ in ins] + list(after)
    n_in = len(meta) + len(ins)
    moved = sum(math.prod(o.shape) * o.dtype.itemsize for o, _ in outs)
    moved += sum(math.prod(s.block_shape or a.shape) * a.dtype.itemsize for a, s in ins)

    def run(*refs):
        body(*refs[:n_in], *refs[n_in + len(after):])

    return pl.pallas_call(
        run,
        name=name,
        out_shape=[o for o, _ in outs],
        grid_spec=pltpu.PrefetchScalarGridSpec(
            num_scalar_prefetch=len(meta),
            grid=grid,
            in_specs=[s for _, s in ins] + [pl.BlockSpec(memory_space=pl.ANY)] * len(after),
            out_specs=[s for _, s in outs],
            scratch_shapes=list(scratch),
        ),
        input_output_aliases=aliases or {},
        compiler_params=pltpu.CompilerParams(vmem_limit_bytes=VMEM_LIMIT),
        cost_estimate=pl.CostEstimate(flops=flops, bytes_accessed=moved, transcendentals=0),
    )(*meta, *arrays)


def plan_sum(plan):
    total = plan[0]
    for r in range(1, plan.shape[0]):
        total = total + plan[r]
    return total


def fragment(plan):
    return lax.rem(plan_sum(plan), 2)


EXTRA = 16


def cast_body(sizes, theta, enc, dec, *parts):
    enc[...] = theta[0, 0].astype(bf16)
    value = theta[0, 1].astype(bf16)
    dec[...] = value
    put_parts(value, sizes, parts)


def put_parts(value, sizes, parts):
    off = 0
    for size, part in zip(sizes, parts):
        part[...] = value[off:off + size, :]
        off += size


def cast_rows(weights, sizes, pos):
    _, _, rows, width = weights.shape
    shapes = [(rows, width)] * 2 + [(size, width) for size in sizes]
    return call(
        functools.partial(cast_body, sizes), "cast_rows", (), [(weights, whole(weights.shape))],
        [(sds(shape, bf16), whole(shape)) for shape in shapes], after=[pos],
    )


def weight_rows(kinds, wide):
    rows = [token_weight(kinds[j:j + wide].reshape(1, wide)) for j in range(0, kinds.shape[0], wide)]
    return jnp.concatenate(rows + [jnp.zeros((EXTRA - len(rows), wide), f32)], 0)


def weigh_body(kinds, other, out):
    wide = other.shape[1]
    lanes = kinds.shape[0] // wide
    own = weight_rows(kinds, wide)
    for h, rows in enumerate((own, other[other.shape[0] - EXTRA:, :].astype(f32))):
        turned = rows.T
        for j in range(lanes):
            out[h, j * wide:(j + 1) * wide, :] = turned[:, j:j + 1]


def weigh(lanes, other, tokens):
    return call(
        weigh_body, "weigh_tokens", (), [(a, whole(a.shape)) for a in (lanes, other)],
        [(sds((2, tokens, 1), f32), whole((2, tokens, 1)))],
    )[0]


def relay_body(cut, x, *refs):
    outs = refs
    if refs[0].dtype != bf16:
        kinds, outs = refs[0], refs[1:]
        outs[-1][cut:, :] = weight_rows(kinds, x.shape[1]).astype(bf16)
    for n, out in enumerate(outs):
        out[:cut, :] = x[n * cut:(n + 1) * cut, :]


def relay(x, cuts, after, lanes=None):
    rows, width = x.shape
    cut = rows // cuts
    shapes = [(cut, width)] * (cuts - 1) + [(cut + (0 if lanes is None else EXTRA), width)]
    ins = [x] if lanes is None else [x, lanes]
    return call(
        functools.partial(relay_body, cut), "relay_rows", (), [(a, whole(a.shape)) for a in ins],
        [(sds(shape, x.dtype), whole(shape)) for shape in shapes], after=after,
    )


def turn_block(pos, x, xt, t, tile):
    rows = x.shape[1] // (pos.shape[0] - 1)
    for s in range(xt.shape[0] // rows):
        xt[s * rows:(s + 1) * rows, t:t + tile] = x[t:t + tile, columns(pos, 1 + s, 0, rows, rows)].T


def columns(pos, slot, off, size, rows):
    return pl.ds(pl.multiple_of(pos[slot] * rows + off, 128), size)


def turn_body(tile, pos, x, xt):
    for t in range(0, x.shape[0], tile):
        turn_block(pos, x, xt, t, tile)


def stage_body(tile, pos, x, held, xt, sems):
    copies = []
    for n, t in enumerate(range(0, x.shape[0], tile)):
        copy = pltpu.make_async_copy(x.at[pl.ds(t, tile), :], held.at[pl.ds(t, tile), :], sems.at[n])
        copy.start()
        copies.append(copy)
    for n, t in enumerate(range(0, x.shape[0], tile)):
        copies[n].wait()
        turn_block(pos, held, xt, t, tile)


def turn(pos, x, chips, stage):
    tokens, depth = x.shape
    tile = min(128, tokens)
    xt = [(sds((depth // 2, tokens), bf16), whole((depth // 2, tokens)))]
    if not stage:
        return x, call(functools.partial(turn_body, tile), "turn_tokens", (pos,), [(x, whole(x.shape))], xt)[0]
    return call(
        functools.partial(stage_body, tile), "stage_tokens", (pos,), [(x, pl.BlockSpec(memory_space=pl.ANY))],
        [(sds(x.shape, bf16), whole(x.shape))] + xt,
        scratch=[pltpu.SemaphoreType.DMA((tokens // tile,))],
    )


def product(pos, x, low, place, rows):
    slot, off, size = place
    return dot(x[:, columns(pos, slot, off, size, rows)], low[:size, :])


def gram_sum(lows, before):
    for low in lows:
        term = dot_rows(low[...], low[...])
        before = term if before is None else before + term
    return before


def forward_body(places, rows, with_gram, first_call, pos, *refs):
    carry = 2 if with_gram else 1
    before = (None, None) if first_call else refs[:carry]
    if not first_call:
        refs = refs[carry:]
    count = len(places)
    lows, xs = refs[:count], refs[count:count + 2]
    outs = refs[count + 2:]
    if with_gram:
        outs[1][...] = gram_sum(lows, None if first_call else before[1][...])
    for h in range(2):
        value = None if first_call else before[0][h]
        for low, place in zip(lows, places):
            term = product(pos, xs[h], low, place, rows)
            value = term if value is None else value + term
        outs[0][h] = value


def forward(pos, carry, pieces, xs, rows, with_gram, after=()):
    tokens = xs[0].shape[0]
    width = pieces[0][0].shape[1]
    ins = [(a, whole(a.shape)) for a in carry]
    ins += [(p[0], whole(p[0].shape)) for p in pieces] + [(x, whole(x.shape)) for x in xs]
    shapes = [(2, tokens, width)] + [(width, width)] * with_gram
    return call(
        functools.partial(forward_body, [p[1:] for p in pieces], rows, with_gram, not carry),
        "forward_decoder" if with_gram else "forward_encoder", (pos,), ins,
        [(sds(shape, f32), whole(shape)) for shape in shapes], after=after,
    )


def split(total):
    hi = total.astype(bf16)
    return hi, (total - hi.astype(f32)).astype(bf16)


def hidden_body(scale, tile, places, rows, pos, acc_in, cw, *refs):
    count = len(places)
    lows, xs = refs[:count], refs[count:count + 2]
    hidden_out, slope_out, counted_out, w_hi, w_lo, acc = refs[count + 2:]
    total = None
    for h in range(2):
        value = acc_in[h]
        for low, place in zip(lows, places):
            value = value + product(pos, xs[h], low, place, rows)
        acc[h] = value
        for t in range(0, acc.shape[1], tile):
            at = pl.ds(t, tile)
            pre = acc[h, at, :]
            sig = 0.5 + 0.5 * jnp.tanh(0.5 * pre)
            hidden = (pre * sig).astype(bf16)
            weight = cw[h, at, :]
            counted = (weight * hidden.astype(f32)).astype(bf16)
            hidden_out[h, at, :] = hidden
            slope_out[h, at, :] = (weight * scale) * (sig * (1.0 + pre * (1.0 - sig)))
            counted_out[h, at, :] = counted
            term = dot_rows(counted, hidden)
            total = term if total is None else total + term
    w_hi[...], w_lo[...] = split(total)


def hidden_rows(pos, acc, cw, pieces, xs, rows, scale):
    shape = acc.shape
    width = shape[2]
    ins = [(a, whole(a.shape)) for a in [acc, cw] + [p[0] for p in pieces] + list(xs)]
    square = (sds((width, width), bf16), whole((width, width)))
    return call(
        functools.partial(hidden_body, scale, min(256, shape[1]), [p[1:] for p in pieces], rows),
        "hidden_units", (pos,), ins,
        [(sds(shape, bf16), whole(shape)), (sds(shape, f32), whole(shape)), (sds(shape, bf16), whole(shape)), square, square],
        scratch=[pltpu.VMEM(shape, f32)],
    )


def slope_body(places, rows, pos, acc_in, gram_in, hidden, slope, *refs):
    count = len(places)
    lows, xs, out = refs[:count], refs[count:count + 2], refs[count + 2]
    g_hi, g_lo = split(gram_sum(lows, gram_in[...]))
    for h in range(2):
        value = acc_in[h]
        for low, place in zip(lows, places):
            value = value + product(pos, xs[h], low, place, rows)
        back = dot(hidden[h], g_hi) + dot(hidden[h], g_lo) - value
        out[h] = (slope[h] * back).astype(bf16)


def slope_rows(pos, acc, gram, hidden, slope, pieces, xs, rows):
    ins = [(a, whole(a.shape)) for a in [acc, gram, hidden, slope] + [p[0] for p in pieces] + list(xs)]
    return call(
        functools.partial(slope_body, [p[1:] for p in pieces], rows), "slope_pre", (pos,), ins,
        [(sds(acc.shape, bf16), whole(acc.shape))],
    )[0]


def token_sum(start, size, xts, weights):
    at = pl.ds(start, size)
    return dot(xts[0][at, :], weights[0]) + dot(xts[1][at, :], weights[1])


def encoder_body(start, xt_own, xt_par, slopes, out):
    out[...] = token_sum(start, out.shape[0], (xt_own, xt_par), slopes).astype(out.dtype)


def decoder_body(scale, start, pieces, front, xt_own, xt_par, counted, w_hi, w_lo, *refs):
    lows, more, out = refs[:pieces], refs[pieces:-1], refs[-1]
    off = 0
    got = more
    if front:
        off = more[0].shape[0]
        out[:off, :] = more[0][...]
        got = ()
    for low in lows:
        size = low.shape[0]
        both = token_sum(start + off, size, (xt_own, xt_par), counted)
        value = scale * (dot(low[...], w_hi[...]) + dot(low[...], w_lo[...]) - both)
        for g in got:
            value = value + g[off:off + size, :].astype(f32)
        out[off:off + size, :] = value.astype(out.dtype)
        off += size


def grad_rows(body, name, size, xt, others, dtype, after=()):
    shape = (size, others[0].shape[2])
    ins = [(a, whole(a.shape)) for a in [*xt, *others]]
    return call(body, name, (), ins, [(sds(shape, dtype), whole(shape))], after=after)[0]


def adam_body(last, count, k, off, n_low, plan, own, *refs):
    got = refs[:count]
    theta, first, second = refs[count:3 + count]
    refs = refs[3 + count:]
    grad = own[...]
    for g in got:
        grad = grad + g[...].astype(f32)
    one = beta_one * first[0, 0] + (1.0 - beta_one) * grad
    two = beta_two * second[0, 0] + (1.0 - beta_two) * grad * grad
    old = theta[0, 0]
    if last:
        old = mixed(plan, k, old, refs[0][...])
    new = old - inner_rate * (one / (jnp.sqrt(two) + adam_eps) + decay_rate * old)
    if n_low is not None:
        anchor, before, lows = refs[0], refs[1:1 + n_low], refs[1 + n_low:-3]
        value = mixed(plan, k, new, anchor[off:off + own.shape[0], :]).astype(bf16)
        for b in before:
            lows[0][:off, :] = b[...]
        lows[0][off:, :] = value
    if last and k:
        refs[-4][...] = jnp.zeros_like(refs[-4])
    theta_out, first_out, second_out = refs[-3:]
    theta_out[0, 0] = new
    first_out[0, 0] = one
    second_out[0, 0] = two


def mixed(plan, k, theta, anchor):
    return jnp.where(fragment(plan) == k, mix_share * theta + (1.0 - mix_share) * anchor, theta)


def adam_rows(plan, key, own, got, state, at, new_anc, prev, full, last, lows=None, after=()):
    k, off, cr = key
    i = off // cr
    width = own.shape[1]
    block = (1, 1, cr, width)
    ins = [(g, whole(g.shape)) for g in [own] + got]
    ins += [(s, once(block, lambda g, m: (0, at[0], at[1], 0))) for s in state]
    aliases = {}
    outs = []
    if last:
        ins.append((new_anc, once((cr, width), lambda g, m: (i, 0))))
        if prev is not None:
            for n, p in enumerate(prev):
                aliases[1 + len(ins)] = n
                ins.append((p, pl.BlockSpec(memory_space=pl.ANY)))
        outs = [(sds(full, f32), once(block, lambda g, m: (0, k, i, 0)))] * 3
        if prev is None:
            outs = [(sds((8, 128), f32), whole((8, 128)))] + outs
    else:
        if lows is not None:
            ins += [(a, whole(a.shape)) for a in [new_anc] + lows]
            shape = (off + cr, width)
            outs = [(sds(shape, bf16), whole(shape))]
        outs += [(sds(block, f32), whole(block))] * 3
    return call(
        functools.partial(adam_body, last, len(got), k, off, None if lows is None else len(lows)), "adam_rows",
        (plan,), ins, outs, aliases=aliases, after=after,
    )


def quarter(pos, m, size):
    where = jnp.bitwise_xor(lax.rem(pos[0], 4), m)
    return pl.ds(pl.multiple_of(where * size, size), size)


def delta_body(pos, plan, anchor, theta, *outs):
    count = plan[pos[0]].astype(f32)
    for m, out in enumerate(outs):
        at = quarter(pos, m, out.shape[0])
        out[...] = (count * (anchor[0, at, :] - theta[0, 0, at, :])).astype(out.dtype)


def outer_start(pos, plan, anchor, weights, after):
    _, rows, width = anchor.shape
    part = (rows // 4, width)
    return call(
        delta_body, "delta_quarters", (pos, plan),
        [
            (anchor, once((1, rows, width), lambda g, p, q: (fragment(q), 0, 0))),
            (weights, once((1, 1, rows, width), lambda g, p, q: (0, fragment(q), 0, 0))),
        ],
        [(sds(part, f32), whole(part))] + [(sds(part, bf16), whole(part))] * 3, after=after,
    )


def add_body(final, plan, *refs):
    total = refs[0][...].astype(f32)
    for r in refs[1:-1]:
        total = total + r[...].astype(f32)
    if final:
        total = total / plan_sum(plan).astype(f32)
    refs[-1][...] = total.astype(bf16)


def outer_add(plan, parts, final, after=()):
    shape = parts[0].shape
    return call(
        functools.partial(add_body, final), "add_quarters", (plan,), [(a, whole(shape)) for a in parts],
        [(sds(shape, bf16), whole(shape))], after=after,
    )[0]


def outer_update(frag, at, anchor, momentum, grad):
    mom = outer_mu * momentum[frag, at, :] + grad
    return anchor[frag, at, :] - outer_rate * (grad + outer_mu * mom), mom


def new_anchor_body(pos, plan, anchor, momentum, *refs):
    for m, piece in enumerate(refs[:4]):
        at = quarter(pos, m, piece.shape[0])
        refs[4][at, :] = outer_update(0, at, anchor, momentum, piece[...].astype(f32))[0]


def outer_anchor(pos, plan, anchor, momentum, quarters, after):
    _, rows, width = anchor.shape
    part = once((1, rows, width), lambda g, p, q: (fragment(q), 0, 0))
    return call(
        new_anchor_body, "new_anchor", (pos, plan),
        [(anchor, part), (momentum, part)] + [(a, whole(a.shape)) for a in quarters],
        [(sds((rows, width), f32), whole((rows, width)))], after=after,
    )[0]


def mix_body(k, sizes, plan, new_anc, theta, low, *parts):
    value = mixed(plan, k, theta[0, 0], new_anc[...]).astype(bf16)
    low[...] = value
    put_parts(value, sizes, parts)


def mix_rows(plan, new_anc, k, theta, sizes, after):
    rows, width = new_anc.shape
    shapes = [(rows, width)] + [(size, width) for size in sizes]
    return call(
        functools.partial(mix_body, k, sizes), "mix_rows", (plan,), [(a, whole(a.shape)) for a in (new_anc, theta)],
        [(sds(shape, bf16), whole(shape)) for shape in shapes], after=after,
    )


def outer_body(pos, plan, anchor, momentum, *refs):
    quarters = refs[:4]
    anchor_out, momentum_out, token = refs[4:]
    token[...] = jnp.zeros_like(token)
    frag = fragment(plan)
    anchor_out[...] = anchor[...]
    momentum_out[...] = momentum[...]
    for m, piece in enumerate(quarters):
        at = quarter(pos, m, piece.shape[0])
        anc, mom = outer_update(frag, at, anchor, momentum, piece[...].astype(f32))
        anchor_out[frag, at, :] = anc
        momentum_out[frag, at, :] = mom


def outer_end(pos, plan, anchor, momentum, quarters, after):
    return call(
        outer_body, "outer_step", (pos, plan),
        [(a, whole(a.shape)) for a in [anchor, momentum] + quarters],
        [(sds(anchor.shape, f32), whole(anchor.shape))] * 2 + [(sds((8, 128), f32), whole((8, 128)))], after=after,
    )


def local(n_rep, n_fsdp, inputs, kinds, weights, first_moment, second_moment, anchor, momentum, plan):
    tokens = inputs.shape[0]
    rows, width = weights.shape[2:]
    chips = n_fsdp // 2
    scale = 1.0 / math.sqrt(tokens * n_fsdp)
    most = rows - rows // 4 if rows >= 1024 else rows
    sizes = [most] + [rows - most] * (most < rows)
    starts = [sum(sizes[:n]) for n in range(len(sizes))]
    others = range(1, chips)

    partner = [(f, f ^ 1) for f in range(n_fsdp)]
    to_partner = lambda a: lax.ppermute(a, "fsdp", partner)
    fetch = lambda a, s: lax.ppermute(
        a, "fsdp", [(((f // 2 + s) % chips) * 2 + f % 2, f) for f in range(n_fsdp)])
    give = lambda a, s: lax.ppermute(
        a, "fsdp", [(f, ((f // 2 + s) % chips) * 2 + f % 2) for f in range(n_fsdp)])
    across = lambda a, bit: lax.ppermute(a, "replica", [(r, r ^ bit) for r in range(n_rep)])

    chip = lax.axis_index("fsdp") // 2
    core = lax.axis_index("fsdp") % 2
    at = [((chip + s) % chips) * 2 for s in range(chips)]
    pos = jnp.stack([lax.axis_index("replica")] + [a + core for a in at] + [a + 1 - core for a in at]).astype(jnp.int32)

    enc, dec, *dec_parts = cast_rows(weights, sizes, pos)
    enc_parts = [enc]
    x_par = to_partner(inputs)
    quarters = outer_start(pos, plan, anchor, weights, [enc])
    xs, xt = zip(*[turn(pos, x, chips, stage) for x, stage in ((inputs, False), (x_par, True))])
    own = outer_add(plan, [quarters[0]] + [across(quarters[m], m) for m in range(1, 4)], n_rep == 4, xt)

    half, rest = (rows // 2, rows // 4) if rows >= 1024 else (rows, rows)
    blocks = [(1, 0, rows), (0, 0, half)] + [(0, off, rest) for off in range(half, rows, rest)]
    state = {key: (weights, first_moment, second_moment) for key in blocks}
    state_at = {(k, off, size): (k, off // size) for k, off, size in blocks}
    new_anc = None
    for step in range(INNER):
        last = step == INNER - 1
        enc_far = [{s: fetch(part, s) for s in others} for part in enc_parts]
        dec_far = [{s: fetch(part, s) for s in others} for part in dec_parts]
        enc_near, dec_near = to_partner(enc), to_partner(dec)

        def take(far, off, after, *riders):
            pieces = []
            for s in others:
                cuts = max(1, far[s].shape[0] // 384)
                cut = far[s].shape[0] // cuts
                got = relay(far[s], cuts, after, *riders)
                pieces += [(p, 1 + s, off + n * cut, cut) for n, p in enumerate(got)]
            return pieces, [(to_partner(p), slot + chips, o, size) for p, slot, o, size in pieces]

        carry = forward(pos, [], [(enc, 1, 0, rows), (enc_near, 1 + chips, 0, rows)], xs, rows, False)
        ready = [own, *xt] if step == 0 else [token]
        pending = []
        off = 0
        for part in enc_far:
            pieces, handed = take(part, off, [*carry, *ready], *([kinds] if step == 0 else []))
            carry = forward(pos, carry, pending + pieces, xs, rows, False)
            pending = handed
            off += part[1].shape[0]
        if step == 0:
            cw = weigh(kinds, pending[-1][0], tokens)
        hidden, slope, counted, w_hi, w_lo = hidden_rows(pos, carry[0], cw, pending, xs, rows, scale)
        dec_grad = lambda s, size, lows, more, front, dtype, after: grad_rows(
            functools.partial(decoder_body, scale, s * rows, len(lows), front), "decoder_grad", size, xt,
            [counted, w_hi, w_lo, *lows, *more], dtype, after)
        enc_grad = lambda s, off, size, dtype, after: grad_rows(
            functools.partial(encoder_body, s * rows + off), "encoder_grad", size, xt, [slopes], dtype, after)
        sent = []
        got = {key: [] for key in blocks}
        part, pending = [], []
        whole_grad = {s: [] for s in others}
        for n, far in enumerate(dec_far):
            pieces, handed = take(far, starts[n], [counted] + sent[-1:])
            part += pieces
            pending += handed
            for s in others:
                rows_in = [p[0] for p in pieces if p[1] == 1 + s]
                whole_grad[s] = [dec_grad(
                    s, starts[n] + sizes[n], rows_in, whole_grad[s], n > 0, bf16, sent[-1:])]
                sent.append(whole_grad[s][0])
        back = [give(whole_grad[s][0], s) for s in others]

        carry = forward(
            pos, [], [(dec, 1, 0, rows), (dec_near, 1 + chips, 0, rows)] + part, xs, rows, True, sent[-1:])
        slopes = slope_rows(pos, *carry, hidden, slope, pending, xs, rows)
        adam = lambda key, prev, *more, after=(): adam_rows(
            plan, key, mine[key], got[key], state[key], state_at[key], new_anc, prev, weights.shape, last,
            *more, after=after)
        prev = None
        mine = {}
        own_dec = lambda after: dec_grad(0, rows, dec_parts, [], False, f32, after)
        for n, key in enumerate(blocks[1:]):
            hold = back if n == 1 else []
            for s in others:
                sent.append(enc_grad(s, *key[1:], bf16, sent[-1:] + hold))
                got[key].append(give(sent[-1], s))
            if n == 0 and step == 0:
                bit = 4
                while bit < n_rep:
                    own = outer_add(plan, [own, across(own, bit)], 2 * bit == n_rep, sent[-1:])
                    bit *= 2
                sent.append(own)
            if n == (0 if last else len(blocks) - 2):
                for other in blocks[1:]:
                    mine[other] = enc_grad(0, *other[1:], f32, sent[-1:])
                    sent.append(mine[other])
                if last:
                    mine[blocks[0]] = own_dec(sent[-1:])
                    sent.append(mine[blocks[0]])
        got[blocks[0]] = back
        if last:
            token, *prev = adam(blocks[0], None, after=sent[-1:])

        if not last:
            quarters = [own] + [across(own, m) for m in range(1, 4)]
            new_anc = outer_anchor(pos, plan, anchor, momentum, quarters, sent[-1:])
        new_state, lows = {}, []
        if last:
            for key in blocks[1:]:
                prev = adam(key, prev)
        else:
            for key in blocks[1:]:
                enc, *new_state[key] = adam(key, None, lows)
                lows = [enc]
            enc_parts = [enc]
            mine[blocks[0]] = own_dec([enc])
            new_state[blocks[0]] = adam(blocks[0], None, after=[enc])
            dec, *dec_parts = mix_rows(plan, new_anc, 1, new_state[blocks[0]][0], sizes, [enc])
            anchor_out, momentum_out, token = outer_end(pos, plan, anchor, momentum, quarters, [dec])
            state, state_at = new_state, {key: (0, 0) for key in blocks}
    return (*prev, anchor_out, momentum_out)


def solution(mesh):
    return jax.shard_map(
        functools.partial(local, mesh.shape["replica"], mesh.shape["fsdp"]),
        mesh=mesh,
        in_specs=(
            P(("replica", "fsdp"), None),
            P(("replica", "fsdp")),
            P("replica", None, "fsdp", None),
            P("replica", None, "fsdp", None),
            P("replica", None, "fsdp", None),
            P(None, "fsdp", None),
            P(None, "fsdp", None),
            P(),
        ),
        out_specs=(
            P("replica", None, "fsdp", None),
            P("replica", None, "fsdp", None),
            P("replica", None, "fsdp", None),
            P(None, "fsdp", None),
            P(None, "fsdp", None),
        ),
        check_vma=False,
    )
```

```python
import functools
import math

import jax
import jax.numpy as jnp
from jax import lax
from jax.experimental import pallas as pl
from jax.experimental.pallas import tpu as pltpu
from jax.sharding import PartitionSpec as P

INNER = 2

inner_rate = 0.003
beta_one = 0.9
beta_two = 0.95
adam_eps = 1e-08
decay_rate = 0.1
outer_rate = 0.7
outer_mu = 0.9
mix_share = 0.5

bf16 = jnp.bfloat16
f32 = jnp.float32
VMEM_LIMIT = 10 * 1024 * 1024


def token_weight(kinds):
    return jnp.where(kinds == 2, 1.0, jnp.where(kinds == 1, 0.25, 0.0)).astype(f32)


def dot(a, b):
    return jnp.dot(a, b, preferred_element_type=f32)


def dot_rows(a, b):
    return lax.dot_general(a, b, (((0,), (0,)), ((), ())), preferred_element_type=f32)


def once(shape, index):
    return pl.BlockSpec(shape, index, pipeline_mode=pl.Buffered(1))


def whole(shape):
    return once(shape, lambda *_: (0,) * len(shape))


def sds(shape, dtype):
    return jax.ShapeDtypeStruct(shape, dtype)


def call(body, name, meta, ins, outs, grid=(1,), scratch=(), aliases=None, flops=0, after=()):
    arrays = [a for a, _ in ins] + list(after)
    n_in = len(meta) + len(ins)
    moved = sum(math.prod(o.shape) * o.dtype.itemsize for o, _ in outs)
    moved += sum(math.prod(s.block_shape or a.shape) * a.dtype.itemsize for a, s in ins)

    def run(*refs):
        body(*refs[:n_in], *refs[n_in + len(after):])

    return pl.pallas_call(
        run,
        name=name,
        out_shape=[o for o, _ in outs],
        grid_spec=pltpu.PrefetchScalarGridSpec(
            num_scalar_prefetch=len(meta),
            grid=grid,
            in_specs=[s for _, s in ins] + [pl.BlockSpec(memory_space=pl.ANY)] * len(after),
            out_specs=[s for _, s in outs],
            scratch_shapes=list(scratch),
        ),
        input_output_aliases=aliases or {},
        compiler_params=pltpu.CompilerParams(vmem_limit_bytes=VMEM_LIMIT),
        cost_estimate=pl.CostEstimate(flops=flops, bytes_accessed=moved, transcendentals=0),
    )(*meta, *arrays)


def plan_sum(plan):
    total = plan[0]
    for r in range(1, plan.shape[0]):
        total = total + plan[r]
    return total


def fragment(plan):
    return lax.rem(plan_sum(plan), 2)


EXTRA = 16


def cast_body(sizes, theta, enc, dec, *parts):
    enc[...] = theta[0, 0].astype(bf16)
    value = theta[0, 1].astype(bf16)
    dec[...] = value
    put_parts(value, sizes, parts)


def put_parts(value, sizes, parts):
    off = 0
    for size, part in zip(sizes, parts):
        part[...] = value[off:off + size, :]
        off += size


def cast_rows(weights, sizes, pos):
    _, _, rows, width = weights.shape
    shapes = [(rows, width)] * 2 + [(size, width) for size in sizes]
    return call(
        functools.partial(cast_body, sizes), "cast_rows", (), [(weights, whole(weights.shape))],
        [(sds(shape, bf16), whole(shape)) for shape in shapes], after=[pos],
    )


def weight_rows(kinds, wide):
    rows = [token_weight(kinds[j:j + wide].reshape(1, wide)) for j in range(0, kinds.shape[0], wide)]
    return jnp.concatenate(rows + [jnp.zeros((EXTRA - len(rows), wide), f32)], 0)


def weigh_body(kinds, other, out):
    wide = other.shape[1]
    lanes = kinds.shape[0] // wide
    own = weight_rows(kinds, wide)
    for h, rows in enumerate((own, other[other.shape[0] - EXTRA:, :].astype(f32))):
        turned = rows.T
        for j in range(lanes):
            out[h, j * wide:(j + 1) * wide, :] = turned[:, j:j + 1]


def weigh(lanes, other, tokens):
    return call(
        weigh_body, "weigh_tokens", (), [(a, whole(a.shape)) for a in (lanes, other)],
        [(sds((2, tokens, 1), f32), whole((2, tokens, 1)))],
    )[0]


def relay_body(cut, x, *refs):
    outs = refs
    if refs[0].dtype != bf16:
        kinds, outs = refs[0], refs[1:]
        outs[-1][cut:, :] = weight_rows(kinds, x.shape[1]).astype(bf16)
    for n, out in enumerate(outs):
        out[:cut, :] = x[n * cut:(n + 1) * cut, :]


def relay(x, cuts, after, lanes=None):
    rows, width = x.shape
    cut = rows // cuts
    shapes = [(cut, width)] * (cuts - 1) + [(cut + (0 if lanes is None else EXTRA), width)]
    ins = [x] if lanes is None else [x, lanes]
    return call(
        functools.partial(relay_body, cut), "relay_rows", (), [(a, whole(a.shape)) for a in ins],
        [(sds(shape, x.dtype), whole(shape)) for shape in shapes], after=after,
    )


def turn_block(pos, x, xt, t, tile):
    rows = x.shape[1] // (pos.shape[0] - 1)
    for s in range(xt.shape[0] // rows):
        xt[s * rows:(s + 1) * rows, t:t + tile] = x[t:t + tile, columns(pos, 1 + s, 0, rows, rows)].T


def columns(pos, slot, off, size, rows):
    return pl.ds(pl.multiple_of(pos[slot] * rows + off, 128), size)


def turn_body(tile, pos, x, xt):
    for t in range(0, x.shape[0], tile):
        turn_block(pos, x, xt, t, tile)


def stage_body(tile, pos, x, held, xt, sems):
    copies = []
    for n, t in enumerate(range(0, x.shape[0], tile)):
        copy = pltpu.make_async_copy(x.at[pl.ds(t, tile), :], held.at[pl.ds(t, tile), :], sems.at[n])
        copy.start()
        copies.append(copy)
    for n, t in enumerate(range(0, x.shape[0], tile)):
        copies[n].wait()
        turn_block(pos, held, xt, t, tile)


def turn(pos, x, chips, stage):
    tokens, depth = x.shape
    tile = min(128, tokens)
    xt = [(sds((depth // 2, tokens), bf16), whole((depth // 2, tokens)))]
    if not stage:
        return x, call(functools.partial(turn_body, tile), "turn_tokens", (pos,), [(x, whole(x.shape))], xt)[0]
    return call(
        functools.partial(stage_body, tile), "stage_tokens", (pos,), [(x, pl.BlockSpec(memory_space=pl.ANY))],
        [(sds(x.shape, bf16), whole(x.shape))] + xt,
        scratch=[pltpu.SemaphoreType.DMA((tokens // tile,))],
    )


def product(pos, x, low, place, rows):
    slot, off, size = place
    return dot(x[:, columns(pos, slot, off, size, rows)], low[:size, :])


def gram_sum(lows, before):
    for low in lows:
        term = dot_rows(low[...], low[...])
        before = term if before is None else before + term
    return before


def forward_body(places, rows, with_gram, first_call, pos, *refs):
    carry = 2 if with_gram else 1
    before = (None, None) if first_call else refs[:carry]
    if not first_call:
        refs = refs[carry:]
    count = len(places)
    lows, xs = refs[:count], refs[count:count + 2]
    outs = refs[count + 2:]
    if with_gram:
        outs[1][...] = gram_sum(lows, None if first_call else before[1][...])
    for h in range(2):
        value = None if first_call else before[0][h]
        for low, place in zip(lows, places):
            term = product(pos, xs[h], low, place, rows)
            value = term if value is None else value + term
        outs[0][h] = value


def forward(pos, carry, pieces, xs, rows, with_gram, after=()):
    tokens = xs[0].shape[0]
    width = pieces[0][0].shape[1]
    ins = [(a, whole(a.shape)) for a in carry]
    ins += [(p[0], whole(p[0].shape)) for p in pieces] + [(x, whole(x.shape)) for x in xs]
    shapes = [(2, tokens, width)] + [(width, width)] * with_gram
    return call(
        functools.partial(forward_body, [p[1:] for p in pieces], rows, with_gram, not carry),
        "forward_decoder" if with_gram else "forward_encoder", (pos,), ins,
        [(sds(shape, f32), whole(shape)) for shape in shapes], after=after,
    )


def split(total):
    hi = total.astype(bf16)
    return hi, (total - hi.astype(f32)).astype(bf16)


def hidden_body(scale, tile, places, rows, pos, acc_in, cw, *refs):
    count = len(places)
    lows, xs = refs[:count], refs[count:count + 2]
    hidden_out, slope_out, counted_out, w_hi, w_lo, acc = refs[count + 2:]
    total = None
    for h in range(2):
        value = acc_in[h]
        for low, place in zip(lows, places):
            value = value + product(pos, xs[h], low, place, rows)
        acc[h] = value
        for t in range(0, acc.shape[1], tile):
            at = pl.ds(t, tile)
            pre = acc[h, at, :]
            sig = 0.5 + 0.5 * jnp.tanh(0.5 * pre)
            hidden = (pre * sig).astype(bf16)
            weight = cw[h, at, :]
            counted = (weight * hidden.astype(f32)).astype(bf16)
            hidden_out[h, at, :] = hidden
            slope_out[h, at, :] = (weight * scale) * (sig * (1.0 + pre * (1.0 - sig)))
            counted_out[h, at, :] = counted
            term = dot_rows(counted, hidden)
            total = term if total is None else total + term
    w_hi[...], w_lo[...] = split(total)


def hidden_rows(pos, acc, cw, pieces, xs, rows, scale):
    shape = acc.shape
    width = shape[2]
    ins = [(a, whole(a.shape)) for a in [acc, cw] + [p[0] for p in pieces] + list(xs)]
    square = (sds((width, width), bf16), whole((width, width)))
    return call(
        functools.partial(hidden_body, scale, min(256, shape[1]), [p[1:] for p in pieces], rows),
        "hidden_units", (pos,), ins,
        [(sds(shape, bf16), whole(shape)), (sds(shape, f32), whole(shape)), (sds(shape, bf16), whole(shape)), square, square],
        scratch=[pltpu.VMEM(shape, f32)],
    )


def slope_body(places, rows, pos, acc_in, gram_in, hidden, slope, *refs):
    count = len(places)
    lows, xs, out = refs[:count], refs[count:count + 2], refs[count + 2]
    g_hi, g_lo = split(gram_sum(lows, gram_in[...]))
    for h in range(2):
        value = acc_in[h]
        for low, place in zip(lows, places):
            value = value + product(pos, xs[h], low, place, rows)
        back = dot(hidden[h], g_hi) + dot(hidden[h], g_lo) - value
        out[h] = (slope[h] * back).astype(bf16)


def slope_rows(pos, acc, gram, hidden, slope, pieces, xs, rows):
    ins = [(a, whole(a.shape)) for a in [acc, gram, hidden, slope] + [p[0] for p in pieces] + list(xs)]
    return call(
        functools.partial(slope_body, [p[1:] for p in pieces], rows), "slope_pre", (pos,), ins,
        [(sds(acc.shape, bf16), whole(acc.shape))],
    )[0]


def token_sum(start, size, xts, weights):
    at = pl.ds(start, size)
    return dot(xts[0][at, :], weights[0]) + dot(xts[1][at, :], weights[1])


def encoder_body(start, xt_own, xt_par, slopes, out):
    out[...] = token_sum(start, out.shape[0], (xt_own, xt_par), slopes).astype(out.dtype)


def decoder_body(scale, start, xt_own, xt_par, counted, w_hi, w_lo, *refs):
    lows, out = refs[:-1], refs[-1]
    off = 0
    for low in lows:
        size = low.shape[0]
        both = token_sum(start + off, size, (xt_own, xt_par), counted)
        value = scale * (dot(low[...], w_hi[...]) + dot(low[...], w_lo[...]) - both)
        out[off:off + size, :] = value.astype(out.dtype)
        off += size


def grad_rows(body, name, size, xt, others, dtype, after=()):
    shape = (size, others[0].shape[2])
    ins = [(a, whole(a.shape)) for a in [*xt, *others]]
    return call(body, name, (), ins, [(sds(shape, dtype), whole(shape))], after=after)[0]


def adam_body(last, count, k, off, n_low, plan, own, *refs):
    got = refs[:count]
    theta, first, second = refs[count:3 + count]
    refs = refs[3 + count:]
    grad = own[...]
    got = [g[...].astype(f32) for g in got]
    while got:
        value = got.pop(0)
        while value.shape[0] < own.shape[0]:
            value = jnp.concatenate([value, got.pop(0)], 0)
        grad = grad + value
    one = beta_one * first[0, 0] + (1.0 - beta_one) * grad
    two = beta_two * second[0, 0] + (1.0 - beta_two) * grad * grad
    old = theta[0, 0]
    if last:
        old = mixed(plan, k, old, refs[0][...])
    new = old - inner_rate * (one / (jnp.sqrt(two) + adam_eps) + decay_rate * old)
    if n_low is not None:
        anchor, before, lows = refs[0], refs[1:1 + n_low], refs[1 + n_low:-3]
        value = mixed(plan, k, new, anchor[off:off + own.shape[0], :]).astype(bf16)
        for b in before:
            lows[0][:off, :] = b[...]
        lows[0][off:, :] = value
    if last and k:
        refs[-4][...] = jnp.zeros_like(refs[-4])
    theta_out, first_out, second_out = refs[-3:]
    theta_out[0, 0] = new
    first_out[0, 0] = one
    second_out[0, 0] = two


def mixed(plan, k, theta, anchor):
    return jnp.where(fragment(plan) == k, mix_share * theta + (1.0 - mix_share) * anchor, theta)


def adam_rows(plan, key, own, got, state, at, new_anc, prev, full, last, lows=None, after=()):
    k, off, cr = key
    i = off // cr
    width = own.shape[1]
    block = (1, 1, cr, width)
    ins = [(g, whole(g.shape)) for g in [own] + got]
    ins += [(s, once(block, lambda g, m: (0, at[0], at[1], 0))) for s in state]
    aliases = {}
    outs = []
    if last:
        ins.append((new_anc, once((cr, width), lambda g, m: (i, 0))))
        if prev is not None:
            for n, p in enumerate(prev):
                aliases[1 + len(ins)] = n
                ins.append((p, pl.BlockSpec(memory_space=pl.ANY)))
        outs = [(sds(full, f32), once(block, lambda g, m: (0, k, i, 0)))] * 3
        if prev is None:
            outs = [(sds((8, 128), f32), whole((8, 128)))] + outs
    else:
        if lows is not None:
            ins += [(a, whole(a.shape)) for a in [new_anc] + lows]
            shape = (off + cr, width)
            outs = [(sds(shape, bf16), whole(shape))]
        outs += [(sds(block, f32), whole(block))] * 3
    return call(
        functools.partial(adam_body, last, len(got), k, off, None if lows is None else len(lows)), "adam_rows",
        (plan,), ins, outs, aliases=aliases, after=after,
    )


def quarter(pos, m, size):
    where = jnp.bitwise_xor(lax.rem(pos[0], 4), m)
    return pl.ds(pl.multiple_of(where * size, size), size)


def delta_body(pos, plan, anchor, theta, *outs):
    count = plan[pos[0]].astype(f32)
    for m, out in enumerate(outs):
        at = quarter(pos, m, out.shape[0])
        out[...] = (count * (anchor[0, at, :] - theta[0, 0, at, :])).astype(out.dtype)


def outer_start(pos, plan, anchor, weights, after):
    _, rows, width = anchor.shape
    part = (rows // 4, width)
    return call(
        delta_body, "delta_quarters", (pos, plan),
        [
            (anchor, once((1, rows, width), lambda g, p, q: (fragment(q), 0, 0))),
            (weights, once((1, 1, rows, width), lambda g, p, q: (0, fragment(q), 0, 0))),
        ],
        [(sds(part, f32), whole(part))] + [(sds(part, bf16), whole(part))] * 3, after=after,
    )


def add_body(final, plan, *refs):
    total = refs[0][...].astype(f32)
    for r in refs[1:-1]:
        total = total + r[...].astype(f32)
    if final:
        total = total / plan_sum(plan).astype(f32)
    refs[-1][...] = total.astype(bf16)


def outer_add(plan, parts, final, after=()):
    shape = parts[0].shape
    return call(
        functools.partial(add_body, final), "add_quarters", (plan,), [(a, whole(shape)) for a in parts],
        [(sds(shape, bf16), whole(shape))], after=after,
    )[0]


def outer_update(frag, at, anchor, momentum, grad):
    mom = outer_mu * momentum[frag, at, :] + grad
    return anchor[frag, at, :] - outer_rate * (grad + outer_mu * mom), mom


def new_anchor_body(pos, plan, anchor, momentum, *refs):
    for m, piece in enumerate(refs[:4]):
        at = quarter(pos, m, piece.shape[0])
        refs[4][at, :] = outer_update(0, at, anchor, momentum, piece[...].astype(f32))[0]


def outer_anchor(pos, plan, anchor, momentum, quarters, after):
    _, rows, width = anchor.shape
    part = once((1, rows, width), lambda g, p, q: (fragment(q), 0, 0))
    return call(
        new_anchor_body, "new_anchor", (pos, plan),
        [(anchor, part), (momentum, part)] + [(a, whole(a.shape)) for a in quarters],
        [(sds((rows, width), f32), whole((rows, width)))], after=after,
    )[0]


def mix_body(k, sizes, plan, new_anc, theta, low, *parts):
    value = mixed(plan, k, theta[0, 0], new_anc[...]).astype(bf16)
    low[...] = value
    put_parts(value, sizes, parts)


def mix_rows(plan, new_anc, k, theta, sizes, after):
    rows, width = new_anc.shape
    shapes = [(rows, width)] + [(size, width) for size in sizes]
    return call(
        functools.partial(mix_body, k, sizes), "mix_rows", (plan,), [(a, whole(a.shape)) for a in (new_anc, theta)],
        [(sds(shape, bf16), whole(shape)) for shape in shapes], after=after,
    )


def outer_body(pos, plan, anchor, momentum, *refs):
    quarters = refs[:4]
    anchor_out, momentum_out, token = refs[4:]
    token[...] = jnp.zeros_like(token)
    frag = fragment(plan)
    anchor_out[...] = anchor[...]
    momentum_out[...] = momentum[...]
    for m, piece in enumerate(quarters):
        at = quarter(pos, m, piece.shape[0])
        anc, mom = outer_update(frag, at, anchor, momentum, piece[...].astype(f32))
        anchor_out[frag, at, :] = anc
        momentum_out[frag, at, :] = mom


def outer_end(pos, plan, anchor, momentum, quarters, after):
    return call(
        outer_body, "outer_step", (pos, plan),
        [(a, whole(a.shape)) for a in [anchor, momentum] + quarters],
        [(sds(anchor.shape, f32), whole(anchor.shape))] * 2 + [(sds((8, 128), f32), whole((8, 128)))], after=after,
    )


def local(n_rep, n_fsdp, inputs, kinds, weights, first_moment, second_moment, anchor, momentum, plan):
    tokens = inputs.shape[0]
    rows, width = weights.shape[2:]
    chips = n_fsdp // 2
    scale = 1.0 / math.sqrt(tokens * n_fsdp)
    most = rows - rows // 4 if rows >= 1024 else rows
    sizes = [most] + [rows - most] * (most < rows)
    starts = [sum(sizes[:n]) for n in range(len(sizes))]
    others = range(1, chips)

    partner = [(f, f ^ 1) for f in range(n_fsdp)]
    to_partner = lambda a: lax.ppermute(a, "fsdp", partner)
    fetch = lambda a, s: lax.ppermute(
        a, "fsdp", [(((f // 2 + s) % chips) * 2 + f % 2, f) for f in range(n_fsdp)])
    give = lambda a, s: lax.ppermute(
        a, "fsdp", [(f, ((f // 2 + s) % chips) * 2 + f % 2) for f in range(n_fsdp)])
    across = lambda a, bit: lax.ppermute(a, "replica", [(r, r ^ bit) for r in range(n_rep)])

    chip = lax.axis_index("fsdp") // 2
    core = lax.axis_index("fsdp") % 2
    at = [((chip + s) % chips) * 2 for s in range(chips)]
    pos = jnp.stack([lax.axis_index("replica")] + [a + core for a in at] + [a + 1 - core for a in at]).astype(jnp.int32)

    enc, dec, *dec_parts = cast_rows(weights, sizes, pos)
    enc_parts = [enc]
    x_par = to_partner(inputs)
    quarters = outer_start(pos, plan, anchor, weights, [enc])
    xs, xt = zip(*[turn(pos, x, chips, stage) for x, stage in ((inputs, False), (x_par, True))])
    own = outer_add(plan, [quarters[0]] + [across(quarters[m], m) for m in range(1, 4)], n_rep == 4, xt)

    half, rest = (rows // 2, rows // 4) if rows >= 1024 else (rows, rows)
    blocks = [(1, 0, rows), (0, 0, half)] + [(0, off, rest) for off in range(half, rows, rest)]
    state = {key: (weights, first_moment, second_moment) for key in blocks}
    state_at = {(k, off, size): (k, off // size) for k, off, size in blocks}
    new_anc = None
    for step in range(INNER):
        last = step == INNER - 1
        enc_far = [{s: fetch(part, s) for s in others} for part in enc_parts]
        dec_far = [{s: fetch(part, s) for s in others} for part in dec_parts]
        enc_near, dec_near = to_partner(enc), to_partner(dec)

        def take(far, off, after, *riders):
            pieces = []
            for s in others:
                cuts = max(1, far[s].shape[0] // 384)
                cut = far[s].shape[0] // cuts
                got = relay(far[s], cuts, after, *riders)
                pieces += [(p, 1 + s, off + n * cut, cut) for n, p in enumerate(got)]
            return pieces, [(to_partner(p), slot + chips, o, size) for p, slot, o, size in pieces]

        carry = forward(pos, [], [(enc, 1, 0, rows), (enc_near, 1 + chips, 0, rows)], xs, rows, False)
        ready = [own, *xt] if step == 0 else [token]
        pending = []
        off = 0
        for part in enc_far:
            pieces, handed = take(part, off, [*carry, *ready], *([kinds] if step == 0 else []))
            carry = forward(pos, carry, pending + pieces, xs, rows, False)
            pending = handed
            off += part[1].shape[0]
        if step == 0:
            cw = weigh(kinds, pending[-1][0], tokens)
        hidden, slope, counted, w_hi, w_lo = hidden_rows(pos, carry[0], cw, pending, xs, rows, scale)
        dec_grad = lambda start, size, lows, dtype, after: grad_rows(
            functools.partial(decoder_body, scale, start), "decoder_grad", size, xt,
            [counted, w_hi, w_lo, *lows], dtype, after)
        enc_grad = lambda s, off, size, dtype, after: grad_rows(
            functools.partial(encoder_body, s * rows + off), "encoder_grad", size, xt, [slopes], dtype, after)
        sent = []
        got = {key: [] for key in blocks}
        part, pending = [], []
        back = {}
        for n, far in enumerate(dec_far):
            pieces, handed = take(far, starts[n], [counted] + sent[-1:])
            part += pieces
            pending += handed
            for s in others:
                rows_in = [p[0] for p in pieces if p[1] == 1 + s]
                sent.append(dec_grad(s * rows + starts[n], sizes[n], rows_in, bf16, sent[-1:]))
                back[s, n] = give(sent[-1], s)
        back = [back[key] for key in sorted(back)]

        carry = forward(
            pos, [], [(dec, 1, 0, rows), (dec_near, 1 + chips, 0, rows)] + part, xs, rows, True, sent[-1:])
        slopes = slope_rows(pos, *carry, hidden, slope, pending, xs, rows)
        adam = lambda key, prev, *more, after=(): adam_rows(
            plan, key, mine[key], got[key], state[key], state_at[key], new_anc, prev, weights.shape, last,
            *more, after=after)
        prev = None
        mine = {}
        own_dec = lambda after: dec_grad(0, rows, dec_parts, f32, after)
        for n, key in enumerate(blocks[1:]):
            hold = back if n == 1 else []
            for s in others:
                sent.append(enc_grad(s, *key[1:], bf16, sent[-1:] + hold))
                got[key].append(give(sent[-1], s))
            if n == 0 and step == 0:
                bit = 4
                while bit < n_rep:
                    own = outer_add(plan, [own, across(own, bit)], 2 * bit == n_rep, sent[-1:])
                    bit *= 2
                sent.append(own)
            if n == (0 if last else len(blocks) - 2):
                for other in blocks[1:]:
                    mine[other] = enc_grad(0, *other[1:], f32, sent[-1:])
                    sent.append(mine[other])
                if last:
                    mine[blocks[0]] = own_dec(sent[-1:])
                    sent.append(mine[blocks[0]])
        got[blocks[0]] = back
        if last:
            token, *prev = adam(blocks[0], None, after=sent[-1:])

        if not last:
            quarters = [own] + [across(own, m) for m in range(1, 4)]
            new_anc = outer_anchor(pos, plan, anchor, momentum, quarters, sent[-1:])
        new_state, lows = {}, []
        if last:
            for key in blocks[1:]:
                prev = adam(key, prev)
        else:
            for key in blocks[1:]:
                enc, *new_state[key] = adam(key, None, lows)
                lows = [enc]
            enc_parts = [enc]
            mine[blocks[0]] = own_dec([enc])
            new_state[blocks[0]] = adam(blocks[0], None, after=[enc])
            dec, *dec_parts = mix_rows(plan, new_anc, 1, new_state[blocks[0]][0], sizes, [enc])
            anchor_out, momentum_out, token = outer_end(pos, plan, anchor, momentum, quarters, [dec])
            state, state_at = new_state, {key: (0, 0) for key in blocks}
    return (*prev, anchor_out, momentum_out)


def solution(mesh):
    return jax.shard_map(
        functools.partial(local, mesh.shape["replica"], mesh.shape["fsdp"]),
        mesh=mesh,
        in_specs=(
            P(("replica", "fsdp"), None),
            P(("replica", "fsdp")),
            P("replica", None, "fsdp", None),
            P("replica", None, "fsdp", None),
            P("replica", None, "fsdp", None),
            P(None, "fsdp", None),
            P(None, "fsdp", None),
            P(),
        ),
        out_specs=(
            P("replica", None, "fsdp", None),
            P("replica", None, "fsdp", None),
            P("replica", None, "fsdp", None),
            P(None, "fsdp", None),
            P(None, "fsdp", None),
        ),
        check_vma=False,
    )
```

```python
import functools
import math

import jax
import jax.numpy as jnp
from jax import lax
from jax.experimental import pallas as pl
from jax.experimental.pallas import tpu as pltpu
from jax.sharding import PartitionSpec as P

INNER = 2

inner_rate = 0.003
beta_one = 0.9
beta_two = 0.95
adam_eps = 1e-08
decay_rate = 0.1
outer_rate = 0.7
outer_mu = 0.9
mix_share = 0.5

bf16 = jnp.bfloat16
f32 = jnp.float32
VMEM_LIMIT = 10 * 1024 * 1024


def token_weight(kinds):
    return jnp.where(kinds == 2, 1.0, jnp.where(kinds == 1, 0.25, 0.0)).astype(f32)


def dot(a, b):
    return jnp.dot(a, b, preferred_element_type=f32)


def dot_rows(a, b):
    return lax.dot_general(a, b, (((0,), (0,)), ((), ())), preferred_element_type=f32)


def once(shape, index):
    return pl.BlockSpec(shape, index, pipeline_mode=pl.Buffered(1))


def whole(shape):
    return once(shape, lambda *_: (0,) * len(shape))


def sds(shape, dtype):
    return jax.ShapeDtypeStruct(shape, dtype)


def call(body, name, meta, ins, outs, grid=(1,), scratch=(), aliases=None, flops=0, after=()):
    arrays = [a for a, _ in ins] + list(after)
    n_in = len(meta) + len(ins)
    moved = sum(math.prod(o.shape) * o.dtype.itemsize for o, _ in outs)
    moved += sum(math.prod(s.block_shape or a.shape) * a.dtype.itemsize for a, s in ins)

    def run(*refs):
        body(*refs[:n_in], *refs[n_in + len(after):])

    return pl.pallas_call(
        run,
        name=name,
        out_shape=[o for o, _ in outs],
        grid_spec=pltpu.PrefetchScalarGridSpec(
            num_scalar_prefetch=len(meta),
            grid=grid,
            in_specs=[s for _, s in ins] + [pl.BlockSpec(memory_space=pl.ANY)] * len(after),
            out_specs=[s for _, s in outs],
            scratch_shapes=list(scratch),
        ),
        input_output_aliases=aliases or {},
        compiler_params=pltpu.CompilerParams(vmem_limit_bytes=VMEM_LIMIT),
        cost_estimate=pl.CostEstimate(flops=flops, bytes_accessed=moved, transcendentals=0),
    )(*meta, *arrays)


def plan_sum(plan):
    total = plan[0]
    for r in range(1, plan.shape[0]):
        total = total + plan[r]
    return total


def fragment(plan):
    return lax.rem(plan_sum(plan), 2)


EXTRA = 16


def cast_body(sizes, theta, enc, dec, *parts):
    enc[...] = theta[0, 0].astype(bf16)
    value = theta[0, 1].astype(bf16)
    dec[...] = value
    put_parts(value, sizes, parts)


def put_parts(value, sizes, parts):
    off = 0
    for size, part in zip(sizes, parts):
        part[...] = value[off:off + size, :]
        off += size


def cast_rows(weights, sizes, pos):
    _, _, rows, width = weights.shape
    shapes = [(rows, width)] * 2 + [(size, width) for size in sizes]
    return call(
        functools.partial(cast_body, sizes), "cast_rows", (), [(weights, whole(weights.shape))],
        [(sds(shape, bf16), whole(shape)) for shape in shapes], after=[pos],
    )


def weight_rows(kinds, wide):
    rows = [token_weight(kinds[j:j + wide].reshape(1, wide)) for j in range(0, kinds.shape[0], wide)]
    return jnp.concatenate(rows + [jnp.zeros((EXTRA - len(rows), wide), f32)], 0)


def weigh_body(kinds, other, out):
    wide = other.shape[1]
    lanes = kinds.shape[0] // wide
    own = weight_rows(kinds, wide)
    for h, rows in enumerate((own, other[other.shape[0] - EXTRA:, :].astype(f32))):
        turned = rows.T
        for j in range(lanes):
            out[h, j * wide:(j + 1) * wide, :] = turned[:, j:j + 1]


def weigh(lanes, other, tokens):
    return call(
        weigh_body, "weigh_tokens", (), [(a, whole(a.shape)) for a in (lanes, other)],
        [(sds((2, tokens, 1), f32), whole((2, tokens, 1)))],
    )[0]


def relay_body(cut, x, *refs):
    outs = refs
    if refs[0].dtype != bf16:
        kinds, outs = refs[0], refs[1:]
        outs[-1][cut:, :] = weight_rows(kinds, x.shape[1]).astype(bf16)
    for n, out in enumerate(outs):
        out[:cut, :] = x[n * cut:(n + 1) * cut, :]


def relay(x, cuts, after, lanes=None):
    rows, width = x.shape
    cut = rows // cuts
    shapes = [(cut, width)] * (cuts - 1) + [(cut + (0 if lanes is None else EXTRA), width)]
    ins = [x] if lanes is None else [x, lanes]
    return call(
        functools.partial(relay_body, cut), "relay_rows", (), [(a, whole(a.shape)) for a in ins],
        [(sds(shape, x.dtype), whole(shape)) for shape in shapes], after=after,
    )


def turn_block(pos, x, xt, t, tile):
    rows = x.shape[1] // (pos.shape[0] - 1)
    for s in range(xt.shape[0] // rows):
        xt[s * rows:(s + 1) * rows, t:t + tile] = x[t:t + tile, columns(pos, 1 + s, 0, rows, rows)].T


def columns(pos, slot, off, size, rows):
    return pl.ds(pl.multiple_of(pos[slot] * rows + off, 128), size)


def turn_body(tile, pos, x, xt):
    for t in range(0, x.shape[0], tile):
        turn_block(pos, x, xt, t, tile)


def stage_body(tile, pos, x, held, xt, sems):
    copies = []
    for n, t in enumerate(range(0, x.shape[0], tile)):
        copy = pltpu.make_async_copy(x.at[pl.ds(t, tile), :], held.at[pl.ds(t, tile), :], sems.at[n])
        copy.start()
        copies.append(copy)
    for n, t in enumerate(range(0, x.shape[0], tile)):
        copies[n].wait()
        turn_block(pos, held, xt, t, tile)


def turn(pos, x, chips, stage):
    tokens, depth = x.shape
    tile = min(128, tokens)
    xt = [(sds((depth // 2, tokens), bf16), whole((depth // 2, tokens)))]
    if not stage:
        return x, call(functools.partial(turn_body, tile), "turn_tokens", (pos,), [(x, whole(x.shape))], xt)[0]
    return call(
        functools.partial(stage_body, tile), "stage_tokens", (pos,), [(x, pl.BlockSpec(memory_space=pl.ANY))],
        [(sds(x.shape, bf16), whole(x.shape))] + xt,
        scratch=[pltpu.SemaphoreType.DMA((tokens // tile,))],
    )


def product(pos, x, low, place, rows):
    slot, off, size = place
    return dot(x[:, columns(pos, slot, off, size, rows)], low[:size, :])


def gram_sum(lows, before):
    for low in lows:
        term = dot_rows(low[...], low[...])
        before = term if before is None else before + term
    return before


def forward_body(places, rows, with_gram, first_call, pos, *refs):
    carry = 2 if with_gram else 1
    before = (None, None) if first_call else refs[:carry]
    if not first_call:
        refs = refs[carry:]
    count = len(places)
    lows, xs = refs[:count], refs[count:count + 2]
    outs = refs[count + 2:]
    if with_gram:
        outs[1][...] = gram_sum(lows, None if first_call else before[1][...])
    for h in range(2):
        value = None if first_call else before[0][h]
        for low, place in zip(lows, places):
            term = product(pos, xs[h], low, place, rows)
            value = term if value is None else value + term
        outs[0][h] = value


def forward(pos, carry, pieces, xs, rows, with_gram, after=()):
    tokens = xs[0].shape[0]
    width = pieces[0][0].shape[1]
    ins = [(a, whole(a.shape)) for a in carry]
    ins += [(p[0], whole(p[0].shape)) for p in pieces] + [(x, whole(x.shape)) for x in xs]
    shapes = [(2, tokens, width)] + [(width, width)] * with_gram
    return call(
        functools.partial(forward_body, [p[1:] for p in pieces], rows, with_gram, not carry),
        "forward_decoder" if with_gram else "forward_encoder", (pos,), ins,
        [(sds(shape, f32), whole(shape)) for shape in shapes], after=after,
    )


def split(total):
    hi = total.astype(bf16)
    return hi, (total - hi.astype(f32)).astype(bf16)


def hidden_body(scale, tile, places, rows, pos, acc_in, cw, *refs):
    count = len(places)
    lows, xs = refs[:count], refs[count:count + 2]
    hidden_out, slope_out, counted_out, w_hi, w_lo, acc = refs[count + 2:]
    total = None
    for h in range(2):
        value = acc_in[h]
        for low, place in zip(lows, places):
            value = value + product(pos, xs[h], low, place, rows)
        acc[h] = value
        for t in range(0, acc.shape[1], tile):
            at = pl.ds(t, tile)
            pre = acc[h, at, :]
            sig = 0.5 + 0.5 * jnp.tanh(0.5 * pre)
            hidden = (pre * sig).astype(bf16)
            weight = cw[h, at, :]
            counted = (weight * hidden.astype(f32)).astype(bf16)
            hidden_out[h, at, :] = hidden
            slope_out[h, at, :] = (weight * scale) * (sig * (1.0 + pre * (1.0 - sig)))
            counted_out[h, at, :] = counted
            term = dot_rows(counted, hidden)
            total = term if total is None else total + term
    w_hi[...], w_lo[...] = split(total)


def hidden_rows(pos, acc, cw, pieces, xs, rows, scale):
    shape = acc.shape
    width = shape[2]
    ins = [(a, whole(a.shape)) for a in [acc, cw] + [p[0] for p in pieces] + list(xs)]
    square = (sds((width, width), bf16), whole((width, width)))
    return call(
        functools.partial(hidden_body, scale, min(256, shape[1]), [p[1:] for p in pieces], rows),
        "hidden_units", (pos,), ins,
        [(sds(shape, bf16), whole(shape)), (sds(shape, f32), whole(shape)), (sds(shape, bf16), whole(shape)), square, square],
        scratch=[pltpu.VMEM(shape, f32)],
    )


def slope_body(places, rows, pos, acc_in, gram_in, hidden, slope, *refs):
    count = len(places)
    lows, xs, out = refs[:count], refs[count:count + 2], refs[count + 2]
    g_hi, g_lo = split(gram_sum(lows, gram_in[...]))
    for h in range(2):
        value = acc_in[h]
        for low, place in zip(lows, places):
            value = value + product(pos, xs[h], low, place, rows)
        back = dot(hidden[h], g_hi) + dot(hidden[h], g_lo) - value
        out[h] = (slope[h] * back).astype(bf16)


def slope_rows(pos, acc, gram, hidden, slope, pieces, xs, rows):
    ins = [(a, whole(a.shape)) for a in [acc, gram, hidden, slope] + [p[0] for p in pieces] + list(xs)]
    return call(
        functools.partial(slope_body, [p[1:] for p in pieces], rows), "slope_pre", (pos,), ins,
        [(sds(acc.shape, bf16), whole(acc.shape))],
    )[0]


def token_sum(start, size, xts, weights):
    at = pl.ds(start, size)
    return dot(xts[0][at, :], weights[0]) + dot(xts[1][at, :], weights[1])


def encoder_body(start, xt_own, xt_par, slopes, out):
    out[...] = token_sum(start, out.shape[0], (xt_own, xt_par), slopes).astype(out.dtype)


def decoder_body(scale, start, xt_own, xt_par, counted, w_hi, w_lo, *refs):
    lows, out = refs[:-1], refs[-1]
    off = 0
    for low in lows:
        size = low.shape[0]
        both = token_sum(start + off, size, (xt_own, xt_par), counted)
        value = scale * (dot(low[...], w_hi[...]) + dot(low[...], w_lo[...]) - both)
        out[off:off + size, :] = value.astype(out.dtype)
        off += size


def grad_rows(body, name, size, xt, others, dtype, after=()):
    shape = (size, others[0].shape[2])
    ins = [(a, whole(a.shape)) for a in [*xt, *others]]
    return call(body, name, (), ins, [(sds(shape, dtype), whole(shape))], after=after)[0]


def adam_body(last, count, k, off, n_low, plan, own, *refs):
    got = refs[:count]
    theta, first, second = refs[count:3 + count]
    refs = refs[3 + count:]
    grad = own[...]
    got = [g[...].astype(f32) for g in got]
    while got:
        value = got.pop(0)
        while value.shape[0] < own.shape[0]:
            value = jnp.concatenate([value, got.pop(0)], 0)
        grad = grad + value
    one = beta_one * first[0, 0] + (1.0 - beta_one) * grad
    two = beta_two * second[0, 0] + (1.0 - beta_two) * grad * grad
    old = theta[0, 0]
    if last:
        old = mixed(plan, k, old, refs[0][...])
    new = old - inner_rate * (one / (jnp.sqrt(two) + adam_eps) + decay_rate * old)
    if n_low is not None:
        anchor, before, lows = refs[0], refs[1:1 + n_low], refs[1 + n_low:-3]
        value = mixed(plan, k, new, anchor[off:off + own.shape[0], :]).astype(bf16)
        for b in before:
            lows[0][:off, :] = b[...]
        lows[0][off:, :] = value
    if last and k:
        refs[-4][...] = jnp.zeros_like(refs[-4])
    theta_out, first_out, second_out = refs[-3:]
    theta_out[0, 0] = new
    first_out[0, 0] = one
    second_out[0, 0] = two


def mixed(plan, k, theta, anchor):
    return jnp.where(fragment(plan) == k, mix_share * theta + (1.0 - mix_share) * anchor, theta)


def adam_rows(plan, key, own, got, state, at, new_anc, prev, full, last, lows=None, after=()):
    k, off, cr = key
    i = off // cr
    width = own.shape[1]
    block = (1, 1, cr, width)
    ins = [(g, whole(g.shape)) for g in [own] + got]
    ins += [(s, once(block, lambda g, m: (0, at[0], at[1], 0))) for s in state]
    aliases = {}
    outs = []
    if last:
        ins.append((new_anc, once((cr, width), lambda g, m: (i, 0))))
        if prev is not None:
            for n, p in enumerate(prev):
                aliases[1 + len(ins)] = n + (k == 1)
                ins.append((p, pl.BlockSpec(memory_space=pl.ANY)))
        outs = [(sds(full, f32), once(block, lambda g, m: (0, k, i, 0)))] * 3
        if k == 1:
            outs = [(sds((8, 128), f32), whole((8, 128)))] + outs
    else:
        if lows is not None:
            ins += [(a, whole(a.shape)) for a in [new_anc] + lows]
            shape = (off + cr, width)
            outs = [(sds(shape, bf16), whole(shape))]
        outs += [(sds(block, f32), whole(block))] * 3
    return call(
        functools.partial(adam_body, last, len(got), k, off, None if lows is None else len(lows)), "adam_rows",
        (plan,), ins, outs, aliases=aliases, after=after,
    )


def quarter(pos, m, size):
    where = jnp.bitwise_xor(lax.rem(pos[0], 4), m)
    return pl.ds(pl.multiple_of(where * size, size), size)


def delta_body(pos, plan, anchor, theta, *outs):
    count = plan[pos[0]].astype(f32)
    for m, out in enumerate(outs):
        at = quarter(pos, m, out.shape[0])
        out[...] = (count * (anchor[0, at, :] - theta[0, 0, at, :])).astype(out.dtype)


def outer_start(pos, plan, anchor, weights, after):
    _, rows, width = anchor.shape
    part = (rows // 4, width)
    return call(
        delta_body, "delta_quarters", (pos, plan),
        [
            (anchor, once((1, rows, width), lambda g, p, q: (fragment(q), 0, 0))),
            (weights, once((1, 1, rows, width), lambda g, p, q: (0, fragment(q), 0, 0))),
        ],
        [(sds(part, f32), whole(part))] + [(sds(part, bf16), whole(part))] * 3, after=after,
    )


def add_body(final, plan, *refs):
    total = refs[0][...].astype(f32)
    for r in refs[1:-1]:
        total = total + r[...].astype(f32)
    if final:
        total = total / plan_sum(plan).astype(f32)
    refs[-1][...] = total.astype(bf16)


def outer_add(plan, parts, final, after=()):
    shape = parts[0].shape
    return call(
        functools.partial(add_body, final), "add_quarters", (plan,), [(a, whole(shape)) for a in parts],
        [(sds(shape, bf16), whole(shape))], after=after,
    )[0]


def outer_update(frag, at, anchor, momentum, grad):
    mom = outer_mu * momentum[frag, at, :] + grad
    return anchor[frag, at, :] - outer_rate * (grad + outer_mu * mom), mom


def new_anchor_body(pos, plan, anchor, momentum, *refs):
    for m, piece in enumerate(refs[:4]):
        at = quarter(pos, m, piece.shape[0])
        refs[4][at, :] = outer_update(0, at, anchor, momentum, piece[...].astype(f32))[0]


def outer_anchor(pos, plan, anchor, momentum, quarters, after):
    _, rows, width = anchor.shape
    part = once((1, rows, width), lambda g, p, q: (fragment(q), 0, 0))
    return call(
        new_anchor_body, "new_anchor", (pos, plan),
        [(anchor, part), (momentum, part)] + [(a, whole(a.shape)) for a in quarters],
        [(sds((rows, width), f32), whole((rows, width)))], after=after,
    )[0]


def mix_body(k, count, plan, new_anc, *refs):
    thetas, low, parts = refs[:count], refs[count], refs[count + 1:]
    off = 0
    for theta, part in zip(thetas, parts):
        size = part.shape[0]
        value = mixed(plan, k, theta[0, 0], new_anc[off:off + size, :]).astype(bf16)
        low[off:off + size, :] = value
        part[...] = value
        off += size


def mix_rows(plan, new_anc, k, thetas, after):
    rows, width = new_anc.shape
    shapes = [(rows, width)] + [theta.shape[2:] for theta in thetas]
    return call(
        functools.partial(mix_body, k, len(thetas)), "mix_rows", (plan,),
        [(a, whole(a.shape)) for a in [new_anc, *thetas]],
        [(sds(shape, bf16), whole(shape)) for shape in shapes], after=after,
    )


def outer_body(pos, plan, anchor, momentum, *refs):
    quarters = refs[:4]
    anchor_out, momentum_out, token = refs[4:]
    token[...] = jnp.zeros_like(token)
    frag = fragment(plan)
    anchor_out[...] = anchor[...]
    momentum_out[...] = momentum[...]
    for m, piece in enumerate(quarters):
        at = quarter(pos, m, piece.shape[0])
        anc, mom = outer_update(frag, at, anchor, momentum, piece[...].astype(f32))
        anchor_out[frag, at, :] = anc
        momentum_out[frag, at, :] = mom


def outer_end(pos, plan, anchor, momentum, quarters, after):
    return call(
        outer_body, "outer_step", (pos, plan),
        [(a, whole(a.shape)) for a in [anchor, momentum] + quarters],
        [(sds(anchor.shape, f32), whole(anchor.shape))] * 2 + [(sds((8, 128), f32), whole((8, 128)))], after=after,
    )


def local(n_rep, n_fsdp, inputs, kinds, weights, first_moment, second_moment, anchor, momentum, plan):
    tokens = inputs.shape[0]
    rows, width = weights.shape[2:]
    chips = n_fsdp // 2
    scale = 1.0 / math.sqrt(tokens * n_fsdp)
    most = rows - rows // 4 if rows >= 1024 else rows
    sizes = [most] + [rows - most] * (most < rows)
    starts = [sum(sizes[:n]) for n in range(len(sizes))]
    others = range(1, chips)

    partner = [(f, f ^ 1) for f in range(n_fsdp)]
    to_partner = lambda a: lax.ppermute(a, "fsdp", partner)
    fetch = lambda a, s: lax.ppermute(
        a, "fsdp", [(((f // 2 + s) % chips) * 2 + f % 2, f) for f in range(n_fsdp)])
    give = lambda a, s: lax.ppermute(
        a, "fsdp", [(f, ((f // 2 + s) % chips) * 2 + f % 2) for f in range(n_fsdp)])
    across = lambda a, bit: lax.ppermute(a, "replica", [(r, r ^ bit) for r in range(n_rep)])

    chip = lax.axis_index("fsdp") // 2
    core = lax.axis_index("fsdp") % 2
    at = [((chip + s) % chips) * 2 for s in range(chips)]
    pos = jnp.stack([lax.axis_index("replica")] + [a + core for a in at] + [a + 1 - core for a in at]).astype(jnp.int32)

    enc, dec, *dec_parts = cast_rows(weights, sizes, pos)
    enc_parts = [enc]
    x_par = to_partner(inputs)
    quarters = outer_start(pos, plan, anchor, weights, [enc])
    xs, xt = zip(*[turn(pos, x, chips, stage) for x, stage in ((inputs, False), (x_par, True))])
    own = outer_add(plan, [quarters[0]] + [across(quarters[m], m) for m in range(1, 4)], n_rep == 4, xt)

    half, rest = (rows // 2, rows // 4) if rows >= 1024 else (rows, rows)
    dec_blocks = [(1, off, size) for off, size in zip(starts, sizes)]
    enc_blocks = [(0, 0, half)] + [(0, off, rest) for off in range(half, rows, rest)]
    blocks = dec_blocks + enc_blocks
    state = {key: (weights, first_moment, second_moment) for key in blocks}
    state_at = {(k, off, size): (k, off // size) for k, off, size in blocks}
    new_anc = None
    for step in range(INNER):
        last = step == INNER - 1
        enc_far = [{s: fetch(part, s) for s in others} for part in enc_parts]
        dec_far = [{s: fetch(part, s) for s in others} for part in dec_parts]
        enc_near, dec_near = to_partner(enc), to_partner(dec)

        def take(far, off, after, *riders):
            pieces = []
            for s in others:
                cuts = max(1, far[s].shape[0] // 384)
                cut = far[s].shape[0] // cuts
                got = relay(far[s], cuts, after, *riders)
                pieces += [(p, 1 + s, off + n * cut, cut) for n, p in enumerate(got)]
            return pieces, [(to_partner(p), slot + chips, o, size) for p, slot, o, size in pieces]

        carry = forward(pos, [], [(enc, 1, 0, rows), (enc_near, 1 + chips, 0, rows)], xs, rows, False)
        ready = [own, *xt] if step == 0 else [token]
        pending = []
        off = 0
        for part in enc_far:
            pieces, handed = take(part, off, [*carry, *ready], *([kinds] if step == 0 else []))
            carry = forward(pos, carry, pending + pieces, xs, rows, False)
            pending = handed
            off += part[1].shape[0]
        if step == 0:
            cw = weigh(kinds, pending[-1][0], tokens)
        hidden, slope, counted, w_hi, w_lo = hidden_rows(pos, carry[0], cw, pending, xs, rows, scale)
        dec_grad = lambda start, size, lows, dtype, after: grad_rows(
            functools.partial(decoder_body, scale, start), "decoder_grad", size, xt,
            [counted, w_hi, w_lo, *lows], dtype, after)
        enc_grad = lambda s, off, size, dtype, after: grad_rows(
            functools.partial(encoder_body, s * rows + off), "encoder_grad", size, xt, [slopes], dtype, after)
        sent = []
        got = {key: [] for key in blocks}
        part, pending = [], []
        for n, far in enumerate(dec_far):
            pieces, handed = take(far, starts[n], [counted] + sent[-1:])
            part += pieces
            pending += handed
            for s in others:
                rows_in = [p[0] for p in pieces if p[1] == 1 + s]
                sent.append(dec_grad(s * rows + starts[n], sizes[n], rows_in, bf16, sent[-1:]))
                got[dec_blocks[n]].append(give(sent[-1], s))
        back = [g for key in dec_blocks for g in got[key]]

        carry = forward(
            pos, [], [(dec, 1, 0, rows), (dec_near, 1 + chips, 0, rows)] + part, xs, rows, True, sent[-1:])
        slopes = slope_rows(pos, *carry, hidden, slope, pending, xs, rows)
        adam = lambda key, prev, *more, after=(): adam_rows(
            plan, key, mine[key], got[key], state[key], state_at[key], new_anc, prev, weights.shape, last,
            *more, after=after)
        prev = None
        mine = {}
        own_dec = lambda n, after: dec_grad(starts[n], sizes[n], [dec_parts[n]], f32, after)
        hold = []
        for n, key in enumerate(enc_blocks):
            for s in others:
                sent.append(enc_grad(s, *key[1:], bf16, sent[-1:] + hold))
                got[key].append(give(sent[-1], s))
            if n == 0 and step == 0:
                bit = 4
                while bit < n_rep:
                    own = outer_add(plan, [own, across(own, bit)], 2 * bit == n_rep, sent[-1:])
                    bit *= 2
                sent.append(own)
            hold = back if n == 0 and not last else []
            if n == (0 if last else len(enc_blocks) - 1):
                for other in enc_blocks:
                    mine[other] = enc_grad(0, *other[1:], f32, sent[-1:])
                    sent.append(mine[other])
            if last:
                for m, other in enumerate(dec_blocks):
                    if n == 0:
                        mine[other] = own_dec(m, sent[-1:])
                        sent.append(mine[other])
                for other in dec_blocks[n:n + 1]:
                    token, *prev = adam(other, prev, after=sent[-1:])
                    sent.append(token)

        if not last:
            quarters = [own] + [across(own, m) for m in range(1, 4)]
            new_anc = outer_anchor(pos, plan, anchor, momentum, quarters, sent[-1:])
        new_state, lows = {}, []
        if last:
            for key in enc_blocks:
                prev = adam(key, prev)
        else:
            for key in enc_blocks:
                enc, *new_state[key] = adam(key, None, lows)
                lows = [enc]
            enc_parts = [enc]
            for n, key in enumerate(dec_blocks):
                mine[key] = own_dec(n, [enc])
                new_state[key] = adam(key, None, after=[enc])
            dec, *dec_parts = mix_rows(plan, new_anc, 1, [new_state[key][0] for key in dec_blocks], [enc])
            anchor_out, momentum_out, token = outer_end(pos, plan, anchor, momentum, quarters, [dec])
            state, state_at = new_state, {key: (0, 0) for key in blocks}
    return (*prev, anchor_out, momentum_out)


def solution(mesh):
    return jax.shard_map(
        functools.partial(local, mesh.shape["replica"], mesh.shape["fsdp"]),
        mesh=mesh,
        in_specs=(
            P(("replica", "fsdp"), None),
            P(("replica", "fsdp")),
            P("replica", None, "fsdp", None),
            P("replica", None, "fsdp", None),
            P("replica", None, "fsdp", None),
            P(None, "fsdp", None),
            P(None, "fsdp", None),
            P(),
        ),
        out_specs=(
            P("replica", None, "fsdp", None),
            P("replica", None, "fsdp", None),
            P("replica", None, "fsdp", None),
            P(None, "fsdp", None),
            P(None, "fsdp", None),
        ),
        check_vma=False,
    )
```

```python
import functools
import math

import jax
import jax.numpy as jnp
from jax import lax
from jax.experimental import pallas as pl
from jax.experimental.pallas import tpu as pltpu
from jax.sharding import PartitionSpec as P

INNER = 2

inner_rate = 0.003
beta_one = 0.9
beta_two = 0.95
adam_eps = 1e-08
decay_rate = 0.1
outer_rate = 0.7
outer_mu = 0.9
mix_share = 0.5

bf16 = jnp.bfloat16
f32 = jnp.float32
VMEM_LIMIT = 10 * 1024 * 1024


def token_weight(kinds):
    return jnp.where(kinds == 2, 1.0, jnp.where(kinds == 1, 0.25, 0.0)).astype(f32)


def dot(a, b):
    return jnp.dot(a, b, preferred_element_type=f32)


def dot_rows(a, b):
    return lax.dot_general(a, b, (((0,), (0,)), ((), ())), preferred_element_type=f32)


def once(shape, index):
    return pl.BlockSpec(shape, index, pipeline_mode=pl.Buffered(1))


def whole(shape):
    return once(shape, lambda *_: (0,) * len(shape))


def sds(shape, dtype):
    return jax.ShapeDtypeStruct(shape, dtype)


def call(body, name, meta, ins, outs, grid=(1,), scratch=(), aliases=None, flops=0, after=()):
    arrays = [a for a, _ in ins] + list(after)
    n_in = len(meta) + len(ins)
    moved = sum(math.prod(o.shape) * o.dtype.itemsize for o, _ in outs)
    moved += sum(math.prod(s.block_shape or a.shape) * a.dtype.itemsize for a, s in ins)

    def run(*refs):
        body(*refs[:n_in], *refs[n_in + len(after):])

    return pl.pallas_call(
        run,
        name=name,
        out_shape=[o for o, _ in outs],
        grid_spec=pltpu.PrefetchScalarGridSpec(
            num_scalar_prefetch=len(meta),
            grid=grid,
            in_specs=[s for _, s in ins] + [pl.BlockSpec(memory_space=pl.ANY)] * len(after),
            out_specs=[s for _, s in outs],
            scratch_shapes=list(scratch),
        ),
        input_output_aliases=aliases or {},
        compiler_params=pltpu.CompilerParams(vmem_limit_bytes=VMEM_LIMIT),
        cost_estimate=pl.CostEstimate(flops=flops, bytes_accessed=moved, transcendentals=0),
    )(*meta, *arrays)


def plan_sum(plan):
    total = plan[0]
    for r in range(1, plan.shape[0]):
        total = total + plan[r]
    return total


def fragment(plan):
    return lax.rem(plan_sum(plan), 2)


EXTRA = 16


def cast_body(sizes, theta, enc, dec, *parts):
    enc[...] = theta[0, 0].astype(bf16)
    value = theta[0, 1].astype(bf16)
    dec[...] = value
    put_parts(value, sizes, parts)


def put_parts(value, sizes, parts):
    off = 0
    for size, part in zip(sizes, parts):
        part[...] = value[off:off + size, :]
        off += size


def cast_rows(weights, sizes, pos):
    _, _, rows, width = weights.shape
    shapes = [(rows, width)] * 2 + [(size, width) for size in sizes]
    return call(
        functools.partial(cast_body, sizes), "cast_rows", (), [(weights, whole(weights.shape))],
        [(sds(shape, bf16), whole(shape)) for shape in shapes], after=[pos],
    )


def weight_rows(kinds, wide):
    rows = [token_weight(kinds[j:j + wide].reshape(1, wide)) for j in range(0, kinds.shape[0], wide)]
    return jnp.concatenate(rows + [jnp.zeros((EXTRA - len(rows), wide), f32)], 0)


def weigh_body(kinds, other, out):
    wide = other.shape[1]
    lanes = kinds.shape[0] // wide
    own = weight_rows(kinds, wide)
    for h, rows in enumerate((own, other[other.shape[0] - EXTRA:, :].astype(f32))):
        turned = rows.T
        for j in range(lanes):
            out[h, j * wide:(j + 1) * wide, :] = turned[:, j:j + 1]


def weigh(lanes, other, tokens):
    return call(
        weigh_body, "weigh_tokens", (), [(a, whole(a.shape)) for a in (lanes, other)],
        [(sds((2, tokens, 1), f32), whole((2, tokens, 1)))],
    )[0]


def relay_body(cut, x, *refs):
    outs = refs
    if refs[0].dtype != bf16:
        kinds, outs = refs[0], refs[1:]
        outs[-1][cut:, :] = weight_rows(kinds, x.shape[1]).astype(bf16)
    for n, out in enumerate(outs):
        out[:cut, :] = x[n * cut:(n + 1) * cut, :]


def relay(x, cuts, after, lanes=None):
    rows, width = x.shape
    cut = rows // cuts
    shapes = [(cut, width)] * (cuts - 1) + [(cut + (0 if lanes is None else EXTRA), width)]
    ins = [x] if lanes is None else [x, lanes]
    return call(
        functools.partial(relay_body, cut), "relay_rows", (), [(a, whole(a.shape)) for a in ins],
        [(sds(shape, x.dtype), whole(shape)) for shape in shapes], after=after,
    )


def turn_block(pos, x, xt, t, tile):
    rows = x.shape[1] // (pos.shape[0] - 1)
    for s in range(xt.shape[0] // rows):
        xt[s * rows:(s + 1) * rows, t:t + tile] = x[t:t + tile, columns(pos, 1 + s, 0, rows, rows)].T


def columns(pos, slot, off, size, rows):
    return pl.ds(pl.multiple_of(pos[slot] * rows + off, 128), size)


def turn_body(tile, pos, x, xt):
    for t in range(0, x.shape[0], tile):
        turn_block(pos, x, xt, t, tile)


def stage_body(tile, pos, x, held, xt, sems):
    copies = []
    for n, t in enumerate(range(0, x.shape[0], tile)):
        copy = pltpu.make_async_copy(x.at[pl.ds(t, tile), :], held.at[pl.ds(t, tile), :], sems.at[n])
        copy.start()
        copies.append(copy)
    for n, t in enumerate(range(0, x.shape[0], tile)):
        copies[n].wait()
        turn_block(pos, held, xt, t, tile)


def turn(pos, x, chips, stage):
    tokens, depth = x.shape
    tile = min(128, tokens)
    xt = [(sds((depth // 2, tokens), bf16), whole((depth // 2, tokens)))]
    if not stage:
        return x, call(functools.partial(turn_body, tile), "turn_tokens", (pos,), [(x, whole(x.shape))], xt)[0]
    return call(
        functools.partial(stage_body, tile), "stage_tokens", (pos,), [(x, pl.BlockSpec(memory_space=pl.ANY))],
        [(sds(x.shape, bf16), whole(x.shape))] + xt,
        scratch=[pltpu.SemaphoreType.DMA((tokens // tile,))],
    )


def product(pos, x, low, place, rows):
    slot, off, size = place
    return dot(x[:, columns(pos, slot, off, size, rows)], low[:size, :])


def gram_sum(lows, before):
    for low in lows:
        term = dot_rows(low[...], low[...])
        before = term if before is None else before + term
    return before


def forward_body(places, rows, with_gram, first_call, pos, *refs):
    carry = 2 if with_gram else 1
    before = (None, None) if first_call else refs[:carry]
    if not first_call:
        refs = refs[carry:]
    count = len(places)
    lows, xs = refs[:count], refs[count:count + 2]
    outs = refs[count + 2:]
    if with_gram:
        outs[1][...] = gram_sum(lows, None if first_call else before[1][...])
    for h in range(2):
        value = None if first_call else before[0][h]
        for low, place in zip(lows, places):
            term = product(pos, xs[h], low, place, rows)
            value = term if value is None else value + term
        outs[0][h] = value


def forward(pos, carry, pieces, xs, rows, with_gram, after=()):
    tokens = xs[0].shape[0]
    width = pieces[0][0].shape[1]
    ins = [(a, whole(a.shape)) for a in carry]
    ins += [(p[0], whole(p[0].shape)) for p in pieces] + [(x, whole(x.shape)) for x in xs]
    shapes = [(2, tokens, width)] + [(width, width)] * with_gram
    return call(
        functools.partial(forward_body, [p[1:] for p in pieces], rows, with_gram, not carry),
        "forward_decoder" if with_gram else "forward_encoder", (pos,), ins,
        [(sds(shape, f32), whole(shape)) for shape in shapes], after=after,
    )


def split(total):
    hi = total.astype(bf16)
    return hi, (total - hi.astype(f32)).astype(bf16)


def hidden_body(scale, tile, places, rows, pos, acc_in, cw, *refs):
    count = len(places)
    lows, xs = refs[:count], refs[count:count + 2]
    hidden_out, slope_out, counted_out, w_hi, w_lo, acc = refs[count + 2:]
    total = None
    for h in range(2):
        value = acc_in[h]
        for low, place in zip(lows, places):
            value = value + product(pos, xs[h], low, place, rows)
        acc[h] = value
        for t in range(0, acc.shape[1], tile):
            at = pl.ds(t, tile)
            pre = acc[h, at, :]
            sig = 0.5 + 0.5 * jnp.tanh(0.5 * pre)
            hidden = (pre * sig).astype(bf16)
            weight = cw[h, at, :]
            counted = (weight * hidden.astype(f32)).astype(bf16)
            hidden_out[h, at, :] = hidden
            slope_out[h, at, :] = (weight * scale) * (sig * (1.0 + pre * (1.0 - sig)))
            counted_out[h, at, :] = counted
            term = dot_rows(counted, hidden)
            total = term if total is None else total + term
    w_hi[...], w_lo[...] = split(total)


def hidden_rows(pos, acc, cw, pieces, xs, rows, scale):
    shape = acc.shape
    width = shape[2]
    ins = [(a, whole(a.shape)) for a in [acc, cw] + [p[0] for p in pieces] + list(xs)]
    square = (sds((width, width), bf16), whole((width, width)))
    return call(
        functools.partial(hidden_body, scale, min(256, shape[1]), [p[1:] for p in pieces], rows),
        "hidden_units", (pos,), ins,
        [(sds(shape, bf16), whole(shape)), (sds(shape, f32), whole(shape)), (sds(shape, bf16), whole(shape)), square, square],
        scratch=[pltpu.VMEM(shape, f32)],
    )


def slope_body(places, rows, pos, acc_in, gram_in, hidden, slope, *refs):
    count = len(places)
    lows, xs, out = refs[:count], refs[count:count + 2], refs[count + 2]
    g_hi, g_lo = split(gram_sum(lows, gram_in[...]))
    for h in range(2):
        value = acc_in[h]
        for low, place in zip(lows, places):
            value = value + product(pos, xs[h], low, place, rows)
        back = dot(hidden[h], g_hi) + dot(hidden[h], g_lo) - value
        out[h] = (slope[h] * back).astype(bf16)


def slope_rows(pos, acc, gram, hidden, slope, pieces, xs, rows):
    ins = [(a, whole(a.shape)) for a in [acc, gram, hidden, slope] + [p[0] for p in pieces] + list(xs)]
    return call(
        functools.partial(slope_body, [p[1:] for p in pieces], rows), "slope_pre", (pos,), ins,
        [(sds(acc.shape, bf16), whole(acc.shape))],
    )[0]


def token_sum(start, size, xts, weights):
    at = pl.ds(start, size)
    return dot(xts[0][at, :], weights[0]) + dot(xts[1][at, :], weights[1])


def encoder_body(start, xt_own, xt_par, slopes, out):
    out[...] = token_sum(start, out.shape[0], (xt_own, xt_par), slopes).astype(out.dtype)


def decoder_body(scale, start, pieces, front, xt_own, xt_par, counted, w_hi, w_lo, *refs):
    lows, more, out = refs[:pieces], refs[pieces:-1], refs[-1]
    off = 0
    got = more
    if front:
        off = more[0].shape[0]
        out[:off, :] = more[0][...]
        got = ()
    for low in lows:
        size = low.shape[0]
        both = token_sum(start + off, size, (xt_own, xt_par), counted)
        value = scale * (dot(low[...], w_hi[...]) + dot(low[...], w_lo[...]) - both)
        for g in got:
            value = value + g[off:off + size, :].astype(f32)
        out[off:off + size, :] = value.astype(out.dtype)
        off += size


def grad_rows(body, name, size, xt, others, dtype, after=()):
    shape = (size, others[0].shape[2])
    ins = [(a, whole(a.shape)) for a in [*xt, *others]]
    return call(body, name, (), ins, [(sds(shape, dtype), whole(shape))], after=after)[0]


def adam_body(last, count, k, off, n_low, plan, own, *refs):
    got = refs[:count]
    theta, first, second = refs[count:3 + count]
    refs = refs[3 + count:]
    grad = own[...]
    got = [g[...].astype(f32) for g in got]
    while got:
        value = got.pop(0)
        while value.shape[0] < own.shape[0]:
            value = jnp.concatenate([value, got.pop(0)], 0)
        grad = grad + value
    one = beta_one * first[0, 0] + (1.0 - beta_one) * grad
    two = beta_two * second[0, 0] + (1.0 - beta_two) * grad * grad
    old = theta[0, 0]
    if last:
        old = mixed(plan, k, old, refs[0][...])
    new = old - inner_rate * (one / (jnp.sqrt(two) + adam_eps) + decay_rate * old)
    if n_low is not None:
        anchor, before, lows = refs[0], refs[1:1 + n_low], refs[1 + n_low:-3]
        value = mixed(plan, k, new, anchor[off:off + own.shape[0], :]).astype(bf16)
        for b in before:
            lows[0][:off, :] = b[...]
        lows[0][off:, :] = value
    if last and k:
        refs[-4][...] = jnp.zeros_like(refs[-4])
    theta_out, first_out, second_out = refs[-3:]
    theta_out[0, 0] = new
    first_out[0, 0] = one
    second_out[0, 0] = two


def mixed(plan, k, theta, anchor):
    return jnp.where(fragment(plan) == k, mix_share * theta + (1.0 - mix_share) * anchor, theta)


def adam_rows(plan, key, own, got, state, at, new_anc, prev, full, last, lows=None, after=()):
    k, off, cr = key
    i = off // cr
    width = own.shape[1]
    block = (1, 1, cr, width)
    ins = [(g, whole(g.shape)) for g in [own] + got]
    ins += [(s, once(block, lambda g, m: (0, at[0], at[1], 0))) for s in state]
    aliases = {}
    outs = []
    if last:
        ins.append((new_anc, once((cr, width), lambda g, m: (i, 0))))
        if prev is not None:
            for n, p in enumerate(prev):
                aliases[1 + len(ins)] = n
                ins.append((p, pl.BlockSpec(memory_space=pl.ANY)))
        outs = [(sds(full, f32), once(block, lambda g, m: (0, k, i, 0)))] * 3
        if prev is None:
            outs = [(sds((8, 128), f32), whole((8, 128)))] + outs
    else:
        if lows is not None:
            ins += [(a, whole(a.shape)) for a in [new_anc] + lows]
            shape = (off + cr, width)
            outs = [(sds(shape, bf16), whole(shape))]
        outs += [(sds(block, f32), whole(block))] * 3
    return call(
        functools.partial(adam_body, last, len(got), k, off, None if lows is None else len(lows)), "adam_rows",
        (plan,), ins, outs, aliases=aliases, after=after,
    )


def quarter(pos, m, size):
    where = jnp.bitwise_xor(lax.rem(pos[0], 4), m)
    return pl.ds(pl.multiple_of(where * size, size), size)


def delta_body(pos, plan, anchor, theta, *outs):
    count = plan[pos[0]].astype(f32)
    for m, out in enumerate(outs):
        at = quarter(pos, m, out.shape[0])
        out[...] = (count * (anchor[0, at, :] - theta[0, 0, at, :])).astype(out.dtype)


def outer_start(pos, plan, anchor, weights, after):
    _, rows, width = anchor.shape
    part = (rows // 4, width)
    return call(
        delta_body, "delta_quarters", (pos, plan),
        [
            (anchor, once((1, rows, width), lambda g, p, q: (fragment(q), 0, 0))),
            (weights, once((1, 1, rows, width), lambda g, p, q: (0, fragment(q), 0, 0))),
        ],
        [(sds(part, f32), whole(part))] + [(sds(part, bf16), whole(part))] * 3, after=after,
    )


def add_body(final, plan, *refs):
    total = refs[0][...].astype(f32)
    for r in refs[1:-1]:
        total = total + r[...].astype(f32)
    if final:
        total = total / plan_sum(plan).astype(f32)
    refs[-1][...] = total.astype(bf16)


def outer_add(plan, parts, final, after=()):
    shape = parts[0].shape
    return call(
        functools.partial(add_body, final), "add_quarters", (plan,), [(a, whole(shape)) for a in parts],
        [(sds(shape, bf16), whole(shape))], after=after,
    )[0]


def outer_update(frag, at, anchor, momentum, grad):
    mom = outer_mu * momentum[frag, at, :] + grad
    return anchor[frag, at, :] - outer_rate * (grad + outer_mu * mom), mom


def new_anchor_body(pos, plan, anchor, momentum, *refs):
    for m, piece in enumerate(refs[:4]):
        at = quarter(pos, m, piece.shape[0])
        refs[4][at, :] = outer_update(0, at, anchor, momentum, piece[...].astype(f32))[0]


def outer_anchor(pos, plan, anchor, momentum, quarters, after):
    _, rows, width = anchor.shape
    part = once((1, rows, width), lambda g, p, q: (fragment(q), 0, 0))
    return call(
        new_anchor_body, "new_anchor", (pos, plan),
        [(anchor, part), (momentum, part)] + [(a, whole(a.shape)) for a in quarters],
        [(sds((rows, width), f32), whole((rows, width)))], after=after,
    )[0]


def mix_body(k, sizes, plan, new_anc, theta, low, *parts):
    value = mixed(plan, k, theta[0, 0], new_anc[...]).astype(bf16)
    low[...] = value
    put_parts(value, sizes, parts)


def mix_rows(plan, new_anc, k, theta, sizes, after):
    rows, width = new_anc.shape
    shapes = [(rows, width)] + [(size, width) for size in sizes]
    return call(
        functools.partial(mix_body, k, sizes), "mix_rows", (plan,), [(a, whole(a.shape)) for a in (new_anc, theta)],
        [(sds(shape, bf16), whole(shape)) for shape in shapes], after=after,
    )


def outer_body(pos, plan, anchor, momentum, *refs):
    quarters = refs[:4]
    anchor_out, momentum_out, token = refs[4:]
    token[...] = jnp.zeros_like(token)
    frag = fragment(plan)
    anchor_out[...] = anchor[...]
    momentum_out[...] = momentum[...]
    for m, piece in enumerate(quarters):
        at = quarter(pos, m, piece.shape[0])
        anc, mom = outer_update(frag, at, anchor, momentum, piece[...].astype(f32))
        anchor_out[frag, at, :] = anc
        momentum_out[frag, at, :] = mom


def outer_end(pos, plan, anchor, momentum, quarters, after):
    return call(
        outer_body, "outer_step", (pos, plan),
        [(a, whole(a.shape)) for a in [anchor, momentum] + quarters],
        [(sds(anchor.shape, f32), whole(anchor.shape))] * 2 + [(sds((8, 128), f32), whole((8, 128)))], after=after,
    )


def local(n_rep, n_fsdp, inputs, kinds, weights, first_moment, second_moment, anchor, momentum, plan):
    tokens = inputs.shape[0]
    rows, width = weights.shape[2:]
    chips = n_fsdp // 2
    scale = 1.0 / math.sqrt(tokens * n_fsdp)
    most = rows - rows // 4 if rows >= 1024 else rows
    sizes = [most] + [rows - most] * (most < rows)
    starts = [sum(sizes[:n]) for n in range(len(sizes))]
    others = range(1, chips)

    partner = [(f, f ^ 1) for f in range(n_fsdp)]
    to_partner = lambda a: lax.ppermute(a, "fsdp", partner)
    fetch = lambda a, s: lax.ppermute(
        a, "fsdp", [(((f // 2 + s) % chips) * 2 + f % 2, f) for f in range(n_fsdp)])
    give = lambda a, s: lax.ppermute(
        a, "fsdp", [(f, ((f // 2 + s) % chips) * 2 + f % 2) for f in range(n_fsdp)])
    across = lambda a, bit: lax.ppermute(a, "replica", [(r, r ^ bit) for r in range(n_rep)])

    chip = lax.axis_index("fsdp") // 2
    core = lax.axis_index("fsdp") % 2
    at = [((chip + s) % chips) * 2 for s in range(chips)]
    pos = jnp.stack([lax.axis_index("replica")] + [a + core for a in at] + [a + 1 - core for a in at]).astype(jnp.int32)

    enc, dec, *dec_parts = cast_rows(weights, sizes, pos)
    enc_parts = [enc]
    x_par = to_partner(inputs)
    quarters = outer_start(pos, plan, anchor, weights, [enc])
    xs, xt = zip(*[turn(pos, x, chips, stage) for x, stage in ((inputs, False), (x_par, True))])
    own = outer_add(plan, [quarters[0]] + [across(quarters[m], m) for m in range(1, 4)], n_rep == 4, xt)

    half, rest = (rows // 2, rows // 4) if rows >= 1024 else (rows, rows)
    blocks = [(1, 0, rows), (0, 0, half)] + [(0, off, rest) for off in range(half, rows, rest)]
    state = {key: (weights, first_moment, second_moment) for key in blocks}
    state_at = {(k, off, size): (k, off // size) for k, off, size in blocks}
    new_anc = None
    for step in range(INNER):
        last = step == INNER - 1
        enc_far = [{s: fetch(part, s) for s in others} for part in enc_parts]
        dec_far = [{s: fetch(part, s) for s in others} for part in dec_parts]
        enc_near, dec_near = to_partner(enc), to_partner(dec)

        def take(far, off, after, *riders):
            pieces = []
            for s in others:
                cuts = max(1, far[s].shape[0] // 384)
                cut = far[s].shape[0] // cuts
                got = relay(far[s], cuts, after, *riders)
                pieces += [(p, 1 + s, off + n * cut, cut) for n, p in enumerate(got)]
            return pieces, [(to_partner(p), slot + chips, o, size) for p, slot, o, size in pieces]

        carry = forward(pos, [], [(enc, 1, 0, rows), (enc_near, 1 + chips, 0, rows)], xs, rows, False)
        ready = [own, *xt] if step == 0 else [token]
        pending = []
        off = 0
        for part in enc_far:
            pieces, handed = take(part, off, [*carry, *ready], *([kinds] if step == 0 else []))
            carry = forward(pos, carry, pending + pieces, xs, rows, False)
            pending = handed
            off += part[1].shape[0]
        if step == 0:
            cw = weigh(kinds, pending[-1][0], tokens)
        hidden, slope, counted, w_hi, w_lo = hidden_rows(pos, carry[0], cw, pending, xs, rows, scale)
        dec_grad = lambda s, size, lows, more, front, dtype, after, off=0: grad_rows(
            functools.partial(decoder_body, scale, s * rows + off, len(lows), front), "decoder_grad", size, xt,
            [counted, w_hi, w_lo, *lows, *more], dtype, after)
        enc_grad = lambda s, off, size, dtype, after: grad_rows(
            functools.partial(encoder_body, s * rows + off), "encoder_grad", size, xt, [slopes], dtype, after)
        sent = []
        got = {key: [] for key in blocks}
        part, pending = [], []
        whole_grad = {s: [] for s in others}
        for n, far in enumerate(dec_far):
            pieces, handed = take(far, starts[n], [counted] + sent[-1:])
            part += pieces
            pending += handed
            for s in others:
                rows_in = [p[0] for p in pieces if p[1] == 1 + s]
                if last:
                    whole_grad[s] = [dec_grad(
                        s, starts[n] + sizes[n], rows_in, whole_grad[s], n > 0, bf16, sent[-1:])]
                else:
                    whole_grad[s].append(dec_grad(s, sizes[n], rows_in, [], False, bf16, sent[-1:], starts[n]))
                sent.append(whole_grad[s][-1])
        back = [give(g, s) for s in others for g in whole_grad[s]]

        carry = forward(
            pos, [], [(dec, 1, 0, rows), (dec_near, 1 + chips, 0, rows)] + part, xs, rows, True, sent[-1:])
        slopes = slope_rows(pos, *carry, hidden, slope, pending, xs, rows)
        adam = lambda key, prev, *more, after=(): adam_rows(
            plan, key, mine[key], got[key], state[key], state_at[key], new_anc, prev, weights.shape, last,
            *more, after=after)
        prev = None
        mine = {}
        own_dec = lambda after: dec_grad(0, rows, dec_parts, [], False, f32, after)
        for n, key in enumerate(blocks[1:]):
            hold = back if n == 1 else []
            for s in others:
                sent.append(enc_grad(s, *key[1:], bf16, sent[-1:] + hold))
                got[key].append(give(sent[-1], s))
            if n == 0 and step == 0:
                bit = 4
                while bit < n_rep:
                    own = outer_add(plan, [own, across(own, bit)], 2 * bit == n_rep, sent[-1:])
                    bit *= 2
                sent.append(own)
            if n == (0 if last else len(blocks) - 2):
                for other in blocks[1:]:
                    mine[other] = enc_grad(0, *other[1:], f32, sent[-1:])
                    sent.append(mine[other])
                if last:
                    mine[blocks[0]] = own_dec(sent[-1:])
                    sent.append(mine[blocks[0]])
        got[blocks[0]] = back
        if last:
            token, *prev = adam(blocks[0], None, after=sent[-1:])

        if not last:
            quarters = [own] + [across(own, m) for m in range(1, 4)]
            new_anc = outer_anchor(pos, plan, anchor, momentum, quarters, sent[-1:])
        new_state, lows = {}, []
        if last:
            for key in blocks[1:]:
                prev = adam(key, prev)
        else:
            for key in blocks[1:]:
                enc, *new_state[key] = adam(key, None, lows)
                lows = [enc]
            enc_parts = [enc]
            mine[blocks[0]] = own_dec([enc])
            new_state[blocks[0]] = adam(blocks[0], None, after=[enc])
            dec, *dec_parts = mix_rows(plan, new_anc, 1, new_state[blocks[0]][0], sizes, [enc])
            anchor_out, momentum_out, token = outer_end(pos, plan, anchor, momentum, quarters, [dec])
            state, state_at = new_state, {key: (0, 0) for key in blocks}
    return (*prev, anchor_out, momentum_out)


def solution(mesh):
    return jax.shard_map(
        functools.partial(local, mesh.shape["replica"], mesh.shape["fsdp"]),
        mesh=mesh,
        in_specs=(
            P(("replica", "fsdp"), None),
            P(("replica", "fsdp")),
            P("replica", None, "fsdp", None),
            P("replica", None, "fsdp", None),
            P("replica", None, "fsdp", None),
            P(None, "fsdp", None),
            P(None, "fsdp", None),
            P(),
        ),
        out_specs=(
            P("replica", None, "fsdp", None),
            P("replica", None, "fsdp", None),
            P("replica", None, "fsdp", None),
            P(None, "fsdp", None),
            P(None, "fsdp", None),
        ),
        check_vma=False,
    )
```
